32 devices in a mesh: seq: 4 (over y, x), fsdp: 8 (over z, core).
Axes of the slice: x: 2, y: 2, z: 4, core: 2. Of those that a mesh axis runs over, the one named last changes fastest.
Arguments:
- layer_input: bfloat16 [8, 1024, 2048], P('fsdp', 'seq'), may hold values from -6 to 6
- mixer_gain: bfloat16 [2048], P('fsdp'), may hold values from 0.099609375 to 1.8984375
- query_weight: bfloat16 [2048, 2048], P('fsdp'), may hold values from -0.125 to 0.125
- key_weight: bfloat16 [2048, 2048], P('fsdp'), may hold values from -0.125 to 0.125
- value_weight: bfloat16 [2048, 3456], P('fsdp'), may hold values from -0.125 to 0.125
- swish_weight: bfloat16 [2048, 3456], P('fsdp'), may hold values from -0.125 to 0.125
- output_weight: bfloat16 [3456, 2048], P('fsdp'), may hold values from -0.21875 to 0.21875
- channel_gain: bfloat16 [2048], P('fsdp'), may hold values from 0.099609375 to 1.8984375
- gelu_weight: bfloat16 [2048, 3456], P('fsdp'), may hold values from -0.125 to 0.125
- linear_weight: bfloat16 [2048, 3456], P('fsdp'), may hold values from -0.125 to 0.125
- down_weight: bfloat16 [3456, 2048], P('fsdp'), may hold values from -0.21875 to 0.21875
- output_cotangent: bfloat16 [8, 1024, 2048], P('fsdp', 'seq'), may hold values from -6 to 6
Outputs:
- layer_output: bfloat16 [8, 1024, 2048], P('fsdp', 'seq')
- input_gradient: bfloat16 [8, 1024, 2048], P('fsdp', 'seq')
- mixer_gradient: float32 [2048], P('fsdp')
- query_gradient: float32 [2048, 2048], P('fsdp')
- key_gradient: float32 [2048, 2048], P('fsdp')
- value_gradient: float32 [2048, 3456], P('fsdp')
- swish_gradient: float32 [2048, 3456], P('fsdp')
- output_gradient: float32 [3456, 2048], P('fsdp')
- channel_gradient: float32 [2048], P('fsdp')
- gelu_gradient: float32 [2048, 3456], P('fsdp')
- linear_gradient: float32 [2048, 3456], P('fsdp')
- down_gradient: float32 [3456, 2048], P('fsdp')
The draws below stay inside these ranges and needn't reach their ends.
All inputs are finite; a program needn't handle non-finite values.
Results may differ from the reference program's by a relative error of at most 0.024.
Values may be sent and summed in bfloat16 or wider, within the bound.
A program may use at most 576 MiB of HBM per device.

```python
import math
import jax
import jax.numpy as jnp
from jax import lax

D = 2048
HEADS = 8
KEY_HEAD = 256
VAL_HEAD = 432
FF = 3456
SEQ_LEN = 1024
QK = 2048
VD = 3456
SEQS = 8


def level_of(rng, dims, shards, least, largest):
    def one(dim, blocks):
        draws = jax.random.uniform(jax.random.fold_in(jax.random.fold_in(rng, 6), dim), (blocks,), jnp.float32, least / len(shards), largest / len(shards))
        return jnp.repeat(jnp.exp(draws), dims[dim] // blocks).reshape((-1,) + (1,) * (len(dims) - dim - 1))

    loudness = one(*shards[0])
    for cut in shards[1:]:
        loudness = loudness * one(*cut)
    return loudness


def normal_values(key, extent, scale, limit, shards=(), kind=jnp.bfloat16):
    values = jax.random.normal(key, extent, jnp.float32) * scale
    if len(shards) > 0:
        values = level_of(key, extent, shards, -0.22, 0.18) * values
    return jnp.clip(values, min=-limit, max=limit).astype(kind)


def setup_inputs(seed: int = 0) -> dict:
    arg_keys = jax.random.split(jax.random.key(seed), 13)
    layer_input = normal_values(arg_keys[0], (SEQS, SEQ_LEN, D), 1.0, 6.0, ((0, 8), (1, 4)))
    mixer_gain = jnp.clip(1.0 + 0.18 * jax.random.normal(arg_keys[1], (D,), jnp.float32), 0.099609375, 1.8984375).astype(jnp.bfloat16)
    query_weight = normal_values(arg_keys[2], (D, QK), D ** -0.5, 0.125, ((0, 8),))
    key_weight = normal_values(arg_keys[3], (D, QK), D ** -0.5, 0.125, ((0, 8),))
    value_weight = normal_values(arg_keys[4], (D, VD), D ** -0.5, 0.125, ((0, 8),))
    swish_weight = normal_values(arg_keys[5], (D, VD), D ** -0.5, 0.125, ((0, 8),))
    output_weight = normal_values(arg_keys[6], (VD, D), (VD // 4) ** -0.5, 0.21875, ((0, 8),))
    channel_gain = jnp.clip(1.0 + 0.18 * jax.random.normal(arg_keys[7], (D,), jnp.float32), 0.099609375, 1.8984375).astype(jnp.bfloat16)
    gelu_weight = normal_values(arg_keys[8], (D, FF), D ** -0.5, 0.125, ((0, 8),))
    linear_weight = normal_values(arg_keys[9], (D, FF), D ** -0.5, 0.125, ((0, 8),))
    down_weight = normal_values(arg_keys[10], (FF, D), (FF // 4) ** -0.5, 0.21875, ((0, 8),))
    output_cotangent = normal_values(arg_keys[11], (SEQS, SEQ_LEN, D), 1.0, 6.0, ((0, 8), (1, 4)))
    return dict(layer_input=layer_input, mixer_gain=mixer_gain, query_weight=query_weight, key_weight=key_weight, value_weight=value_weight, swish_weight=swish_weight, output_weight=output_weight, channel_gain=channel_gain, gelu_weight=gelu_weight, linear_weight=linear_weight, down_weight=down_weight, output_cotangent=output_cotangent)


EPSILON = 1e-05

@jax.custom_vjp
def low(v):
    return lax.optimization_barrier(v.astype(jnp.bfloat16)).astype(jnp.float32)

@jax.custom_vjp
def low_back(v):
    return v

def low_keep(v):
    return (low(v), None)

def low_pass(kept, grad):
    return (grad,)

def back_keep(v):
    return (v, None)

def back_low(kept, grad):
    return (low(grad),)
low.defvjp(low_keep, low_pass)
low_back.defvjp(back_keep, back_low)

def matmul(left, right):
    return jnp.dot(left, right, precision=lax.Precision.HIGHEST)

def normalize(values, gain):
    centered = values - lax.optimization_barrier(jnp.mean(values, axis=-1, keepdims=True))
    spread = lax.rsqrt(lax.optimization_barrier(jnp.mean(centered * centered, axis=-1, keepdims=True)) + EPSILON)
    return centered * spread * gain

def group_norm(values):
    shaped = values.reshape(values.shape[0], HEADS, VAL_HEAD)
    centered = shaped - lax.optimization_barrier(jnp.mean(shaped, axis=-1, keepdims=True))
    spread = lax.rsqrt(jnp.maximum(lax.optimization_barrier(jnp.mean(centered * centered, axis=-1, keepdims=True)), 1.0))
    return (centered * spread).reshape(values.shape)

def rotation_tables(positions, half_width):
    rates = jnp.exp(-math.log(10000.0) * jnp.arange(half_width, dtype=jnp.float32) / (half_width - 1))
    turned = positions.astype(jnp.float32)[:, None] * rates[None, :]
    return (jnp.cos(turned), jnp.sin(turned))

def rotate(values, cosine_table, sine_table, heads_count):
    shaped = values.reshape(values.shape[0], heads_count, -1)
    half_width = shaped.shape[-1] // 2
    first_half = shaped[..., :half_width]
    second_half = shaped[..., half_width:]
    cosine_part = cosine_table[:, None, :]
    sine_part = sine_table[:, None, :]
    turned = jnp.concatenate([first_half * cosine_part - second_half * sine_part, second_half * cosine_part + first_half * sine_part], axis=-1)
    return turned.reshape(values.shape)

def decay_mask(head_ids, length):
    rates = jnp.log1p(-jnp.exp2(-5.0 - head_ids.astype(jnp.float32)))
    row_gaps = jnp.arange(length, dtype=jnp.int32)[:, None] - jnp.arange(length, dtype=jnp.int32)[None, :]
    gaps = jnp.maximum(row_gaps, 0).astype(jnp.float32)
    return jnp.where(row_gaps[None] >= 0, jnp.exp(gaps[None] * rates[:, None, None]), 0.0)

def retention(query, key, value, count, length):
    masks = decay_mask(jnp.arange(HEADS, dtype=jnp.int32), length)
    query_heads = query.reshape(count, length, HEADS, KEY_HEAD).transpose(2, 0, 1, 3)
    key_heads = key.reshape(count, length, HEADS, KEY_HEAD).transpose(2, 0, 1, 3)
    value_heads = value.reshape(count, length, HEADS, VAL_HEAD).transpose(2, 0, 1, 3)

    def one_head(pieces):
        query_one, key_one, value_one, mask_one = pieces
        scores = jnp.einsum('glk,gmk->glm', query_one, key_one, precision=lax.Precision.HIGHEST)
        weights = low(low_back(scores) * mask_one[None])
        return jnp.einsum('glm,gme->gle', weights, value_one, precision=lax.Precision.HIGHEST)
    outcome = lax.map(jax.checkpoint(one_head), (query_heads, key_heads, value_heads, masks))
    return outcome.transpose(1, 2, 0, 3).reshape(count * length, HEADS * VAL_HEAD)

def forward(inputs, mixer_gain, query_weight, key_weight, value_weight, swish_weight, output_weight, channel_gain, gelu_weight, linear_weight, down_weight):
    count, length, width = inputs.shape
    flat = inputs.reshape(count * length, width)
    positions = jnp.tile(jnp.arange(length, dtype=jnp.int32), count)
    cosine_table, sine_table = rotation_tables(positions, KEY_HEAD // 2)
    mixed = low(normalize(flat, mixer_gain))
    query = low(low_back(rotate(low_back(matmul(mixed, query_weight)), cosine_table, sine_table, HEADS)))
    key = low(low_back(rotate(low_back(matmul(mixed, key_weight)), cosine_table, sine_table, HEADS) * KEY_HEAD ** (-0.5)))
    value = low(low_back(matmul(mixed, value_weight)))
    swish = low_back(matmul(mixed, swish_weight))
    retained = low(low_back(retention(query, key, value, count, length)))
    gated = low(jax.nn.silu(swish) * group_norm(retained))
    middle = flat + low_back(matmul(gated, output_weight))
    channel = low(normalize(middle, channel_gain))
    gate = low_back(matmul(channel, gelu_weight))
    up_part = low_back(matmul(channel, linear_weight))
    hidden = low(jax.nn.gelu(gate, approximate=False) * up_part)
    return (middle + matmul(hidden, down_weight)).reshape(count, length, width)

def reference(layer_input, mixer_gain, query_weight, key_weight, value_weight, swish_weight, output_weight, channel_gain, gelu_weight, linear_weight, down_weight, output_cotangent):
    params = tuple((weight.astype(jnp.float32) for weight in (mixer_gain, query_weight, key_weight, value_weight, swish_weight, output_weight, channel_gain, gelu_weight, linear_weight, down_weight)))
    group_size = 4 if SEQS % 4 == 0 else 1
    grouped_input = layer_input.reshape(SEQS // group_size, group_size, SEQ_LEN, D)
    grouped_cot = output_cotangent.reshape(SEQS // group_size, group_size, SEQ_LEN, D)

    def step(totals, pieces):
        block_input, block_cot = pieces
        outputs, pullback = jax.vjp(forward, block_input.astype(jnp.float32), *params)
        grads = pullback(block_cot.astype(jnp.float32))
        updated = tuple((total + grad for total, grad in zip(totals, grads[1:])))
        return (updated, (outputs.astype(jnp.bfloat16), grads[0].astype(jnp.bfloat16)))
    zeros = tuple((jnp.zeros(weight.shape, jnp.float32) for weight in params))
    totals, (outputs, input_grads) = lax.scan(step, zeros, (grouped_input, grouped_cot))
    layer_output = outputs.reshape(SEQS, SEQ_LEN, D)
    input_gradient = input_grads.reshape(SEQS, SEQ_LEN, D)
    return (layer_output, input_gradient, totals[0], totals[1], totals[2], totals[3], totals[4], totals[5], totals[6], totals[7], totals[8], totals[9])
```

```python
import functools
import math

import jax
import jax.numpy as jnp
from jax import lax
from jax.experimental import pallas as pl
from jax.experimental.pallas import tpu as pltpu
from jax.sharding import PartitionSpec as P

HEADS = 8
KEY_HEAD = 256
VAL_HEAD = 432
EPSILON = 1e-05
MESH = pl.DeviceIdType.MESH
BF = jnp.bfloat16
F32 = jnp.float32


def product(left, right):
    return jnp.dot(left, right, preferred_element_type=F32)


def times_transposed(left, right):
    return lax.dot_general(left, right, (((1,), (1,)), ((), ())), preferred_element_type=F32)


def transposed_times(left, right):
    return lax.dot_general(left, right, (((0,), (0,)), ((), ())), preferred_element_type=F32)


def normalize(values, gain):
    centered = values - jnp.mean(values, axis=-1, keepdims=True)
    spread = lax.rsqrt(jnp.mean(centered * centered, axis=-1, keepdims=True) + EPSILON)
    return centered * spread * gain


def group_norm_head(values):
    centered = values - jnp.mean(values, axis=-1, keepdims=True)
    return centered * lax.rsqrt(
        jnp.maximum(jnp.mean(centered * centered, axis=-1, keepdims=True), 1.0)
    )


def swish_mix(swish_value, retained_value):
    parts = [
        group_norm_head(retained_value[:, at : at + VAL_HEAD])
        for at in range(0, retained_value.shape[1], VAL_HEAD)
    ]
    return jax.nn.silu(swish_value) * jnp.concatenate(parts, axis=-1)


def gelu_mix(gate_value, up_value):
    return jax.nn.gelu(gate_value, approximate=False) * up_value


def rotation_tables(length, half_width):
    rates = jnp.exp(-math.log(10000.0) * jnp.arange(half_width, dtype=F32) / (half_width - 1))
    turned = jnp.arange(length, dtype=F32)[:, None] * rates[None, :]
    return (jnp.cos(turned), jnp.sin(turned))


def rotate(values, cosine, sine, back=False):
    half = KEY_HEAD // 2
    pieces = []
    for at in range(0, values.shape[1], KEY_HEAD):
        first = values[:, at : at + half]
        second = values[:, at + half : at + KEY_HEAD]
        if back:
            pieces += [first * cosine + second * sine, second * cosine - first * sine]
        else:
            pieces += [first * cosine - second * sine, second * cosine + first * sine]
    return jnp.concatenate(pieces, axis=-1)


def decay_mask(head_ids, length):
    rates = jnp.log1p(-jnp.exp2(-5.0 - head_ids.astype(F32)))
    row_gaps = (
        jnp.arange(length, dtype=jnp.int32)[:, None] - jnp.arange(length, dtype=jnp.int32)[None, :]
    )
    gaps = jnp.maximum(row_gaps, 0).astype(F32)
    return jnp.where(row_gaps[None] >= 0, jnp.exp(gaps[None] * rates[:, None, None]), 0.0)


def greet(peers):
    barrier = pltpu.get_barrier_semaphore()
    for peer in peers:
        pl.semaphore_signal(barrier, inc=1, device_id={"seq": peer}, device_id_type=MESH)
    pl.semaphore_wait(barrier, len(peers))


def remote(source, target, sends, recvs, k, to):
    return pltpu.make_async_remote_copy(
        src_ref=source,
        dst_ref=target,
        send_sem=sends.at[k],
        recv_sem=recvs.at[k],
        device_id={"seq": to},
        device_id_type=MESH,
    )


def gather_square_kernel(x_ref, o_ref, sends, recvs, local):
    me = lax.axis_index("seq")
    across, along = me ^ 1, me ^ 2
    half = x_ref.shape[0] // 2
    greet((across, along))
    own = pltpu.make_async_copy(x_ref, o_ref.at[me], local)
    own.start()

    def part(ref, i):
        return ref.at[pl.ds(i * half, half)]

    first = (
        remote(part(x_ref, 0), part(o_ref.at[me], 0), sends, recvs, 0, across),
        remote(part(x_ref, 1), part(o_ref.at[me], 1), sends, recvs, 1, along),
        remote(part(x_ref, 1), part(o_ref.at[me], 1), sends, recvs, 2, across),
        remote(part(x_ref, 0), part(o_ref.at[me], 0), sends, recvs, 3, along),
    )
    for copy in first:
        copy.start()
    first[0].wait_recv()
    on_along = remote(part(o_ref.at[across], 0), part(o_ref.at[across], 0), sends, recvs, 4, along)
    on_along.start()
    first[1].wait_recv()
    on_across = remote(part(o_ref.at[along], 1), part(o_ref.at[along], 1), sends, recvs, 5, across)
    on_across.start()
    first[2].wait_recv()
    first[3].wait_recv()
    on_along.wait_recv()
    on_across.wait_recv()
    for copy in first + (on_along, on_across):
        copy.wait_send()
    own.wait()


def gather_kernel(count, x_ref, o_ref, sends, recvs, local):
    me = lax.axis_index("seq")
    peers = [lax.rem(me + step, count) for step in range(1, count)]
    greet(peers)
    own = pltpu.make_async_copy(x_ref, o_ref.at[me], local)
    own.start()
    copies = [remote(x_ref, o_ref.at[me], sends, recvs, k, to) for k, to in enumerate(peers)]
    for copy in copies:
        copy.start()
    for copy in copies:
        copy.wait()
    own.wait()


def gather_seq(values, call):
    count = lax.axis_size("seq")
    square = count == 4 and values.shape[0] % 32 == 0
    body = gather_square_kernel if square else functools.partial(gather_kernel, count)
    copies = 6 if square else count - 1
    return pl.pallas_call(
        body,
        out_shape=jax.ShapeDtypeStruct((count,) + values.shape, values.dtype),
        in_specs=[pl.BlockSpec(memory_space=pl.ANY)],
        out_specs=pl.BlockSpec(memory_space=pl.ANY),
        scratch_shapes=[
            pltpu.SemaphoreType.DMA((copies,)),
            pltpu.SemaphoreType.DMA((copies,)),
            pltpu.SemaphoreType.DMA,
        ],
        compiler_params=pltpu.CompilerParams(collective_id=call, has_side_effects=True),
        name=f"gather_seq_{call}",
    )(values)


def exchange_kernel(count, x_ref, o_ref, sends, recvs, local):
    me = lax.axis_index("seq")
    peers = [lax.rem(me + step, count) for step in range(1, count)]
    greet(peers)
    own = pltpu.make_async_copy(x_ref.at[me], o_ref.at[me], local)
    own.start()
    copies = [remote(x_ref.at[to], o_ref.at[me], sends, recvs, k, to) for k, to in enumerate(peers)]
    for copy in copies:
        copy.start()
    for copy in copies:
        copy.wait()
    own.wait()


def exchange_seq(values, call):
    count = lax.axis_size("seq")
    return pl.pallas_call(
        functools.partial(exchange_kernel, count),
        out_shape=jax.ShapeDtypeStruct(values.shape, values.dtype),
        in_specs=[pl.BlockSpec(memory_space=pl.ANY)],
        out_specs=pl.BlockSpec(memory_space=pl.ANY),
        scratch_shapes=[
            pltpu.SemaphoreType.DMA((count - 1,)),
            pltpu.SemaphoreType.DMA((count - 1,)),
            pltpu.SemaphoreType.DMA,
        ],
        compiler_params=pltpu.CompilerParams(collective_id=call, has_side_effects=True),
        name=f"exchange_seq_{call}",
    )(values)


def scatter_square_kernel(p_ref, o_ref, inbox_x, inbox_y, via_x, via_y, out_x, out_y, sends, recvs):
    me = lax.axis_index("seq")
    across, along, corner = me ^ 1, me ^ 2, me ^ 3
    half = p_ref.shape[1] // 2
    low, high = pl.ds(0, half), pl.ds(half, half)
    greet((across, along))
    first = (
        remote(p_ref.at[corner, low], via_x, sends, recvs, 0, across),
        remote(p_ref.at[corner, high], via_y, sends, recvs, 1, along),
        remote(p_ref.at[across, low], inbox_x.at[low], sends, recvs, 2, across),
        remote(p_ref.at[along, high], inbox_y.at[high], sends, recvs, 3, along),
    )
    for copy in first:
        copy.start()
    first[0].wait_recv()
    out_y[...] = (p_ref[along, :half].astype(F32) + via_x[...].astype(F32)).astype(BF)
    to_along = remote(out_y, inbox_y.at[low], sends, recvs, 4, along)
    to_along.start()
    first[1].wait_recv()
    out_x[...] = (p_ref[across, half:].astype(F32) + via_y[...].astype(F32)).astype(BF)
    to_across = remote(out_x, inbox_x.at[high], sends, recvs, 5, across)
    to_across.start()
    first[2].wait_recv()
    first[3].wait_recv()
    to_along.wait_recv()
    to_across.wait_recv()
    o_ref[...] = (
        p_ref[me].astype(F32) + inbox_x[...].astype(F32) + inbox_y[...].astype(F32)
    )
    for copy in first + (to_along, to_across):
        copy.wait_send()


def scatter_kernel(count, p_ref, o_ref, inbox, sends, recvs):
    me = lax.axis_index("seq")
    peers = [lax.rem(me + step, count) for step in range(1, count)]
    greet(peers)
    copies = [remote(p_ref.at[to], inbox.at[k], sends, recvs, k, to) for k, to in enumerate(peers)]
    for copy in copies:
        copy.start()
    total = p_ref[me].astype(F32)
    for k, copy in enumerate(copies):
        copy.wait_recv()
        total = total + inbox[k].astype(F32)
    o_ref[...] = total
    for copy in copies:
        copy.wait_send()


def scatter_seq(parts, call):
    count = lax.axis_size("seq")
    rows, width = parts.shape[0] // count, parts.shape[1]
    parts = parts.reshape(count, rows, width)
    if count == 4 and rows % 32 == 0:
        body = scatter_square_kernel
        scratch = [pltpu.VMEM((rows, width), BF)] * 2 + [pltpu.VMEM((rows // 2, width), BF)] * 4
        copies = 6
    else:
        body = functools.partial(scatter_kernel, count)
        scratch = [pltpu.VMEM((count - 1, rows, width), BF)]
        copies = count - 1
    return pl.pallas_call(
        body,
        out_shape=jax.ShapeDtypeStruct((rows, width), F32),
        in_specs=[pl.BlockSpec(memory_space=pltpu.VMEM)],
        out_specs=pl.BlockSpec(memory_space=pltpu.VMEM),
        scratch_shapes=scratch
        + [pltpu.SemaphoreType.DMA((copies,)), pltpu.SemaphoreType.DMA((copies,))],
        compiler_params=pltpu.CompilerParams(
            collective_id=call, has_side_effects=True, vmem_limit_bytes=32 * 1024 * 1024
        ),
        name=f"scatter_seq_{call}",
    )(parts)


class Cut:
    def __init__(self, rows, count):
        self.rows, self.count = rows, count
        self.width = -(-rows // (count * 16)) * 16

    def start(self, piece):
        if isinstance(piece, int):
            return min(piece * self.width, self.rows - self.width)
        return jnp.minimum(piece * self.width, self.rows - self.width)

    def skip(self, piece):
        if isinstance(piece, int):
            return min(piece * self.width - self.start(piece), self.width)
        return jnp.minimum(piece * self.width - self.start(piece), self.width)

    def assemble(self, pieces, axis):
        kept = []
        for k, piece in enumerate(pieces):
            if self.skip(k) < self.width:
                kept.append(lax.slice_in_dim(piece, self.skip(k), self.width, axis=axis))
        return jnp.concatenate(kept, axis=axis)


def columns_of(weight, index, width, padded):
    piece = lax.dynamic_slice_in_dim(weight, index * width, width, axis=1)
    return jnp.pad(piece, ((0, 0), (0, padded - width)))


def on_device(
    layer_input,
    mixer_gain,
    query_weight,
    key_weight,
    value_weight,
    swish_weight,
    output_weight,
    channel_gain,
    gelu_weight,
    linear_weight,
    down_weight,
    output_cotangent,
):
    groups, local_length, width = layer_input.shape
    seq_count = lax.axis_size("seq")
    shards = lax.axis_size("fsdp")
    me = lax.axis_index("seq")
    per_device = HEADS // seq_count
    rows_count = groups * local_length
    length = local_length * seq_count
    key_scale = KEY_HEAD ** (-0.5)
    qk = query_weight.shape[1] // seq_count
    vd = value_weight.shape[1] // seq_count
    vd_pad = -(-vd // 128) * 128
    hidden_units = gelu_weight.shape[1]
    own_rows = down_weight.shape[0]
    cut = Cut(own_rows, seq_count)
    ff = shards * cut.width

    def gather_rows(values):
        return lax.all_gather(values, "fsdp", axis=0, tiled=True)

    def scatter_rows(values):
        return lax.psum_scatter(values.astype(BF), "fsdp", scatter_dimension=0, tiled=True)

    attention_piece = jnp.concatenate(
        [
            columns_of(query_weight, me, qk, qk),
            columns_of(key_weight, me, qk, qk),
            columns_of(value_weight, me, vd, vd_pad),
            columns_of(swish_weight, me, vd, vd_pad),
        ],
        axis=1,
    )
    attention_weight = gather_rows(attention_piece)
    output_piece = lax.dynamic_slice_in_dim(output_weight, cut.start(me), cut.width, axis=0)
    output_pieces = gather_rows(output_piece)
    column = lax.broadcasted_iota(jnp.int32, (hidden_units, ff), 0)
    slot = lax.broadcasted_iota(jnp.int32, (hidden_units, ff), 1)
    chosen = (slot // cut.width) * own_rows + cut.start(me) + slot % cut.width
    selector = (column == chosen).astype(BF)
    gate_piece = product(gelu_weight, selector).astype(BF)
    up_piece = product(linear_weight, selector).astype(BF)
    feed_weight = gather_rows(jnp.concatenate([gate_piece, up_piece], axis=1))
    gate_full, up_full = feed_weight[:, :ff], feed_weight[:, ff:]
    down_piece = lax.dynamic_slice_in_dim(down_weight, cut.start(me), cut.width, axis=0)
    kept_rows = lax.broadcasted_iota(jnp.int32, down_piece.shape, 0) >= cut.skip(me)
    down_full = gather_rows(jnp.where(kept_rows, down_piece, jnp.zeros_like(down_piece)))
    gains = lax.all_gather(jnp.stack([mixer_gain, channel_gain]), "fsdp", axis=1, tiled=True)
    mixer_scale, channel_scale = gains[0].astype(F32), gains[1].astype(F32)

    local_input = layer_input.reshape(rows_count, width)
    upstream = output_cotangent.reshape(rows_count, width)

    def whole(values, call):
        gathered = gather_seq(values, call)
        return gathered.reshape(length * groups, width)

    input_full = whole(local_input, 0)
    upstream_full = whole(upstream, 1)
    inputs = local_input.astype(F32)

    mixed_low = normalize(input_full.astype(F32), mixer_scale).astype(BF)
    projected = product(mixed_low, attention_weight)
    cosine, sine = rotation_tables(length, KEY_HEAD // 2)
    query_low = rotate(projected[:, :qk], cosine, sine).astype(BF)
    key_low = (rotate(projected[:, qk : 2 * qk], cosine, sine) * key_scale).astype(BF)
    value_low = projected[:, 2 * qk : 2 * qk + vd].astype(BF)
    swish_pre = projected[:, 2 * qk + vd_pad : 2 * qk + vd_pad + vd]
    head_ids = me * per_device + jnp.arange(per_device, dtype=jnp.int32)
    masks = decay_mask(head_ids, length)
    weights_low, retained_parts = [], []

    def key_of(values, head):
        return values[:, head * KEY_HEAD : (head + 1) * KEY_HEAD]

    def value_of(values, head):
        return values[:, head * VAL_HEAD : (head + 1) * VAL_HEAD]

    for head in range(per_device):
        scores = times_transposed(key_of(query_low, head), key_of(key_low, head))
        weights_low.append((scores * masks[head]).astype(BF))
        retained_parts.append(product(weights_low[head], value_of(value_low, head)).astype(BF))
    retained = jnp.concatenate(retained_parts, axis=1).astype(F32)
    gated_low = swish_mix(swish_pre, retained).astype(BF)

    blocks = shards // seq_count
    swapped = exchange_seq(output_pieces.reshape(seq_count, blocks, cut.width, width), 2)
    output_full = jnp.concatenate(
        [
            cut.assemble([swapped[piece, block] for piece in range(seq_count)], 0)
            for block in range(blocks)
        ],
        axis=0,
    )
    middle = inputs + scatter_seq(product(gated_low, output_full).astype(BF), 3)

    channel_low = normalize(middle, channel_scale).astype(BF)
    channel_full = whole(channel_low, 4)
    gate_pre = product(channel_full, gate_full)
    up_pre = product(channel_full, up_full)
    hidden_low = gelu_mix(gate_pre, up_pre).astype(BF)
    result = middle + scatter_seq(product(hidden_low, down_full).astype(BF), 5)
    layer_output = result.astype(BF).reshape(groups, local_length, width)

    hidden_grad = times_transposed(upstream_full, down_full)
    _, gelu_back = jax.vjp(gelu_mix, gate_pre, up_pre)
    gate_grad, up_grad = gelu_back(hidden_grad)
    gate_low_grad, up_low_grad = gate_grad.astype(BF), up_grad.astype(BF)
    channel_part = times_transposed(gate_low_grad, gate_full) + times_transposed(
        up_low_grad, up_full
    )
    channel_grad = scatter_seq(channel_part.astype(BF), 6)
    _, channel_back = jax.vjp(normalize, middle, channel_scale)
    middle_local, channel_term = channel_back(channel_grad)
    middle_grad = upstream.astype(F32) + middle_local
    down_share = scatter_rows(transposed_times(hidden_low, upstream_full))
    feed_share = scatter_rows(
        jnp.concatenate(
            [
                transposed_times(channel_full, gate_low_grad).astype(BF),
                transposed_times(channel_full, up_low_grad).astype(BF),
            ],
            axis=1,
        )
    )

    branch_full = whole(middle_grad.astype(BF), 7)
    gated_grad = times_transposed(branch_full, output_full)
    output_term = transposed_times(gated_low, branch_full).astype(BF)
    output_term = output_term.reshape(blocks, own_rows, width)
    output_send = jnp.stack(
        [
            lax.slice_in_dim(output_term, cut.start(k), cut.start(k) + cut.width, axis=1)
            for k in range(seq_count)
        ]
    )
    output_swapped = exchange_seq(output_send, 8)
    output_share = scatter_rows(output_swapped.reshape(shards * cut.width, width))
    _, swish_back = jax.vjp(swish_mix, swish_pre, retained)
    swish_grad, retained_grad = swish_back(gated_grad)
    swish_low_grad = swish_grad.astype(BF)
    retained_low_grad = retained_grad.astype(BF)
    query_parts, key_parts, value_parts = [], [], []
    for head in range(per_device):
        head_grad = value_of(retained_low_grad, head)
        weights_grad = times_transposed(head_grad, value_of(value_low, head))
        value_parts.append(transposed_times(weights_low[head], head_grad).astype(BF))
        score_low = (weights_grad * masks[head]).astype(BF)
        query_parts.append(product(score_low, key_of(key_low, head)).astype(BF))
        key_parts.append(transposed_times(score_low, key_of(query_low, head)).astype(BF))
    query_grad = jnp.concatenate(query_parts, axis=1).astype(F32)
    key_grad = jnp.concatenate(key_parts, axis=1).astype(F32)
    query_pre_grad = rotate(query_grad, cosine, sine, back=True).astype(BF)
    key_pre_grad = (rotate(key_grad, cosine, sine, back=True) * key_scale).astype(BF)
    gap = jnp.zeros((length, vd_pad - vd), BF)
    projected_grad = jnp.concatenate(
        [query_pre_grad, key_pre_grad] + value_parts + [gap, swish_low_grad, gap], axis=1
    )
    attention_share = scatter_rows(transposed_times(mixed_low, projected_grad))
    mixed_grad = scatter_seq(times_transposed(projected_grad, attention_weight).astype(BF), 9)
    _, mixer_back = jax.vjp(normalize, inputs, mixer_scale)
    input_local, mixer_term = mixer_back(mixed_grad)
    input_gradient = (middle_grad + input_local).astype(BF)
    input_gradient = input_gradient.reshape(groups, local_length, width)

    down_all = gather_seq(down_share, 10)
    feed_all = gather_seq(feed_share, 11)
    output_all = gather_seq(output_share, 12)
    attention_all = gather_seq(attention_share, 13)
    down_gradient = cut.assemble([down_all[k] for k in range(seq_count)], 0).astype(F32)
    output_gradient = cut.assemble([output_all[k] for k in range(seq_count)], 0).astype(F32)

    def hidden_order(at):
        pieces = [feed_all[k][:, at : at + ff] for k in range(seq_count)]
        return jnp.concatenate(
            [
                cut.assemble(
                    [piece[:, f * cut.width : (f + 1) * cut.width] for piece in pieces], 1
                )
                for f in range(shards)
            ],
            axis=1,
        ).astype(F32)

    def attention_order(at, wide):
        pieces = [attention_all[k][:, at : at + wide] for k in range(seq_count)]
        return jnp.concatenate(pieces, axis=1).astype(F32)

    gain_terms = lax.psum(jnp.stack([mixer_term, channel_term]), ("seq", "fsdp"))
    own_gain = width // shards
    gain_own = lax.dynamic_slice_in_dim(
        gain_terms, lax.axis_index("fsdp") * own_gain, own_gain, axis=1
    )
    return (
        layer_output,
        input_gradient,
        gain_own[0],
        attention_order(0, qk),
        attention_order(qk, qk),
        attention_order(2 * qk, vd),
        attention_order(2 * qk + vd_pad, vd),
        output_gradient,
        gain_own[1],
        hidden_order(0),
        hidden_order(ff),
        down_gradient,
    )


def solution(mesh):
    tokens, rows, vector = P("fsdp", "seq", None), P("fsdp", None), P("fsdp")
    return jax.shard_map(
        on_device,
        mesh=mesh,
        in_specs=(
            tokens, vector, rows, rows, rows, rows, rows, vector, rows, rows, rows, tokens,
        ),
        out_specs=(
            tokens, tokens, vector, rows, rows, rows, rows, rows, vector, rows, rows, rows,
        ),
        check_vma=False,
    )
```

```python
import functools
import math

import jax
import jax.numpy as jnp
from jax import lax
from jax.experimental import pallas as pl
from jax.experimental.pallas import tpu as pltpu
from jax.sharding import PartitionSpec as P

HEADS = 8
KEY_HEAD = 256
VAL_HEAD = 432
EPSILON = 1e-05
MESH = pl.DeviceIdType.MESH
BF = jnp.bfloat16
F32 = jnp.float32


def product(left, right):
    return jnp.dot(left, right, preferred_element_type=F32)


def times_transposed(left, right):
    return lax.dot_general(left, right, (((1,), (1,)), ((), ())), preferred_element_type=F32)


def transposed_times(left, right):
    return lax.dot_general(left, right, (((0,), (0,)), ((), ())), preferred_element_type=F32)


def normalize(values, gain):
    centered = values - jnp.mean(values, axis=-1, keepdims=True)
    spread = lax.rsqrt(jnp.mean(centered * centered, axis=-1, keepdims=True) + EPSILON)
    return centered * spread * gain


def rotation_tables(length, half_width):
    rates = jnp.exp(-math.log(10000.0) * jnp.arange(half_width, dtype=F32) / (half_width - 1))
    turned = jnp.arange(length, dtype=F32)[:, None] * rates[None, :]
    return (jnp.cos(turned), jnp.sin(turned))


def pad_lanes(pieces, width):
    have = sum(piece.shape[1] for piece in pieces)
    if have < width:
        pieces = pieces + [jnp.zeros((pieces[0].shape[0], width - have), pieces[0].dtype)]
    return jnp.concatenate(pieces, axis=1) if len(pieces) > 1 else pieces[0]


def rotate_pair(values, cosine, sine, back=False):
    half = KEY_HEAD // 2
    first, second = values[:, :half], values[:, half:]
    if back:
        return jnp.concatenate([first * cosine + second * sine, second * cosine - first * sine], 1)
    return jnp.concatenate([first * cosine - second * sine, second * cosine + first * sine], 1)


BLOCK = 256


def head_rate(head):
    ids = jnp.full((1, 1), head, jnp.int32).astype(F32)
    return jnp.log1p(-jnp.exp2(-5.0 - ids))


def decay_tile(rate):
    gap = lax.broadcasted_iota(jnp.int32, (BLOCK, BLOCK), 0) - lax.broadcasted_iota(
        jnp.int32, (BLOCK, BLOCK), 1
    )
    full = jnp.exp(gap.astype(F32) * rate)
    return full, jnp.where(gap >= 0, full, 0.0)


def norm_parts(values):
    centered = values - jnp.mean(values, axis=-1, keepdims=True)
    variance = jnp.mean(centered * centered, axis=-1, keepdims=True)
    factor = lax.rsqrt(jnp.maximum(variance, 1.0))
    return centered * factor, factor, variance > 1.0


def rows_of(block):
    return pl.ds(pl.multiple_of(block * BLOCK, BLOCK), BLOCK)


def retention_kernel(
    heads, offsets, x_ref, gain_ref, w_ref, cos_ref, sin_ref,
    mixed_ref, q_ref, k_ref, v_ref, swish_ref, retained_ref, gated_ref,
):
    first_head = lax.axis_index("seq") * heads
    at_key, at_value, at_swish = offsets
    value_width = heads * VAL_HEAD
    blocks = x_ref.shape[0] // BLOCK
    rates = [head_rate(first_head + h) for h in range(heads)]

    @pl.loop(0, blocks)
    def _(i):
        rows = rows_of(i)
        x = x_ref[rows, :].astype(F32)
        mixed = normalize(x, gain_ref[...]).astype(BF)
        mixed_ref[rows, :] = mixed
        cosine, sine = cos_ref[rows, :], sin_ref[rows, :]
        query = product(mixed, w_ref[:, :at_key])
        for h in range(heads):
            lanes = slice(h * KEY_HEAD, (h + 1) * KEY_HEAD)
            q_ref[rows, lanes] = rotate_pair(query[:, lanes], cosine, sine).astype(BF)
        key = product(mixed, w_ref[:, at_key:at_value])
        for h in range(heads):
            lanes = slice(h * KEY_HEAD, (h + 1) * KEY_HEAD)
            turned = rotate_pair(key[:, lanes], cosine, sine) * (KEY_HEAD**-0.5)
            k_ref[rows, lanes] = turned.astype(BF)
        value = product(mixed, w_ref[:, at_value:at_swish])
        for h in range(heads):
            v_ref[h, rows, :] = value[:, h * VAL_HEAD : (h + 1) * VAL_HEAD].astype(BF)
        swish = product(mixed, w_ref[:, at_swish:])[:, :value_width]
        swish_ref[rows, :] = swish

        gated = []
        for h in range(heads):
            lanes = slice(h * KEY_HEAD, (h + 1) * KEY_HEAD)
            full, lower = decay_tile(rates[h])
            q = q_ref[rows, lanes]
            scores = times_transposed(q, k_ref[rows, lanes])
            total = product((scores * lower).astype(BF), v_ref[h, rows, :])

            def earlier(j, total):
                there = rows_of(j)
                scores = times_transposed(q, k_ref[there, lanes])
                far = jnp.exp(rates[h] * ((i - j) * BLOCK).astype(F32))
                return total + product((scores * (full * far)).astype(BF), v_ref[h, there, :])

            total = lax.fori_loop(0, i, earlier, total)
            retained = total.astype(BF)
            retained_ref[h, rows, :] = retained
            unit, _, _ = norm_parts(retained.astype(F32))
            s = swish[:, h * VAL_HEAD : (h + 1) * VAL_HEAD]
            gated.append((s * jax.nn.sigmoid(s) * unit).astype(BF))
        gated_ref[rows, :] = jnp.concatenate(gated, axis=1) if heads > 1 else gated[0]


def vmem_call(body, out_shapes, scratch, limit, cost, name):
    return pl.pallas_call(
        body,
        out_shape=out_shapes,
        scratch_shapes=scratch,
        compiler_params=pltpu.CompilerParams(vmem_limit_bytes=limit * 1024 * 1024),
        cost_estimate=pl.CostEstimate(flops=cost, bytes_accessed=0, transcendentals=0),
        name=name,
    )


def retention_forward(x, gain, weight, cosine, sine, heads, offsets):
    length, width = x.shape
    qk, vd = heads * KEY_HEAD, heads * VAL_HEAD
    return vmem_call(
        functools.partial(retention_kernel, heads, offsets),
        (
            jax.ShapeDtypeStruct((length, width), BF),
            jax.ShapeDtypeStruct((length, qk), BF),
            jax.ShapeDtypeStruct((length, qk), BF),
            jax.ShapeDtypeStruct((heads, length, VAL_HEAD), BF),
            jax.ShapeDtypeStruct((length, vd), F32),
            jax.ShapeDtypeStruct((heads, length, VAL_HEAD), BF),
            jax.ShapeDtypeStruct((length, vd), BF),
        ),
        [],
        56,
        30_000_000_000,
        "retention",
    )(x, gain, weight, cosine, sine)


def gate_back_kernel(heads, branch_ref, w_ref, swish_ref, retained_ref, dswish_ref, dret_ref):
    blocks = branch_ref.shape[0] // BLOCK

    @pl.loop(0, blocks)
    def _(i):
        rows = rows_of(i)
        gated_grad = times_transposed(branch_ref[rows, :], w_ref[...])
        swish_parts = []
        for h in range(heads):
            lanes = slice(h * VAL_HEAD, (h + 1) * VAL_HEAD)
            grad, s = gated_grad[:, lanes], swish_ref[rows, lanes]
            gate = jax.nn.sigmoid(s)
            unit, factor, above = norm_parts(retained_ref[h, rows, :].astype(F32))
            swish_parts.append((grad * unit * (gate * (1.0 + s * (1.0 - gate)))).astype(BF))
            g = grad * (s * gate)
            along = jnp.where(above, jnp.mean(g * unit, axis=-1, keepdims=True), 0.0)
            back = factor * (g - jnp.mean(g, axis=-1, keepdims=True) - unit * along)
            dret_ref[h, rows, :] = back.astype(BF)
        dswish_ref[rows, :] = pad_lanes(swish_parts, dswish_ref.shape[1])


def gate_backward(branch, weight, swish, retained, heads, padded):
    length = branch.shape[0]
    return vmem_call(
        functools.partial(gate_back_kernel, heads),
        (
            jax.ShapeDtypeStruct((length, padded), BF),
            jax.ShapeDtypeStruct((heads, length, VAL_HEAD), BF),
        ),
        [],
        48,
        12_000_000_000,
        "gate_back",
    )(branch, weight, swish, retained)


def retention_back_kernel(
    heads, q_ref, k_ref, v_ref, dret_ref, cos_ref, sin_ref, dqk_ref, dv_ref, dq_sum, dv_sum
):
    first_head = lax.axis_index("seq") * heads
    blocks = q_ref.shape[0] // BLOCK
    qk = heads * KEY_HEAD
    dq_sum[...] = jnp.zeros_like(dq_sum)
    for h in range(heads):
        rate = head_rate(first_head + h)
        lanes = slice(h * KEY_HEAD, (h + 1) * KEY_HEAD)

        @pl.loop(0, blocks)
        def _(j):
            there = rows_of(j)
            full, lower = decay_tile(rate)
            key, value = k_ref[there, lanes], v_ref[h, there, :]

            def step(i, decay, sums):
                rows = rows_of(i)
                query, grad = q_ref[rows, lanes], dret_ref[h, rows, :]
                weights = (times_transposed(query, key) * decay).astype(BF)
                score = (times_transposed(grad, value) * decay).astype(BF)
                dq_sum[rows, lanes] += product(score, key)
                return (
                    sums[0] + transposed_times(score, query),
                    sums[1] + transposed_times(weights, grad),
                )

            sums = (jnp.zeros((BLOCK, KEY_HEAD), F32), jnp.zeros((BLOCK, VAL_HEAD), F32))
            sums = step(j, lower, sums)

            def later(i, sums):
                return step(i, full * jnp.exp(rate * ((i - j) * BLOCK).astype(F32)), sums)

            dk, dv = lax.fori_loop(j + 1, blocks, later, sums)
            dk = rotate_pair(
                dk.astype(BF).astype(F32), cos_ref[there, :], sin_ref[there, :], back=True
            )
            dqk_ref[there, qk + h * KEY_HEAD : qk + (h + 1) * KEY_HEAD] = (
                dk * (KEY_HEAD**-0.5)
            ).astype(BF)
            dv_sum[h, there, :] = dv.astype(BF)

    @pl.loop(0, blocks)
    def _(i):
        rows = rows_of(i)
        cosine, sine = cos_ref[rows, :], sin_ref[rows, :]
        for h in range(heads):
            lanes = slice(h * KEY_HEAD, (h + 1) * KEY_HEAD)
            dq = dq_sum[rows, lanes].astype(BF).astype(F32)
            dqk_ref[rows, lanes] = rotate_pair(dq, cosine, sine, back=True).astype(BF)
        dv_ref[rows, :] = pad_lanes([dv_sum[h, rows, :] for h in range(heads)], dv_ref.shape[1])


def retention_backward(q, k, v, dret, cosine, sine, heads, padded):
    length = q.shape[0]
    qk = heads * KEY_HEAD
    return vmem_call(
        functools.partial(retention_back_kernel, heads),
        (
            jax.ShapeDtypeStruct((length, 2 * qk), BF),
            jax.ShapeDtypeStruct((length, padded), BF),
        ),
        [pltpu.VMEM((length, qk), F32), pltpu.VMEM((heads, length, VAL_HEAD), BF)],
        48,
        12_000_000_000,
        "retention_back",
    )(q, k, v, dret, cosine, sine)


def transfer_cost(elements):
    return pl.CostEstimate(flops=0, bytes_accessed=elements * 240, transcendentals=0)


def greet(peers):
    barrier = pltpu.get_barrier_semaphore()
    for peer in peers:
        pl.semaphore_signal(barrier, inc=1, device_id={"seq": peer}, device_id_type=MESH)
    pl.semaphore_wait(barrier, len(peers))


def remote(source, target, sends, recvs, k, to):
    return pltpu.make_async_remote_copy(
        src_ref=source,
        dst_ref=target,
        send_sem=sends.at[k],
        recv_sem=recvs.at[k],
        device_id={"seq": to},
        device_id_type=MESH,
    )


def gather_square_kernel(x_ref, o_ref, sends, recvs, local):
    me = lax.axis_index("seq")
    across, along = me ^ 1, me ^ 2
    half = x_ref.shape[0] // 2
    greet((across, along))
    own = pltpu.make_async_copy(x_ref, o_ref.at[me], local)
    own.start()

    def part(ref, i):
        return ref.at[pl.ds(i * half, half)]

    first = (
        remote(part(x_ref, 0), part(o_ref.at[me], 0), sends, recvs, 0, across),
        remote(part(x_ref, 1), part(o_ref.at[me], 1), sends, recvs, 1, along),
        remote(part(x_ref, 1), part(o_ref.at[me], 1), sends, recvs, 2, across),
        remote(part(x_ref, 0), part(o_ref.at[me], 0), sends, recvs, 3, along),
    )
    for copy in first:
        copy.start()
    first[0].wait_recv()
    on_along = remote(part(o_ref.at[across], 0), part(o_ref.at[across], 0), sends, recvs, 4, along)
    on_along.start()
    first[1].wait_recv()
    on_across = remote(part(o_ref.at[along], 1), part(o_ref.at[along], 1), sends, recvs, 5, across)
    on_across.start()
    first[2].wait_recv()
    first[3].wait_recv()
    on_along.wait_recv()
    on_across.wait_recv()
    for copy in first + (on_along, on_across):
        copy.wait_send()
    own.wait()


def gather_kernel(count, x_ref, o_ref, sends, recvs, local):
    me = lax.axis_index("seq")
    peers = [lax.rem(me + step, count) for step in range(1, count)]
    greet(peers)
    own = pltpu.make_async_copy(x_ref, o_ref.at[me], local)
    own.start()
    copies = [remote(x_ref, o_ref.at[me], sends, recvs, k, to) for k, to in enumerate(peers)]
    for copy in copies:
        copy.start()
    for copy in copies:
        copy.wait()
    own.wait()


def gather_seq(values, call):
    count = lax.axis_size("seq")
    square = count == 4 and values.shape[0] % 32 == 0
    body = gather_square_kernel if square else functools.partial(gather_kernel, count)
    copies = 6 if square else count - 1
    return pl.pallas_call(
        body,
        out_shape=jax.ShapeDtypeStruct((count,) + values.shape, values.dtype),
        in_specs=[pl.BlockSpec(memory_space=pl.ANY)],
        out_specs=pl.BlockSpec(memory_space=pl.ANY),
        scratch_shapes=[
            pltpu.SemaphoreType.DMA((copies,)),
            pltpu.SemaphoreType.DMA((copies,)),
            pltpu.SemaphoreType.DMA,
        ],
        compiler_params=pltpu.CompilerParams(collective_id=call, has_side_effects=True),
        cost_estimate=transfer_cost(values.size),
        name=f"gather_seq_{call}",
    )(values)


def exchange_kernel(count, x_ref, o_ref, sends, recvs, local):
    me = lax.axis_index("seq")
    peers = [lax.rem(me + step, count) for step in range(1, count)]
    greet(peers)
    own = pltpu.make_async_copy(x_ref.at[me], o_ref.at[me], local)
    own.start()
    copies = [remote(x_ref.at[to], o_ref.at[me], sends, recvs, k, to) for k, to in enumerate(peers)]
    for copy in copies:
        copy.start()
    for copy in copies:
        copy.wait()
    own.wait()


def exchange_seq(values, call):
    count = lax.axis_size("seq")
    return pl.pallas_call(
        functools.partial(exchange_kernel, count),
        out_shape=jax.ShapeDtypeStruct(values.shape, values.dtype),
        in_specs=[pl.BlockSpec(memory_space=pl.ANY)],
        out_specs=pl.BlockSpec(memory_space=pl.ANY),
        scratch_shapes=[
            pltpu.SemaphoreType.DMA((count - 1,)),
            pltpu.SemaphoreType.DMA((count - 1,)),
            pltpu.SemaphoreType.DMA,
        ],
        compiler_params=pltpu.CompilerParams(collective_id=call, has_side_effects=True),
        cost_estimate=transfer_cost(values.size),
        name=f"exchange_seq_{call}",
    )(values)


def scatter_square_kernel(p_ref, o_ref, inbox_x, inbox_y, via_x, via_y, out_x, out_y, sends, recvs):
    me = lax.axis_index("seq")
    across, along, corner = me ^ 1, me ^ 2, me ^ 3
    half = p_ref.shape[1] // 2
    low, high = pl.ds(0, half), pl.ds(half, half)
    greet((across, along))
    first = (
        remote(p_ref.at[corner, low], via_x, sends, recvs, 0, across),
        remote(p_ref.at[corner, high], via_y, sends, recvs, 1, along),
        remote(p_ref.at[across, low], inbox_x.at[low], sends, recvs, 2, across),
        remote(p_ref.at[along, high], inbox_y.at[high], sends, recvs, 3, along),
    )
    for copy in first:
        copy.start()
    first[0].wait_recv()
    out_y[...] = (p_ref[along, :half].astype(F32) + via_x[...].astype(F32)).astype(BF)
    to_along = remote(out_y, inbox_y.at[low], sends, recvs, 4, along)
    to_along.start()
    first[1].wait_recv()
    out_x[...] = (p_ref[across, half:].astype(F32) + via_y[...].astype(F32)).astype(BF)
    to_across = remote(out_x, inbox_x.at[high], sends, recvs, 5, across)
    to_across.start()
    first[2].wait_recv()
    first[3].wait_recv()
    to_along.wait_recv()
    to_across.wait_recv()
    o_ref[...] = (
        p_ref[me].astype(F32) + inbox_x[...].astype(F32) + inbox_y[...].astype(F32)
    )
    for copy in first + (to_along, to_across):
        copy.wait_send()


def scatter_kernel(count, p_ref, o_ref, inbox, sends, recvs):
    me = lax.axis_index("seq")
    peers = [lax.rem(me + step, count) for step in range(1, count)]
    greet(peers)
    copies = [remote(p_ref.at[to], inbox.at[k], sends, recvs, k, to) for k, to in enumerate(peers)]
    for copy in copies:
        copy.start()
    total = p_ref[me].astype(F32)
    for k, copy in enumerate(copies):
        copy.wait_recv()
        total = total + inbox[k].astype(F32)
    o_ref[...] = total
    for copy in copies:
        copy.wait_send()


def scatter_seq(parts, call):
    count = lax.axis_size("seq")
    rows, width = parts.shape[0] // count, parts.shape[1]
    parts = parts.reshape(count, rows, width)
    if count == 4 and rows % 32 == 0:
        body = scatter_square_kernel
        scratch = [pltpu.VMEM((rows, width), BF)] * 2 + [pltpu.VMEM((rows // 2, width), BF)] * 4
        copies = 6
    else:
        body = functools.partial(scatter_kernel, count)
        scratch = [pltpu.VMEM((count - 1, rows, width), BF)]
        copies = count - 1
    return pl.pallas_call(
        body,
        out_shape=jax.ShapeDtypeStruct((rows, width), F32),
        in_specs=[pl.BlockSpec(memory_space=pltpu.VMEM)],
        out_specs=pl.BlockSpec(memory_space=pltpu.VMEM),
        scratch_shapes=scratch
        + [pltpu.SemaphoreType.DMA((copies,)), pltpu.SemaphoreType.DMA((copies,))],
        compiler_params=pltpu.CompilerParams(
            collective_id=call, has_side_effects=True, vmem_limit_bytes=32 * 1024 * 1024
        ),
        cost_estimate=transfer_cost(rows * width),
        name=f"scatter_seq_{call}",
    )(parts)


def feed_forward_kernel(ff, x_ref, w_ref, gate_ref, up_ref, hidden_ref):
    both = product(x_ref[...], w_ref[...])
    gate, up = both[:, :ff], both[:, ff:]
    gate_ref[...] = gate
    up_ref[...] = up
    hidden_ref[...] = (gate * (0.5 + 0.5 * lax.erf(gate * math.sqrt(0.5))) * up).astype(BF)


def feed_back_kernel(
    ff, c_ref, gate_ref, up_ref, hidden_ref, w_ref, down_ref, both_ref, part_ref, out_ref
):
    gate, up = gate_ref[...], up_ref[...]
    out_ref[...] = product(hidden_ref[...], down_ref[...]).astype(BF)
    hidden_grad = times_transposed(c_ref[...], down_ref[...])
    bell = 0.5 + 0.5 * lax.erf(gate * math.sqrt(0.5))
    slope = bell + gate * (math.sqrt(0.5 / math.pi) * jnp.exp(-0.5 * gate * gate))
    both = jnp.concatenate([hidden_grad * up * slope, hidden_grad * (gate * bell)], axis=1)
    both = both.astype(BF)
    both_ref[...] = both
    part_ref[...] = times_transposed(both, w_ref[...]).astype(BF)


def by_rows(block, width):
    return pl.BlockSpec((block, width), lambda i: (i, 0))


def kept(shape):
    return pl.BlockSpec(shape, lambda i: (0, 0), pipeline_mode=pl.Buffered(1))


FEED_BLOCK = 256


def feed_forward(x, weight):
    length, width = x.shape
    ff = weight.shape[1] // 2
    return pl.pallas_call(
        functools.partial(feed_forward_kernel, ff),
        grid=(length // FEED_BLOCK,),
        in_specs=[by_rows(FEED_BLOCK, width), kept(weight.shape)],
        out_specs=[by_rows(FEED_BLOCK, ff)] * 3,
        out_shape=(
            jax.ShapeDtypeStruct((length, ff), F32),
            jax.ShapeDtypeStruct((length, ff), F32),
            jax.ShapeDtypeStruct((length, ff), BF),
        ),
        compiler_params=pltpu.CompilerParams(vmem_limit_bytes=48 * 1024 * 1024),
        cost_estimate=pl.CostEstimate(
            flops=4 * length * width * ff, bytes_accessed=weight.size * 4, transcendentals=0
        ),
        name="feed_forward",
    )(x, weight)


def feed_backward(cotangent, gate, up, hidden, weight, down):
    length, width = cotangent.shape
    ff = weight.shape[1] // 2
    return pl.pallas_call(
        functools.partial(feed_back_kernel, ff),
        grid=(length // FEED_BLOCK,),
        in_specs=[by_rows(FEED_BLOCK, width)]
        + [by_rows(FEED_BLOCK, ff)] * 3
        + [kept(weight.shape), kept(down.shape)],
        out_specs=[
            by_rows(FEED_BLOCK, 2 * ff),
            by_rows(FEED_BLOCK, width),
            by_rows(FEED_BLOCK, width),
        ],
        out_shape=(
            jax.ShapeDtypeStruct((length, 2 * ff), BF),
            jax.ShapeDtypeStruct((length, width), BF),
            jax.ShapeDtypeStruct((length, width), BF),
        ),
        compiler_params=pltpu.CompilerParams(vmem_limit_bytes=56 * 1024 * 1024),
        cost_estimate=pl.CostEstimate(
            flops=8 * length * width * ff, bytes_accessed=weight.size * 4, transcendentals=0
        ),
        name="feed_back",
    )(cotangent, gate, up, hidden, weight, down)


def square_parts(parts, boxes, sends, recvs, first):
    me = lax.axis_index("seq")
    across, along = me ^ 1, me ^ 2
    inbox_x, inbox_y, via_x, via_y, out_x, out_y = boxes
    half = via_x.shape[0]
    low, high = pl.ds(0, half), pl.ds(half, half)
    copies = [
        remote(parts.at[3, low], via_x, sends, recvs, first, across),
        remote(parts.at[3, high], via_y, sends, recvs, first + 1, along),
        remote(parts.at[1, low], inbox_x.at[low], sends, recvs, first + 2, across),
        remote(parts.at[2, high], inbox_y.at[high], sends, recvs, first + 3, along),
        remote(out_y, inbox_y.at[low], sends, recvs, first + 4, along),
        remote(out_x, inbox_x.at[high], sends, recvs, first + 5, across),
    ]

    def finish():
        copies[0].wait_recv()
        out_y[...] = (parts[2, :half].astype(F32) + via_x[...].astype(F32)).astype(BF)
        copies[4].start()
        copies[1].wait_recv()
        out_x[...] = (parts[1, half:].astype(F32) + via_y[...].astype(F32)).astype(BF)
        copies[5].start()
        for copy in copies[2:]:
            copy.wait_recv()

    def total(rows):
        return (
            parts[0, rows].astype(F32)
            + inbox_x[rows, :].astype(F32)
            + inbox_y[rows, :].astype(F32)
        )

    return copies, finish, total


def square_gather(own, out_ref, sends, recvs, first):
    me = lax.axis_index("seq")
    across, along = me ^ 1, me ^ 2
    half = own.shape[0] // 2

    def part(ref, i):
        return ref.at[pl.ds(i * half, half)]

    copies = [
        remote(part(own, 0), part(out_ref.at[me], 0), sends, recvs, first, across),
        remote(part(own, 1), part(out_ref.at[me], 1), sends, recvs, first + 1, along),
        remote(part(own, 1), part(out_ref.at[me], 1), sends, recvs, first + 2, across),
        remote(part(own, 0), part(out_ref.at[me], 0), sends, recvs, first + 3, along),
        remote(
            part(out_ref.at[across], 0), part(out_ref.at[across], 0), sends, recvs, first + 4, along
        ),
        remote(
            part(out_ref.at[along], 1), part(out_ref.at[along], 1), sends, recvs, first + 5, across
        ),
    ]

    def finish():
        copies[0].wait_recv()
        copies[4].start()
        copies[1].wait_recv()
        copies[5].start()
        for copy in copies[2:]:
            copy.wait_recv()

    return copies, finish


def block_rows(k, rows):
    return pl.ds(pl.multiple_of((lax.axis_index("seq") ^ k) * rows, rows), rows)


def project_kernel(
    g_ref, w_ref, x_ref, gain_ref, middle_ref, full_ref,
    parts, inbox_x, inbox_y, via_x, via_y, out_x, out_y, own, sends, recvs, local,
):
    me = lax.axis_index("seq")
    rows = x_ref.shape[0]
    half = rows // 2
    greet((me ^ 1, me ^ 2))
    boxes = (inbox_x, inbox_y, via_x, via_y, out_x, out_y)
    copies, finish, total = square_parts(parts, boxes, sends, recvs, 0)

    def part(k):
        parts[k] = product(g_ref[block_rows(k, rows), :], w_ref[...]).astype(BF)

    part(3)
    copies[0].start()
    copies[1].start()
    part(1)
    copies[2].start()
    part(2)
    copies[3].start()
    part(0)
    finish()
    spread, finish_gather = square_gather(own, full_ref, sends, recvs, 6)
    for i in range(2):
        here = slice(i * half, (i + 1) * half)
        middle = x_ref[here, :].astype(F32) + total(here)
        middle_ref[here, :] = middle
        own[here, :] = normalize(middle, gain_ref[...]).astype(BF)
        spread[i].start()
    spread[2].start()
    spread[3].start()
    keep = pltpu.make_async_copy(own, full_ref.at[me], local)
    keep.start()
    finish_gather()
    for copy in copies + spread:
        copy.wait_send()
    keep.wait()


def square_scratch(rows, width):
    return [
        pltpu.VMEM((4, rows, width), BF),
        pltpu.VMEM((rows, width), BF),
        pltpu.VMEM((rows, width), BF),
        pltpu.VMEM((rows // 2, width), BF),
        pltpu.VMEM((rows // 2, width), BF),
        pltpu.VMEM((rows // 2, width), BF),
        pltpu.VMEM((rows // 2, width), BF),
    ]


IN_VMEM = pl.BlockSpec(memory_space=pltpu.VMEM)
ANYWHERE = pl.BlockSpec(memory_space=pl.ANY)


def square_call(body, out_shape, out_specs, scratch, inputs, call, cost, name):
    return pl.pallas_call(
        body,
        out_shape=out_shape,
        in_specs=[IN_VMEM] * len(inputs),
        out_specs=out_specs,
        scratch_shapes=scratch,
        compiler_params=pltpu.CompilerParams(
            collective_id=call, has_side_effects=True, vmem_limit_bytes=56 * 1024 * 1024
        ),
        cost_estimate=transfer_cost(cost),
        name=name,
    )(*inputs)


def project_and_norm(gated, weight, x, gain, call):
    rows, width = x.shape
    middle, full = square_call(
        project_kernel,
        (
            jax.ShapeDtypeStruct((rows, width), F32),
            jax.ShapeDtypeStruct((4, rows, width), BF),
        ),
        (IN_VMEM, ANYWHERE),
        square_scratch(rows, width)
        + [
            pltpu.VMEM((rows, width), BF),
            pltpu.SemaphoreType.DMA((12,)),
            pltpu.SemaphoreType.DMA((12,)),
            pltpu.SemaphoreType.DMA,
        ],
        (gated, weight, x, gain[None, :]),
        call,
        2 * x.size,
        "project_and_norm",
    )
    return middle, full.reshape(4 * rows, width)


def norm_back(values, grad, gain):
    centered = values - jnp.mean(values, axis=-1, keepdims=True)
    spread = lax.rsqrt(jnp.mean(centered * centered, axis=-1, keepdims=True) + EPSILON)
    unit = centered * spread
    g = grad * gain
    back = g - jnp.mean(g, axis=-1, keepdims=True)
    back = spread * (back - unit * jnp.mean(g * unit, axis=-1, keepdims=True))
    return back, grad * unit


def middle_back_kernel(
    p_ref, m_ref, c_ref, gain_ref, grad_ref, term_ref, full_ref,
    parts, inbox_x, inbox_y, via_x, via_y, out_x, out_y, own, sends, recvs, local,
):
    me = lax.axis_index("seq")
    rows = c_ref.shape[0]
    half = rows // 2
    greet((me ^ 1, me ^ 2))
    boxes = (inbox_x, inbox_y, via_x, via_y, out_x, out_y)
    copies, finish, total = square_parts(parts, boxes, sends, recvs, 0)
    for k in (3, 1, 2, 0):
        parts[k] = p_ref[block_rows(k, rows), :]
        if k == 3:
            copies[0].start()
            copies[1].start()
        if k == 1:
            copies[2].start()
        if k == 2:
            copies[3].start()
    finish()
    spread, finish_gather = square_gather(own, full_ref, sends, recvs, 6)
    term = jnp.zeros((1, p_ref.shape[1]), F32)
    for i in range(2):
        here = slice(i * half, (i + 1) * half)
        back, terms = norm_back(m_ref[here, :], total(here), gain_ref[...])
        grad = c_ref[here, :].astype(F32) + back
        grad_ref[here, :] = grad
        own[here, :] = grad.astype(BF)
        spread[i].start()
        term = term + jnp.sum(terms, axis=0, keepdims=True)
    spread[2].start()
    spread[3].start()
    keep = pltpu.make_async_copy(own, full_ref.at[me], local)
    keep.start()
    term_ref[...] = term
    finish_gather()
    for copy in copies + spread:
        copy.wait_send()
    keep.wait()


def middle_backward(part, middle, cotangent, gain, call):
    rows, width = cotangent.shape
    grad, term, full = square_call(
        middle_back_kernel,
        (
            jax.ShapeDtypeStruct((rows, width), F32),
            jax.ShapeDtypeStruct((1, width), F32),
            jax.ShapeDtypeStruct((4, rows, width), BF),
        ),
        (IN_VMEM, IN_VMEM, ANYWHERE),
        square_scratch(rows, width)
        + [
            pltpu.VMEM((rows, width), BF),
            pltpu.SemaphoreType.DMA((12,)),
            pltpu.SemaphoreType.DMA((12,)),
            pltpu.SemaphoreType.DMA,
        ],
        (part, middle, cotangent, gain[None, :]),
        call,
        2 * cotangent.size,
        "middle_backward",
    )
    return grad, term[0], full.reshape(4 * rows, width)


def input_back_kernel(
    at_value, at_swish, dqk_ref, dv_ref, ds_ref, w_ref, x_ref, grad_ref, gain_ref, dx_ref, term_ref,
    parts, inbox_x, inbox_y, via_x, via_y, out_x, out_y, sends, recvs,
):
    me = lax.axis_index("seq")
    rows = x_ref.shape[0]
    half = rows // 2
    greet((me ^ 1, me ^ 2))
    boxes = (inbox_x, inbox_y, via_x, via_y, out_x, out_y)
    copies, finish, total = square_parts(parts, boxes, sends, recvs, 0)

    def part(k):
        here = block_rows(k, rows)
        parts[k] = (
            times_transposed(dqk_ref[here, :], w_ref[:, :at_value])
            + times_transposed(dv_ref[here, :], w_ref[:, at_value:at_swish])
            + times_transposed(ds_ref[here, :], w_ref[:, at_swish:])
        ).astype(BF)

    part(3)
    copies[0].start()
    copies[1].start()
    part(1)
    copies[2].start()
    part(2)
    copies[3].start()
    part(0)
    finish()
    term = jnp.zeros((1, x_ref.shape[1]), F32)
    for i in range(2):
        here = slice(i * half, (i + 1) * half)
        back, terms = norm_back(x_ref[here, :].astype(F32), total(here), gain_ref[...])
        dx_ref[here, :] = (grad_ref[here, :] + back).astype(BF)
        term = term + jnp.sum(terms, axis=0, keepdims=True)
    term_ref[...] = term
    for copy in copies:
        copy.wait_send()


def input_backward(dqk, dv, ds, weight, x, grad, gain, at_value, at_swish, call):
    rows, width = x.shape
    dx, term = square_call(
        functools.partial(input_back_kernel, at_value, at_swish),
        (
            jax.ShapeDtypeStruct((rows, width), BF),
            jax.ShapeDtypeStruct((1, width), F32),
        ),
        (IN_VMEM, IN_VMEM),
        square_scratch(rows, width)
        + [pltpu.SemaphoreType.DMA((6,)), pltpu.SemaphoreType.DMA((6,))],
        (dqk, dv, ds, weight, x, grad, gain[None, :]),
        call,
        x.size,
        "input_backward",
    )
    return dx, term[0]


def weight_rows(left_ref, right, out_ref):
    @pl.loop(0, out_ref.shape[0] // BLOCK)
    def _(b):
        lanes = rows_of(b)
        out_ref[lanes, :] = transposed_times(left_ref[:, lanes], right).astype(BF)


def gate_back_gather_kernel(
    heads, starts, branch_ref, w_ref, swish_ref, retained_ref, mixed_ref, gated_ref, column_ref,
    share_ref, dswish_ref, dret_ref, dws_ref, dwo_ref, full_ref, wide, sends, recvs, local,
):
    me = lax.axis_index("seq")
    greet((me ^ 1, me ^ 2))
    keep = pltpu.make_async_copy(share_ref, full_ref.at[me], local)
    keep.start()
    copies, finish = square_gather_whole(share_ref, full_ref, sends, recvs, 0)
    for copy in copies[:4]:
        copy.start()
    gate_back_kernel(heads, branch_ref, w_ref, swish_ref, retained_ref, dswish_ref, dret_ref)
    padded = dswish_ref.shape[1]
    spare = lax.broadcasted_iota(jnp.int32, (BLOCK, padded), 1) == heads * VAL_HEAD

    @pl.loop(0, dws_ref.shape[0] // BLOCK)
    def _(b):
        lanes = rows_of(b)
        term = transposed_times(mixed_ref[:, lanes], dswish_ref[...])
        dws_ref[lanes, :] = jnp.where(spare, column_ref[lanes, :], term).astype(BF)

    finish()
    for h in range(heads):
        value_lanes = slice(h * VAL_HEAD, (h + 1) * VAL_HEAD)

        @pl.loop(0, branch_ref.shape[1] // (2 * BLOCK))
        def _(b):
            lanes = pl.ds(pl.multiple_of(b * 2 * BLOCK, 2 * BLOCK), 2 * BLOCK)
            wide[...] = transposed_times(gated_ref[:, value_lanes], branch_ref[:, lanes]).astype(BF)
            for k, start in enumerate(starts):
                dwo_ref[k, h, :, lanes] = wide[start : start + dwo_ref.shape[2], :]

    for copy in copies:
        copy.wait_send()
    keep.wait()


def square_gather_whole(own, out_ref, sends, recvs, first):
    rows = own.shape[0]
    half = -(-rows // 32) * 16
    me = lax.axis_index("seq")
    across, along = me ^ 1, me ^ 2
    spans = (pl.ds(0, half), pl.ds(half, rows - half))

    def part(ref, i):
        return ref.at[spans[i]]

    copies = [
        remote(part(own, 0), part(out_ref.at[me], 0), sends, recvs, first, across),
        remote(part(own, 1), part(out_ref.at[me], 1), sends, recvs, first + 1, along),
        remote(part(own, 1), part(out_ref.at[me], 1), sends, recvs, first + 2, across),
        remote(part(own, 0), part(out_ref.at[me], 0), sends, recvs, first + 3, along),
        remote(
            part(out_ref.at[across], 0), part(out_ref.at[across], 0), sends, recvs, first + 4, along
        ),
        remote(
            part(out_ref.at[along], 1), part(out_ref.at[along], 1), sends, recvs, first + 5, across
        ),
    ]

    def finish():
        copies[0].wait_recv()
        copies[4].start()
        copies[1].wait_recv()
        copies[5].start()
        for copy in copies[2:]:
            copy.wait_recv()

    return copies, finish


def gate_backward_gather(
    branch, weight, swish, retained, mixed, gated, column, share, heads, padded, cut, call
):
    length, width = branch.shape
    starts = [cut.start(k) for k in range(4)]
    return pl.pallas_call(
        functools.partial(gate_back_gather_kernel, heads, starts),
        out_shape=(
            jax.ShapeDtypeStruct((length, padded), BF),
            jax.ShapeDtypeStruct((heads, length, VAL_HEAD), BF),
            jax.ShapeDtypeStruct((width, padded), BF),
            jax.ShapeDtypeStruct((4, heads, cut.width, width), BF),
            jax.ShapeDtypeStruct((4,) + share.shape, BF),
        ),
        in_specs=[IN_VMEM] * 7 + [ANYWHERE],
        out_specs=(IN_VMEM,) * 4 + (ANYWHERE,),
        scratch_shapes=[
            pltpu.VMEM((VAL_HEAD, 2 * BLOCK), BF),
            pltpu.SemaphoreType.DMA((6,)),
            pltpu.SemaphoreType.DMA((6,)),
            pltpu.SemaphoreType.DMA,
        ],
        compiler_params=pltpu.CompilerParams(
            collective_id=call, has_side_effects=True, vmem_limit_bytes=56 * 1024 * 1024
        ),
        cost_estimate=transfer_cost(share.size),
        name="gate_back_gather",
    )(branch, weight, swish, retained, mixed, gated, column, share)


def retention_back_exchange_kernel(
    heads, q_ref, k_ref, v_ref, dret_ref, cos_ref, sin_ref, mixed_ref, send_ref,
    dqk_ref, dv_ref, dwqk_ref, came_ref, dq_sum, dv_sum, sends, recvs, local,
):
    me = lax.axis_index("seq")
    greet((me ^ 1, me ^ 2, me ^ 3))
    keep = pltpu.make_async_copy(send_ref.at[me], came_ref.at[me], local)
    keep.start()
    copies = [
        remote(send_ref.at[me ^ k], came_ref.at[me], sends, recvs, k - 1, me ^ k) for k in (3, 1, 2)
    ]
    for copy in copies:
        copy.start()
    retention_back_kernel(
        heads, q_ref, k_ref, v_ref, dret_ref, cos_ref, sin_ref, dqk_ref, dv_ref, dq_sum, dv_sum
    )
    weight_rows(mixed_ref, dqk_ref[...], dwqk_ref)
    for copy in copies:
        copy.wait()
    keep.wait()


def retention_backward_exchange(q, k, v, dret, cosine, sine, mixed, send, heads, padded, call):
    length, width = mixed.shape
    qk = heads * KEY_HEAD
    return pl.pallas_call(
        functools.partial(retention_back_exchange_kernel, heads),
        out_shape=(
            jax.ShapeDtypeStruct((length, 2 * qk), BF),
            jax.ShapeDtypeStruct((length, padded), BF),
            jax.ShapeDtypeStruct((width, 2 * qk), BF),
            jax.ShapeDtypeStruct(send.shape, BF),
        ),
        in_specs=[IN_VMEM] * 7 + [ANYWHERE],
        out_specs=(IN_VMEM,) * 3 + (ANYWHERE,),
        scratch_shapes=[
            pltpu.VMEM((length, qk), F32),
            pltpu.VMEM((heads, length, VAL_HEAD), BF),
            pltpu.SemaphoreType.DMA((3,)),
            pltpu.SemaphoreType.DMA((3,)),
            pltpu.SemaphoreType.DMA,
        ],
        compiler_params=pltpu.CompilerParams(
            collective_id=call, has_side_effects=True, vmem_limit_bytes=56 * 1024 * 1024
        ),
        cost_estimate=transfer_cost(send.size // 4 * 3 // 2),
        name="retention_back_exchange",
    )(q, k, v, dret, cosine, sine, mixed, send)


def after(values, *others):
    return lax.optimization_barrier((values,) + others)[0]


class Cut:
    def __init__(self, rows, count):
        self.rows, self.count = rows, count
        self.width = -(-rows // (count * 16)) * 16

    def start(self, piece):
        if isinstance(piece, int):
            return min(piece * self.width, self.rows - self.width)
        return jnp.minimum(piece * self.width, self.rows - self.width)

    def skip(self, piece):
        if isinstance(piece, int):
            return min(piece * self.width - self.start(piece), self.width)
        return jnp.minimum(piece * self.width - self.start(piece), self.width)

    def assemble(self, pieces, axis):
        kept = []
        for k, piece in enumerate(pieces):
            if self.skip(k) < self.width:
                kept.append(lax.slice_in_dim(piece, self.skip(k), self.width, axis=axis))
        return jnp.concatenate(kept, axis=axis)


def columns_of(weight, index, width, padded):
    piece = lax.dynamic_slice_in_dim(weight, index * width, width, axis=1)
    return jnp.pad(piece, ((0, 0), (0, padded - width)))


def on_device(
    layer_input,
    mixer_gain,
    query_weight,
    key_weight,
    value_weight,
    swish_weight,
    output_weight,
    channel_gain,
    gelu_weight,
    linear_weight,
    down_weight,
    output_cotangent,
):
    groups, local_length, width = layer_input.shape
    seq_count = lax.axis_size("seq")
    shards = lax.axis_size("fsdp")
    me = lax.axis_index("seq")
    per_device = HEADS // seq_count
    rows_count = groups * local_length
    square = seq_count == 4 and rows_count % 32 == 0
    length = local_length * seq_count
    key_scale = KEY_HEAD ** (-0.5)
    qk = query_weight.shape[1] // seq_count
    vd = value_weight.shape[1] // seq_count
    vd_pad = -(-vd // 128) * 128
    hidden_units = gelu_weight.shape[1]
    own_rows = down_weight.shape[0]
    cut = Cut(own_rows, seq_count)
    ff = shards * cut.width

    def gather_rows(values):
        return lax.all_gather(values, "fsdp", axis=0, tiled=True)

    def scatter_rows(values):
        return lax.psum_scatter(values.astype(BF), "fsdp", scatter_dimension=0, tiled=True)

    attention_piece = jnp.concatenate(
        [
            columns_of(query_weight, me, qk, qk),
            columns_of(key_weight, me, qk, qk),
            columns_of(value_weight, me, vd, vd_pad),
            columns_of(swish_weight, me, vd, vd_pad),
        ],
        axis=1,
    )
    attention_weight = gather_rows(attention_piece)
    output_piece = lax.dynamic_slice_in_dim(output_weight, cut.start(me), cut.width, axis=0)
    output_pieces = gather_rows(output_piece)
    column = lax.broadcasted_iota(jnp.int32, (hidden_units, ff), 0)
    slot = lax.broadcasted_iota(jnp.int32, (hidden_units, ff), 1)
    chosen = (slot // cut.width) * own_rows + cut.start(me) + slot % cut.width
    selector = (column == chosen).astype(BF)
    gate_piece = product(gelu_weight, selector).astype(BF)
    up_piece = product(linear_weight, selector).astype(BF)
    feed_piece = jnp.concatenate([gate_piece, up_piece], axis=1)
    down_piece = lax.dynamic_slice_in_dim(down_weight, cut.start(me), cut.width, axis=0)
    gains = lax.all_gather(jnp.stack([mixer_gain, channel_gain]), "fsdp", axis=1, tiled=True)
    mixer_scale, channel_scale = gains[0].astype(F32), gains[1].astype(F32)

    local_input = layer_input.reshape(rows_count, width)
    upstream = output_cotangent.reshape(rows_count, width)

    def whole(values, call):
        gathered = gather_seq(values, call)
        return gathered.reshape(length * groups, width)

    input_full = whole(local_input, 0)
    upstream_full = whole(after(upstream, input_full), 1)
    inputs = local_input.astype(F32)

    blocks = shards // seq_count
    output_pieces = after(output_pieces, upstream_full)
    swapped = exchange_seq(output_pieces.reshape(seq_count, blocks, cut.width, width), 2)
    output_full = jnp.concatenate(
        [
            cut.assemble([swapped[piece, block] for piece in range(seq_count)], 0)
            for block in range(blocks)
        ],
        axis=0,
    )
    feed_weight = gather_rows(after(feed_piece, swapped))

    cosine, sine = rotation_tables(length, KEY_HEAD // 2)
    mixed_low, query_low, key_low, value_low, swish_pre, retained, gated_low = retention_forward(
        input_full, mixer_scale[None, :], attention_weight, cosine, sine, per_device,
        (qk, 2 * qk, 2 * qk + vd_pad),
    )

    kept_rows = lax.broadcasted_iota(jnp.int32, down_piece.shape, 0) >= cut.skip(me)
    down_full = gather_rows(after(jnp.where(kept_rows, down_piece, jnp.zeros_like(down_piece)), gated_low))
    if square:
        middle, channel_full = project_and_norm(
            gated_low, output_full, local_input, channel_scale, 3
        )
    else:
        middle = inputs + scatter_seq(product(gated_low, output_full).astype(BF), 3)
        channel_full = whole(normalize(middle, channel_scale).astype(BF), 4)

    gate_pre, up_pre, hidden_low = feed_forward(channel_full, feed_weight)
    down_term = transposed_times(hidden_low, upstream_full).astype(BF)
    down_share = scatter_rows(down_term)

    feed_low_grad, channel_part, hidden_part = feed_backward(
        after(upstream_full, down_term), gate_pre, up_pre, hidden_low, feed_weight, down_full
    )
    feed_term = transposed_times(channel_full, feed_low_grad).astype(BF)
    feed_share = scatter_rows(feed_term)
    channel_part = after(channel_part, feed_term)
    if square:
        middle_grad, channel_term, branch_full = middle_backward(
            channel_part, middle, upstream, channel_scale, 6
        )
    else:
        middle_local, channel_terms = norm_back(
            middle, scatter_seq(channel_part, 6), channel_scale
        )
        channel_term = jnp.sum(channel_terms, axis=0)
        middle_grad = upstream.astype(F32) + middle_local
        branch_full = whole(middle_grad.astype(BF), 7)

    at_value, at_swish = 2 * qk, 2 * qk + vd_pad
    spare = lax.broadcasted_iota(jnp.int32, (width, vd_pad), 1) == vd
    if square:
        swish_grad, retained_grad, swish_term, output_send, down_all = gate_backward_gather(
            branch_full, output_full, swish_pre, retained, mixed_low, gated_low,
            channel_term[:, None], down_share, per_device, vd_pad, cut, 10,
        )
        swish_share = scatter_rows(swish_term)
        key_grad, value_grad, key_term, output_swapped = retention_backward_exchange(
            query_low, key_low, value_low, retained_grad, cosine, sine, mixed_low,
            after(output_send, feed_share), per_device, vd_pad, 8,
        )
        output_share = scatter_rows(output_swapped.reshape(shards * cut.width, width))
        key_share = scatter_rows(key_term)
        input_gradient, mixer_term = input_backward(
            key_grad, value_grad, swish_grad, attention_weight, local_input, middle_grad,
            mixer_scale, at_value, at_swish, 9,
        )
    else:
        swish_grad, retained_grad = gate_backward(
            branch_full, output_full, swish_pre, retained, per_device, vd_pad
        )
        swish_term = transposed_times(mixed_low, swish_grad)
        swish_term = jnp.where(spare, channel_term[:, None], swish_term).astype(BF)
        swish_share = scatter_rows(swish_term)
        down_all = gather_seq(down_share, 10)
        key_grad, value_grad = retention_backward(
            query_low, key_low, value_low, retained_grad, cosine, sine, per_device, vd_pad
        )
        key_term = transposed_times(mixed_low, key_grad).astype(BF)
        key_share = scatter_rows(key_term)
        mixed_part = (
            times_transposed(key_grad, attention_weight[:, :at_value])
            + times_transposed(value_grad, attention_weight[:, at_value:at_swish])
            + times_transposed(swish_grad, attention_weight[:, at_swish:])
        )
        input_local, mixer_terms = norm_back(
            inputs, scatter_seq(mixed_part.astype(BF), 9), mixer_scale
        )
        mixer_term = jnp.sum(mixer_terms, axis=0)
        input_gradient = (middle_grad + input_local).astype(BF)
        output_term = transposed_times(gated_low, branch_full).astype(BF)
        output_term = output_term.reshape(blocks, own_rows, width)
        output_send = jnp.stack(
            [
                lax.slice_in_dim(output_term, cut.start(k), cut.start(k) + cut.width, axis=1)
                for k in range(seq_count)
            ]
        )
        output_swapped = exchange_seq(output_send, 8)
        output_share = scatter_rows(output_swapped.reshape(shards * cut.width, width))
    input_gradient = input_gradient.reshape(groups, local_length, width)
    value_term = transposed_times(mixed_low, value_grad)
    value_term = jnp.where(spare, mixer_term[:, None], value_term).astype(BF)
    value_share = scatter_rows(value_term)

    result = middle + scatter_seq(after(hidden_part, value_term), 5)
    layer_output = result.astype(BF).reshape(groups, local_length, width)
    feed_all = gather_seq(after(feed_share, layer_output), 11)
    swish_all = gather_seq(after(swish_share, feed_all), 13)
    output_all = gather_seq(after(output_share, swish_all), 12)
    key_all = gather_seq(after(key_share, output_all), 15)
    value_all = gather_seq(after(value_share, key_all), 14)
    down_gradient = cut.assemble([down_all[k] for k in range(seq_count)], 0).astype(F32)
    output_gradient = cut.assemble([output_all[k] for k in range(seq_count)], 0).astype(F32)

    def hidden_order(at):
        pieces = [feed_all[k][:, at : at + ff] for k in range(seq_count)]
        return jnp.concatenate(
            [
                cut.assemble(
                    [piece[:, f * cut.width : (f + 1) * cut.width] for piece in pieces], 1
                )
                for f in range(shards)
            ],
            axis=1,
        ).astype(F32)

    def attention_order(gathered, at, wide):
        pieces = [gathered[k][:, at : at + wide] for k in range(seq_count)]
        return jnp.concatenate(pieces, axis=1).astype(F32)

    def gain_order(gathered):
        return sum(gathered[k][:, vd].astype(F32) for k in range(seq_count))

    return (
        layer_output,
        input_gradient,
        gain_order(value_all),
        attention_order(key_all, 0, qk),
        attention_order(key_all, qk, qk),
        attention_order(value_all, 0, vd),
        attention_order(swish_all, 0, vd),
        output_gradient,
        gain_order(swish_all),
        hidden_order(0),
        hidden_order(ff),
        down_gradient,
    )


def solution(mesh):
    tokens, rows, vector = P("fsdp", "seq", None), P("fsdp", None), P("fsdp")
    return jax.shard_map(
        on_device,
        mesh=mesh,
        in_specs=(
            tokens, vector, rows, rows, rows, rows, rows, vector, rows, rows, rows, tokens,
        ),
        out_specs=(
            tokens, tokens, vector, rows, rows, rows, rows, rows, vector, rows, rows, rows,
        ),
        check_vma=False,
    )
```

```python
import functools
import math

import jax
import jax.numpy as jnp
from jax import lax
from jax.experimental import pallas as pl
from jax.experimental.pallas import tpu as pltpu
from jax.sharding import PartitionSpec as P

HEADS = 8
KEY_HEAD = 256
VAL_HEAD = 432
EPSILON = 1e-05
MESH = pl.DeviceIdType.MESH
BF = jnp.bfloat16
F32 = jnp.float32


def product(left, right):
    return jnp.dot(left, right, preferred_element_type=F32)


def times_transposed(left, right):
    return lax.dot_general(left, right, (((1,), (1,)), ((), ())), preferred_element_type=F32)


def transposed_times(left, right):
    return lax.dot_general(left, right, (((0,), (0,)), ((), ())), preferred_element_type=F32)


def normalize(values, gain):
    centered = values - jnp.mean(values, axis=-1, keepdims=True)
    spread = lax.rsqrt(jnp.mean(centered * centered, axis=-1, keepdims=True) + EPSILON)
    return centered * spread * gain


def rotation_tables(length, half_width):
    rates = jnp.exp(-math.log(10000.0) * jnp.arange(half_width, dtype=F32) / (half_width - 1))
    turned = jnp.arange(length, dtype=F32)[:, None] * rates[None, :]
    return (jnp.cos(turned), jnp.sin(turned))


def pad_lanes(pieces, width):
    have = sum(piece.shape[1] for piece in pieces)
    if have < width:
        pieces = pieces + [jnp.zeros((pieces[0].shape[0], width - have), pieces[0].dtype)]
    return jnp.concatenate(pieces, axis=1) if len(pieces) > 1 else pieces[0]


def rotate_pair(values, cosine, sine, back=False):
    half = KEY_HEAD // 2
    first, second = values[:, :half], values[:, half:]
    if back:
        return jnp.concatenate([first * cosine + second * sine, second * cosine - first * sine], 1)
    return jnp.concatenate([first * cosine - second * sine, second * cosine + first * sine], 1)


BLOCK = 256


def head_rate(head):
    ids = jnp.full((1, 1), head, jnp.int32).astype(F32)
    return jnp.log1p(-jnp.exp2(-5.0 - ids))


def decay_tile(rate):
    gap = lax.broadcasted_iota(jnp.int32, (BLOCK, BLOCK), 0) - lax.broadcasted_iota(
        jnp.int32, (BLOCK, BLOCK), 1
    )
    full = jnp.exp(gap.astype(F32) * rate)
    return full, jnp.where(gap >= 0, full, 0.0)


def norm_parts(values):
    centered = values - jnp.mean(values, axis=-1, keepdims=True)
    variance = jnp.mean(centered * centered, axis=-1, keepdims=True)
    factor = lax.rsqrt(jnp.maximum(variance, 1.0))
    return centered * factor, factor, variance > 1.0


def rows_of(block):
    return pl.ds(pl.multiple_of(block * BLOCK, BLOCK), BLOCK)


def retention_kernel(
    heads, offsets, x_ref, gain_ref, w_ref, cos_ref, sin_ref,
    mixed_ref, q_ref, k_ref, v_ref, swish_ref, retained_ref, gated_ref,
):
    first_head = lax.axis_index("seq") * heads
    at_key, at_value, at_swish = offsets
    value_width = heads * VAL_HEAD
    blocks = x_ref.shape[0] // BLOCK
    rates = [head_rate(first_head + h) for h in range(heads)]

    @pl.loop(0, blocks)
    def _(i):
        rows = rows_of(i)
        x = x_ref[rows, :].astype(F32)
        mixed = normalize(x, gain_ref[...]).astype(BF)
        mixed_ref[rows, :] = mixed
        cosine, sine = cos_ref[rows, :], sin_ref[rows, :]
        query = product(mixed, w_ref[:, :at_key])
        for h in range(heads):
            lanes = slice(h * KEY_HEAD, (h + 1) * KEY_HEAD)
            q_ref[rows, lanes] = rotate_pair(query[:, lanes], cosine, sine).astype(BF)
        key = product(mixed, w_ref[:, at_key:at_value])
        for h in range(heads):
            lanes = slice(h * KEY_HEAD, (h + 1) * KEY_HEAD)
            turned = rotate_pair(key[:, lanes], cosine, sine) * (KEY_HEAD**-0.5)
            k_ref[rows, lanes] = turned.astype(BF)
        value = product(mixed, w_ref[:, at_value:at_swish])
        for h in range(heads):
            v_ref[h, rows, :] = value[:, h * VAL_HEAD : (h + 1) * VAL_HEAD].astype(BF)
        swish = product(mixed, w_ref[:, at_swish:])[:, :value_width]
        swish_ref[rows, :] = swish

        gated = []
        for h in range(heads):
            lanes = slice(h * KEY_HEAD, (h + 1) * KEY_HEAD)
            full, lower = decay_tile(rates[h])
            q = q_ref[rows, lanes]
            scores = times_transposed(q, k_ref[rows, lanes])
            total = product((scores * lower).astype(BF), v_ref[h, rows, :])

            def earlier(j, total):
                there = rows_of(j)
                scores = times_transposed(q, k_ref[there, lanes])
                far = jnp.exp(rates[h] * ((i - j) * BLOCK).astype(F32))
                return total + product((scores * (full * far)).astype(BF), v_ref[h, there, :])

            total = lax.fori_loop(0, i, earlier, total)
            retained = total.astype(BF)
            retained_ref[h, rows, :] = retained
            unit, _, _ = norm_parts(retained.astype(F32))
            s = swish[:, h * VAL_HEAD : (h + 1) * VAL_HEAD]
            gated.append((s * jax.nn.sigmoid(s) * unit).astype(BF))
        gated_ref[rows, :] = jnp.concatenate(gated, axis=1) if heads > 1 else gated[0]


def vmem_call(body, out_shapes, scratch, limit, cost, name):
    return pl.pallas_call(
        body,
        out_shape=out_shapes,
        scratch_shapes=scratch,
        compiler_params=pltpu.CompilerParams(vmem_limit_bytes=limit * 1024 * 1024),
        cost_estimate=pl.CostEstimate(flops=cost, bytes_accessed=0, transcendentals=0),
        name=name,
    )


def retention_forward(x, gain, weight, cosine, sine, heads, offsets):
    length, width = x.shape
    qk, vd = heads * KEY_HEAD, heads * VAL_HEAD
    return vmem_call(
        functools.partial(retention_kernel, heads, offsets),
        (
            jax.ShapeDtypeStruct((length, width), BF),
            jax.ShapeDtypeStruct((length, qk), BF),
            jax.ShapeDtypeStruct((length, qk), BF),
            jax.ShapeDtypeStruct((heads, length, VAL_HEAD), BF),
            jax.ShapeDtypeStruct((length, vd), F32),
            jax.ShapeDtypeStruct((heads, length, VAL_HEAD), BF),
            jax.ShapeDtypeStruct((length, vd), BF),
        ),
        [],
        56,
        30_000_000_000,
        "retention",
    )(x, gain, weight, cosine, sine)


def gate_back_kernel(heads, branch_ref, w_ref, swish_ref, retained_ref, dswish_ref, dret_ref):
    blocks = branch_ref.shape[0] // BLOCK

    @pl.loop(0, blocks)
    def _(i):
        rows = rows_of(i)
        gated_grad = times_transposed(branch_ref[rows, :], w_ref[...])
        swish_parts = []
        for h in range(heads):
            lanes = slice(h * VAL_HEAD, (h + 1) * VAL_HEAD)
            grad, s = gated_grad[:, lanes], swish_ref[rows, lanes]
            gate = jax.nn.sigmoid(s)
            unit, factor, above = norm_parts(retained_ref[h, rows, :].astype(F32))
            swish_parts.append((grad * unit * (gate * (1.0 + s * (1.0 - gate)))).astype(BF))
            g = grad * (s * gate)
            along = jnp.where(above, jnp.mean(g * unit, axis=-1, keepdims=True), 0.0)
            back = factor * (g - jnp.mean(g, axis=-1, keepdims=True) - unit * along)
            dret_ref[h, rows, :] = back.astype(BF)
        dswish_ref[rows, :] = pad_lanes(swish_parts, dswish_ref.shape[1])


def gate_backward(branch, weight, swish, retained, heads, padded):
    length = branch.shape[0]
    return vmem_call(
        functools.partial(gate_back_kernel, heads),
        (
            jax.ShapeDtypeStruct((length, padded), BF),
            jax.ShapeDtypeStruct((heads, length, VAL_HEAD), BF),
        ),
        [],
        48,
        12_000_000_000,
        "gate_back",
    )(branch, weight, swish, retained)


def retention_back_kernel(
    heads, q_ref, k_ref, v_ref, dret_ref, cos_ref, sin_ref, dqk_ref, dv_ref, dq_sum, dv_sum
):
    first_head = lax.axis_index("seq") * heads
    blocks = q_ref.shape[0] // BLOCK
    qk = heads * KEY_HEAD
    dq_sum[...] = jnp.zeros_like(dq_sum)
    for h in range(heads):
        rate = head_rate(first_head + h)
        lanes = slice(h * KEY_HEAD, (h + 1) * KEY_HEAD)

        @pl.loop(0, blocks)
        def _(j):
            there = rows_of(j)
            full, lower = decay_tile(rate)
            key, value = k_ref[there, lanes], v_ref[h, there, :]

            def step(i, decay, sums):
                rows = rows_of(i)
                query, grad = q_ref[rows, lanes], dret_ref[h, rows, :]
                weights = (times_transposed(query, key) * decay).astype(BF)
                score = (times_transposed(grad, value) * decay).astype(BF)
                dq_sum[rows, lanes] += product(score, key)
                return (
                    sums[0] + transposed_times(score, query),
                    sums[1] + transposed_times(weights, grad),
                )

            sums = (jnp.zeros((BLOCK, KEY_HEAD), F32), jnp.zeros((BLOCK, VAL_HEAD), F32))
            sums = step(j, lower, sums)

            def later(i, sums):
                return step(i, full * jnp.exp(rate * ((i - j) * BLOCK).astype(F32)), sums)

            dk, dv = lax.fori_loop(j + 1, blocks, later, sums)
            dk = rotate_pair(
                dk.astype(BF).astype(F32), cos_ref[there, :], sin_ref[there, :], back=True
            )
            dqk_ref[there, qk + h * KEY_HEAD : qk + (h + 1) * KEY_HEAD] = (
                dk * (KEY_HEAD**-0.5)
            ).astype(BF)
            dv_sum[h, there, :] = dv.astype(BF)

    @pl.loop(0, blocks)
    def _(i):
        rows = rows_of(i)
        cosine, sine = cos_ref[rows, :], sin_ref[rows, :]
        for h in range(heads):
            lanes = slice(h * KEY_HEAD, (h + 1) * KEY_HEAD)
            dq = dq_sum[rows, lanes].astype(BF).astype(F32)
            dqk_ref[rows, lanes] = rotate_pair(dq, cosine, sine, back=True).astype(BF)
        dv_ref[rows, :] = pad_lanes([dv_sum[h, rows, :] for h in range(heads)], dv_ref.shape[1])


def retention_backward(q, k, v, dret, cosine, sine, heads, padded):
    length = q.shape[0]
    qk = heads * KEY_HEAD
    return vmem_call(
        functools.partial(retention_back_kernel, heads),
        (
            jax.ShapeDtypeStruct((length, 2 * qk), BF),
            jax.ShapeDtypeStruct((length, padded), BF),
        ),
        [pltpu.VMEM((length, qk), F32), pltpu.VMEM((heads, length, VAL_HEAD), BF)],
        48,
        12_000_000_000,
        "retention_back",
    )(q, k, v, dret, cosine, sine)


def transfer_cost(elements):
    return pl.CostEstimate(flops=0, bytes_accessed=elements * 240, transcendentals=0)


def greet(peers):
    barrier = pltpu.get_barrier_semaphore()
    for peer in peers:
        pl.semaphore_signal(barrier, inc=1, device_id={"seq": peer}, device_id_type=MESH)
    pl.semaphore_wait(barrier, len(peers))


def remote(source, target, sends, recvs, k, to):
    return pltpu.make_async_remote_copy(
        src_ref=source,
        dst_ref=target,
        send_sem=sends.at[k],
        recv_sem=recvs.at[k],
        device_id={"seq": to},
        device_id_type=MESH,
    )


def gather_square_kernel(x_ref, o_ref, sends, recvs, local):
    me = lax.axis_index("seq")
    across, along = me ^ 1, me ^ 2
    half = x_ref.shape[0] // 2
    greet((across, along))
    own = pltpu.make_async_copy(x_ref, o_ref.at[me], local)
    own.start()

    def part(ref, i):
        return ref.at[pl.ds(i * half, half)]

    first = (
        remote(part(x_ref, 0), part(o_ref.at[me], 0), sends, recvs, 0, across),
        remote(part(x_ref, 1), part(o_ref.at[me], 1), sends, recvs, 1, along),
        remote(part(x_ref, 1), part(o_ref.at[me], 1), sends, recvs, 2, across),
        remote(part(x_ref, 0), part(o_ref.at[me], 0), sends, recvs, 3, along),
    )
    for copy in first:
        copy.start()
    first[0].wait_recv()
    on_along = remote(part(o_ref.at[across], 0), part(o_ref.at[across], 0), sends, recvs, 4, along)
    on_along.start()
    first[1].wait_recv()
    on_across = remote(part(o_ref.at[along], 1), part(o_ref.at[along], 1), sends, recvs, 5, across)
    on_across.start()
    first[2].wait_recv()
    first[3].wait_recv()
    on_along.wait_recv()
    on_across.wait_recv()
    for copy in first + (on_along, on_across):
        copy.wait_send()
    own.wait()


def gather_kernel(count, x_ref, o_ref, sends, recvs, local):
    me = lax.axis_index("seq")
    peers = [lax.rem(me + step, count) for step in range(1, count)]
    greet(peers)
    own = pltpu.make_async_copy(x_ref, o_ref.at[me], local)
    own.start()
    copies = [remote(x_ref, o_ref.at[me], sends, recvs, k, to) for k, to in enumerate(peers)]
    for copy in copies:
        copy.start()
    for copy in copies:
        copy.wait()
    own.wait()


def gather_seq(values, call):
    count = lax.axis_size("seq")
    square = count == 4 and values.shape[0] % 32 == 0
    body = gather_square_kernel if square else functools.partial(gather_kernel, count)
    copies = 6 if square else count - 1
    return pl.pallas_call(
        body,
        out_shape=jax.ShapeDtypeStruct((count,) + values.shape, values.dtype),
        in_specs=[pl.BlockSpec(memory_space=pl.ANY)],
        out_specs=pl.BlockSpec(memory_space=pl.ANY),
        scratch_shapes=[
            pltpu.SemaphoreType.DMA((copies,)),
            pltpu.SemaphoreType.DMA((copies,)),
            pltpu.SemaphoreType.DMA,
        ],
        compiler_params=pltpu.CompilerParams(collective_id=call, has_side_effects=True),
        cost_estimate=transfer_cost(values.size),
        name=f"gather_seq_{call}",
    )(values)


def exchange_kernel(count, x_ref, o_ref, sends, recvs, local):
    me = lax.axis_index("seq")
    peers = [lax.rem(me + step, count) for step in range(1, count)]
    greet(peers)
    own = pltpu.make_async_copy(x_ref.at[me], o_ref.at[me], local)
    own.start()
    copies = [remote(x_ref.at[to], o_ref.at[me], sends, recvs, k, to) for k, to in enumerate(peers)]
    for copy in copies:
        copy.start()
    for copy in copies:
        copy.wait()
    own.wait()


def exchange_seq(values, call):
    count = lax.axis_size("seq")
    return pl.pallas_call(
        functools.partial(exchange_kernel, count),
        out_shape=jax.ShapeDtypeStruct(values.shape, values.dtype),
        in_specs=[pl.BlockSpec(memory_space=pl.ANY)],
        out_specs=pl.BlockSpec(memory_space=pl.ANY),
        scratch_shapes=[
            pltpu.SemaphoreType.DMA((count - 1,)),
            pltpu.SemaphoreType.DMA((count - 1,)),
            pltpu.SemaphoreType.DMA,
        ],
        compiler_params=pltpu.CompilerParams(collective_id=call, has_side_effects=True),
        cost_estimate=transfer_cost(values.size),
        name=f"exchange_seq_{call}",
    )(values)


def scatter_square_kernel(p_ref, o_ref, inbox_x, inbox_y, via_x, via_y, out_x, out_y, sends, recvs):
    me = lax.axis_index("seq")
    across, along, corner = me ^ 1, me ^ 2, me ^ 3
    half = p_ref.shape[1] // 2
    low, high = pl.ds(0, half), pl.ds(half, half)
    greet((across, along))
    first = (
        remote(p_ref.at[corner, low], via_x, sends, recvs, 0, across),
        remote(p_ref.at[corner, high], via_y, sends, recvs, 1, along),
        remote(p_ref.at[across, low], inbox_x.at[low], sends, recvs, 2, across),
        remote(p_ref.at[along, high], inbox_y.at[high], sends, recvs, 3, along),
    )
    for copy in first:
        copy.start()
    first[0].wait_recv()
    out_y[...] = (p_ref[along, :half].astype(F32) + via_x[...].astype(F32)).astype(BF)
    to_along = remote(out_y, inbox_y.at[low], sends, recvs, 4, along)
    to_along.start()
    first[1].wait_recv()
    out_x[...] = (p_ref[across, half:].astype(F32) + via_y[...].astype(F32)).astype(BF)
    to_across = remote(out_x, inbox_x.at[high], sends, recvs, 5, across)
    to_across.start()
    first[2].wait_recv()
    first[3].wait_recv()
    to_along.wait_recv()
    to_across.wait_recv()
    o_ref[...] = (
        p_ref[me].astype(F32) + inbox_x[...].astype(F32) + inbox_y[...].astype(F32)
    )
    for copy in first + (to_along, to_across):
        copy.wait_send()


def scatter_kernel(count, p_ref, o_ref, inbox, sends, recvs):
    me = lax.axis_index("seq")
    peers = [lax.rem(me + step, count) for step in range(1, count)]
    greet(peers)
    copies = [remote(p_ref.at[to], inbox.at[k], sends, recvs, k, to) for k, to in enumerate(peers)]
    for copy in copies:
        copy.start()
    total = p_ref[me].astype(F32)
    for k, copy in enumerate(copies):
        copy.wait_recv()
        total = total + inbox[k].astype(F32)
    o_ref[...] = total
    for copy in copies:
        copy.wait_send()


def scatter_seq(parts, call):
    count = lax.axis_size("seq")
    rows, width = parts.shape[0] // count, parts.shape[1]
    parts = parts.reshape(count, rows, width)
    if count == 4 and rows % 32 == 0:
        body = scatter_square_kernel
        scratch = [pltpu.VMEM((rows, width), BF)] * 2 + [pltpu.VMEM((rows // 2, width), BF)] * 4
        copies = 6
    else:
        body = functools.partial(scatter_kernel, count)
        scratch = [pltpu.VMEM((count - 1, rows, width), BF)]
        copies = count - 1
    return pl.pallas_call(
        body,
        out_shape=jax.ShapeDtypeStruct((rows, width), F32),
        in_specs=[pl.BlockSpec(memory_space=pltpu.VMEM)],
        out_specs=pl.BlockSpec(memory_space=pltpu.VMEM),
        scratch_shapes=scratch
        + [pltpu.SemaphoreType.DMA((copies,)), pltpu.SemaphoreType.DMA((copies,))],
        compiler_params=pltpu.CompilerParams(
            collective_id=call, has_side_effects=True, vmem_limit_bytes=32 * 1024 * 1024
        ),
        cost_estimate=transfer_cost(rows * width),
        name=f"scatter_seq_{call}",
    )(parts)


def feed_forward_kernel(ff, x_ref, w_ref, gate_ref, up_ref, hidden_ref):
    both = product(x_ref[...], w_ref[...])
    gate, up = both[:, :ff], both[:, ff:]
    gate_ref[...] = gate
    up_ref[...] = up
    hidden_ref[...] = (gate * (0.5 + 0.5 * lax.erf(gate * math.sqrt(0.5))) * up).astype(BF)


def feed_back_kernel(
    ff, c_ref, gate_ref, up_ref, hidden_ref, w_ref, down_ref, both_ref, part_ref, out_ref
):
    gate, up = gate_ref[...], up_ref[...]
    out_ref[...] = product(hidden_ref[...], down_ref[...]).astype(BF)
    hidden_grad = times_transposed(c_ref[...], down_ref[...])
    bell = 0.5 + 0.5 * lax.erf(gate * math.sqrt(0.5))
    slope = bell + gate * (math.sqrt(0.5 / math.pi) * jnp.exp(-0.5 * gate * gate))
    both = jnp.concatenate([hidden_grad * up * slope, hidden_grad * (gate * bell)], axis=1)
    both = both.astype(BF)
    both_ref[...] = both
    part_ref[...] = times_transposed(both, w_ref[...]).astype(BF)


def by_rows(block, width):
    return pl.BlockSpec((block, width), lambda i: (i, 0))


def kept(shape):
    return pl.BlockSpec(shape, lambda i: (0, 0), pipeline_mode=pl.Buffered(1))


FEED_BLOCK = 256


def feed_forward(x, weight):
    length, width = x.shape
    ff = weight.shape[1] // 2
    return pl.pallas_call(
        functools.partial(feed_forward_kernel, ff),
        grid=(length // FEED_BLOCK,),
        in_specs=[by_rows(FEED_BLOCK, width), kept(weight.shape)],
        out_specs=[by_rows(FEED_BLOCK, ff)] * 3,
        out_shape=(
            jax.ShapeDtypeStruct((length, ff), F32),
            jax.ShapeDtypeStruct((length, ff), F32),
            jax.ShapeDtypeStruct((length, ff), BF),
        ),
        compiler_params=pltpu.CompilerParams(vmem_limit_bytes=48 * 1024 * 1024),
        cost_estimate=pl.CostEstimate(
            flops=4 * length * width * ff, bytes_accessed=weight.size * 4, transcendentals=0
        ),
        name="feed_forward",
    )(x, weight)


def feed_backward(cotangent, gate, up, hidden, weight, down):
    length, width = cotangent.shape
    ff = weight.shape[1] // 2
    return pl.pallas_call(
        functools.partial(feed_back_kernel, ff),
        grid=(length // FEED_BLOCK,),
        in_specs=[by_rows(FEED_BLOCK, width)]
        + [by_rows(FEED_BLOCK, ff)] * 3
        + [kept(weight.shape), kept(down.shape)],
        out_specs=[
            by_rows(FEED_BLOCK, 2 * ff),
            by_rows(FEED_BLOCK, width),
            by_rows(FEED_BLOCK, width),
        ],
        out_shape=(
            jax.ShapeDtypeStruct((length, 2 * ff), BF),
            jax.ShapeDtypeStruct((length, width), BF),
            jax.ShapeDtypeStruct((length, width), BF),
        ),
        compiler_params=pltpu.CompilerParams(vmem_limit_bytes=56 * 1024 * 1024),
        cost_estimate=pl.CostEstimate(
            flops=8 * length * width * ff, bytes_accessed=weight.size * 4, transcendentals=0
        ),
        name="feed_back",
    )(cotangent, gate, up, hidden, weight, down)


def square_parts(parts, boxes, sends, recvs, first):
    me = lax.axis_index("seq")
    across, along = me ^ 1, me ^ 2
    inbox_x, inbox_y, via_x, via_y, out_x, out_y = boxes
    half = via_x.shape[0]
    low, high = pl.ds(0, half), pl.ds(half, half)
    copies = [
        remote(parts.at[3, low], via_x, sends, recvs, first, across),
        remote(parts.at[3, high], via_y, sends, recvs, first + 1, along),
        remote(parts.at[1, low], inbox_x.at[low], sends, recvs, first + 2, across),
        remote(parts.at[2, high], inbox_y.at[high], sends, recvs, first + 3, along),
        remote(out_y, inbox_y.at[low], sends, recvs, first + 4, along),
        remote(out_x, inbox_x.at[high], sends, recvs, first + 5, across),
    ]

    def finish():
        copies[0].wait_recv()
        out_y[...] = (parts[2, :half].astype(F32) + via_x[...].astype(F32)).astype(BF)
        copies[4].start()
        copies[1].wait_recv()
        out_x[...] = (parts[1, half:].astype(F32) + via_y[...].astype(F32)).astype(BF)
        copies[5].start()
        for copy in copies[2:]:
            copy.wait_recv()

    def total(rows):
        return (
            parts[0, rows].astype(F32)
            + inbox_x[rows, :].astype(F32)
            + inbox_y[rows, :].astype(F32)
        )

    return copies, finish, total


def square_gather(own, out_ref, sends, recvs, first):
    me = lax.axis_index("seq")
    across, along = me ^ 1, me ^ 2
    half = own.shape[0] // 2

    def part(ref, i):
        return ref.at[pl.ds(i * half, half)]

    copies = [
        remote(part(own, 0), part(out_ref.at[me], 0), sends, recvs, first, across),
        remote(part(own, 1), part(out_ref.at[me], 1), sends, recvs, first + 1, along),
        remote(part(own, 1), part(out_ref.at[me], 1), sends, recvs, first + 2, across),
        remote(part(own, 0), part(out_ref.at[me], 0), sends, recvs, first + 3, along),
        remote(
            part(out_ref.at[across], 0), part(out_ref.at[across], 0), sends, recvs, first + 4, along
        ),
        remote(
            part(out_ref.at[along], 1), part(out_ref.at[along], 1), sends, recvs, first + 5, across
        ),
    ]

    def finish():
        copies[0].wait_recv()
        copies[4].start()
        copies[1].wait_recv()
        copies[5].start()
        for copy in copies[2:]:
            copy.wait_recv()

    return copies, finish


def block_rows(k, rows):
    return pl.ds(pl.multiple_of((lax.axis_index("seq") ^ k) * rows, rows), rows)


class Moves:
    def __init__(self, sems):
        self.sems, self.used, self.open = sems, 0, []

    def start(self, source, target):
        copy = pltpu.make_async_copy(source, target, self.sems.at[self.used])
        self.used += 1
        copy.start()
        return copy

    def store(self, source, target):
        self.open.append(self.start(source, target))

    def close(self):
        for copy in self.open:
            copy.wait()


def project_kernel(
    g_any, w_any, x_ref, gain_ref, middle_ref, own_ref,
    g_ref, w_ref, parts, inbox_x, inbox_y, via_x, via_y, out_x, out_y, sends, recvs, locals_,
):
    me = lax.axis_index("seq")
    rows = x_ref.shape[0]
    half = rows // 2
    moves = Moves(locals_)
    load_w = moves.start(w_any, w_ref)
    load_g = moves.start(g_any, g_ref)
    greet((me ^ 1, me ^ 2))
    boxes = (inbox_x, inbox_y, via_x, via_y, out_x, out_y)
    copies, finish, total = square_parts(parts, boxes, sends, recvs, 0)

    def part(k):
        parts[k] = product(g_ref[block_rows(k, rows), :], w_ref[...]).astype(BF)

    load_w.wait()
    load_g.wait()
    part(3)
    copies[0].start()
    copies[1].start()
    part(1)
    copies[2].start()
    part(2)
    copies[3].start()
    part(0)
    finish()
    for i in range(2):
        here = slice(i * half, (i + 1) * half)
        middle = x_ref[here, :].astype(F32) + total(here)
        middle_ref[here, :] = middle
        own_ref[here, :] = normalize(middle, gain_ref[...]).astype(BF)
    for copy in copies:
        copy.wait_send()


def square_scratch(rows, width):
    return [
        pltpu.VMEM((4, rows, width), BF),
        pltpu.VMEM((rows, width), BF),
        pltpu.VMEM((rows, width), BF),
        pltpu.VMEM((rows // 2, width), BF),
        pltpu.VMEM((rows // 2, width), BF),
        pltpu.VMEM((rows // 2, width), BF),
        pltpu.VMEM((rows // 2, width), BF),
    ]


IN_VMEM = pl.BlockSpec(memory_space=pltpu.VMEM)
ANYWHERE = pl.BlockSpec(memory_space=pl.ANY)


def square_call(body, out_shape, out_specs, scratch, inputs, call, cost, name):
    return pl.pallas_call(
        body,
        out_shape=out_shape,
        in_specs=[IN_VMEM] * len(inputs),
        out_specs=out_specs,
        scratch_shapes=scratch,
        compiler_params=pltpu.CompilerParams(
            collective_id=call, has_side_effects=True, vmem_limit_bytes=56 * 1024 * 1024
        ),
        cost_estimate=transfer_cost(cost),
        name=name,
    )(*inputs)


def comm_call(body, inputs, outputs, scratch, remotes, moves, call, cost, name):
    return pl.pallas_call(
        body,
        out_shape=tuple(jax.ShapeDtypeStruct(shape, kind) for shape, kind, _ in outputs),
        in_specs=[IN_VMEM if whole else ANYWHERE for _, whole in inputs],
        out_specs=tuple(IN_VMEM if whole else ANYWHERE for _, _, whole in outputs),
        scratch_shapes=scratch
        + [
            pltpu.SemaphoreType.DMA((remotes,)),
            pltpu.SemaphoreType.DMA((remotes,)),
            pltpu.SemaphoreType.DMA((moves,)),
        ],
        compiler_params=pltpu.CompilerParams(
            collective_id=call, has_side_effects=True, vmem_limit_bytes=60 * 1024 * 1024
        ),
        cost_estimate=transfer_cost(cost),
        name=name,
    )(*[value for value, _ in inputs])


def project_and_norm(gated, weight, x, gain, call):
    rows, width = x.shape
    return comm_call(
        project_kernel,
        [(gated, False), (weight, False), (x, True), (gain[None, :], True)],
        [((rows, width), F32, True), ((rows, width), BF, True)],
        [pltpu.VMEM(gated.shape, BF), pltpu.VMEM(weight.shape, BF)] + square_scratch(rows, width),
        6,
        2,
        call,
        x.size,
        "project_and_norm",
    )


def feed_forward_gather_kernel(
    ff, x_any, w_any, c_any, both_any, hidden_any, down_any, full_any,
    full, w_ref, c_ref, both_ref, hidden_ref, total, down_ref, sends, recvs, locals_,
):
    me = lax.axis_index("seq")
    rows = x_any.shape[0]
    moves = Moves(locals_)
    load_x = moves.start(x_any, full.at[me])
    load_w = moves.start(w_any, w_ref)
    load_c = moves.start(c_any, c_ref)
    greet((me ^ 1, me ^ 2))
    load_x.wait()
    copies, _ = square_gather(full.at[me], full, sends, recvs, 0)
    for copy in copies[:4]:
        copy.start()

    def block(k):
        here = block_rows(k, rows)
        x = full[me ^ k]
        moves.store(full.at[me ^ k], full_any.at[me ^ k])
        both = product(x, w_ref[...])
        gate, up = both[:, :ff], both[:, ff:]
        both_ref[here, :] = both
        moves.store(both_ref.at[here], both_any.at[here])
        hidden = (gate * (0.5 + 0.5 * lax.erf(gate * math.sqrt(0.5))) * up).astype(BF)
        hidden_ref[here, :] = hidden
        moves.store(hidden_ref.at[here], hidden_any.at[here])
        term = transposed_times(hidden, c_ref[here, :])
        if k == 0:
            total[...] = term
        elif k < 3:
            total[...] += term
        else:
            down_ref[...] = (total[...] + term).astype(BF)

    load_w.wait()
    load_c.wait()
    block(0)
    copies[0].wait_recv()
    copies[4].start()
    copies[1].wait_recv()
    copies[5].start()
    copies[2].wait_recv()
    block(1)
    copies[3].wait_recv()
    block(2)
    copies[4].wait_recv()
    copies[5].wait_recv()
    block(3)
    moves.store(down_ref, down_any)
    moves.close()
    for copy in copies:
        copy.wait_send()


def feed_forward_gather(own, weight, cotangent, call):
    rows, width = own.shape
    length, ff = 4 * rows, weight.shape[1] // 2
    both, hidden, down, full = comm_call(
        functools.partial(feed_forward_gather_kernel, ff),
        [(own, False), (weight, False), (cotangent, False)],
        [
            ((length, 2 * ff), F32, False),
            ((length, ff), BF, False),
            ((ff, width), BF, False),
            ((4, rows, width), BF, False),
        ],
        [
            pltpu.VMEM((4, rows, width), BF),
            pltpu.VMEM(weight.shape, BF),
            pltpu.VMEM(cotangent.shape, BF),
            pltpu.VMEM((length, 2 * ff), F32),
            pltpu.VMEM((length, ff), BF),
            pltpu.VMEM((ff, width), F32),
            pltpu.VMEM((ff, width), BF),
        ],
        6,
        16,
        call,
        own.size,
        "feed_forward_gather",
    )
    return both, hidden, down, full.reshape(length, width)


def feed_back_scatter_kernel(
    ff, c_any, both_any, w_any, down_any, x_any, m_ref, own_c_ref, gain_ref,
    grad_ref, term_ref, branch_ref, dw_any,
    c_ref, both_ref, w_ref, down_ref, x_ref, low, dw_ref,
    parts, inbox_x, inbox_y, via_x, via_y, out_x, out_y, sends, recvs, locals_,
):
    me = lax.axis_index("seq")
    rows = own_c_ref.shape[0]
    half = rows // 2
    moves = Moves(locals_)
    load_down = moves.start(down_any, down_ref)
    load_w = moves.start(w_any, w_ref)
    order = (3, 1, 2, 0)
    loads = []
    for k in order:
        here = block_rows(k, rows)
        loads.append(moves.start(c_any.at[here], c_ref.at[here]))
        loads.append(moves.start(both_any.at[here], both_ref.at[here]))
    load_x = moves.start(x_any, x_ref)
    greet((me ^ 1, me ^ 2))
    boxes = (inbox_x, inbox_y, via_x, via_y, out_x, out_y)
    copies, _, total = square_parts(parts, boxes, sends, recvs, 0)

    def part(k):
        here = block_rows(k, rows)
        at = order.index(k)
        loads[2 * at].wait()
        loads[2 * at + 1].wait()
        gate, up = both_ref[here, :ff], both_ref[here, ff:]
        hidden_grad = times_transposed(c_ref[here, :], down_ref[...])
        bell = 0.5 + 0.5 * lax.erf(gate * math.sqrt(0.5))
        slope = bell + gate * (math.sqrt(0.5 / math.pi) * jnp.exp(-0.5 * gate * gate))
        grads = jnp.concatenate([hidden_grad * up * slope, hidden_grad * (gate * bell)], axis=1)
        grads = grads.astype(BF)
        low[here, :] = grads
        parts[k] = times_transposed(grads, w_ref[...]).astype(BF)

    load_down.wait()
    load_w.wait()
    part(3)
    copies[0].start()
    copies[1].start()
    part(1)
    copies[2].start()
    part(2)
    copies[3].start()
    copies[0].wait_recv()
    out_y[...] = (parts[2, :half].astype(F32) + via_x[...].astype(F32)).astype(BF)
    copies[4].start()
    copies[1].wait_recv()
    out_x[...] = (parts[1, half:].astype(F32) + via_y[...].astype(F32)).astype(BF)
    copies[5].start()
    part(0)
    load_x.wait()
    for b in range(x_ref.shape[1] // BLOCK):
        lanes = slice(b * BLOCK, (b + 1) * BLOCK)
        dw_ref[lanes, :] = transposed_times(x_ref[:, lanes], low[...]).astype(BF)
        moves.store(dw_ref.at[lanes], dw_any.at[lanes])
    for copy in copies[2:]:
        copy.wait_recv()
    term = jnp.zeros((1, gain_ref.shape[1]), F32)
    for i in range(2):
        here = slice(i * half, (i + 1) * half)
        back, terms = norm_back(m_ref[here, :], total(here), gain_ref[...])
        grad = own_c_ref[here, :].astype(F32) + back
        grad_ref[here, :] = grad
        branch_ref[here, :] = grad.astype(BF)
        term = term + jnp.sum(terms, axis=0, keepdims=True)
    term_ref[...] = term
    moves.close()
    for copy in copies:
        copy.wait_send()


def feed_back_scatter(cotangent, both, weight, down, x, middle, own_cotangent, gain, call):
    rows, width = own_cotangent.shape
    length, ff = cotangent.shape[0], weight.shape[1] // 2
    grad, term, branch, dw = comm_call(
        functools.partial(feed_back_scatter_kernel, ff),
        [
            (cotangent, False),
            (both, False),
            (weight, False),
            (down, False),
            (x, False),
            (middle, True),
            (own_cotangent, True),
            (gain[None, :], True),
        ],
        [
            ((rows, width), F32, True),
            ((1, width), F32, True),
            ((rows, width), BF, True),
            ((width, 2 * ff), BF, False),
        ],
        [
            pltpu.VMEM(cotangent.shape, BF),
            pltpu.VMEM(both.shape, F32),
            pltpu.VMEM(weight.shape, BF),
            pltpu.VMEM(down.shape, BF),
            pltpu.VMEM(x.shape, BF),
            pltpu.VMEM((length, 2 * ff), BF),
            pltpu.VMEM((width, 2 * ff), BF),
        ]
        + square_scratch(rows, width),
        6,
        11 + width // BLOCK,
        call,
        own_cotangent.size,
        "feed_back_scatter",
    )
    return grad, term[0], branch, dw


def norm_back(values, grad, gain):
    centered = values - jnp.mean(values, axis=-1, keepdims=True)
    spread = lax.rsqrt(jnp.mean(centered * centered, axis=-1, keepdims=True) + EPSILON)
    unit = centered * spread
    g = grad * gain
    back = g - jnp.mean(g, axis=-1, keepdims=True)
    back = spread * (back - unit * jnp.mean(g * unit, axis=-1, keepdims=True))
    return back, grad * unit


def input_back_kernel(
    at_value, at_swish, dqk_ref, dv_ref, ds_ref, w_ref, x_ref, grad_ref, gain_ref, dx_ref, term_ref,
    parts, inbox_x, inbox_y, via_x, via_y, out_x, out_y, sends, recvs,
):
    me = lax.axis_index("seq")
    rows = x_ref.shape[0]
    half = rows // 2
    greet((me ^ 1, me ^ 2))
    boxes = (inbox_x, inbox_y, via_x, via_y, out_x, out_y)
    copies, finish, total = square_parts(parts, boxes, sends, recvs, 0)

    def part(k):
        here = block_rows(k, rows)
        parts[k] = (
            times_transposed(dqk_ref[here, :], w_ref[:, :at_value])
            + times_transposed(dv_ref[here, :], w_ref[:, at_value:at_swish])
            + times_transposed(ds_ref[here, :], w_ref[:, at_swish:])
        ).astype(BF)

    part(3)
    copies[0].start()
    copies[1].start()
    part(1)
    copies[2].start()
    part(2)
    copies[3].start()
    part(0)
    finish()
    term = jnp.zeros((1, x_ref.shape[1]), F32)
    for i in range(2):
        here = slice(i * half, (i + 1) * half)
        back, terms = norm_back(x_ref[here, :].astype(F32), total(here), gain_ref[...])
        dx_ref[here, :] = (grad_ref[here, :] + back).astype(BF)
        term = term + jnp.sum(terms, axis=0, keepdims=True)
    term_ref[...] = term
    for copy in copies:
        copy.wait_send()


def input_backward(dqk, dv, ds, weight, x, grad, gain, at_value, at_swish, call):
    rows, width = x.shape
    dx, term = square_call(
        functools.partial(input_back_kernel, at_value, at_swish),
        (
            jax.ShapeDtypeStruct((rows, width), BF),
            jax.ShapeDtypeStruct((1, width), F32),
        ),
        (IN_VMEM, IN_VMEM),
        square_scratch(rows, width)
        + [pltpu.SemaphoreType.DMA((6,)), pltpu.SemaphoreType.DMA((6,))],
        (dqk, dv, ds, weight, x, grad, gain[None, :]),
        call,
        x.size,
        "input_backward",
    )
    return dx, term[0]


def weight_rows(left_ref, right, out_ref):
    @pl.loop(0, out_ref.shape[0] // BLOCK)
    def _(b):
        lanes = rows_of(b)
        out_ref[lanes, :] = transposed_times(left_ref[:, lanes], right).astype(BF)


def gate_back_scatter_kernel(
    heads, starts, branch_ref, w_ref, swish_ref, retained_ref, column_ref, hidden_any, down_any,
    mixed_any, gated_any, m_any, dswish_ref, dret_ref, dws_any, dwo_any, out_ref,
    hidden_ref, down_ref, mixed_ref, gated_ref, m_ref, dws_ref, dwo_ref, wide,
    parts, inbox_x, inbox_y, via_x, via_y, out_x, out_y, sends, recvs, locals_,
):
    me = lax.axis_index("seq")
    rows = out_ref.shape[0]
    moves = Moves(locals_)
    load_hidden = moves.start(hidden_any, hidden_ref)
    load_down = moves.start(down_any, down_ref)
    load_mixed = moves.start(mixed_any, mixed_ref)
    load_gated = moves.start(gated_any, gated_ref)
    load_m = moves.start(m_any, m_ref)
    greet((me ^ 1, me ^ 2))
    boxes = (inbox_x, inbox_y, via_x, via_y, out_x, out_y)
    copies, finish, total = square_parts(parts, boxes, sends, recvs, 0)

    def part(k):
        here = block_rows(k, rows)
        parts[k] = product(hidden_ref[here, :], down_ref[...]).astype(BF)

    load_hidden.wait()
    load_down.wait()
    part(3)
    copies[0].start()
    copies[1].start()
    part(1)
    copies[2].start()
    part(2)
    copies[3].start()
    part(0)
    gate_back_kernel(heads, branch_ref, w_ref, swish_ref, retained_ref, dswish_ref, dret_ref)
    half = rows // 2
    copies[0].wait_recv()
    out_y[...] = (parts[2, :half].astype(F32) + via_x[...].astype(F32)).astype(BF)
    copies[4].start()
    copies[1].wait_recv()
    out_x[...] = (parts[1, half:].astype(F32) + via_y[...].astype(F32)).astype(BF)
    copies[5].start()
    padded = dswish_ref.shape[1]
    spare = lax.broadcasted_iota(jnp.int32, (BLOCK, padded), 1) == heads * VAL_HEAD
    load_mixed.wait()
    for b in range(dws_ref.shape[0] // BLOCK):
        lanes = slice(b * BLOCK, (b + 1) * BLOCK)
        term = transposed_times(mixed_ref[:, lanes], dswish_ref[...])
        dws_ref[lanes, :] = jnp.where(spare, column_ref[lanes, :], term).astype(BF)
        moves.store(dws_ref.at[lanes], dws_any.at[lanes])
    load_gated.wait()
    step = 2 * BLOCK
    for h in range(heads):
        value_lanes = slice(h * VAL_HEAD, (h + 1) * VAL_HEAD)
        for b in range(branch_ref.shape[1] // step):
            lanes = slice(b * step, (b + 1) * step)
            wide[...] = transposed_times(gated_ref[:, value_lanes], branch_ref[:, lanes]).astype(BF)
            for k, start in enumerate(starts):
                dwo_ref[k, h, :, lanes] = wide[start : start + dwo_ref.shape[2], :]
    moves.store(dwo_ref, dwo_any)
    load_m.wait()
    for copy in copies[2:]:
        copy.wait_recv()
    out_ref[...] = (m_ref[...] + total(slice(0, rows))).astype(BF)
    moves.close()
    for copy in copies:
        copy.wait_send()


def gate_backward_scatter(
    branch, weight, swish, retained, column, hidden, down, mixed, gated, middle, heads, padded, cut,
    call,
):
    length, width = branch.shape
    rows = middle.shape[0]
    starts = [cut.start(k) for k in range(4)]
    dwo = (4, heads, cut.width, width)
    return comm_call(
        functools.partial(gate_back_scatter_kernel, heads, starts),
        [
            (branch, True),
            (weight, True),
            (swish, True),
            (retained, True),
            (column, True),
            (hidden, False),
            (down, False),
            (mixed, False),
            (gated, False),
            (middle, False),
        ],
        [
            ((length, padded), BF, True),
            ((heads, length, VAL_HEAD), BF, True),
            ((width, padded), BF, False),
            (dwo, BF, False),
            ((rows, width), BF, True),
        ],
        [
            pltpu.VMEM(hidden.shape, BF),
            pltpu.VMEM(down.shape, BF),
            pltpu.VMEM(mixed.shape, BF),
            pltpu.VMEM(gated.shape, BF),
            pltpu.VMEM(middle.shape, F32),
            pltpu.VMEM((width, padded), BF),
            pltpu.VMEM(dwo, BF),
            pltpu.VMEM((VAL_HEAD, 2 * BLOCK), BF),
        ]
        + square_scratch(rows, width),
        6,
        6 + width // BLOCK,
        call,
        middle.size,
        "gate_back_scatter",
    )


def retention_back_exchange_kernel(
    heads, q_ref, k_ref, v_ref, dret_ref, cos_ref, sin_ref, mixed_ref, send_ref,
    dqk_ref, dv_ref, dwqk_ref, came_ref, dq_sum, dv_sum, sends, recvs, local,
):
    me = lax.axis_index("seq")
    greet((me ^ 1, me ^ 2, me ^ 3))
    keep = pltpu.make_async_copy(send_ref.at[me], came_ref.at[me], local)
    keep.start()
    copies = [
        remote(send_ref.at[me ^ k], came_ref.at[me], sends, recvs, k - 1, me ^ k) for k in (3, 1, 2)
    ]
    for copy in copies:
        copy.start()
    retention_back_kernel(
        heads, q_ref, k_ref, v_ref, dret_ref, cos_ref, sin_ref, dqk_ref, dv_ref, dq_sum, dv_sum
    )
    weight_rows(mixed_ref, dqk_ref[...], dwqk_ref)
    for copy in copies:
        copy.wait()
    keep.wait()


def retention_backward_exchange(q, k, v, dret, cosine, sine, mixed, send, heads, padded, call):
    length, width = mixed.shape
    qk = heads * KEY_HEAD
    return pl.pallas_call(
        functools.partial(retention_back_exchange_kernel, heads),
        out_shape=(
            jax.ShapeDtypeStruct((length, 2 * qk), BF),
            jax.ShapeDtypeStruct((length, padded), BF),
            jax.ShapeDtypeStruct((width, 2 * qk), BF),
            jax.ShapeDtypeStruct(send.shape, BF),
        ),
        in_specs=[IN_VMEM] * 7 + [ANYWHERE],
        out_specs=(IN_VMEM,) * 3 + (ANYWHERE,),
        scratch_shapes=[
            pltpu.VMEM((length, qk), F32),
            pltpu.VMEM((heads, length, VAL_HEAD), BF),
            pltpu.SemaphoreType.DMA((3,)),
            pltpu.SemaphoreType.DMA((3,)),
            pltpu.SemaphoreType.DMA,
        ],
        compiler_params=pltpu.CompilerParams(
            collective_id=call, has_side_effects=True, vmem_limit_bytes=56 * 1024 * 1024
        ),
        cost_estimate=transfer_cost(send.size // 4 * 3 // 2),
        name="retention_back_exchange",
    )(q, k, v, dret, cosine, sine, mixed, send)


def after(values, *others):
    return lax.optimization_barrier((values,) + others)[0]


class Cut:
    def __init__(self, rows, count):
        self.rows, self.count = rows, count
        self.width = -(-rows // (count * 16)) * 16

    def start(self, piece):
        if isinstance(piece, int):
            return min(piece * self.width, self.rows - self.width)
        return jnp.minimum(piece * self.width, self.rows - self.width)

    def skip(self, piece):
        if isinstance(piece, int):
            return min(piece * self.width - self.start(piece), self.width)
        return jnp.minimum(piece * self.width - self.start(piece), self.width)

    def assemble(self, pieces, axis):
        kept = []
        for k, piece in enumerate(pieces):
            if self.skip(k) < self.width:
                kept.append(lax.slice_in_dim(piece, self.skip(k), self.width, axis=axis))
        return jnp.concatenate(kept, axis=axis)


def columns_of(weight, index, width, padded):
    piece = lax.dynamic_slice_in_dim(weight, index * width, width, axis=1)
    return jnp.pad(piece, ((0, 0), (0, padded - width)))


def on_device(
    layer_input,
    mixer_gain,
    query_weight,
    key_weight,
    value_weight,
    swish_weight,
    output_weight,
    channel_gain,
    gelu_weight,
    linear_weight,
    down_weight,
    output_cotangent,
):
    groups, local_length, width = layer_input.shape
    seq_count = lax.axis_size("seq")
    shards = lax.axis_size("fsdp")
    me = lax.axis_index("seq")
    per_device = HEADS // seq_count
    rows_count = groups * local_length
    square = seq_count == 4 and rows_count % 32 == 0
    length = local_length * seq_count
    key_scale = KEY_HEAD ** (-0.5)
    qk = query_weight.shape[1] // seq_count
    vd = value_weight.shape[1] // seq_count
    vd_pad = -(-vd // 128) * 128
    hidden_units = gelu_weight.shape[1]
    own_rows = down_weight.shape[0]
    cut = Cut(own_rows, seq_count)
    ff = shards * cut.width

    def gather_rows(values):
        return lax.all_gather(values, "fsdp", axis=0, tiled=True)

    def scatter_rows(values):
        return lax.psum_scatter(values.astype(BF), "fsdp", scatter_dimension=0, tiled=True)

    attention_piece = jnp.concatenate(
        [
            columns_of(query_weight, me, qk, qk),
            columns_of(key_weight, me, qk, qk),
            columns_of(value_weight, me, vd, vd_pad),
            columns_of(swish_weight, me, vd, vd_pad),
        ],
        axis=1,
    )
    attention_weight = gather_rows(attention_piece)
    output_piece = lax.dynamic_slice_in_dim(output_weight, cut.start(me), cut.width, axis=0)
    output_pieces = gather_rows(output_piece)
    column = lax.broadcasted_iota(jnp.int32, (hidden_units, ff), 0)
    slot = lax.broadcasted_iota(jnp.int32, (hidden_units, ff), 1)
    chosen = (slot // cut.width) * own_rows + cut.start(me) + slot % cut.width
    selector = (column == chosen).astype(BF)
    gate_piece = product(gelu_weight, selector).astype(BF)
    up_piece = product(linear_weight, selector).astype(BF)
    feed_piece = jnp.concatenate([gate_piece, up_piece], axis=1)
    down_piece = lax.dynamic_slice_in_dim(down_weight, cut.start(me), cut.width, axis=0)
    gains = lax.all_gather(jnp.stack([mixer_gain, channel_gain]), "fsdp", axis=1, tiled=True)
    mixer_scale, channel_scale = gains[0].astype(F32), gains[1].astype(F32)

    local_input = layer_input.reshape(rows_count, width)
    upstream = output_cotangent.reshape(rows_count, width)

    def whole(values, call):
        gathered = gather_seq(values, call)
        return gathered.reshape(length * groups, width)

    input_full = whole(local_input, 0)
    upstream_full = whole(after(upstream, input_full), 1)
    inputs = local_input.astype(F32)

    blocks = shards // seq_count
    output_pieces = after(output_pieces, upstream_full)
    swapped = exchange_seq(output_pieces.reshape(seq_count, blocks, cut.width, width), 2)
    output_full = jnp.concatenate(
        [
            cut.assemble([swapped[piece, block] for piece in range(seq_count)], 0)
            for block in range(blocks)
        ],
        axis=0,
    )
    feed_weight = gather_rows(after(feed_piece, swapped))

    cosine, sine = rotation_tables(length, KEY_HEAD // 2)
    mixed_low, query_low, key_low, value_low, swish_pre, retained, gated_low = retention_forward(
        input_full, mixer_scale[None, :], attention_weight, cosine, sine, per_device,
        (qk, 2 * qk, 2 * qk + vd_pad),
    )

    kept_rows = lax.broadcasted_iota(jnp.int32, down_piece.shape, 0) >= cut.skip(me)
    down_full = gather_rows(after(jnp.where(kept_rows, down_piece, jnp.zeros_like(down_piece)), gated_low))
    if square:
        middle, channel_own = project_and_norm(
            gated_low, output_full, local_input, channel_scale, 3
        )
        both_pre, hidden_low, down_term, channel_full = feed_forward_gather(
            channel_own, feed_weight, upstream_full, 4
        )
        down_share = scatter_rows(down_term)
        middle_grad, channel_term, branch_own, feed_term = feed_back_scatter(
            after(upstream_full, down_term), both_pre, feed_weight, down_full, channel_full,
            middle, upstream, channel_scale, 6,
        )
        feed_share = scatter_rows(feed_term)
        branch_full = whole(branch_own, 7)
    else:
        middle = inputs + scatter_seq(product(gated_low, output_full).astype(BF), 3)
        channel_full = whole(normalize(middle, channel_scale).astype(BF), 4)
        gate_pre, up_pre, hidden_low = feed_forward(channel_full, feed_weight)
        down_share = scatter_rows(transposed_times(hidden_low, upstream_full).astype(BF))
        feed_low_grad, channel_part, hidden_part = feed_backward(
            upstream_full, gate_pre, up_pre, hidden_low, feed_weight, down_full
        )
        feed_share = scatter_rows(transposed_times(channel_full, feed_low_grad).astype(BF))
        middle_local, channel_terms = norm_back(
            middle, scatter_seq(channel_part, 6), channel_scale
        )
        channel_term = jnp.sum(channel_terms, axis=0)
        middle_grad = upstream.astype(F32) + middle_local
        branch_full = whole(middle_grad.astype(BF), 7)

    at_value, at_swish = 2 * qk, 2 * qk + vd_pad
    spare = lax.broadcasted_iota(jnp.int32, (width, vd_pad), 1) == vd
    if square:
        swish_grad, retained_grad, swish_term, output_send, layer_output = gate_backward_scatter(
            after(branch_full, down_share), output_full, swish_pre, retained,
            channel_term[:, None], hidden_low, down_full, mixed_low, gated_low, middle,
            per_device, vd_pad, cut, 5,
        )
        swish_share = scatter_rows(swish_term)
        key_grad, value_grad, key_term, output_swapped = retention_backward_exchange(
            query_low, key_low, value_low, retained_grad, cosine, sine, mixed_low,
            after(output_send, feed_share), per_device, vd_pad, 8,
        )
        output_share = scatter_rows(output_swapped.reshape(shards * cut.width, width))
        key_share = scatter_rows(key_term)
        input_gradient, mixer_term = input_backward(
            key_grad, value_grad, swish_grad, attention_weight, local_input, middle_grad,
            mixer_scale, at_value, at_swish, 9,
        )
    else:
        swish_grad, retained_grad = gate_backward(
            branch_full, output_full, swish_pre, retained, per_device, vd_pad
        )
        swish_term = transposed_times(mixed_low, swish_grad)
        swish_term = jnp.where(spare, channel_term[:, None], swish_term).astype(BF)
        swish_share = scatter_rows(swish_term)
        result = middle + scatter_seq(hidden_part, 5)
        layer_output = result.astype(BF)
        key_grad, value_grad = retention_backward(
            query_low, key_low, value_low, retained_grad, cosine, sine, per_device, vd_pad
        )
        key_term = transposed_times(mixed_low, key_grad).astype(BF)
        key_share = scatter_rows(key_term)
        mixed_part = (
            times_transposed(key_grad, attention_weight[:, :at_value])
            + times_transposed(value_grad, attention_weight[:, at_value:at_swish])
            + times_transposed(swish_grad, attention_weight[:, at_swish:])
        )
        input_local, mixer_terms = norm_back(
            inputs, scatter_seq(mixed_part.astype(BF), 9), mixer_scale
        )
        mixer_term = jnp.sum(mixer_terms, axis=0)
        input_gradient = (middle_grad + input_local).astype(BF)
        output_term = transposed_times(gated_low, branch_full).astype(BF)
        output_term = output_term.reshape(blocks, own_rows, width)
        output_send = jnp.stack(
            [
                lax.slice_in_dim(output_term, cut.start(k), cut.start(k) + cut.width, axis=1)
                for k in range(seq_count)
            ]
        )
        output_swapped = exchange_seq(output_send, 8)
        output_share = scatter_rows(output_swapped.reshape(shards * cut.width, width))
    input_gradient = input_gradient.reshape(groups, local_length, width)
    value_term = transposed_times(mixed_low, value_grad)
    value_term = jnp.where(spare, mixer_term[:, None], value_term).astype(BF)
    value_share = scatter_rows(value_term)

    layer_output = layer_output.reshape(groups, local_length, width)
    down_all = gather_seq(after(down_share, value_term), 10)
    feed_all = gather_seq(after(feed_share, down_all), 11)
    swish_all = gather_seq(after(swish_share, feed_all), 13)
    output_all = gather_seq(after(output_share, swish_all), 12)
    key_all = gather_seq(after(key_share, output_all), 15)
    value_all = gather_seq(after(value_share, key_all), 14)
    down_gradient = cut.assemble([down_all[k] for k in range(seq_count)], 0).astype(F32)
    output_gradient = cut.assemble([output_all[k] for k in range(seq_count)], 0).astype(F32)

    def hidden_order(at):
        pieces = [feed_all[k][:, at : at + ff] for k in range(seq_count)]
        return jnp.concatenate(
            [
                cut.assemble(
                    [piece[:, f * cut.width : (f + 1) * cut.width] for piece in pieces], 1
                )
                for f in range(shards)
            ],
            axis=1,
        ).astype(F32)

    def attention_order(gathered, at, wide):
        pieces = [gathered[k][:, at : at + wide] for k in range(seq_count)]
        return jnp.concatenate(pieces, axis=1).astype(F32)

    def gain_order(gathered):
        return sum(gathered[k][:, vd].astype(F32) for k in range(seq_count))

    return (
        layer_output,
        input_gradient,
        gain_order(value_all),
        attention_order(key_all, 0, qk),
        attention_order(key_all, qk, qk),
        attention_order(value_all, 0, vd),
        attention_order(swish_all, 0, vd),
        output_gradient,
        gain_order(swish_all),
        hidden_order(0),
        hidden_order(ff),
        down_gradient,
    )


def solution(mesh):
    tokens, rows, vector = P("fsdp", "seq", None), P("fsdp", None), P("fsdp")
    return jax.shard_map(
        on_device,
        mesh=mesh,
        in_specs=(
            tokens, vector, rows, rows, rows, rows, rows, vector, rows, rows, rows, tokens,
        ),
        out_specs=(
            tokens, tokens, vector, rows, rows, rows, rows, rows, vector, rows, rows, rows,
        ),
        check_vma=False,
    )
```

```python
import functools
import math

import jax
import jax.numpy as jnp
from jax import lax
from jax.experimental import pallas as pl
from jax.experimental.pallas import tpu as pltpu
from jax.sharding import PartitionSpec as P

HEADS = 8
KEY_HEAD = 256
VAL_HEAD = 432
EPSILON = 1e-05
MESH = pl.DeviceIdType.MESH
BF = jnp.bfloat16
F32 = jnp.float32
IN_VMEM = pl.BlockSpec(memory_space=pltpu.VMEM)
ANYWHERE = pl.BlockSpec(memory_space=pl.ANY)


def product(left, right):
    return jnp.dot(left, right, preferred_element_type=F32)


def times_transposed(left, right):
    return lax.dot_general(left, right, (((1,), (1,)), ((), ())), preferred_element_type=F32)


def transposed_times(left, right):
    return lax.dot_general(left, right, (((0,), (0,)), ((), ())), preferred_element_type=F32)


def normalize(values, gain):
    centered = values - jnp.mean(values, axis=-1, keepdims=True)
    spread = lax.rsqrt(jnp.mean(centered * centered, axis=-1, keepdims=True) + EPSILON)
    return centered * spread * gain


def rotation_tables(length, half_width):
    rates = jnp.exp(-math.log(10000.0) * jnp.arange(half_width, dtype=F32) / (half_width - 1))
    turned = jnp.arange(length, dtype=F32)[:, None] * rates[None, :]
    return (jnp.cos(turned), jnp.sin(turned))


def pad_lanes(pieces, width):
    have = sum(piece.shape[1] for piece in pieces)
    if have < width:
        pieces = pieces + [jnp.zeros((pieces[0].shape[0], width - have), pieces[0].dtype)]
    return jnp.concatenate(pieces, axis=1) if len(pieces) > 1 else pieces[0]


def rotate_pair(values, cosine, sine, back=False):
    half = KEY_HEAD // 2
    first, second = values[:, :half], values[:, half:]
    if back:
        return jnp.concatenate([first * cosine + second * sine, second * cosine - first * sine], 1)
    return jnp.concatenate([first * cosine - second * sine, second * cosine + first * sine], 1)


BLOCK = 256


def decay_table(head_ids, length):
    rates = jnp.log1p(-jnp.exp2(-5.0 - head_ids.astype(F32)))
    gap = (
        jnp.arange(length - BLOCK, length, dtype=jnp.int32)[:, None]
        - jnp.arange(length, dtype=jnp.int32)[None, :]
    )
    decay = jnp.exp(jnp.maximum(gap, 0).astype(F32)[None] * rates[:, None, None])
    return jnp.where(gap[None] >= 0, decay, 0.0)


def norm_parts(values):
    centered = values - jnp.mean(values, axis=-1, keepdims=True)
    variance = jnp.mean(centered * centered, axis=-1, keepdims=True)
    factor = lax.rsqrt(jnp.maximum(variance, 1.0))
    return centered * factor, factor, variance > 1.0


def rows_of(block):
    return pl.ds(pl.multiple_of(block * BLOCK, BLOCK), BLOCK)


def head_lanes(head, width):
    return slice(head * width, (head + 1) * width)


class Moves:
    def __init__(self, sems):
        self.sems, self.used, self.open = sems, 0, []

    def start(self, source, target):
        copy = pltpu.make_async_copy(source, target, self.sems.at[self.used])
        self.used += 1
        copy.start()
        return copy

    def store(self, source, target):
        self.open.append(self.start(source, target))

    def close(self):
        for copy in self.open:
            copy.wait()


def retention_kernel(
    heads, offsets, mixed_any, w_any, cos_ref, sin_ref, table_ref,
    q_any, k_any, v_any, swish_any, retained_any, gated_any,
    mixed_ref, w_ref, q_ref, k_ref, v_ref, swish_ref, retained_ref, gated_ref, sems,
):
    at_key, at_value, at_swish = offsets
    blocks = mixed_ref.shape[0] // BLOCK
    moves = Moves(sems)
    spans = (
        slice(0, at_key), slice(at_key, at_value), slice(at_value, at_swish),
        slice(at_swish, w_ref.shape[1]),
    )
    loads = []
    for i in range(blocks):
        rows = slice(i * BLOCK, (i + 1) * BLOCK)
        loads.append(moves.start(mixed_any.at[rows], mixed_ref.at[rows]))
        if i == 0:
            weights = [moves.start(w_any.at[:, span], w_ref.at[:, span]) for span in spans]
    for i in range(blocks):
        rows = slice(i * BLOCK, (i + 1) * BLOCK)
        seen = slice(0, (i + 1) * BLOCK)
        loads[i].wait()
        mixed = mixed_ref[rows, :]
        cosine, sine = cos_ref[rows, :], sin_ref[rows, :]
        for n, (target, scale) in enumerate(((q_ref, 1.0), (k_ref, KEY_HEAD**-0.5))):
            if i == 0:
                weights[n].wait()
            pre = product(mixed, w_ref[:, spans[n]])
            for h in range(heads):
                lanes = head_lanes(h, KEY_HEAD)
                turned = rotate_pair(pre[:, lanes], cosine, sine)
                target[rows, lanes] = (turned * scale if n else turned).astype(BF)
        if i == 0:
            weights[2].wait()
        value = product(mixed, w_ref[:, spans[2]])
        for h in range(heads):
            v_ref[h, rows, :] = value[:, head_lanes(h, VAL_HEAD)].astype(BF)
        if i == 0:
            weights[3].wait()
        swish = product(mixed, w_ref[:, spans[3]])[:, : heads * VAL_HEAD]
        swish_ref[rows, :] = swish
        gated = []
        for h in range(heads):
            lanes = head_lanes(h, KEY_HEAD)
            scores = times_transposed(q_ref[rows, lanes], k_ref[seen, lanes])
            decay = table_ref[h, :, (blocks - 1 - i) * BLOCK :]
            retained = product((scores * decay).astype(BF), v_ref[h, seen, :]).astype(BF)
            retained_ref[h, rows, :] = retained
            unit, _, _ = norm_parts(retained.astype(F32))
            s = swish[:, head_lanes(h, VAL_HEAD)]
            gated.append((s * jax.nn.sigmoid(s) * unit).astype(BF))
        gated_ref[rows, :] = jnp.concatenate(gated, axis=1) if heads > 1 else gated[0]
        for ref, out in (
            (q_ref, q_any), (k_ref, k_any), (swish_ref, swish_any), (gated_ref, gated_any)
        ):
            moves.store(ref.at[rows], out.at[rows])
        moves.store(v_ref.at[:, rows], v_any.at[:, rows])
        moves.store(retained_ref.at[:, rows], retained_any.at[:, rows])
    moves.close()


def retention_forward(mixed, weight, cosine, sine, table, heads, offsets):
    length, width = mixed.shape
    qk, vd = heads * KEY_HEAD, heads * VAL_HEAD
    outputs = (
        ((length, qk), BF),
        ((length, qk), BF),
        ((heads, length, VAL_HEAD), BF),
        ((length, vd), F32),
        ((heads, length, VAL_HEAD), BF),
        ((length, vd), BF),
    )
    blocks = length // BLOCK
    return pl.pallas_call(
        functools.partial(retention_kernel, heads, offsets),
        out_shape=tuple(jax.ShapeDtypeStruct(*out) for out in outputs),
        in_specs=[ANYWHERE, ANYWHERE, IN_VMEM, IN_VMEM, IN_VMEM],
        out_specs=(ANYWHERE,) * 6,
        scratch_shapes=[pltpu.VMEM(mixed.shape, BF), pltpu.VMEM(weight.shape, BF)]
        + [pltpu.VMEM(*out) for out in outputs]
        + [pltpu.SemaphoreType.DMA((4 + 7 * blocks,))],
        compiler_params=pltpu.CompilerParams(vmem_limit_bytes=60 * 1024 * 1024),
        cost_estimate=pl.CostEstimate(
            flops=30_000_000_000, bytes_accessed=0, transcendentals=0
        ),
        name="retention",
    )(mixed, weight, cosine, sine, table)


def gate_back_rows(heads, rows, branch, w_ref, swish_ref, retained_ref, dswish_ref, dret_ref):
    gated_grad = times_transposed(branch, w_ref[...])
    swish_parts = []
    for h in range(heads):
        lanes = head_lanes(h, VAL_HEAD)
        grad, s = gated_grad[:, lanes], swish_ref[rows, lanes]
        gate = jax.nn.sigmoid(s)
        unit, factor, above = norm_parts(retained_ref[h, rows, :].astype(F32))
        swish_parts.append((grad * unit * (gate * (1.0 + s * (1.0 - gate)))).astype(BF))
        g = grad * (s * gate)
        along = jnp.where(above, jnp.mean(g * unit, axis=-1, keepdims=True), 0.0)
        back = factor * (g - jnp.mean(g, axis=-1, keepdims=True) - unit * along)
        dret_ref[h, rows, :] = back.astype(BF)
    dswish_ref[rows, :] = pad_lanes(swish_parts, dswish_ref.shape[1])


def gate_back_kernel(heads, branch_ref, w_ref, swish_ref, retained_ref, dswish_ref, dret_ref):
    for i in range(branch_ref.shape[0] // BLOCK):
        rows = slice(i * BLOCK, (i + 1) * BLOCK)
        gate_back_rows(
            heads, rows, branch_ref[rows, :], w_ref, swish_ref, retained_ref, dswish_ref, dret_ref
        )


def gate_backward(branch, weight, swish, retained, heads, padded):
    length = branch.shape[0]
    return pl.pallas_call(
        functools.partial(gate_back_kernel, heads),
        out_shape=(
            jax.ShapeDtypeStruct((length, padded), BF),
            jax.ShapeDtypeStruct((heads, length, VAL_HEAD), BF),
        ),
        compiler_params=pltpu.CompilerParams(vmem_limit_bytes=48 * 1024 * 1024),
        name="gate_back",
    )(branch, weight, swish, retained)


def retention_back_head(
    h, heads, q_ref, k_ref, v_ref, dret_ref, table_ref, cos_ref, sin_ref, dqk_ref, dv_ref,
    dk_sum, dv_sum,
):
    blocks = q_ref.shape[0] // BLOCK
    lanes = head_lanes(h, KEY_HEAD)
    for i in reversed(range(blocks)):
        rows = slice(i * BLOCK, (i + 1) * BLOCK)
        seen = slice(0, (i + 1) * BLOCK)
        query, grad = q_ref[rows, lanes], dret_ref[h, rows, :]
        key, value = k_ref[seen, lanes], v_ref[h, seen, :]
        decay = table_ref[h, :, (blocks - 1 - i) * BLOCK :]
        weights = (times_transposed(query, key) * decay).astype(BF)
        score = (times_transposed(grad, value) * decay).astype(BF)
        dq = product(score, key).astype(BF).astype(F32)
        dqk_ref[rows, lanes] = rotate_pair(
            dq, cos_ref[rows, :], sin_ref[rows, :], back=True
        ).astype(BF)
        if i == blocks - 1:
            dk_sum[...] = transposed_times(score, query)
            dv_sum[...] = transposed_times(weights, grad)
        else:
            dk_sum[seen, :] += transposed_times(score, query)
            dv_sum[seen, :] += transposed_times(weights, grad)
    dk = rotate_pair(
        dk_sum[...].astype(BF).astype(F32), cos_ref[...], sin_ref[...], back=True
    ) * (KEY_HEAD**-0.5)
    dqk_ref[:, head_lanes(heads + h, KEY_HEAD)] = dk.astype(BF)
    return dv_sum[...].astype(BF)


def retention_back_kernel(
    heads, q_ref, k_ref, v_ref, dret_ref, table_ref, cos_ref, sin_ref, dqk_ref, dv_ref,
    dk_sum, dv_sum,
):
    parts = [
        retention_back_head(
            h, heads, q_ref, k_ref, v_ref, dret_ref, table_ref, cos_ref, sin_ref, dqk_ref, dv_ref,
            dk_sum, dv_sum,
        )
        for h in range(heads)
    ]
    dv_ref[...] = pad_lanes(parts, dv_ref.shape[1])


def retention_backward(q, k, v, dret, table, cosine, sine, heads, padded):
    length = q.shape[0]
    qk = heads * KEY_HEAD
    return pl.pallas_call(
        functools.partial(retention_back_kernel, heads),
        out_shape=(
            jax.ShapeDtypeStruct((length, 2 * qk), BF),
            jax.ShapeDtypeStruct((length, padded), BF),
        ),
        scratch_shapes=[
            pltpu.VMEM((length, KEY_HEAD), F32),
            pltpu.VMEM((length, VAL_HEAD), F32),
        ],
        compiler_params=pltpu.CompilerParams(vmem_limit_bytes=48 * 1024 * 1024),
        name="retention_back",
    )(q, k, v, dret, table, cosine, sine)


def transfer_cost(elements):
    return pl.CostEstimate(flops=0, bytes_accessed=elements * 240, transcendentals=0)


def greet(peers):
    barrier = pltpu.get_barrier_semaphore()
    for peer in peers:
        pl.semaphore_signal(barrier, inc=1, device_id={"seq": peer}, device_id_type=MESH)
    pl.semaphore_wait(barrier, len(peers))


def remote(source, target, sends, recvs, k, to):
    return pltpu.make_async_remote_copy(
        src_ref=source,
        dst_ref=target,
        send_sem=sends.at[k],
        recv_sem=recvs.at[k],
        device_id={"seq": to},
        device_id_type=MESH,
    )


def gather_square_kernel(x_ref, o_ref, sends, recvs, local):
    me = lax.axis_index("seq")
    across, along = me ^ 1, me ^ 2
    half = x_ref.shape[0] // 2
    greet((across, along))
    own = pltpu.make_async_copy(x_ref, o_ref.at[me], local)
    own.start()

    def part(ref, i):
        return ref.at[pl.ds(i * half, half)]

    first = (
        remote(part(x_ref, 0), part(o_ref.at[me], 0), sends, recvs, 0, across),
        remote(part(x_ref, 1), part(o_ref.at[me], 1), sends, recvs, 1, along),
        remote(part(x_ref, 1), part(o_ref.at[me], 1), sends, recvs, 2, across),
        remote(part(x_ref, 0), part(o_ref.at[me], 0), sends, recvs, 3, along),
    )
    for copy in first:
        copy.start()
    first[0].wait_recv()
    on_along = remote(part(o_ref.at[across], 0), part(o_ref.at[across], 0), sends, recvs, 4, along)
    on_along.start()
    first[1].wait_recv()
    on_across = remote(part(o_ref.at[along], 1), part(o_ref.at[along], 1), sends, recvs, 5, across)
    on_across.start()
    first[2].wait_recv()
    first[3].wait_recv()
    on_along.wait_recv()
    on_across.wait_recv()
    for copy in first + (on_along, on_across):
        copy.wait_send()
    own.wait()


def gather_kernel(count, x_ref, o_ref, sends, recvs, local):
    me = lax.axis_index("seq")
    peers = [lax.rem(me + step, count) for step in range(1, count)]
    greet(peers)
    own = pltpu.make_async_copy(x_ref, o_ref.at[me], local)
    own.start()
    copies = [remote(x_ref, o_ref.at[me], sends, recvs, k, to) for k, to in enumerate(peers)]
    for copy in copies:
        copy.start()
    for copy in copies:
        copy.wait()
    own.wait()


def gather_seq(values, call):
    count = lax.axis_size("seq")
    square = count == 4 and values.shape[0] % 32 == 0
    body = gather_square_kernel if square else functools.partial(gather_kernel, count)
    copies = 6 if square else count - 1
    return pl.pallas_call(
        body,
        out_shape=jax.ShapeDtypeStruct((count,) + values.shape, values.dtype),
        in_specs=[pl.BlockSpec(memory_space=pl.ANY)],
        out_specs=pl.BlockSpec(memory_space=pl.ANY),
        scratch_shapes=[
            pltpu.SemaphoreType.DMA((copies,)),
            pltpu.SemaphoreType.DMA((copies,)),
            pltpu.SemaphoreType.DMA,
        ],
        compiler_params=pltpu.CompilerParams(collective_id=call, has_side_effects=True),
        cost_estimate=transfer_cost(values.size),
        name=f"gather_seq_{call}",
    )(values)


def exchange_kernel(count, x_ref, o_ref, sends, recvs, local):
    me = lax.axis_index("seq")
    peers = [lax.rem(me + step, count) for step in range(1, count)]
    greet(peers)
    own = pltpu.make_async_copy(x_ref.at[me], o_ref.at[me], local)
    own.start()
    copies = [remote(x_ref.at[to], o_ref.at[me], sends, recvs, k, to) for k, to in enumerate(peers)]
    for copy in copies:
        copy.start()
    for copy in copies:
        copy.wait()
    own.wait()


def exchange_seq(values, call):
    count = lax.axis_size("seq")
    return pl.pallas_call(
        functools.partial(exchange_kernel, count),
        out_shape=jax.ShapeDtypeStruct(values.shape, values.dtype),
        in_specs=[pl.BlockSpec(memory_space=pl.ANY)],
        out_specs=pl.BlockSpec(memory_space=pl.ANY),
        scratch_shapes=[
            pltpu.SemaphoreType.DMA((count - 1,)),
            pltpu.SemaphoreType.DMA((count - 1,)),
            pltpu.SemaphoreType.DMA,
        ],
        compiler_params=pltpu.CompilerParams(collective_id=call, has_side_effects=True),
        cost_estimate=transfer_cost(values.size),
        name=f"exchange_seq_{call}",
    )(values)


def scatter_square_kernel(p_ref, o_ref, inbox_x, inbox_y, via_x, via_y, out_x, out_y, sends, recvs):
    me = lax.axis_index("seq")
    across, along, corner = me ^ 1, me ^ 2, me ^ 3
    half = p_ref.shape[1] // 2
    low, high = pl.ds(0, half), pl.ds(half, half)
    greet((across, along))
    first = (
        remote(p_ref.at[corner, low], via_x, sends, recvs, 0, across),
        remote(p_ref.at[corner, high], via_y, sends, recvs, 1, along),
        remote(p_ref.at[across, low], inbox_x.at[low], sends, recvs, 2, across),
        remote(p_ref.at[along, high], inbox_y.at[high], sends, recvs, 3, along),
    )
    for copy in first:
        copy.start()
    first[0].wait_recv()
    out_y[...] = (p_ref[along, :half].astype(F32) + via_x[...].astype(F32)).astype(BF)
    to_along = remote(out_y, inbox_y.at[low], sends, recvs, 4, along)
    to_along.start()
    first[1].wait_recv()
    out_x[...] = (p_ref[across, half:].astype(F32) + via_y[...].astype(F32)).astype(BF)
    to_across = remote(out_x, inbox_x.at[high], sends, recvs, 5, across)
    to_across.start()
    first[2].wait_recv()
    first[3].wait_recv()
    to_along.wait_recv()
    to_across.wait_recv()
    o_ref[...] = (
        p_ref[me].astype(F32) + inbox_x[...].astype(F32) + inbox_y[...].astype(F32)
    )
    for copy in first + (to_along, to_across):
        copy.wait_send()


def scatter_kernel(count, p_ref, o_ref, inbox, sends, recvs):
    me = lax.axis_index("seq")
    peers = [lax.rem(me + step, count) for step in range(1, count)]
    greet(peers)
    copies = [remote(p_ref.at[to], inbox.at[k], sends, recvs, k, to) for k, to in enumerate(peers)]
    for copy in copies:
        copy.start()
    total = p_ref[me].astype(F32)
    for k, copy in enumerate(copies):
        copy.wait_recv()
        total = total + inbox[k].astype(F32)
    o_ref[...] = total
    for copy in copies:
        copy.wait_send()


def scatter_seq(parts, call):
    count = lax.axis_size("seq")
    rows, width = parts.shape[0] // count, parts.shape[1]
    parts = parts.reshape(count, rows, width)
    if count == 4 and rows % 32 == 0:
        body = scatter_square_kernel
        scratch = [pltpu.VMEM((rows, width), BF)] * 2 + [pltpu.VMEM((rows // 2, width), BF)] * 4
        copies = 6
    else:
        body = functools.partial(scatter_kernel, count)
        scratch = [pltpu.VMEM((count - 1, rows, width), BF)]
        copies = count - 1
    return pl.pallas_call(
        body,
        out_shape=jax.ShapeDtypeStruct((rows, width), F32),
        in_specs=[pl.BlockSpec(memory_space=pltpu.VMEM)],
        out_specs=pl.BlockSpec(memory_space=pltpu.VMEM),
        scratch_shapes=scratch
        + [pltpu.SemaphoreType.DMA((copies,)), pltpu.SemaphoreType.DMA((copies,))],
        compiler_params=pltpu.CompilerParams(
            collective_id=call, has_side_effects=True, vmem_limit_bytes=32 * 1024 * 1024
        ),
        cost_estimate=transfer_cost(rows * width),
        name=f"scatter_seq_{call}",
    )(parts)


def feed_forward_kernel(ff, x_ref, w_ref, gate_ref, up_ref, hidden_ref):
    both = product(x_ref[...], w_ref[...])
    gate, up = both[:, :ff], both[:, ff:]
    gate_ref[...] = gate
    up_ref[...] = up
    hidden_ref[...] = (gate * (0.5 + 0.5 * lax.erf(gate * math.sqrt(0.5))) * up).astype(BF)


def feed_back_kernel(
    ff, c_ref, gate_ref, up_ref, hidden_ref, w_ref, down_ref, both_ref, part_ref, out_ref
):
    gate, up = gate_ref[...], up_ref[...]
    out_ref[...] = product(hidden_ref[...], down_ref[...]).astype(BF)
    hidden_grad = times_transposed(c_ref[...], down_ref[...])
    bell = 0.5 + 0.5 * lax.erf(gate * math.sqrt(0.5))
    slope = bell + gate * (math.sqrt(0.5 / math.pi) * jnp.exp(-0.5 * gate * gate))
    both = jnp.concatenate([hidden_grad * up * slope, hidden_grad * (gate * bell)], axis=1)
    both = both.astype(BF)
    both_ref[...] = both
    part_ref[...] = times_transposed(both, w_ref[...]).astype(BF)


def by_rows(block, width):
    return pl.BlockSpec((block, width), lambda i: (i, 0))


def kept(shape):
    return pl.BlockSpec(shape, lambda i: (0, 0), pipeline_mode=pl.Buffered(1))


FEED_BLOCK = 256


def feed_forward(x, weight):
    length, width = x.shape
    ff = weight.shape[1] // 2
    return pl.pallas_call(
        functools.partial(feed_forward_kernel, ff),
        grid=(length // FEED_BLOCK,),
        in_specs=[by_rows(FEED_BLOCK, width), kept(weight.shape)],
        out_specs=[by_rows(FEED_BLOCK, ff)] * 3,
        out_shape=(
            jax.ShapeDtypeStruct((length, ff), F32),
            jax.ShapeDtypeStruct((length, ff), F32),
            jax.ShapeDtypeStruct((length, ff), BF),
        ),
        compiler_params=pltpu.CompilerParams(vmem_limit_bytes=48 * 1024 * 1024),
        cost_estimate=pl.CostEstimate(
            flops=4 * length * width * ff, bytes_accessed=weight.size * 4, transcendentals=0
        ),
        name="feed_forward",
    )(x, weight)


def feed_backward(cotangent, gate, up, hidden, weight, down):
    length, width = cotangent.shape
    ff = weight.shape[1] // 2
    return pl.pallas_call(
        functools.partial(feed_back_kernel, ff),
        grid=(length // FEED_BLOCK,),
        in_specs=[by_rows(FEED_BLOCK, width)]
        + [by_rows(FEED_BLOCK, ff)] * 3
        + [kept(weight.shape), kept(down.shape)],
        out_specs=[
            by_rows(FEED_BLOCK, 2 * ff),
            by_rows(FEED_BLOCK, width),
            by_rows(FEED_BLOCK, width),
        ],
        out_shape=(
            jax.ShapeDtypeStruct((length, 2 * ff), BF),
            jax.ShapeDtypeStruct((length, width), BF),
            jax.ShapeDtypeStruct((length, width), BF),
        ),
        compiler_params=pltpu.CompilerParams(vmem_limit_bytes=56 * 1024 * 1024),
        cost_estimate=pl.CostEstimate(
            flops=8 * length * width * ff, bytes_accessed=weight.size * 4, transcendentals=0
        ),
        name="feed_back",
    )(cotangent, gate, up, hidden, weight, down)


def square_parts(parts, boxes, sends, recvs, first):
    me = lax.axis_index("seq")
    across, along = me ^ 1, me ^ 2
    inbox_x, inbox_y, via_x, via_y, out_x, out_y = boxes
    half = via_x.shape[0]
    low, high = pl.ds(0, half), pl.ds(half, half)
    copies = [
        remote(parts.at[3, low], via_x, sends, recvs, first, across),
        remote(parts.at[3, high], via_y, sends, recvs, first + 1, along),
        remote(parts.at[1, low], inbox_x.at[low], sends, recvs, first + 2, across),
        remote(parts.at[2, high], inbox_y.at[high], sends, recvs, first + 3, along),
        remote(out_y, inbox_y.at[low], sends, recvs, first + 4, along),
        remote(out_x, inbox_x.at[high], sends, recvs, first + 5, across),
    ]

    def finish():
        copies[0].wait_recv()
        out_y[...] = (parts[2, :half].astype(F32) + via_x[...].astype(F32)).astype(BF)
        copies[4].start()
        copies[1].wait_recv()
        out_x[...] = (parts[1, half:].astype(F32) + via_y[...].astype(F32)).astype(BF)
        copies[5].start()
        for copy in copies[2:]:
            copy.wait_recv()

    def total(rows):
        return (
            parts[0, rows].astype(F32)
            + inbox_x[rows, :].astype(F32)
            + inbox_y[rows, :].astype(F32)
        )

    return copies, finish, total


def square_gather(own, out_ref, sends, recvs, first):
    me = lax.axis_index("seq")
    across, along = me ^ 1, me ^ 2
    half = own.shape[0] // 2

    def part(ref, i):
        return ref.at[pl.ds(i * half, half)]

    copies = [
        remote(part(own, 0), part(out_ref.at[me], 0), sends, recvs, first, across),
        remote(part(own, 1), part(out_ref.at[me], 1), sends, recvs, first + 1, along),
        remote(part(own, 1), part(out_ref.at[me], 1), sends, recvs, first + 2, across),
        remote(part(own, 0), part(out_ref.at[me], 0), sends, recvs, first + 3, along),
        remote(
            part(out_ref.at[across], 0), part(out_ref.at[across], 0), sends, recvs, first + 4, along
        ),
        remote(
            part(out_ref.at[along], 1), part(out_ref.at[along], 1), sends, recvs, first + 5, across
        ),
    ]

    def finish():
        copies[0].wait_recv()
        copies[4].start()
        copies[1].wait_recv()
        copies[5].start()
        for copy in copies[2:]:
            copy.wait_recv()

    return copies, finish


def block_rows(k, rows):
    return pl.ds(pl.multiple_of((lax.axis_index("seq") ^ k) * rows, rows), rows)


def load_output(moves, cut, swapped_any, w_ref):
    loads = []
    for block in range(swapped_any.shape[1]):
        for k in range(swapped_any.shape[0]):
            skip, at = cut.skip(k), block * cut.rows + cut.start(k)
            loads.append(
                moves.start(
                    swapped_any.at[k, block, slice(skip, cut.width)],
                    w_ref.at[slice(at + skip, at + cut.width)],
                )
            )
    return loads


def project_kernel(
    cut, g_any, w_any, x_ref, gain_ref, middle_ref, own_ref,
    g_ref, w_ref, parts, inbox_x, inbox_y, via_x, via_y, out_x, out_y, sends, recvs, locals_,
):
    me = lax.axis_index("seq")
    rows = x_ref.shape[0]
    half = rows // 2
    moves = Moves(locals_)
    loads = load_output(moves, cut, w_any, w_ref)
    loads.append(moves.start(g_any, g_ref))
    greet((me ^ 1, me ^ 2))
    boxes = (inbox_x, inbox_y, via_x, via_y, out_x, out_y)
    copies, finish, total = square_parts(parts, boxes, sends, recvs, 0)

    def part(k):
        parts[k] = product(g_ref[block_rows(k, rows), :], w_ref[...]).astype(BF)

    for load in loads:
        load.wait()
    part(3)
    copies[0].start()
    copies[1].start()
    part(1)
    copies[2].start()
    part(2)
    copies[3].start()
    part(0)
    finish()
    for i in range(2):
        here = slice(i * half, (i + 1) * half)
        middle = x_ref[here, :].astype(F32) + total(here)
        middle_ref[here, :] = middle
        own_ref[here, :] = normalize(middle, gain_ref[...]).astype(BF)
    for copy in copies:
        copy.wait_send()


def square_scratch(rows, width):
    return [
        pltpu.VMEM((4, rows, width), BF),
        pltpu.VMEM((rows, width), BF),
        pltpu.VMEM((rows, width), BF),
        pltpu.VMEM((rows // 2, width), BF),
        pltpu.VMEM((rows // 2, width), BF),
        pltpu.VMEM((rows // 2, width), BF),
        pltpu.VMEM((rows // 2, width), BF),
    ]


def square_call(body, out_shape, out_specs, scratch, inputs, call, cost, name):
    return pl.pallas_call(
        body,
        out_shape=out_shape,
        in_specs=[IN_VMEM] * len(inputs),
        out_specs=out_specs,
        scratch_shapes=scratch,
        compiler_params=pltpu.CompilerParams(
            collective_id=call, has_side_effects=True, vmem_limit_bytes=56 * 1024 * 1024
        ),
        cost_estimate=transfer_cost(cost),
        name=name,
    )(*inputs)


def comm_call(body, inputs, outputs, scratch, remotes, moves, call, cost, name):
    return pl.pallas_call(
        body,
        out_shape=tuple(jax.ShapeDtypeStruct(shape, kind) for shape, kind, _ in outputs),
        in_specs=[IN_VMEM if whole else ANYWHERE for _, whole in inputs],
        out_specs=tuple(IN_VMEM if whole else ANYWHERE for _, _, whole in outputs),
        scratch_shapes=scratch
        + [
            pltpu.SemaphoreType.DMA((remotes,)),
            pltpu.SemaphoreType.DMA((remotes,)),
            pltpu.SemaphoreType.DMA((moves,)),
        ],
        compiler_params=pltpu.CompilerParams(
            collective_id=call, has_side_effects=True, vmem_limit_bytes=60 * 1024 * 1024
        ),
        cost_estimate=transfer_cost(cost),
        name=name,
    )(*[value for value, _ in inputs])


def project_and_norm(gated, swapped, x, gain, cut, call):
    rows, width = x.shape
    return comm_call(
        functools.partial(project_kernel, cut),
        [(gated, False), (swapped, False), (x, True), (gain[None, :], True)],
        [((rows, width), F32, True), ((rows, width), BF, True)],
        [pltpu.VMEM(gated.shape, BF), pltpu.VMEM((gated.shape[1], width), BF)]
        + square_scratch(rows, width),
        6,
        9,
        call,
        x.size,
        "project_and_norm",
    )


def feed_forward_gather_kernel(
    ff, x_any, w_any, c_any, both_any, hidden_any, down_any, full_any,
    full, w_ref, c_ref, both_ref, hidden_ref, total, down_ref, sends, recvs, locals_,
):
    me = lax.axis_index("seq")
    rows = x_any.shape[0]
    moves = Moves(locals_)
    load_x = moves.start(x_any, full.at[me])
    load_w = moves.start(w_any, w_ref)
    load_c = moves.start(c_any, c_ref)
    greet((me ^ 1, me ^ 2))
    load_x.wait()
    copies, _ = square_gather(full.at[me], full, sends, recvs, 0)
    for copy in copies[:4]:
        copy.start()

    def block(k):
        here = block_rows(k, rows)
        x = full[me ^ k]
        moves.store(full.at[me ^ k], full_any.at[me ^ k])
        both = product(x, w_ref[...])
        gate, up = both[:, :ff], both[:, ff:]
        both_ref[here, :] = both
        moves.store(both_ref.at[here], both_any.at[here])
        hidden = (gate * (0.5 + 0.5 * lax.erf(gate * math.sqrt(0.5))) * up).astype(BF)
        hidden_ref[here, :] = hidden
        moves.store(hidden_ref.at[here], hidden_any.at[here])
        term = transposed_times(hidden, c_ref[here, :])
        if k == 0:
            total[...] = term
        elif k < 3:
            total[...] += term
        else:
            down_ref[...] = (total[...] + term).astype(BF)

    load_w.wait()
    load_c.wait()
    block(0)
    copies[0].wait_recv()
    copies[4].start()
    copies[1].wait_recv()
    copies[5].start()
    copies[2].wait_recv()
    block(1)
    copies[3].wait_recv()
    block(2)
    copies[4].wait_recv()
    copies[5].wait_recv()
    block(3)
    moves.store(down_ref, down_any)
    moves.close()
    for copy in copies:
        copy.wait_send()


def feed_forward_gather(own, weight, cotangent, call):
    rows, width = own.shape
    length, ff = 4 * rows, weight.shape[1] // 2
    both, hidden, down, full = comm_call(
        functools.partial(feed_forward_gather_kernel, ff),
        [(own, False), (weight, False), (cotangent, False)],
        [
            ((length, 2 * ff), F32, False),
            ((length, ff), BF, False),
            ((ff, width), BF, False),
            ((4, rows, width), BF, False),
        ],
        [
            pltpu.VMEM((4, rows, width), BF),
            pltpu.VMEM(weight.shape, BF),
            pltpu.VMEM(cotangent.shape, BF),
            pltpu.VMEM((length, 2 * ff), F32),
            pltpu.VMEM((length, ff), BF),
            pltpu.VMEM((ff, width), F32),
            pltpu.VMEM((ff, width), BF),
        ],
        6,
        16,
        call,
        own.size,
        "feed_forward_gather",
    )
    return both, hidden, down, full.reshape(length, width)


def feed_back_scatter_kernel(
    ff, c_any, both_any, w_any, down_any, x_any, m_ref, own_c_ref, gain_ref,
    grad_ref, term_ref, branch_ref, dw_any,
    c_ref, both_ref, w_ref, down_ref, x_ref, low, dw_ref,
    parts, inbox_x, inbox_y, via_x, via_y, out_x, out_y, sends, recvs, locals_,
):
    me = lax.axis_index("seq")
    rows = own_c_ref.shape[0]
    half = rows // 2
    moves = Moves(locals_)
    load_down = moves.start(down_any, down_ref)
    load_w = moves.start(w_any, w_ref)
    order = (3, 1, 2, 0)
    loads = []
    for k in order:
        here = block_rows(k, rows)
        loads.append(moves.start(c_any.at[here], c_ref.at[here]))
        loads.append(moves.start(both_any.at[here], both_ref.at[here]))
    load_x = moves.start(x_any, x_ref)
    greet((me ^ 1, me ^ 2))
    boxes = (inbox_x, inbox_y, via_x, via_y, out_x, out_y)
    copies, _, total = square_parts(parts, boxes, sends, recvs, 0)

    def part(k):
        here = block_rows(k, rows)
        at = order.index(k)
        loads[2 * at].wait()
        loads[2 * at + 1].wait()
        gate, up = both_ref[here, :ff], both_ref[here, ff:]
        hidden_grad = times_transposed(c_ref[here, :], down_ref[...])
        bell = 0.5 + 0.5 * lax.erf(gate * math.sqrt(0.5))
        slope = bell + gate * (math.sqrt(0.5 / math.pi) * jnp.exp(-0.5 * gate * gate))
        grads = jnp.concatenate([hidden_grad * up * slope, hidden_grad * (gate * bell)], axis=1)
        grads = grads.astype(BF)
        low[here, :] = grads
        parts[k] = times_transposed(grads, w_ref[...]).astype(BF)

    load_down.wait()
    load_w.wait()
    part(3)
    copies[0].start()
    copies[1].start()
    part(1)
    copies[2].start()
    part(2)
    copies[3].start()
    copies[0].wait_recv()
    out_y[...] = (parts[2, :half].astype(F32) + via_x[...].astype(F32)).astype(BF)
    copies[4].start()
    copies[1].wait_recv()
    out_x[...] = (parts[1, half:].astype(F32) + via_y[...].astype(F32)).astype(BF)
    copies[5].start()
    part(0)
    load_x.wait()
    for b in range(x_ref.shape[1] // BLOCK):
        lanes = slice(b * BLOCK, (b + 1) * BLOCK)
        dw_ref[lanes, :] = transposed_times(x_ref[:, lanes], low[...]).astype(BF)
        moves.store(dw_ref.at[lanes], dw_any.at[lanes])
    for copy in copies[2:]:
        copy.wait_recv()
    term = jnp.zeros((1, gain_ref.shape[1]), F32)
    for i in range(2):
        here = slice(i * half, (i + 1) * half)
        back, terms = norm_back(m_ref[here, :], total(here), gain_ref[...])
        grad = own_c_ref[here, :].astype(F32) + back
        grad_ref[here, :] = grad
        branch_ref[here, :] = grad.astype(BF)
        term = term + jnp.sum(terms, axis=0, keepdims=True)
    term_ref[...] = term
    moves.close()
    for copy in copies:
        copy.wait_send()


def feed_back_scatter(cotangent, both, weight, down, x, middle, own_cotangent, gain, call):
    rows, width = own_cotangent.shape
    length, ff = cotangent.shape[0], weight.shape[1] // 2
    grad, term, branch, dw = comm_call(
        functools.partial(feed_back_scatter_kernel, ff),
        [
            (cotangent, False),
            (both, False),
            (weight, False),
            (down, False),
            (x, False),
            (middle, True),
            (own_cotangent, True),
            (gain[None, :], True),
        ],
        [
            ((rows, width), F32, True),
            ((1, width), F32, True),
            ((rows, width), BF, True),
            ((width, 2 * ff), BF, False),
        ],
        [
            pltpu.VMEM(cotangent.shape, BF),
            pltpu.VMEM(both.shape, F32),
            pltpu.VMEM(weight.shape, BF),
            pltpu.VMEM(down.shape, BF),
            pltpu.VMEM(x.shape, BF),
            pltpu.VMEM((length, 2 * ff), BF),
            pltpu.VMEM((width, 2 * ff), BF),
        ]
        + square_scratch(rows, width),
        6,
        11 + width // BLOCK,
        call,
        own_cotangent.size,
        "feed_back_scatter",
    )
    return grad, term[0], branch, dw


def norm_back(values, grad, gain):
    centered = values - jnp.mean(values, axis=-1, keepdims=True)
    spread = lax.rsqrt(jnp.mean(centered * centered, axis=-1, keepdims=True) + EPSILON)
    unit = centered * spread
    g = grad * gain
    back = g - jnp.mean(g, axis=-1, keepdims=True)
    back = spread * (back - unit * jnp.mean(g * unit, axis=-1, keepdims=True))
    return back, grad * unit


def square_pass(own, out_ref, sends, recvs, first, half):
    me = lax.axis_index("seq")
    across, along = me ^ 1, me ^ 2
    spans = (slice(0, half), slice(half, own.shape[0]))

    def part(ref, i):
        return ref.at[spans[i]]

    return [
        remote(part(own, 0), part(out_ref.at[me], 0), sends, recvs, first, across),
        remote(part(own, 1), part(out_ref.at[me], 1), sends, recvs, first + 1, along),
        remote(part(own, 1), part(out_ref.at[me], 1), sends, recvs, first + 2, across),
        remote(part(own, 0), part(out_ref.at[me], 0), sends, recvs, first + 3, along),
        remote(
            part(out_ref.at[across], 0), part(out_ref.at[across], 0), sends, recvs, first + 4, along
        ),
        remote(
            part(out_ref.at[along], 1), part(out_ref.at[along], 1), sends, recvs, first + 5, across
        ),
    ]


def pass_on(copies):
    copies[0].wait_recv()
    copies[4].start()
    copies[1].wait_recv()
    copies[5].start()


def half_rows(rows):
    return -(-rows // 32) * 16


def gate_back_scatter_kernel(
    heads, cut, branch_any, w_any, swish_any, retained_any, column_any, hidden_any, down_any,
    mixed_any, gated_any, m_any, dswish_any, dret_any, dws_any, dwo_any, out_ref,
    branch_ref, w_ref, swish_ref, retained_ref, column_ref, hidden_ref, down_ref, mixed_ref,
    gated_ref, m_ref, dswish_ref, dret_ref, dws_ref, dwo_ref,
    parts, inbox_x, inbox_y, via_x, via_y, out_x, out_y, sends, recvs, locals_,
):
    me = lax.axis_index("seq")
    rows = out_ref.shape[0]
    half = rows // 2
    moves = Moves(locals_)
    load_down = moves.start(down_any, down_ref)
    load_hidden = moves.start(hidden_any, hidden_ref)
    load_gate = load_output(moves, cut, w_any, w_ref)
    blocks = branch_ref.shape[0] // BLOCK
    load_rows = []
    for i in range(blocks):
        here = slice(i * BLOCK, (i + 1) * BLOCK)
        load_rows.append(
            [
                moves.start(branch_any.at[here], branch_ref.at[here]),
                moves.start(swish_any.at[here], swish_ref.at[here]),
                moves.start(retained_any.at[:, here], retained_ref.at[:, here]),
            ]
        )
    load_mixed = moves.start(mixed_any, mixed_ref)
    load_column = moves.start(column_any, column_ref)
    load_gated = moves.start(gated_any, gated_ref)
    load_m = moves.start(m_any, m_ref)
    greet((me ^ 1, me ^ 2))
    boxes = (inbox_x, inbox_y, via_x, via_y, out_x, out_y)
    copies, _, total = square_parts(parts, boxes, sends, recvs, 0)

    def part(k):
        here = block_rows(k, rows)
        parts[k] = product(hidden_ref[here, :], down_ref[...]).astype(BF)

    load_hidden.wait()
    load_down.wait()
    part(3)
    copies[0].start()
    copies[1].start()
    part(1)
    copies[2].start()
    part(2)
    copies[3].start()
    for load in load_gate:
        load.wait()
    for i in range(blocks):
        here = slice(i * BLOCK, (i + 1) * BLOCK)
        for load in load_rows[i]:
            load.wait()
        gate_back_rows(
            heads, here, branch_ref[here, :], w_ref, swish_ref, retained_ref, dswish_ref, dret_ref
        )
    moves.store(dswish_ref, dswish_any)
    moves.store(dret_ref, dret_any)
    copies[0].wait_recv()
    out_y[...] = (parts[2, :half].astype(F32) + via_x[...].astype(F32)).astype(BF)
    copies[4].start()
    copies[1].wait_recv()
    out_x[...] = (parts[1, half:].astype(F32) + via_y[...].astype(F32)).astype(BF)
    copies[5].start()
    padded = dswish_ref.shape[1]
    spare = lax.broadcasted_iota(jnp.int32, (BLOCK, padded), 1) == heads * VAL_HEAD
    load_mixed.wait()
    load_column.wait()
    for b in range(dws_ref.shape[0] // BLOCK):
        here = slice(b * BLOCK, (b + 1) * BLOCK)
        term = product(mixed_ref[here, :], dswish_ref[...])
        dws_ref[here, :] = jnp.where(spare, column_ref[here, :], term).astype(BF)
        moves.store(dws_ref.at[here], dws_any.at[here])
    load_gated.wait()
    step, tile, lane = 2 * BLOCK, 16, 128
    for h in range(heads):
        value_lanes = head_lanes(h, VAL_HEAD)
        for b in range(branch_ref.shape[1] // step):
            lanes = slice(b * step, (b + 1) * step)
            wide = transposed_times(gated_ref[:, value_lanes], branch_ref[:, lanes]).astype(BF)
            for k in range(4):
                for r in range(cut.width // tile):
                    at = cut.start(k) + r * tile
                    for c in range(step // lane):
                        dwo_ref[
                            h, k,
                            (b * step // lane + c) * tile : (b * step // lane + c + 1) * tile,
                            r * lane : (r + 1) * lane,
                        ] = wide[at : at + tile, c * lane : (c + 1) * lane]
        moves.store(dwo_ref.at[h], dwo_any.at[h])
    part(0)
    load_m.wait()
    for copy in copies[2:]:
        copy.wait_recv()
    out_ref[...] = (m_ref[...] + total(slice(0, rows))).astype(BF)
    moves.close()
    for copy in copies:
        copy.wait_send()


def gate_backward_scatter(
    branch, swapped, swish, retained, column, hidden, down, mixed_t, gated, middle, heads, padded,
    cut, call,
):
    length, width = branch.shape
    rows = middle.shape[0]
    dwo = (heads, 4, width // 8, cut.width * 8)
    inputs = (branch, swapped, swish, retained, column, hidden, down, mixed_t, gated, middle)
    weight = jax.ShapeDtypeStruct((heads * VAL_HEAD, width), BF)
    outputs = [
        ((length, padded), BF, False),
        ((heads, length, VAL_HEAD), BF, False),
        ((width, padded), BF, False),
        (dwo, BF, False),
        ((rows, width), BF, True),
    ]
    return comm_call(
        functools.partial(gate_back_scatter_kernel, heads, cut),
        [(value, False) for value in inputs],
        outputs,
        [pltpu.VMEM(v.shape, v.dtype) for v in (branch, weight) + inputs[2:]]
        + [pltpu.VMEM(shape, kind) for shape, kind, _ in outputs[:4]]
        + square_scratch(rows, width),
        6,
        20 + 3 * length // BLOCK + width // BLOCK,
        call,
        middle.size,
        "gate_back_scatter",
    )


def retention_back_exchange_kernel(
    heads, q_any, k_any, v_any, dret_any, table_ref, cos_ref, sin_ref, mixed_any, send_any, share_any,
    dqk_any, dv_any, merged_any, full_any,
    q_ref, k_ref, v_ref, dret_ref, mixed_ref, send_ref, dqk_ref, dv_ref, dwqk_ref, twin_ref, sum_ref,
    zero_ref, dk_sum, dv_sum, sends, recvs, locals_,
):
    me = lax.axis_index("seq")
    shard = lax.axis_index("fsdp")
    core = lax.rem(shard, 2)
    moves = Moves(locals_)
    load_send = moves.start(send_any, send_ref)
    loads = [
        moves.start(source, target)
        for source, target in (
            (q_any, q_ref), (k_any, k_ref), (v_any, v_ref), (dret_any, dret_ref)
        )
    ]
    load_mixed = moves.start(mixed_any, mixed_ref)
    barrier = pltpu.get_barrier_semaphore()
    for k in (1, 2, 3):
        pl.semaphore_signal(barrier, inc=1, device_id={"seq": me ^ k}, device_id_type=MESH)
    pl.semaphore_signal(barrier, inc=1, device_id={"fsdp": shard ^ 1}, device_id_type=MESH)
    pl.semaphore_wait(barrier, 4)
    load_send.wait()
    twin = pltpu.make_async_remote_copy(
        src_ref=send_ref.at[1 - core],
        dst_ref=twin_ref,
        send_sem=sends.at[9],
        recv_sem=recvs.at[9],
        device_id={"fsdp": shard ^ 1},
        device_id_type=MESH,
    )
    twin.start()
    passed = square_pass(share_any, full_any, sends, recvs, 0, half_rows(share_any.shape[0]))
    for copy in passed[:4]:
        copy.start()
    moves.store(share_any, full_any.at[me])
    step, wide = sum_ref.shape[1:]
    at = dqk_ref.shape[1]

    def place(column, parity):
        return merged_any.at[
            pl.ds(pl.multiple_of((2 * column + parity) * step, step), step), pl.ds(at, wide)
        ]

    zero_ref[...] = jnp.zeros_like(zero_ref)
    for column in range(4):
        moves.store(zero_ref, place(column, 1 - core))
    for load in loads:
        load.wait()
    parts = []
    swaps = [
        remote(sum_ref.at[me ^ k], place(me, core), sends, recvs, 5 + k, me ^ k) for k in (3, 1, 2)
    ]
    for h in range(heads):
        parts.append(
            retention_back_head(
                h, heads, q_ref, k_ref, v_ref, dret_ref, table_ref, cos_ref, sin_ref, dqk_ref,
                dv_ref, dk_sum, dv_sum,
            )
        )
        if h == 0:
            twin.wait_recv()
            for k in range(4):
                sum_ref[k] = (send_ref[core, k].astype(F32) + twin_ref[k].astype(F32)).astype(BF)
            for copy in swaps:
                copy.start()
            moves.store(sum_ref.at[me], place(me, core))
            pass_on(passed)
    dv_ref[...] = pad_lanes(parts, dv_ref.shape[1])
    moves.store(dv_ref, dv_any)
    moves.store(dqk_ref, dqk_any)
    load_mixed.wait()
    for b in range(mixed_ref.shape[0] // BLOCK):
        here = slice(b * BLOCK, (b + 1) * BLOCK)
        dwqk_ref[here, :] = product(mixed_ref[here, :], dqk_ref[...]).astype(BF)
        moves.store(dwqk_ref.at[here], merged_any.at[here, slice(0, at)])
    for copy in passed[2:] + swaps:
        copy.wait_recv()
    moves.close()
    for copy in passed + swaps + [twin]:
        copy.wait_send()


def retention_backward_exchange(
    q, k, v, dret, table, cosine, sine, mixed_t, send, share, heads, padded, call
):
    width, length = mixed_t.shape
    qk = heads * KEY_HEAD
    inputs = (
        (q, False), (k, False), (v, False), (dret, False), (table, True), (cosine, True),
        (sine, True), (mixed_t, False), (send, False), (share, False),
    )
    staged = (q, k, v, dret, mixed_t, send)
    block = send.shape[1:]
    return comm_call(
        functools.partial(retention_back_exchange_kernel, heads),
        inputs,
        [
            ((length, 2 * qk), BF, False),
            ((length, padded), BF, False),
            ((width, 2 * qk + block[2]), BF, False),
            ((4,) + share.shape, BF, False),
        ],
        [pltpu.VMEM(value.shape, BF) for value in staged]
        + [
            pltpu.VMEM((length, 2 * qk), BF),
            pltpu.VMEM((length, padded), BF),
            pltpu.VMEM((width, 2 * qk), BF),
            pltpu.VMEM(block, BF),
            pltpu.VMEM(block, BF),
            pltpu.VMEM(block[1:], BF),
            pltpu.VMEM((length, KEY_HEAD), F32),
            pltpu.VMEM((length, VAL_HEAD), F32),
        ],
        10,
        16 + width // BLOCK,
        call,
        send.size // 4,
        "retention_back_exchange",
    )


def input_back_kernel(
    offsets, dqk_any, dv_any, ds_any, w_any, x_any, grad_any, gain_ref, share_any,
    dx_ref, term_ref, full_any, dqk_ref, dv_ref, ds_ref, w_ref, x_ref, grad_ref,
    parts, inbox_x, inbox_y, via_x, via_y, out_x, out_y, sends, recvs, locals_,
):
    at_value, at_swish = offsets
    me = lax.axis_index("seq")
    rows = x_ref.shape[0]
    half = rows // 2
    moves = Moves(locals_)
    spans = (slice(0, at_value), slice(at_value, at_swish), slice(at_swish, w_ref.shape[1]))
    grads = ((dqk_any, dqk_ref), (dv_any, dv_ref), (ds_any, ds_ref))
    loads = []
    for span, (source, target) in zip(spans, grads, strict=True):
        loads.append(moves.start(source, target))
        loads.append(moves.start(w_any.at[:, span], w_ref.at[:, span]))
    load_x = moves.start(x_any, x_ref)
    load_grad = moves.start(grad_any, grad_ref)
    greet((me ^ 1, me ^ 2))
    boxes = (inbox_x, inbox_y, via_x, via_y, out_x, out_y)
    copies, _, total = square_parts(parts, boxes, sends, recvs, 0)
    passed = square_pass(share_any, full_any, sends, recvs, 6, half_rows(share_any.shape[0]))
    passed[0].start()
    passed[1].start()
    moves.store(share_any, full_any.at[me])

    def part(k):
        here = block_rows(k, rows)
        whole = 0.0
        for n, (_, ref) in enumerate(grads):
            if k == 3:
                loads[2 * n].wait()
                loads[2 * n + 1].wait()
            whole = whole + times_transposed(ref[here, :], w_ref[:, spans[n]])
        parts[k] = whole.astype(BF)

    part(3)
    copies[0].start()
    copies[1].start()
    part(1)
    copies[2].start()
    part(2)
    copies[3].start()
    pass_on(passed)
    copies[0].wait_recv()
    out_y[...] = (parts[2, :half].astype(F32) + via_x[...].astype(F32)).astype(BF)
    copies[4].start()
    copies[1].wait_recv()
    out_x[...] = (parts[1, half:].astype(F32) + via_y[...].astype(F32)).astype(BF)
    copies[5].start()
    passed[2].start()
    passed[3].start()
    part(0)
    for copy in copies[2:]:
        copy.wait_recv()
    load_x.wait()
    load_grad.wait()
    term = jnp.zeros((1, x_ref.shape[1]), F32)
    for i in range(2):
        here = slice(i * half, (i + 1) * half)
        back, terms = norm_back(x_ref[here, :].astype(F32), total(here), gain_ref[...])
        dx_ref[here, :] = (grad_ref[here, :] + back).astype(BF)
        term = term + jnp.sum(terms, axis=0, keepdims=True)
    term_ref[...] = term
    for copy in passed[2:]:
        copy.wait_recv()
    moves.close()
    for copy in copies + passed:
        copy.wait_send()


def input_backward(dqk, dv, ds, weight, x, grad, gain, share, offsets, call):
    rows, width = x.shape
    staged = (dqk, dv, ds, weight, x, grad)
    dx, term, full = comm_call(
        functools.partial(input_back_kernel, offsets),
        [(value, False) for value in staged] + [(gain[None, :], True), (share, False)],
        [
            ((rows, width), BF, True),
            ((1, width), F32, True),
            ((4,) + share.shape, BF, False),
        ],
        [pltpu.VMEM(value.shape, value.dtype) for value in staged] + square_scratch(rows, width),
        12,
        9,
        call,
        x.size + share.size,
        "input_backward",
    )
    return dx, term[0], full


def join(pieces):
    return jnp.concatenate(pieces, axis=1) if len(pieces) > 1 else pieces[0]


def unpack_columns_kernel(width, in_ref, out_ref):
    out_ref[...] = join([in_ref[k][:, :width].astype(F32) for k in range(in_ref.shape[0])])


def unpack_columns(gathered, at, width):
    count, rows, whole = gathered.shape
    block = rows // 4 if rows % 64 == 0 else rows
    padded = -(-width // 128) * 128
    return pl.pallas_call(
        functools.partial(unpack_columns_kernel, width),
        grid=(rows // block,),
        in_specs=[pl.BlockSpec((count, block, padded), lambda i: (0, i, at // padded))],
        out_specs=pl.BlockSpec((block, count * width), lambda i: (i, 0)),
        out_shape=jax.ShapeDtypeStruct((rows, count * width), F32),
        name="unpack_columns",
    )(gathered)


def unpack_hidden_kernel(cut, shards, in_ref, gate_ref, up_ref):
    count = in_ref.shape[0]
    for n, out_ref in enumerate((gate_ref, up_ref)):
        pieces = []
        for f in range(shards):
            for k in range(count):
                at = (n * shards + f) * cut.width
                if cut.skip(k) < cut.width:
                    piece = in_ref[k][:, at + cut.skip(k) : at + cut.width]
                    pieces.append(piece.astype(F32))
        out_ref[...] = join(pieces)


def unpack_hidden(gathered, cut, shards):
    count, rows, whole = gathered.shape
    block = rows // 4 if rows % 64 == 0 else rows
    wide = shards * cut.rows
    return pl.pallas_call(
        functools.partial(unpack_hidden_kernel, cut, shards),
        grid=(rows // block,),
        in_specs=[pl.BlockSpec((count, block, whole), lambda i: (0, i, 0))],
        out_specs=[pl.BlockSpec((block, wide), lambda i: (i, 0))] * 2,
        out_shape=[jax.ShapeDtypeStruct((rows, wide), F32)] * 2,
        name="unpack_hidden",
    )(gathered)


def unpack_output_kernel(cut, in_ref, out_ref):
    tile, lane = 16, 128
    for k in range(in_ref.shape[0]):
        for r in range(cut.skip(k) // tile, cut.width // tile):
            at = cut.start(k) + r * tile
            for c in range(out_ref.shape[1] // lane):
                out_ref[at : at + tile, c * lane : (c + 1) * lane] = in_ref[
                    k, c * tile : (c + 1) * tile, r * lane : (r + 1) * lane
                ].astype(F32)


def unpack_output(gathered, at, cut, width):
    count, rows, whole = gathered.shape
    wide = whole - at
    return pl.pallas_call(
        functools.partial(unpack_output_kernel, cut),
        out_shape=jax.ShapeDtypeStruct((cut.rows, width), F32),
        compiler_params=pltpu.CompilerParams(vmem_limit_bytes=32 * 1024 * 1024),
        name="unpack_output",
    )(gathered[:, :, at:])


def after(values, *others, all_of=False):
    held = lax.optimization_barrier((values,) + others)
    return held if all_of else held[0]


class Cut:
    def __init__(self, rows, count):
        self.rows, self.count = rows, count
        self.width = -(-rows // (count * 16)) * 16

    def start(self, piece):
        if isinstance(piece, int):
            return min(piece * self.width, self.rows - self.width)
        return jnp.minimum(piece * self.width, self.rows - self.width)

    def skip(self, piece):
        if isinstance(piece, int):
            return min(piece * self.width - self.start(piece), self.width)
        return jnp.minimum(piece * self.width - self.start(piece), self.width)

    def assemble(self, pieces, axis):
        kept = []
        for k, piece in enumerate(pieces):
            if self.skip(k) < self.width:
                kept.append(lax.slice_in_dim(piece, self.skip(k), self.width, axis=axis))
        return jnp.concatenate(kept, axis=axis)


def columns_of(weight, index, width, padded):
    piece = lax.dynamic_slice_in_dim(weight, index * width, width, axis=1)
    return jnp.pad(piece, ((0, 0), (0, padded - width)))


def on_device(
    layer_input,
    mixer_gain,
    query_weight,
    key_weight,
    value_weight,
    swish_weight,
    output_weight,
    channel_gain,
    gelu_weight,
    linear_weight,
    down_weight,
    output_cotangent,
):
    groups, local_length, width = layer_input.shape
    seq_count = lax.axis_size("seq")
    shards = lax.axis_size("fsdp")
    me = lax.axis_index("seq")
    per_device = HEADS // seq_count
    rows_count = groups * local_length
    square = seq_count == 4 and rows_count % 32 == 0
    length = local_length * seq_count
    key_scale = KEY_HEAD ** (-0.5)
    qk = query_weight.shape[1] // seq_count
    vd = value_weight.shape[1] // seq_count
    vd_pad = -(-vd // 128) * 128
    hidden_units = gelu_weight.shape[1]
    own_rows = down_weight.shape[0]
    cut = Cut(own_rows, seq_count)
    ff = shards * cut.width

    def gather_rows(values):
        return lax.all_gather(values, "fsdp", axis=0, tiled=True)

    def scatter_rows(values):
        return lax.psum_scatter(values.astype(BF), "fsdp", scatter_dimension=0, tiled=True)

    attention_piece = jnp.concatenate(
        [
            columns_of(query_weight, me, qk, qk),
            columns_of(key_weight, me, qk, qk),
            columns_of(value_weight, me, vd, vd_pad),
            columns_of(swish_weight, me, vd, vd_pad),
        ],
        axis=1,
    )
    attention_weight = gather_rows(attention_piece)
    output_piece = lax.dynamic_slice_in_dim(output_weight, cut.start(me), cut.width, axis=0)
    output_pieces = gather_rows(output_piece)
    column = lax.broadcasted_iota(jnp.int32, (hidden_units, ff), 0)
    slot = lax.broadcasted_iota(jnp.int32, (hidden_units, ff), 1)
    chosen = (slot // cut.width) * own_rows + cut.start(me) + slot % cut.width
    selector = (column == chosen).astype(BF)
    gate_piece = product(gelu_weight, selector).astype(BF)
    up_piece = product(linear_weight, selector).astype(BF)
    feed_piece = jnp.concatenate([gate_piece, up_piece], axis=1)
    down_piece = lax.dynamic_slice_in_dim(down_weight, cut.start(me), cut.width, axis=0)
    gains = lax.all_gather(jnp.stack([mixer_gain, channel_gain]), "fsdp", axis=1, tiled=True)
    mixer_scale, channel_scale = gains[0].astype(F32), gains[1].astype(F32)

    local_input = layer_input.reshape(rows_count, width)
    upstream = output_cotangent.reshape(rows_count, width)

    def whole(values, call):
        gathered = gather_seq(values, call)
        return gathered.reshape(length * groups, width)

    input_full = whole(local_input, 0)
    upstream_full = whole(after(upstream, input_full), 1)
    inputs = local_input.astype(F32)

    blocks = shards // seq_count
    mixed_low = normalize(input_full.astype(F32), mixer_scale).astype(BF)
    mixed_turned = mixed_low.T
    output_pieces = after(output_pieces, upstream_full, gains)
    swapped = exchange_seq(output_pieces.reshape(seq_count, blocks, cut.width, width), 2)
    feed_weight = gather_rows(after(feed_piece, swapped))

    cosine, sine = rotation_tables(length, KEY_HEAD // 2)
    head_ids = me * per_device + jnp.arange(per_device, dtype=jnp.int32)
    table = decay_table(head_ids, length)
    attention_weight, mixed_low, mixed_turned, table = after(
        attention_weight, mixed_low, mixed_turned, table, all_of=True
    )
    query_low, key_low, value_low, swish_pre, retained, gated_low = retention_forward(
        mixed_low, attention_weight, cosine, sine, table, per_device, (qk, 2 * qk, 2 * qk + vd_pad)
    )

    kept_rows = lax.broadcasted_iota(jnp.int32, down_piece.shape, 0) >= cut.skip(me)
    down_full = gather_rows(after(jnp.where(kept_rows, down_piece, jnp.zeros_like(down_piece)), gated_low))
    if square:
        middle, channel_own = project_and_norm(
            gated_low, swapped, local_input, channel_scale, cut, 3
        )
        both_pre, hidden_low, down_term, channel_full = feed_forward_gather(
            channel_own, feed_weight, upstream_full, 4
        )
        down_share = scatter_rows(down_term)
        middle_grad, channel_term, branch_own, feed_term = feed_back_scatter(
            after(upstream_full, down_term), both_pre, feed_weight, down_full, channel_full,
            middle, upstream, channel_scale, 6,
        )
        feed_share = scatter_rows(feed_term)
        branch_full = whole(branch_own, 7)
    else:
        output_full = jnp.concatenate(
            [
                cut.assemble([swapped[piece, block] for piece in range(seq_count)], 0)
                for block in range(blocks)
            ],
            axis=0,
        )
        middle = inputs + scatter_seq(product(gated_low, output_full).astype(BF), 3)
        channel_full = whole(normalize(middle, channel_scale).astype(BF), 4)
        gate_pre, up_pre, hidden_low = feed_forward(channel_full, feed_weight)
        down_share = scatter_rows(transposed_times(hidden_low, upstream_full).astype(BF))
        feed_low_grad, channel_part, hidden_part = feed_backward(
            upstream_full, gate_pre, up_pre, hidden_low, feed_weight, down_full
        )
        feed_share = scatter_rows(transposed_times(channel_full, feed_low_grad).astype(BF))
        middle_local, channel_terms = norm_back(
            middle, scatter_seq(channel_part, 6), channel_scale
        )
        channel_term = jnp.sum(channel_terms, axis=0)
        middle_grad = upstream.astype(F32) + middle_local
        branch_full = whole(middle_grad.astype(BF), 7)

    at_value, at_swish = 2 * qk, 2 * qk + vd_pad
    spare = lax.broadcasted_iota(jnp.int32, (width, vd_pad), 1) == vd
    if square:
        swish_grad, retained_grad, swish_term, output_send, layer_output = gate_backward_scatter(
            after(branch_full, down_share), swapped, swish_pre, retained,
            channel_term[:, None], hidden_low, down_full, mixed_turned, gated_low, middle,
            per_device, vd_pad, cut, 5,
        )
        swish_share = scatter_rows(swish_term)
        key_grad, value_grad, merged_term, down_all = retention_backward_exchange(
            query_low, key_low, value_low, after(retained_grad, feed_share), table, cosine, sine,
            mixed_turned, output_send, down_share, per_device, vd_pad, 8,
        )
        merged_share = scatter_rows(merged_term)
        input_gradient, mixer_term, feed_all = input_backward(
            key_grad, value_grad, swish_grad, attention_weight, local_input, middle_grad,
            mixer_scale, feed_share, (at_value, at_swish), 9,
        )
    else:
        swish_grad, retained_grad = gate_backward(
            branch_full, output_full, swish_pre, retained, per_device, vd_pad
        )
        swish_term = transposed_times(mixed_low, swish_grad)
        swish_term = jnp.where(spare, channel_term[:, None], swish_term).astype(BF)
        swish_share = scatter_rows(swish_term)
        result = middle + scatter_seq(hidden_part, 5)
        layer_output = result.astype(BF)
        key_grad, value_grad = retention_backward(
            query_low, key_low, value_low, retained_grad, table, cosine, sine, per_device, vd_pad
        )
        key_term = transposed_times(mixed_low, key_grad).astype(BF)
        key_share = scatter_rows(key_term)
        mixed_part = (
            times_transposed(key_grad, attention_weight[:, :at_value])
            + times_transposed(value_grad, attention_weight[:, at_value:at_swish])
            + times_transposed(swish_grad, attention_weight[:, at_swish:])
        )
        input_local, mixer_terms = norm_back(
            inputs, scatter_seq(mixed_part.astype(BF), 9), mixer_scale
        )
        mixer_term = jnp.sum(mixer_terms, axis=0)
        input_gradient = (middle_grad + input_local).astype(BF)
        output_term = transposed_times(gated_low, branch_full).astype(BF)
        output_term = output_term.reshape(blocks, own_rows, width)
        output_send = jnp.stack(
            [
                lax.slice_in_dim(output_term, cut.start(k), cut.start(k) + cut.width, axis=1)
                for k in range(seq_count)
            ]
        )
        output_swapped = exchange_seq(output_send, 8)
        output_share = scatter_rows(output_swapped.reshape(shards * cut.width, width))
    input_gradient = input_gradient.reshape(groups, local_length, width)
    value_term = transposed_times(mixed_low, value_grad)
    value_term = jnp.where(spare, mixer_term[:, None], value_term).astype(BF)
    value_share = scatter_rows(value_term)

    layer_output = layer_output.reshape(groups, local_length, width)
    if square:
        down_gradient = cut.assemble([down_all[k] for k in range(seq_count)], 0).astype(F32)
        gelu_gradient, linear_gradient = unpack_hidden(after(feed_all, value_term), cut, shards)
        swish_all = gather_seq(after(swish_share, gelu_gradient), 13)
        merged_all = gather_seq(after(merged_share, swish_all), 15)
        output_gradient = unpack_output(merged_all, at_value, cut, width)
        query_gradient = unpack_columns(merged_all, 0, qk)
        key_gradient = unpack_columns(merged_all, qk, qk)
        value_share = after(value_share, merged_all)
    else:
        down_all = gather_seq(down_share, 10)
        feed_all = gather_seq(after(feed_share, down_all), 11)
        swish_all = gather_seq(after(swish_share, feed_all), 13)
        output_all = gather_seq(after(output_share, swish_all), 12)
        key_all = gather_seq(after(key_share, output_all), 15)
        value_share = after(value_share, key_all)
        down_gradient = cut.assemble([down_all[k] for k in range(seq_count)], 0).astype(F32)
        output_gradient = cut.assemble([output_all[k] for k in range(seq_count)], 0).astype(F32)
        gelu_gradient, linear_gradient = unpack_hidden(feed_all, cut, shards)
        query_gradient = unpack_columns(key_all, 0, qk)
        key_gradient = unpack_columns(key_all, qk, qk)
    value_all = gather_seq(value_share, 14)

    def gain_order(gathered):
        return jnp.sum(gathered[:, :, vd].astype(F32), axis=0)

    return (
        layer_output,
        input_gradient,
        gain_order(value_all),
        query_gradient,
        key_gradient,
        unpack_columns(value_all, 0, vd),
        unpack_columns(swish_all, 0, vd),
        output_gradient,
        gain_order(swish_all),
        gelu_gradient,
        linear_gradient,
        down_gradient,
    )


def solution(mesh):
    tokens, rows, vector = P("fsdp", "seq", None), P("fsdp", None), P("fsdp")
    return jax.shard_map(
        on_device,
        mesh=mesh,
        in_specs=(
            tokens, vector, rows, rows, rows, rows, rows, vector, rows, rows, rows, tokens,
        ),
        out_specs=(
            tokens, tokens, vector, rows, rows, rows, rows, rows, vector, rows, rows, rows,
        ),
        check_vma=False,
    )
```

```python
import functools
import math

import jax
import jax.numpy as jnp
from jax import lax
from jax.experimental import pallas as pl
from jax.experimental.pallas import tpu as pltpu
from jax.sharding import PartitionSpec as P

HEADS = 8
KEY_HEAD = 256
VAL_HEAD = 432
EPSILON = 1e-05
MESH = pl.DeviceIdType.MESH
BF = jnp.bfloat16
F32 = jnp.float32
IN_VMEM = pl.BlockSpec(memory_space=pltpu.VMEM)
ANYWHERE = pl.BlockSpec(memory_space=pl.ANY)


def product(left, right):
    return jnp.dot(left, right, preferred_element_type=F32)


def times_transposed(left, right):
    return lax.dot_general(left, right, (((1,), (1,)), ((), ())), preferred_element_type=F32)


def transposed_times(left, right):
    return lax.dot_general(left, right, (((0,), (0,)), ((), ())), preferred_element_type=F32)


def normalize(values, gain):
    centered = values - jnp.mean(values, axis=-1, keepdims=True)
    spread = lax.rsqrt(jnp.mean(centered * centered, axis=-1, keepdims=True) + EPSILON)
    return centered * spread * gain


def rotation_tables(length, half_width):
    rates = jnp.exp(-math.log(10000.0) * jnp.arange(half_width, dtype=F32) / (half_width - 1))
    turned = jnp.arange(length, dtype=F32)[:, None] * rates[None, :]
    return (jnp.cos(turned), jnp.sin(turned))


def pad_lanes(pieces, width):
    have = sum(piece.shape[1] for piece in pieces)
    if have < width:
        pieces = pieces + [jnp.zeros((pieces[0].shape[0], width - have), pieces[0].dtype)]
    return jnp.concatenate(pieces, axis=1) if len(pieces) > 1 else pieces[0]


def rotate_pair(values, cosine, sine, back=False):
    half = KEY_HEAD // 2
    first, second = values[:, :half], values[:, half:]
    if back:
        return jnp.concatenate([first * cosine + second * sine, second * cosine - first * sine], 1)
    return jnp.concatenate([first * cosine - second * sine, second * cosine + first * sine], 1)


BLOCK = 256


def decay_tables(head_ids, length):
    rates = jnp.log1p(-jnp.exp2(-5.0 - head_ids.astype(F32)))[:, None, None]
    short = jnp.arange(BLOCK, dtype=jnp.int32)
    long = jnp.arange(2 * length - BLOCK, dtype=jnp.int32)

    def decay(gap):
        far = jnp.exp(jnp.maximum(gap, 0).astype(F32)[None] * rates)
        return jnp.where(gap[None] >= 0, far, 0.0)

    by_row = decay(length - BLOCK + short[:, None] - long[None, :])
    by_column = decay(long[:, None] - (length - BLOCK) - short[None, :])
    return by_row, by_column


def norm_parts(values):
    centered = values - jnp.mean(values, axis=-1, keepdims=True)
    variance = jnp.mean(centered * centered, axis=-1, keepdims=True)
    factor = lax.rsqrt(jnp.maximum(variance, 1.0))
    return centered * factor, factor, variance > 1.0


def rows_of(block):
    return pl.ds(pl.multiple_of(block * BLOCK, BLOCK), BLOCK)


def head_lanes(head, width):
    return slice(head * width, (head + 1) * width)


class Moves:
    def __init__(self, sems):
        self.sems, self.used, self.open = sems, 0, []

    def start(self, source, target):
        copy = pltpu.make_async_copy(source, target, self.sems.at[self.used])
        self.used += 1
        copy.start()
        return copy

    def store(self, source, target):
        self.open.append(self.start(source, target))

    def close(self):
        for copy in self.open:
            copy.wait()


def norm_kernel(x_ref, gain_ref, out_ref, turned_ref):
    normed = normalize(x_ref[...].astype(F32), gain_ref[...])
    out_ref[...] = normed.astype(BF)
    turned_ref[...] = normed.T.astype(BF)


def norm_and_turn(x, gain):
    length, width = x.shape
    return pl.pallas_call(
        norm_kernel,
        grid=(length // BLOCK,),
        in_specs=[
            pl.BlockSpec((BLOCK, width), lambda i: (i, 0)),
            pl.BlockSpec((1, width), lambda i: (0, 0)),
        ],
        out_specs=[
            pl.BlockSpec((BLOCK, width), lambda i: (i, 0)),
            pl.BlockSpec((width, BLOCK), lambda i: (0, i)),
        ],
        out_shape=[
            jax.ShapeDtypeStruct((length, width), BF),
            jax.ShapeDtypeStruct((width, length), BF),
        ],
        compiler_params=pltpu.CompilerParams(vmem_limit_bytes=32 * 1024 * 1024),
        name="norm_and_turn",
    )(x, gain[None, :])


class Series:
    def __init__(self, moves, count, ends):
        self.sems, self.first, self.count, self.ends = moves.sems, moves.used, count, ends
        moves.used += count

    def copy(self, i):
        return pltpu.make_async_copy(*self.ends(i), self.sems.at[self.first + i])

    def start_all(self):
        for i in range(self.count):
            self.copy(i).start()
        return self

    def wait_all(self):
        for i in range(self.count):
            self.copy(i).wait()


def by_block(moves, count, source, target, rows=BLOCK):
    def ends(i):
        here = pl.ds(i * rows if isinstance(i, int) else pl.multiple_of(i * rows, rows), rows)
        if len(source.shape) == 3:
            return source.at[:, here], target.at[:, here]
        return source.at[here], target.at[here]

    return Series(moves, count, ends)


def retention_kernel(
    heads, offsets, mixed_any, w_any, cos_ref, sin_ref, table_ref,
    q_any, k_any, v_any, swish_any, retained_any, gated_any,
    mixed_ref, w_ref, q_ref, k_ref, v_ref, swish_ref, retained_ref, gated_ref, sems,
    between=None,
):
    at_key, at_value, at_swish = offsets
    length = mixed_ref.shape[0]
    blocks = length // BLOCK
    moves = sems if isinstance(sems, Moves) else Moves(sems)
    spans = (
        slice(0, at_key), slice(at_key, at_value), slice(at_value, at_swish),
        slice(at_swish, w_ref.shape[1]),
    )
    loads = by_block(moves, blocks, mixed_any, mixed_ref)
    loads.copy(0).start()
    weights = [moves.start(w_any.at[:, span], w_ref.at[:, span]) for span in spans]
    for i in range(1, blocks):
        loads.copy(i).start()
    stores = [
        by_block(moves, blocks, source, target)
        for source, target in (
            (q_ref, q_any), (k_ref, k_any), (v_ref, v_any), (swish_ref, swish_any),
            (retained_ref, retained_any), (gated_ref, gated_any),
        )
    ]
    k_ref[...] = jnp.zeros_like(k_ref)
    v_ref[...] = jnp.zeros_like(v_ref)
    if between is not None:
        between(-1)

    @pl.loop(0, blocks)
    def _(i):
        rows = rows_of(i)
        loads.copy(i).wait()
        mixed = mixed_ref[rows, :]
        cosine, sine = cos_ref[rows, :], sin_ref[rows, :]

        def projected(n):
            @pl.when(i == 0)
            def _():
                weights[n].wait()

            return product(mixed, w_ref[:, spans[n]])

        for n, (target, scale) in enumerate(((q_ref, 1.0), (k_ref, KEY_HEAD**-0.5))):
            pre = projected(n)
            for h in range(heads):
                lanes = head_lanes(h, KEY_HEAD)
                turned = rotate_pair(pre[:, lanes], cosine, sine)
                target[rows, lanes] = (turned * scale if n else turned).astype(BF)
        value = projected(2)
        for h in range(heads):
            v_ref[h, rows, :] = value[:, head_lanes(h, VAL_HEAD)].astype(BF)
        swish_ref[rows, :] = projected(3)[:, : heads * VAL_HEAD]
        gated = []
        for h in range(heads):
            lanes = head_lanes(h, KEY_HEAD)
            scores = times_transposed(q_ref[rows, lanes], k_ref[:, lanes])
            decay = table_ref[
                h, :, pl.ds(pl.multiple_of((blocks - 1 - i) * BLOCK, BLOCK), length)
            ]
            retained = product((scores * decay).astype(BF), v_ref[h]).astype(BF)
            retained_ref[h, rows, :] = retained
            unit, _, _ = norm_parts(retained.astype(F32))
            s = swish_ref[rows, head_lanes(h, VAL_HEAD)]
            gated.append((s * jax.nn.sigmoid(s) * unit).astype(BF))
        gated_ref[rows, :] = jnp.concatenate(gated, axis=1) if heads > 1 else gated[0]
        for store in stores:
            store.copy(i).start()
        if between is not None:
            between(i)

    for store in stores:
        store.wait_all()


def retention_outputs(length, heads):
    qk, vd = heads * KEY_HEAD, heads * VAL_HEAD
    return (
        ((length, qk), BF),
        ((length, qk), BF),
        ((heads, length, VAL_HEAD), BF),
        ((length, vd), F32),
        ((heads, length, VAL_HEAD), BF),
        ((length, vd), BF),
    )


def retention_forward(mixed, weight, cosine, sine, table, heads, offsets):
    length, width = mixed.shape
    outputs = retention_outputs(length, heads)
    blocks = length // BLOCK
    return pl.pallas_call(
        functools.partial(retention_kernel, heads, offsets),
        out_shape=tuple(jax.ShapeDtypeStruct(*out) for out in outputs),
        in_specs=[ANYWHERE, ANYWHERE, IN_VMEM, IN_VMEM, IN_VMEM],
        out_specs=(ANYWHERE,) * 6,
        scratch_shapes=[pltpu.VMEM(mixed.shape, BF), pltpu.VMEM(weight.shape, BF)]
        + [pltpu.VMEM(*out) for out in outputs]
        + [pltpu.SemaphoreType.DMA((4 + 7 * blocks,))],
        compiler_params=pltpu.CompilerParams(vmem_limit_bytes=60 * 1024 * 1024),
        cost_estimate=pl.CostEstimate(
            flops=30_000_000_000, bytes_accessed=0, transcendentals=0
        ),
        name="retention",
    )(mixed, weight, cosine, sine, table)


def gate_back_rows(heads, rows, branch, w_ref, swish_ref, retained_ref, dswish_ref, dret_ref):
    gated_grad = times_transposed(branch, w_ref[...])
    swish_parts = []
    for h in range(heads):
        lanes = head_lanes(h, VAL_HEAD)
        grad, s = gated_grad[:, lanes], swish_ref[rows, lanes]
        gate = jax.nn.sigmoid(s)
        unit, factor, above = norm_parts(retained_ref[h, rows, :].astype(F32))
        swish_parts.append((grad * unit * (gate * (1.0 + s * (1.0 - gate)))).astype(BF))
        g = grad * (s * gate)
        along = jnp.where(above, jnp.mean(g * unit, axis=-1, keepdims=True), 0.0)
        back = factor * (g - jnp.mean(g, axis=-1, keepdims=True) - unit * along)
        dret_ref[h, rows, :] = back.astype(BF)
    dswish_ref[rows, :] = pad_lanes(swish_parts, dswish_ref.shape[1])


def gate_back_kernel(heads, branch_ref, w_ref, swish_ref, retained_ref, dswish_ref, dret_ref):
    @pl.loop(0, branch_ref.shape[0] // BLOCK)
    def _(i):
        rows = rows_of(i)
        gate_back_rows(
            heads, rows, branch_ref[rows, :], w_ref, swish_ref, retained_ref, dswish_ref, dret_ref
        )


def gate_backward(branch, weight, swish, retained, heads, padded):
    length = branch.shape[0]
    return pl.pallas_call(
        functools.partial(gate_back_kernel, heads),
        out_shape=(
            jax.ShapeDtypeStruct((length, padded), BF),
            jax.ShapeDtypeStruct((heads, length, VAL_HEAD), BF),
        ),
        compiler_params=pltpu.CompilerParams(vmem_limit_bytes=48 * 1024 * 1024),
        name="gate_back",
    )(branch, weight, swish, retained)


def retention_back_head(
    h, heads, q_ref, k_ref, v_ref, dret_ref, table_ref, cos_ref, sin_ref, dqk_ref, dv_head,
    dq_sum,
):
    length = q_ref.shape[0]
    blocks = length // BLOCK
    lanes = head_lanes(h, KEY_HEAD)
    dq_sum[...] = jnp.zeros_like(dq_sum)

    @pl.loop(0, blocks)
    def _(j):
        there = rows_of(j)
        query, grad = q_ref[:, lanes], dret_ref[h]
        key, value = k_ref[there, lanes], v_ref[h, there, :]
        decay = table_ref[h, pl.ds(pl.multiple_of((blocks - 1 - j) * BLOCK, BLOCK), length), :]
        weights = (times_transposed(query, key) * decay).astype(BF)
        score = (times_transposed(grad, value) * decay).astype(BF)
        dq_sum[...] += product(score, key)
        dk = transposed_times(score, query).astype(BF).astype(F32)
        dk = rotate_pair(dk, cos_ref[there, :], sin_ref[there, :], back=True)
        dqk_ref[there, head_lanes(heads + h, KEY_HEAD)] = (dk * (KEY_HEAD**-0.5)).astype(BF)
        dv_head[there, :] = transposed_times(weights, grad).astype(BF)

    @pl.loop(0, blocks)
    def _(i):
        rows = rows_of(i)
        dq = dq_sum[rows, :].astype(BF).astype(F32)
        dqk_ref[rows, lanes] = rotate_pair(
            dq, cos_ref[rows, :], sin_ref[rows, :], back=True
        ).astype(BF)


def retention_back_kernel(
    heads, q_ref, k_ref, v_ref, dret_ref, table_ref, cos_ref, sin_ref, dqk_ref, dv_ref,
    dv_heads, dq_sum,
):
    for h in range(heads):
        retention_back_head(
            h, heads, q_ref, k_ref, v_ref, dret_ref, table_ref, cos_ref, sin_ref, dqk_ref,
            dv_heads.at[h], dq_sum,
        )
    dv_ref[...] = pad_lanes([dv_heads[h] for h in range(heads)], dv_ref.shape[1])


def retention_backward(q, k, v, dret, table, cosine, sine, heads, padded):
    length = q.shape[0]
    qk = heads * KEY_HEAD
    return pl.pallas_call(
        functools.partial(retention_back_kernel, heads),
        out_shape=(
            jax.ShapeDtypeStruct((length, 2 * qk), BF),
            jax.ShapeDtypeStruct((length, padded), BF),
        ),
        scratch_shapes=[
            pltpu.VMEM((heads, length, VAL_HEAD), BF),
            pltpu.VMEM((length, KEY_HEAD), F32),
        ],
        compiler_params=pltpu.CompilerParams(vmem_limit_bytes=48 * 1024 * 1024),
        name="retention_back",
    )(q, k, v, dret, table, cosine, sine)


def transfer_cost(elements):
    return pl.CostEstimate(flops=0, bytes_accessed=elements * 240, transcendentals=0)


def greet(peers):
    barrier = pltpu.get_barrier_semaphore()
    for peer in peers:
        pl.semaphore_signal(barrier, inc=1, device_id={"seq": peer}, device_id_type=MESH)
    pl.semaphore_wait(barrier, len(peers))


def remote(source, target, sends, recvs, k, to):
    return pltpu.make_async_remote_copy(
        src_ref=source,
        dst_ref=target,
        send_sem=sends.at[k],
        recv_sem=recvs.at[k],
        device_id={"seq": to},
        device_id_type=MESH,
    )


def gather_square_kernel(x_ref, o_ref, sends, recvs, local):
    me = lax.axis_index("seq")
    across, along = me ^ 1, me ^ 2
    half = x_ref.shape[0] // 2
    greet((across, along))
    own = pltpu.make_async_copy(x_ref, o_ref.at[me], local)
    own.start()

    def part(ref, i):
        return ref.at[pl.ds(i * half, half)]

    first = (
        remote(part(x_ref, 0), part(o_ref.at[me], 0), sends, recvs, 0, across),
        remote(part(x_ref, 1), part(o_ref.at[me], 1), sends, recvs, 1, along),
        remote(part(x_ref, 1), part(o_ref.at[me], 1), sends, recvs, 2, across),
        remote(part(x_ref, 0), part(o_ref.at[me], 0), sends, recvs, 3, along),
    )
    for copy in first:
        copy.start()
    first[0].wait_recv()
    on_along = remote(part(o_ref.at[across], 0), part(o_ref.at[across], 0), sends, recvs, 4, along)
    on_along.start()
    first[1].wait_recv()
    on_across = remote(part(o_ref.at[along], 1), part(o_ref.at[along], 1), sends, recvs, 5, across)
    on_across.start()
    first[2].wait_recv()
    first[3].wait_recv()
    on_along.wait_recv()
    on_across.wait_recv()
    for copy in first + (on_along, on_across):
        copy.wait_send()
    own.wait()


def gather_kernel(count, x_ref, o_ref, sends, recvs, local):
    me = lax.axis_index("seq")
    peers = [lax.rem(me + step, count) for step in range(1, count)]
    greet(peers)
    own = pltpu.make_async_copy(x_ref, o_ref.at[me], local)
    own.start()
    copies = [remote(x_ref, o_ref.at[me], sends, recvs, k, to) for k, to in enumerate(peers)]
    for copy in copies:
        copy.start()
    for copy in copies:
        copy.wait()
    own.wait()


def gather_seq(values, call):
    count = lax.axis_size("seq")
    square = count == 4 and values.shape[0] % 32 == 0
    body = gather_square_kernel if square else functools.partial(gather_kernel, count)
    copies = 6 if square else count - 1
    return pl.pallas_call(
        body,
        out_shape=jax.ShapeDtypeStruct((count,) + values.shape, values.dtype),
        in_specs=[pl.BlockSpec(memory_space=pl.ANY)],
        out_specs=pl.BlockSpec(memory_space=pl.ANY),
        scratch_shapes=[
            pltpu.SemaphoreType.DMA((copies,)),
            pltpu.SemaphoreType.DMA((copies,)),
            pltpu.SemaphoreType.DMA,
        ],
        compiler_params=pltpu.CompilerParams(collective_id=call, has_side_effects=True),
        cost_estimate=transfer_cost(values.size),
        name=f"gather_seq_{call}",
    )(values)


def exchange_kernel(count, x_ref, o_ref, sends, recvs, local):
    me = lax.axis_index("seq")
    peers = [lax.rem(me + step, count) for step in range(1, count)]
    greet(peers)
    own = pltpu.make_async_copy(x_ref.at[me], o_ref.at[me], local)
    own.start()
    copies = [remote(x_ref.at[to], o_ref.at[me], sends, recvs, k, to) for k, to in enumerate(peers)]
    for copy in copies:
        copy.start()
    for copy in copies:
        copy.wait()
    own.wait()


def exchange_seq(values, call):
    count = lax.axis_size("seq")
    return pl.pallas_call(
        functools.partial(exchange_kernel, count),
        out_shape=jax.ShapeDtypeStruct(values.shape, values.dtype),
        in_specs=[pl.BlockSpec(memory_space=pl.ANY)],
        out_specs=pl.BlockSpec(memory_space=pl.ANY),
        scratch_shapes=[
            pltpu.SemaphoreType.DMA((count - 1,)),
            pltpu.SemaphoreType.DMA((count - 1,)),
            pltpu.SemaphoreType.DMA,
        ],
        compiler_params=pltpu.CompilerParams(collective_id=call, has_side_effects=True),
        cost_estimate=transfer_cost(values.size),
        name=f"exchange_seq_{call}",
    )(values)


def scatter_square_kernel(p_ref, o_ref, inbox_x, inbox_y, via_x, via_y, out_x, out_y, sends, recvs):
    me = lax.axis_index("seq")
    across, along, corner = me ^ 1, me ^ 2, me ^ 3
    half = p_ref.shape[1] // 2
    low, high = pl.ds(0, half), pl.ds(half, half)
    greet((across, along))
    first = (
        remote(p_ref.at[corner, low], via_x, sends, recvs, 0, across),
        remote(p_ref.at[corner, high], via_y, sends, recvs, 1, along),
        remote(p_ref.at[across, low], inbox_x.at[low], sends, recvs, 2, across),
        remote(p_ref.at[along, high], inbox_y.at[high], sends, recvs, 3, along),
    )
    for copy in first:
        copy.start()
    first[0].wait_recv()
    out_y[...] = (p_ref[along, :half].astype(F32) + via_x[...].astype(F32)).astype(BF)
    to_along = remote(out_y, inbox_y.at[low], sends, recvs, 4, along)
    to_along.start()
    first[1].wait_recv()
    out_x[...] = (p_ref[across, half:].astype(F32) + via_y[...].astype(F32)).astype(BF)
    to_across = remote(out_x, inbox_x.at[high], sends, recvs, 5, across)
    to_across.start()
    first[2].wait_recv()
    first[3].wait_recv()
    to_along.wait_recv()
    to_across.wait_recv()
    o_ref[...] = (
        p_ref[me].astype(F32) + inbox_x[...].astype(F32) + inbox_y[...].astype(F32)
    )
    for copy in first + (to_along, to_across):
        copy.wait_send()


def scatter_kernel(count, p_ref, o_ref, inbox, sends, recvs):
    me = lax.axis_index("seq")
    peers = [lax.rem(me + step, count) for step in range(1, count)]
    greet(peers)
    copies = [remote(p_ref.at[to], inbox.at[k], sends, recvs, k, to) for k, to in enumerate(peers)]
    for copy in copies:
        copy.start()
    total = p_ref[me].astype(F32)
    for k, copy in enumerate(copies):
        copy.wait_recv()
        total = total + inbox[k].astype(F32)
    o_ref[...] = total
    for copy in copies:
        copy.wait_send()


def scatter_seq(parts, call):
    count = lax.axis_size("seq")
    rows, width = parts.shape[0] // count, parts.shape[1]
    parts = parts.reshape(count, rows, width)
    if count == 4 and rows % 32 == 0:
        body = scatter_square_kernel
        scratch = [pltpu.VMEM((rows, width), BF)] * 2 + [pltpu.VMEM((rows // 2, width), BF)] * 4
        copies = 6
    else:
        body = functools.partial(scatter_kernel, count)
        scratch = [pltpu.VMEM((count - 1, rows, width), BF)]
        copies = count - 1
    return pl.pallas_call(
        body,
        out_shape=jax.ShapeDtypeStruct((rows, width), F32),
        in_specs=[pl.BlockSpec(memory_space=pltpu.VMEM)],
        out_specs=pl.BlockSpec(memory_space=pltpu.VMEM),
        scratch_shapes=scratch
        + [pltpu.SemaphoreType.DMA((copies,)), pltpu.SemaphoreType.DMA((copies,))],
        compiler_params=pltpu.CompilerParams(
            collective_id=call, has_side_effects=True, vmem_limit_bytes=32 * 1024 * 1024
        ),
        cost_estimate=transfer_cost(rows * width),
        name=f"scatter_seq_{call}",
    )(parts)


def feed_forward_kernel(ff, x_ref, w_ref, gate_ref, up_ref, hidden_ref):
    both = product(x_ref[...], w_ref[...])
    gate, up = both[:, :ff], both[:, ff:]
    gate_ref[...] = gate
    up_ref[...] = up
    hidden_ref[...] = (gate * (0.5 + 0.5 * lax.erf(gate * math.sqrt(0.5))) * up).astype(BF)


def feed_back_kernel(
    ff, c_ref, gate_ref, up_ref, hidden_ref, w_ref, down_ref, both_ref, part_ref, out_ref
):
    gate, up = gate_ref[...], up_ref[...]
    out_ref[...] = product(hidden_ref[...], down_ref[...]).astype(BF)
    hidden_grad = times_transposed(c_ref[...], down_ref[...])
    bell = 0.5 + 0.5 * lax.erf(gate * math.sqrt(0.5))
    slope = bell + gate * (math.sqrt(0.5 / math.pi) * jnp.exp(-0.5 * gate * gate))
    both = jnp.concatenate([hidden_grad * up * slope, hidden_grad * (gate * bell)], axis=1)
    both = both.astype(BF)
    both_ref[...] = both
    part_ref[...] = times_transposed(both, w_ref[...]).astype(BF)


def by_rows(block, width):
    return pl.BlockSpec((block, width), lambda i: (i, 0))


def kept(shape):
    return pl.BlockSpec(shape, lambda i: (0, 0), pipeline_mode=pl.Buffered(1))


FEED_BLOCK = 256


def feed_forward(x, weight):
    length, width = x.shape
    ff = weight.shape[1] // 2
    return pl.pallas_call(
        functools.partial(feed_forward_kernel, ff),
        grid=(length // FEED_BLOCK,),
        in_specs=[by_rows(FEED_BLOCK, width), kept(weight.shape)],
        out_specs=[by_rows(FEED_BLOCK, ff)] * 3,
        out_shape=(
            jax.ShapeDtypeStruct((length, ff), F32),
            jax.ShapeDtypeStruct((length, ff), F32),
            jax.ShapeDtypeStruct((length, ff), BF),
        ),
        compiler_params=pltpu.CompilerParams(vmem_limit_bytes=48 * 1024 * 1024),
        cost_estimate=pl.CostEstimate(
            flops=4 * length * width * ff, bytes_accessed=weight.size * 4, transcendentals=0
        ),
        name="feed_forward",
    )(x, weight)


def feed_backward(cotangent, gate, up, hidden, weight, down):
    length, width = cotangent.shape
    ff = weight.shape[1] // 2
    return pl.pallas_call(
        functools.partial(feed_back_kernel, ff),
        grid=(length // FEED_BLOCK,),
        in_specs=[by_rows(FEED_BLOCK, width)]
        + [by_rows(FEED_BLOCK, ff)] * 3
        + [kept(weight.shape), kept(down.shape)],
        out_specs=[
            by_rows(FEED_BLOCK, 2 * ff),
            by_rows(FEED_BLOCK, width),
            by_rows(FEED_BLOCK, width),
        ],
        out_shape=(
            jax.ShapeDtypeStruct((length, 2 * ff), BF),
            jax.ShapeDtypeStruct((length, width), BF),
            jax.ShapeDtypeStruct((length, width), BF),
        ),
        compiler_params=pltpu.CompilerParams(vmem_limit_bytes=56 * 1024 * 1024),
        cost_estimate=pl.CostEstimate(
            flops=8 * length * width * ff, bytes_accessed=weight.size * 4, transcendentals=0
        ),
        name="feed_back",
    )(cotangent, gate, up, hidden, weight, down)


def square_parts(parts, boxes, sends, recvs, first):
    me = lax.axis_index("seq")
    across, along = me ^ 1, me ^ 2
    inbox_x, inbox_y, via_x, via_y, out_x, out_y = boxes
    half = via_x.shape[0]
    low, high = pl.ds(0, half), pl.ds(half, half)
    copies = [
        remote(parts.at[3, low], via_x, sends, recvs, first, across),
        remote(parts.at[3, high], via_y, sends, recvs, first + 1, along),
        remote(parts.at[1, low], inbox_x.at[low], sends, recvs, first + 2, across),
        remote(parts.at[2, high], inbox_y.at[high], sends, recvs, first + 3, along),
        remote(out_y, inbox_y.at[low], sends, recvs, first + 4, along),
        remote(out_x, inbox_x.at[high], sends, recvs, first + 5, across),
    ]

    def finish():
        forward_sums(copies, parts, boxes)
        for copy in copies[2:]:
            copy.wait_recv()

    def total(rows):
        return (
            parts[0, rows].astype(F32)
            + inbox_x[rows, :].astype(F32)
            + inbox_y[rows, :].astype(F32)
        )

    return copies, finish, total


def square_gather(own, out_ref, sends, recvs, first):
    me = lax.axis_index("seq")
    across, along = me ^ 1, me ^ 2
    half = own.shape[0] // 2

    def part(ref, i):
        return ref.at[pl.ds(i * half, half)]

    copies = [
        remote(part(own, 0), part(out_ref.at[me], 0), sends, recvs, first, across),
        remote(part(own, 1), part(out_ref.at[me], 1), sends, recvs, first + 1, along),
        remote(part(own, 1), part(out_ref.at[me], 1), sends, recvs, first + 2, across),
        remote(part(own, 0), part(out_ref.at[me], 0), sends, recvs, first + 3, along),
        remote(
            part(out_ref.at[across], 0), part(out_ref.at[across], 0), sends, recvs, first + 4, along
        ),
        remote(
            part(out_ref.at[along], 1), part(out_ref.at[along], 1), sends, recvs, first + 5, across
        ),
    ]

    def finish():
        copies[0].wait_recv()
        copies[4].start()
        copies[1].wait_recv()
        copies[5].start()
        for copy in copies[2:]:
            copy.wait_recv()

    return copies, finish


def block_rows(k, rows):
    return pl.ds(pl.multiple_of((lax.axis_index("seq") ^ k) * rows, rows), rows)


def forward_sums(copies, parts, boxes):
    inbox_x, inbox_y, via_x, via_y, out_x, out_y = boxes
    half = via_x.shape[0]
    copies[0].wait_recv()
    out_y[...] = (parts[2, :half].astype(F32) + via_x[...].astype(F32)).astype(BF)
    copies[4].start()
    copies[1].wait_recv()
    out_x[...] = (parts[1, half:].astype(F32) + via_y[...].astype(F32)).astype(BF)
    copies[5].start()


def send_parts(part, copies, then=None):
    @pl.loop(0, 4)
    def _(i):
        if then is not None:
            pl.when(i == 3)(then)
        part(jnp.where(i == 0, 3, jnp.where(i == 3, 0, i)))

        @pl.when(i == 0)
        def _():
            copies[0].start()
            copies[1].start()

        @pl.when(i == 1)
        def _():
            copies[2].start()

        @pl.when(i == 2)
        def _():
            copies[3].start()


def project_kernel(
    g_any, w_any, x_ref, gain_ref, middle_ref, own_ref,
    g_ref, w_ref, parts, inbox_x, inbox_y, via_x, via_y, out_x, out_y, sends, recvs, locals_,
):
    me = lax.axis_index("seq")
    rows = x_ref.shape[0]
    half = rows // 2
    moves = Moves(locals_)
    loads = [moves.start(w_any, w_ref), moves.start(g_any, g_ref)]
    greet((me ^ 1, me ^ 2))
    boxes = (inbox_x, inbox_y, via_x, via_y, out_x, out_y)
    copies, finish, total = square_parts(parts, boxes, sends, recvs, 0)

    def part(k):
        parts[k] = product(g_ref[block_rows(k, rows), :], w_ref[...]).astype(BF)

    for load in loads:
        load.wait()
    send_parts(part, copies)
    finish()

    @pl.loop(0, 2)
    def _(i):
        here = pl.ds(pl.multiple_of(i * half, half), half)
        middle = x_ref[here, :].astype(F32) + total(here)
        middle_ref[here, :] = middle
        own_ref[here, :] = normalize(middle, gain_ref[...]).astype(BF)

    for copy in copies:
        copy.wait_send()


def square_scratch(rows, width):
    return [
        pltpu.VMEM((4, rows, width), BF),
        pltpu.VMEM((rows, width), BF),
        pltpu.VMEM((rows, width), BF),
        pltpu.VMEM((rows // 2, width), BF),
        pltpu.VMEM((rows // 2, width), BF),
        pltpu.VMEM((rows // 2, width), BF),
        pltpu.VMEM((rows // 2, width), BF),
    ]


def square_call(body, out_shape, out_specs, scratch, inputs, call, cost, name):
    return pl.pallas_call(
        body,
        out_shape=out_shape,
        in_specs=[IN_VMEM] * len(inputs),
        out_specs=out_specs,
        scratch_shapes=scratch,
        compiler_params=pltpu.CompilerParams(
            collective_id=call, has_side_effects=True, vmem_limit_bytes=56 * 1024 * 1024
        ),
        cost_estimate=transfer_cost(cost),
        name=name,
    )(*inputs)


def comm_call(body, inputs, outputs, scratch, remotes, moves, call, cost, name):
    return pl.pallas_call(
        body,
        out_shape=tuple(jax.ShapeDtypeStruct(shape, kind) for shape, kind, _ in outputs),
        in_specs=[IN_VMEM if whole else ANYWHERE for _, whole in inputs],
        out_specs=tuple(IN_VMEM if whole else ANYWHERE for _, _, whole in outputs),
        scratch_shapes=scratch
        + [
            pltpu.SemaphoreType.DMA((remotes,)),
            pltpu.SemaphoreType.DMA((remotes,)),
            pltpu.SemaphoreType.DMA((moves,)),
        ],
        compiler_params=pltpu.CompilerParams(
            collective_id=call, has_side_effects=True, vmem_limit_bytes=60 * 1024 * 1024
        ),
        cost_estimate=transfer_cost(cost),
        name=name,
    )(*[value for value, _ in inputs])


def retention_exchange_kernel(
    heads, offsets, cut, mixed_any, w_any, cos_ref, sin_ref, table_ref,
    q_any, k_any, v_any, swish_any, retained_any, gated_any, wo_any,
    mixed_ref, w_ref, q_ref, k_ref, v_ref, swish_ref, retained_ref, gated_ref, both_ref, wo_ref,
    via_x, via_y, sends, recvs, locals_,
):
    me = lax.axis_index("seq")
    shard = lax.axis_index("fsdp")
    core = lax.rem(shard, 2)
    step, wide = both_ref.shape[2:]
    moves = Moves(locals_)

    def piece(column):
        rows = pl.ds(pl.multiple_of((2 * column + core) * step, step), step)
        return w_any.at[rows, slice(w_ref.shape[1], w_ref.shape[1] + wide)]

    across, along, corner = me ^ 1, me ^ 2, me ^ 3
    half = step // 2
    low, high = slice(0, half), slice(half, step)
    swaps = [
        remote(piece(corner).at[low], via_x, sends, recvs, 0, across),
        remote(piece(corner).at[high], via_y, sends, recvs, 1, along),
        remote(piece(across), both_ref.at[core, me], sends, recvs, 2, across),
        remote(piece(along), both_ref.at[core, me], sends, recvs, 3, along),
        remote(via_x, both_ref.at[core, across, low], sends, recvs, 4, along),
        remote(via_y, both_ref.at[core, along, high], sends, recvs, 5, across),
    ]
    kept_here = []

    def twin(k):
        return pltpu.make_async_remote_copy(
            src_ref=both_ref.at[core, me ^ k],
            dst_ref=both_ref.at[core, me ^ k],
            send_sem=sends.at[6 + k],
            recv_sem=recvs.at[6 + k],
            device_id={"fsdp": shard ^ 1},
            device_id_type=MESH,
        )

    def between(i):
        if isinstance(i, int):
            greet_all(me, shard)
            for copy in swaps[:4]:
                copy.start()
            kept_here.append(moves.start(piece(me), both_ref.at[core, me]))
            return

        @pl.when(i == 0)
        def _():
            swaps[0].wait_recv()
            swaps[4].start()
            swaps[1].wait_recv()
            swaps[5].start()
            kept_here[0].wait()
            twin(0).start()

        @pl.when(i == 2)
        def _():
            for k in (1, 2):
                swaps[1 + k].wait_recv()
                twin(k).start()

        @pl.when(i == 3)
        def _():
            swaps[4].wait_recv()
            swaps[5].wait_recv()
            twin(3).start()

    retention_kernel(
        heads, offsets, mixed_any, w_any, cos_ref, sin_ref, table_ref,
        q_any, k_any, v_any, swish_any, retained_any, gated_any,
        mixed_ref, w_ref, q_ref, k_ref, v_ref, swish_ref, retained_ref, gated_ref, moves, between,
    )
    for k in range(4):
        twin(k).wait_recv()
    tile, lane = 16, 128

    @pl.loop(0, heads * (wo_ref.shape[1] // lane))
    def _(n):
        h, c = n // (wo_ref.shape[1] // lane), lax.rem(n, wo_ref.shape[1] // lane)
        lanes = pl.ds(pl.multiple_of(c * lane, lane), lane)
        for k in range(4):
            for r in range(cut.skip(k) // tile, cut.width // tile):
                at = pl.multiple_of(h * cut.rows + (cut.start(k) + r * tile), tile)
                wo_ref[pl.ds(at, tile), lanes] = both_ref[
                    h, k, pl.ds(pl.multiple_of(c * tile, tile), tile), head_lanes(r, lane)
                ]

    moves.start(wo_ref, wo_any).wait()
    for copy in swaps + [twin(k) for k in range(4)]:
        copy.wait_send()


def greet_all(me, shard):
    barrier = pltpu.get_barrier_semaphore()
    for k in (1, 2, 3):
        pl.semaphore_signal(barrier, inc=1, device_id={"seq": me ^ k}, device_id_type=MESH)
    pl.semaphore_signal(barrier, inc=1, device_id={"fsdp": shard ^ 1}, device_id_type=MESH)
    pl.semaphore_wait(barrier, 4)


def retention_exchange(mixed, weight, cosine, sine, table, heads, offsets, cut, call):
    length, width = mixed.shape
    wide = cut.width * width // 256
    outputs = retention_outputs(length, heads) + (((heads * VAL_HEAD, width), BF),)
    return comm_call(
        functools.partial(retention_exchange_kernel, heads, offsets, cut),
        [(mixed, False), (weight, False), (cosine, True), (sine, True), (table, True)],
        [(shape, kind, False) for shape, kind in outputs],
        [pltpu.VMEM(mixed.shape, BF), pltpu.VMEM((width, weight.shape[1] - wide), BF)]
        + [pltpu.VMEM(*out) for out in outputs[:-1]]
        + [pltpu.VMEM((heads, 4, 256, wide), BF), pltpu.VMEM(outputs[-1][0], BF)]
        + [pltpu.VMEM((128, wide), BF)] * 2,
        10,
        6 + 7 * (length // BLOCK),
        call,
        mixed.size // 2,
        "retention_exchange",
    )


def project_and_norm(gated, weight, x, gain, call):
    rows, width = x.shape
    return comm_call(
        project_kernel,
        [(gated, False), (weight, False), (x, True), (gain[None, :], True)],
        [((rows, width), F32, True), ((rows, width), BF, True)],
        [pltpu.VMEM(gated.shape, BF), pltpu.VMEM(weight.shape, BF)] + square_scratch(rows, width),
        6,
        2,
        call,
        x.size,
        "project_and_norm",
    )


def feed_forward_gather_kernel(
    ff, x_any, w_any, c_any, both_any, hidden_any, down_any, full_any,
    full, w_ref, c_ref, both_ref, hidden_ref, total, down_ref, sends, recvs, locals_,
):
    me = lax.axis_index("seq")
    rows = x_any.shape[0]
    moves = Moves(locals_)
    load_x = moves.start(x_any, full.at[me])
    load_w = moves.start(w_any, w_ref)
    load_c = moves.start(c_any, c_ref)
    greet((me ^ 1, me ^ 2))
    load_x.wait()
    copies, _ = square_gather(full.at[me], full, sends, recvs, 0)
    for copy in copies[:4]:
        copy.start()
    stores = [
        by_block(moves, 4, both_ref, both_any, rows),
        by_block(moves, 4, hidden_ref, hidden_any, rows),
        Series(moves, 4, lambda n: (full.at[n], full_any.at[n])),
    ]
    total[...] = jnp.zeros_like(total)
    load_w.wait()
    load_c.wait()

    @pl.loop(0, 4)
    def _(k):
        @pl.when(k == 1)
        def _():
            copies[0].wait_recv()
            copies[4].start()
            copies[1].wait_recv()
            copies[5].start()
            copies[2].wait_recv()

        @pl.when(k == 2)
        def _():
            copies[3].wait_recv()

        @pl.when(k == 3)
        def _():
            copies[4].wait_recv()
            copies[5].wait_recv()

        here = block_rows(k, rows)
        both = product(full[me ^ k], w_ref[...])
        gate, up = both[:, :ff], both[:, ff:]
        both_ref[here, :] = both
        hidden = (gate * (0.5 + 0.5 * lax.erf(gate * math.sqrt(0.5))) * up).astype(BF)
        hidden_ref[here, :] = hidden
        for store in stores:
            store.copy(me ^ k).start()
        total[...] += transposed_times(hidden, c_ref[here, :])

    down_ref[...] = total[...].astype(BF)
    moves.store(down_ref, down_any)
    for store in stores:
        store.wait_all()
    moves.close()
    for copy in copies:
        copy.wait_send()


def feed_forward_gather(own, weight, cotangent, call):
    rows, width = own.shape
    length, ff = 4 * rows, weight.shape[1] // 2
    both, hidden, down, full = comm_call(
        functools.partial(feed_forward_gather_kernel, ff),
        [(own, False), (weight, False), (cotangent, False)],
        [
            ((length, 2 * ff), F32, False),
            ((length, ff), BF, False),
            ((ff, width), BF, False),
            ((4, rows, width), BF, False),
        ],
        [
            pltpu.VMEM((4, rows, width), BF),
            pltpu.VMEM(weight.shape, BF),
            pltpu.VMEM(cotangent.shape, BF),
            pltpu.VMEM((length, 2 * ff), F32),
            pltpu.VMEM((length, ff), BF),
            pltpu.VMEM((ff, width), F32),
            pltpu.VMEM((ff, width), BF),
        ],
        6,
        16,
        call,
        own.size,
        "feed_forward_gather",
    )
    return both, hidden, down, full.reshape(length, width)


def column_of(halves):
    total = 0.0
    for terms in halves:
        ones = jnp.ones((terms.shape[0], 128), BF)
        total = total + transposed_times(terms.astype(BF), ones)
    return total


def feed_back_scatter_kernel(
    ff, c_any, both_any, w_any, down_any, x_any, m_ref, own_c_ref, gain_ref,
    grad_ref, term_ref, branch_ref, dw_any,
    c_ref, both_ref, w_ref, down_ref, x_ref, low, dw_ref,
    parts, inbox_x, inbox_y, via_x, via_y, out_x, out_y, sends, recvs, locals_,
):
    me = lax.axis_index("seq")
    rows = own_c_ref.shape[0]
    half = rows // 2
    moves = Moves(locals_)
    load_c = by_block(moves, 4, c_any, c_ref, rows)
    load_both = by_block(moves, 4, both_any, both_ref, rows)
    load_c.copy(me ^ 3).start()
    load_down = moves.start(down_any, down_ref)
    load_both.copy(me ^ 3).start()
    load_w = moves.start(w_any, w_ref)
    for k in (1, 2, 0):
        load_c.copy(me ^ k).start()
        load_both.copy(me ^ k).start()
    load_x = moves.start(x_any, x_ref)
    greet((me ^ 1, me ^ 2))
    boxes = (inbox_x, inbox_y, via_x, via_y, out_x, out_y)
    copies, _, total = square_parts(parts, boxes, sends, recvs, 0)

    def part(k):
        here = block_rows(k, rows)
        load_c.copy(me ^ k).wait()
        load_both.copy(me ^ k).wait()
        gate, up = both_ref[here, :ff], both_ref[here, ff:]
        hidden_grad = times_transposed(c_ref[here, :], down_ref[...])
        bell = 0.5 + 0.5 * lax.erf(gate * math.sqrt(0.5))
        slope = bell + gate * (math.sqrt(0.5 / math.pi) * jnp.exp(-0.5 * gate * gate))
        low[here, :ff] = (hidden_grad * up * slope).astype(BF)
        low[here, ff:] = (hidden_grad * (gate * bell)).astype(BF)
        pl.when(k == 3)(load_w.wait)
        parts[k] = times_transposed(low[here, :], w_ref[...]).astype(BF)

    load_down.wait()
    send_parts(part, copies, lambda: forward_sums(copies, parts, boxes))
    load_x.wait()
    stores = by_block(moves, x_ref.shape[1] // BLOCK, dw_ref, dw_any)

    @pl.loop(0, stores.count)
    def _(b):
        lanes = rows_of(b)
        dw_ref[lanes, :] = transposed_times(x_ref[:, lanes], low[...]).astype(BF)
        stores.copy(b).start()

    for copy in copies[2:]:
        copy.wait_recv()

    def back_half(i):
        here = slice(i * half, (i + 1) * half)
        back, term = norm_back(m_ref[here, :], total(here), gain_ref[...])
        grad = own_c_ref[here, :].astype(F32) + back
        grad_ref[here, :] = grad
        branch_ref[here, :] = grad.astype(BF)
        return term

    term_ref[...] = column_of([back_half(i) for i in range(2)])
    stores.wait_all()
    for copy in copies:
        copy.wait_send()


def feed_back_scatter(cotangent, both, weight, down, x, middle, own_cotangent, gain, call):
    rows, width = own_cotangent.shape
    length, ff = cotangent.shape[0], weight.shape[1] // 2
    grad, term, branch, dw = comm_call(
        functools.partial(feed_back_scatter_kernel, ff),
        [
            (cotangent, False),
            (both, False),
            (weight, False),
            (down, False),
            (x, False),
            (middle, True),
            (own_cotangent, True),
            (gain[None, :], True),
        ],
        [
            ((rows, width), F32, True),
            ((width, 128), F32, True),
            ((rows, width), BF, True),
            ((width, 2 * ff), BF, False),
        ],
        [
            pltpu.VMEM(cotangent.shape, BF),
            pltpu.VMEM(both.shape, F32),
            pltpu.VMEM(weight.shape, BF),
            pltpu.VMEM(down.shape, BF),
            pltpu.VMEM(x.shape, BF),
            pltpu.VMEM((length, 2 * ff), BF),
            pltpu.VMEM((width, 2 * ff), BF),
        ]
        + square_scratch(rows, width),
        6,
        11 + width // BLOCK,
        call,
        own_cotangent.size,
        "feed_back_scatter",
    )
    return grad, term, branch, dw


def norm_back(values, grad, gain):
    centered = values - jnp.mean(values, axis=-1, keepdims=True)
    spread = lax.rsqrt(jnp.mean(centered * centered, axis=-1, keepdims=True) + EPSILON)
    unit = centered * spread
    g = grad * gain
    back = g - jnp.mean(g, axis=-1, keepdims=True)
    back = spread * (back - unit * jnp.mean(g * unit, axis=-1, keepdims=True))
    return back, grad * unit


def square_pass(own, out_ref, sends, recvs, first, half):
    me = lax.axis_index("seq")
    across, along = me ^ 1, me ^ 2
    spans = (slice(0, half), slice(half, own.shape[0]))

    def part(ref, i):
        return ref.at[spans[i]]

    return [
        remote(part(own, 0), part(out_ref.at[me], 0), sends, recvs, first, across),
        remote(part(own, 1), part(out_ref.at[me], 1), sends, recvs, first + 1, along),
        remote(part(own, 1), part(out_ref.at[me], 1), sends, recvs, first + 2, across),
        remote(part(own, 0), part(out_ref.at[me], 0), sends, recvs, first + 3, along),
        remote(
            part(out_ref.at[across], 0), part(out_ref.at[across], 0), sends, recvs, first + 4, along
        ),
        remote(
            part(out_ref.at[along], 1), part(out_ref.at[along], 1), sends, recvs, first + 5, across
        ),
    ]


def pass_on(copies):
    copies[0].wait_recv()
    copies[4].start()
    copies[1].wait_recv()
    copies[5].start()


def half_rows(rows):
    return -(-rows // 32) * 16


def put_column(ref, rows, at, column):
    first = ref.shape[1] - 128
    spare = lax.broadcasted_iota(jnp.int32, column.shape, 1) == at - first
    ref[rows, first:] = jnp.where(spare, column, ref[rows, first:].astype(F32)).astype(BF)


def gate_back_scatter_kernel(
    heads, cut, branch_any, w_any, swish_any, retained_any, column_any, hidden_any, down_any,
    mixed_any, gated_any, m_any, dswish_any, dret_any, dws_any, dwo_any, out_ref,
    branch_ref, w_ref, swish_ref, retained_ref, column_ref, hidden_ref, down_ref, mixed_ref,
    gated_ref, m_ref, dswish_ref, dret_ref, dws_ref, dwo_ref,
    parts, inbox_x, inbox_y, via_x, via_y, out_x, out_y, sends, recvs, locals_,
):
    me = lax.axis_index("seq")
    rows = out_ref.shape[0]
    moves = Moves(locals_)
    load_down = moves.start(down_any, down_ref)
    load_hidden = moves.start(hidden_any, hidden_ref)
    load_gate = moves.start(w_any, w_ref)
    blocks = branch_ref.shape[0] // BLOCK
    load_rows = [
        by_block(moves, blocks, branch_any, branch_ref).start_all(),
        by_block(moves, blocks, swish_any, swish_ref).start_all(),
        by_block(moves, blocks, retained_any, retained_ref).start_all(),
    ]
    load_mixed = moves.start(mixed_any, mixed_ref)
    load_column = moves.start(column_any, column_ref)
    load_gated = moves.start(gated_any, gated_ref)
    load_m = moves.start(m_any, m_ref)
    greet((me ^ 1, me ^ 2))
    boxes = (inbox_x, inbox_y, via_x, via_y, out_x, out_y)
    copies, _, total = square_parts(parts, boxes, sends, recvs, 0)

    def part(k):
        here = block_rows(k, rows)
        parts[k] = product(hidden_ref[here, :], down_ref[...]).astype(BF)

    load_hidden.wait()
    load_down.wait()
    send_parts(part, copies)
    load_gate.wait()

    @pl.loop(0, blocks)
    def _(i):
        here = rows_of(i)
        for load in load_rows:
            load.copy(i).wait()
        gate_back_rows(
            heads, here, branch_ref[here, :], w_ref, swish_ref, retained_ref, dswish_ref, dret_ref
        )

    moves.store(dswish_ref, dswish_any)
    moves.store(dret_ref, dret_any)
    forward_sums(copies, parts, boxes)
    load_mixed.wait()
    load_column.wait()
    stores = by_block(moves, dws_ref.shape[0] // BLOCK, dws_ref, dws_any)

    @pl.loop(0, stores.count)
    def _(b):
        here = rows_of(b)
        dws_ref[here, :] = product(mixed_ref[here, :], dswish_ref[...]).astype(BF)
        put_column(dws_ref, here, heads * VAL_HEAD, column_ref[here, :])
        stores.copy(b).start()

    load_gated.wait()
    step, tile, lane = 2 * BLOCK, 16, 128
    for h in range(heads):
        value_lanes = head_lanes(h, VAL_HEAD)

        @pl.loop(0, branch_ref.shape[1] // step)
        def _(b):
            lanes = pl.ds(pl.multiple_of(b * step, step), step)
            wide = transposed_times(gated_ref[:, value_lanes], branch_ref[:, lanes]).astype(BF)
            for k in range(4):
                for r in range(cut.width // tile):
                    at = cut.start(k) + r * tile
                    for c in range(step // lane):
                        to = pl.ds(pl.multiple_of((b * (step // lane) + c) * tile, tile), tile)
                        dwo_ref[h, k, to, head_lanes(r, lane)] = wide[
                            at : at + tile, head_lanes(c, lane)
                        ]

    moves.store(dwo_ref, dwo_any)
    load_m.wait()
    for copy in copies[2:]:
        copy.wait_recv()
    out_ref[...] = m_ref[...] + total(slice(0, rows))
    stores.wait_all()
    moves.close()
    for copy in copies:
        copy.wait_send()


def gate_backward_scatter(
    branch, weight, swish, retained, column, hidden, down, mixed_t, gated, middle, heads, padded,
    cut, call,
):
    length, width = branch.shape
    rows = middle.shape[0]
    dwo = (heads, 4, width // 8, cut.width * 8)
    inputs = (branch, weight, swish, retained, column, hidden, down, mixed_t, gated, middle)
    outputs = [
        ((length, padded), BF, False),
        ((heads, length, VAL_HEAD), BF, False),
        ((width, padded), BF, False),
        (dwo, BF, False),
        ((rows, width), F32, True),
    ]
    return comm_call(
        functools.partial(gate_back_scatter_kernel, heads, cut),
        [(value, False) for value in inputs],
        outputs,
        [pltpu.VMEM(v.shape, v.dtype) for v in inputs]
        + [pltpu.VMEM(shape, kind) for shape, kind, _ in outputs[:4]]
        + square_scratch(rows, width),
        6,
        20 + 3 * length // BLOCK + width // BLOCK,
        call,
        middle.size,
        "gate_back_scatter",
    )


def retention_back_exchange_kernel(
    heads, q_any, k_any, v_any, dret_any, table_ref, cos_ref, sin_ref, mixed_any, send_any, share_any,
    dqk_any, dv_any, merged_any, full_any,
    q_ref, k_ref, v_ref, dret_ref, mixed_ref, send_ref, dqk_ref, dv_ref, dwqk_ref, twin_ref, sum_ref,
    zero_ref, dv_heads, dq_sum, sends, recvs, locals_,
):
    me = lax.axis_index("seq")
    shard = lax.axis_index("fsdp")
    core = lax.rem(shard, 2)
    moves = Moves(locals_)
    load_send = moves.start(send_any, send_ref)
    loads = [
        moves.start(source, target)
        for source, target in (
            (q_any, q_ref), (k_any, k_ref), (v_any, v_ref), (dret_any, dret_ref)
        )
    ]
    load_mixed = moves.start(mixed_any, mixed_ref)
    greet_all(me, shard)
    load_send.wait()
    twin = pltpu.make_async_remote_copy(
        src_ref=send_ref.at[1 - core],
        dst_ref=twin_ref,
        send_sem=sends.at[9],
        recv_sem=recvs.at[9],
        device_id={"fsdp": shard ^ 1},
        device_id_type=MESH,
    )
    twin.start()
    passed = square_pass(share_any, full_any, sends, recvs, 0, half_rows(share_any.shape[0]))
    for copy in passed[:4]:
        copy.start()
    moves.store(share_any, full_any.at[me])
    step, wide = sum_ref.shape[1:]
    at = dqk_ref.shape[1]

    def place(column, parity):
        return merged_any.at[
            pl.ds(pl.multiple_of((2 * column + parity) * step, step), step), pl.ds(at, wide)
        ]

    zero_ref[...] = jnp.zeros_like(zero_ref)
    for column in range(4):
        moves.store(zero_ref, place(column, 1 - core))
    for load in loads:
        load.wait()
    swaps = [
        remote(sum_ref.at[me ^ k], place(me, core), sends, recvs, 5 + k, me ^ k) for k in (3, 1, 2)
    ]
    for h in range(heads):
        retention_back_head(
            h, heads, q_ref, k_ref, v_ref, dret_ref, table_ref, cos_ref, sin_ref, dqk_ref,
            dv_heads.at[h], dq_sum,
        )
        if h == 0:
            twin.wait_recv()

            @pl.loop(0, 4)
            def _(k):
                sum_ref[k] = (send_ref[core, k].astype(F32) + twin_ref[k].astype(F32)).astype(BF)

            for copy in swaps:
                copy.start()
            moves.store(sum_ref.at[me], place(me, core))
            pass_on(passed)
    dv_ref[...] = pad_lanes([dv_heads[h] for h in range(heads)], dv_ref.shape[1])
    moves.store(dv_ref, dv_any)
    moves.store(dqk_ref, dqk_any)
    load_mixed.wait()
    stores = Series(
        moves,
        mixed_ref.shape[0] // BLOCK,
        lambda b: (dwqk_ref.at[rows_of(b)], merged_any.at[rows_of(b), slice(0, at)]),
    )

    @pl.loop(0, stores.count)
    def _(b):
        here = rows_of(b)
        dwqk_ref[here, :] = product(mixed_ref[here, :], dqk_ref[...]).astype(BF)
        stores.copy(b).start()

    for copy in passed[2:] + swaps:
        copy.wait_recv()
    stores.wait_all()
    moves.close()
    for copy in passed + swaps + [twin]:
        copy.wait_send()


def retention_backward_exchange(
    q, k, v, dret, table, cosine, sine, mixed_t, send, share, heads, padded, call
):
    width, length = mixed_t.shape
    qk = heads * KEY_HEAD
    inputs = (
        (q, False), (k, False), (v, False), (dret, False), (table, True), (cosine, True),
        (sine, True), (mixed_t, False), (send, False), (share, False),
    )
    staged = (q, k, v, dret, mixed_t, send)
    block = send.shape[1:]
    return comm_call(
        functools.partial(retention_back_exchange_kernel, heads),
        inputs,
        [
            ((length, 2 * qk), BF, False),
            ((length, padded), BF, False),
            ((width, 2 * qk + block[2]), BF, False),
            ((4,) + share.shape, BF, False),
        ],
        [pltpu.VMEM(value.shape, BF) for value in staged]
        + [
            pltpu.VMEM((length, 2 * qk), BF),
            pltpu.VMEM((length, padded), BF),
            pltpu.VMEM((width, 2 * qk), BF),
            pltpu.VMEM(block, BF),
            pltpu.VMEM(block, BF),
            pltpu.VMEM(block[1:], BF),
            pltpu.VMEM((heads, length, VAL_HEAD), BF),
            pltpu.VMEM((length, KEY_HEAD), F32),
        ],
        10,
        16 + width // BLOCK,
        call,
        send.size // 4,
        "retention_back_exchange",
    )


def input_back_kernel(
    offsets, spare, dqk_any, dv_any, ds_any, w_any, x_any, grad_any, mixed_any, gain_ref, share_any,
    dx_ref, dwv_any, full_any, dqk_ref, dv_ref, ds_ref, w_ref, x_ref, grad_ref, mixed_ref, dwv_ref,
    parts, inbox_x, inbox_y, via_x, via_y, out_x, out_y, sends, recvs, locals_,
):
    at_value, at_swish = offsets
    me = lax.axis_index("seq")
    rows = x_ref.shape[0]
    half = rows // 2
    moves = Moves(locals_)
    spans = (slice(0, at_value), slice(at_value, at_swish), slice(at_swish, w_ref.shape[1]))
    grads = ((dqk_any, dqk_ref), (dv_any, dv_ref), (ds_any, ds_ref))
    loads = []
    for span, (source, target) in zip(spans, grads, strict=True):
        loads.append(moves.start(source, target))
        loads.append(moves.start(w_any.at[:, span], w_ref.at[:, span]))
    load_x = moves.start(x_any, x_ref)
    load_grad = moves.start(grad_any, grad_ref)
    load_mixed = moves.start(mixed_any, mixed_ref)
    greet((me ^ 1, me ^ 2))
    boxes = (inbox_x, inbox_y, via_x, via_y, out_x, out_y)
    copies, _, total = square_parts(parts, boxes, sends, recvs, 0)
    passed = square_pass(share_any, full_any, sends, recvs, 6, half_rows(share_any.shape[0]))
    passed[0].start()
    passed[1].start()
    moves.store(share_any, full_any.at[me])

    def part(k):
        here = block_rows(k, rows)
        whole = 0.0
        for n, (_, ref) in enumerate(grads):

            @pl.when(k == 3)
            def _():
                loads[2 * n].wait()
                loads[2 * n + 1].wait()

            whole = whole + times_transposed(ref[here, :], w_ref[:, spans[n]])
        parts[k] = whole.astype(BF)

    def pass_all():
        pass_on(passed)
        forward_sums(copies, parts, boxes)
        passed[2].start()
        passed[3].start()

    send_parts(part, copies, pass_all)
    load_mixed.wait()

    @pl.loop(0, dwv_ref.shape[0] // BLOCK)
    def _(b):
        here = rows_of(b)
        dwv_ref[here, :] = product(mixed_ref[here, :], dv_ref[...]).astype(BF)

    for copy in copies[2:]:
        copy.wait_recv()
    load_x.wait()
    load_grad.wait()
    terms = []
    for i in range(2):
        here = slice(i * half, (i + 1) * half)
        back, term = norm_back(x_ref[here, :].astype(F32), total(here), gain_ref[...])
        dx_ref[here, :] = grad_ref[here, :] + back
        terms.append(term)
    put_column(dwv_ref, slice(0, dwv_ref.shape[0]), spare, column_of(terms))
    moves.store(dwv_ref, dwv_any)
    for copy in passed[2:]:
        copy.wait_recv()
    moves.close()
    for copy in copies + passed:
        copy.wait_send()


def input_backward(dqk, dv, ds, weight, x, grad, mixed_t, gain, share, offsets, spare, call):
    rows, width = x.shape
    staged = (dqk, dv, ds, weight, x, grad, mixed_t)
    return comm_call(
        functools.partial(input_back_kernel, offsets, spare),
        [(value, False) for value in staged] + [(gain[None, :], True), (share, False)],
        [
            ((rows, width), F32, True),
            ((width, dv.shape[1]), BF, False),
            ((4,) + share.shape, BF, False),
        ],
        [pltpu.VMEM(value.shape, value.dtype) for value in staged[:3]]
        + [pltpu.VMEM((width, dqk.shape[1] + dv.shape[1] + ds.shape[1]), BF)]
        + [pltpu.VMEM(value.shape, value.dtype) for value in staged[4:]]
        + [pltpu.VMEM((width, dv.shape[1]), BF)]
        + square_scratch(rows, width),
        12,
        11,
        call,
        x.size + share.size,
        "input_backward",
    )


def join(pieces):
    return jnp.concatenate(pieces, axis=1) if len(pieces) > 1 else pieces[0]


def unpack_columns_kernel(width, in_ref, out_ref, gain_ref):
    count = in_ref.shape[0]
    out_ref[...] = join([in_ref[k][:, :width].astype(F32) for k in range(count)])
    last = in_ref.shape[2] - 128
    tile = sum(in_ref[k][:, last:].astype(F32) for k in range(count))
    gain_ref[...] = tile.T[width - last : width - last + 1, :]


def unpack_columns(gathered, width):
    count, rows, whole = gathered.shape
    block = min(rows, 128)
    out, gain = pl.pallas_call(
        functools.partial(unpack_columns_kernel, width),
        grid=(rows // block,),
        in_specs=[pl.BlockSpec((count, block, whole), lambda i: (0, i, 0))],
        out_specs=[
            pl.BlockSpec((block, count * width), lambda i: (i, 0)),
            pl.BlockSpec((1, block), lambda i: (0, i)),
        ],
        out_shape=[
            jax.ShapeDtypeStruct((rows, count * width), F32),
            jax.ShapeDtypeStruct((1, rows), F32),
        ],
        name="unpack_columns",
    )(gathered)
    return out, gain[0]


def unpack_feed_kernel(cut, shards, in_ref, down_ref, gate_ref, up_ref, out_ref):
    count = in_ref.shape[0]

    @pl.when(pl.program_id(0) == 0)
    def _():
        for k in range(count):
            if cut.skip(k) < cut.width:
                at = cut.start(k)
                out_ref[at + cut.skip(k) : at + cut.width, :] = down_ref[
                    k, cut.skip(k) : cut.width, :
                ].astype(F32)

    for n, target in enumerate((gate_ref, up_ref)):
        pieces = []
        for f in range(shards):
            for k in range(count):
                at = (n * shards + f) * cut.width
                if cut.skip(k) < cut.width:
                    piece = in_ref[k][:, at + cut.skip(k) : at + cut.width]
                    pieces.append(piece.astype(F32))
        target[...] = join(pieces)


def unpack_feed(gathered, down, cut, shards):
    count, rows, whole = gathered.shape
    block = rows // 4 if rows % 64 == 0 else rows
    wide, width = shards * cut.rows, down.shape[2]
    return pl.pallas_call(
        functools.partial(unpack_feed_kernel, cut, shards),
        grid=(rows // block,),
        in_specs=[
            pl.BlockSpec((count, block, whole), lambda i: (0, i, 0)),
            pl.BlockSpec(down.shape, lambda i: (0, 0, 0)),
        ],
        out_specs=[
            pl.BlockSpec((block, wide), lambda i: (i, 0)),
            pl.BlockSpec((block, wide), lambda i: (i, 0)),
            pl.BlockSpec((cut.rows, width), lambda i: (0, 0)),
        ],
        out_shape=[
            jax.ShapeDtypeStruct((rows, wide), F32),
            jax.ShapeDtypeStruct((rows, wide), F32),
            jax.ShapeDtypeStruct((cut.rows, width), F32),
        ],
        compiler_params=pltpu.CompilerParams(vmem_limit_bytes=40 * 1024 * 1024),
        name="unpack_feed",
    )(gathered, down)


def unpack_merged_kernel(cut, in_ref, query_ref, key_ref, out_ref):
    tile, lane, count = 16, 128, in_ref.shape[0]
    wide = query_ref.shape[1] // count
    for k in range(count):
        query_ref[:, head_lanes(k, wide)] = in_ref[k, :, :wide].astype(F32)
        key_ref[:, head_lanes(k, wide)] = in_ref[k, :, wide : 2 * wide].astype(F32)
        for r in range(cut.skip(k) // tile, cut.width // tile):
            at = cut.start(k) + r * tile
            lanes = slice(2 * wide + r * lane, 2 * wide + (r + 1) * lane)
            for c in range(out_ref.shape[1] // lane):
                out_ref[at : at + tile, head_lanes(c, lane)] = in_ref[
                    k, c * tile : (c + 1) * tile, lanes
                ].astype(F32)


def unpack_merged(gathered, wide, cut, width):
    count, rows, _ = gathered.shape
    return pl.pallas_call(
        functools.partial(unpack_merged_kernel, cut),
        out_shape=(
            jax.ShapeDtypeStruct((rows, count * wide), F32),
            jax.ShapeDtypeStruct((rows, count * wide), F32),
            jax.ShapeDtypeStruct((cut.rows, width), F32),
        ),
        compiler_params=pltpu.CompilerParams(vmem_limit_bytes=40 * 1024 * 1024),
        name="unpack_merged",
    )(gathered)


def after(values, *others, all_of=False):
    held = lax.optimization_barrier((values,) + others)
    return held if all_of else held[0]


class Cut:
    def __init__(self, rows, count):
        self.rows, self.count = rows, count
        self.width = -(-rows // (count * 16)) * 16

    def start(self, piece):
        if isinstance(piece, int):
            return min(piece * self.width, self.rows - self.width)
        return jnp.minimum(piece * self.width, self.rows - self.width)

    def skip(self, piece):
        if isinstance(piece, int):
            return min(piece * self.width - self.start(piece), self.width)
        return jnp.minimum(piece * self.width - self.start(piece), self.width)

    def assemble(self, pieces, axis):
        kept = []
        for k, piece in enumerate(pieces):
            if self.skip(k) < self.width:
                kept.append(lax.slice_in_dim(piece, self.skip(k), self.width, axis=axis))
        return jnp.concatenate(kept, axis=axis)


def columns_of(weight, index, width, padded):
    piece = lax.dynamic_slice_in_dim(weight, index * width, width, axis=1)
    return jnp.pad(piece, ((0, 0), (0, padded - width)))


def on_device(
    layer_input,
    mixer_gain,
    query_weight,
    key_weight,
    value_weight,
    swish_weight,
    output_weight,
    channel_gain,
    gelu_weight,
    linear_weight,
    down_weight,
    output_cotangent,
):
    groups, local_length, width = layer_input.shape
    seq_count = lax.axis_size("seq")
    shards = lax.axis_size("fsdp")
    me = lax.axis_index("seq")
    per_device = HEADS // seq_count
    rows_count = groups * local_length
    square = seq_count == 4 and shards == 8 and rows_count % 32 == 0
    length = local_length * seq_count
    key_scale = KEY_HEAD ** (-0.5)
    qk = query_weight.shape[1] // seq_count
    vd = value_weight.shape[1] // seq_count
    vd_pad = -(-vd // 128) * 128
    hidden_units = gelu_weight.shape[1]
    own_rows = down_weight.shape[0]
    cut = Cut(own_rows, seq_count)
    ff = shards * cut.width

    def gather_rows(values):
        return lax.all_gather(values, "fsdp", axis=0, tiled=True)

    def scatter_rows(values):
        return lax.psum_scatter(values.astype(BF), "fsdp", scatter_dimension=0, tiled=True)

    output_piece = lax.dynamic_slice_in_dim(output_weight, cut.start(me), cut.width, axis=0)
    attention_pieces = [
        columns_of(query_weight, me, qk, qk),
        columns_of(key_weight, me, qk, qk),
        columns_of(value_weight, me, vd, vd_pad),
        columns_of(swish_weight, me, vd, vd_pad),
    ]
    if square:
        tiles = output_piece.reshape(cut.width // 16, 16, width // 128, 128)
        attention_pieces.append(tiles.transpose(2, 1, 0, 3).reshape(width // 8, cut.width * 8))
    else:
        output_pieces = gather_rows(output_piece)
    attention_weight = gather_rows(jnp.concatenate(attention_pieces, axis=1))
    column = lax.broadcasted_iota(jnp.int32, (hidden_units, ff), 0)
    slot = lax.broadcasted_iota(jnp.int32, (hidden_units, ff), 1)
    chosen = (slot // cut.width) * own_rows + cut.start(me) + slot % cut.width
    selector = (column == chosen).astype(BF)
    gate_piece = product(gelu_weight, selector).astype(BF)
    up_piece = product(linear_weight, selector).astype(BF)
    feed_piece = jnp.concatenate([gate_piece, up_piece], axis=1)
    down_piece = lax.dynamic_slice_in_dim(down_weight, cut.start(me), cut.width, axis=0)
    gains = lax.all_gather(jnp.stack([mixer_gain, channel_gain]), "fsdp", axis=1, tiled=True)
    mixer_scale, channel_scale = gains[0].astype(F32), gains[1].astype(F32)

    local_input = layer_input.reshape(rows_count, width)
    upstream = output_cotangent.reshape(rows_count, width)

    upstream = after(upstream, gains)

    def whole(values, call):
        gathered = gather_seq(values, call)
        return gathered.reshape(length * groups, width)

    input_full = whole(local_input, 0)
    upstream_full = whole(after(upstream, input_full), 1)
    inputs = local_input.astype(F32)

    blocks = shards // seq_count
    mixed_low, mixed_turned = norm_and_turn(input_full, mixer_scale)
    head_ids = me * per_device + jnp.arange(per_device, dtype=jnp.int32)
    table, table_back = decay_tables(head_ids, length)
    cosine, sine = rotation_tables(length, KEY_HEAD // 2)
    feed_weight = gather_rows(after(feed_piece, upstream_full))

    offsets = (qk, 2 * qk, 2 * qk + vd_pad)
    attention_weight = after(
        attention_weight, mixed_low, mixed_turned, table, table_back, cosine, feed_piece
    )
    if square:
        query_low, key_low, value_low, swish_pre, retained, gated_low, output_full = (
            retention_exchange(
                mixed_low, attention_weight, cosine, sine, table, per_device, offsets, cut, 2
            )
        )
    else:
        query_low, key_low, value_low, swish_pre, retained, gated_low = retention_forward(
            mixed_low, attention_weight, cosine, sine, table, per_device, offsets
        )
        swapped = exchange_seq(
            output_pieces.reshape(seq_count, blocks, cut.width, width), 2
        )
        output_full = jnp.concatenate(
            [
                cut.assemble([swapped[piece, block] for piece in range(seq_count)], 0)
                for block in range(blocks)
            ],
            axis=0,
        )

    kept_rows = lax.broadcasted_iota(jnp.int32, down_piece.shape, 0) >= cut.skip(me)
    down_full = gather_rows(after(jnp.where(kept_rows, down_piece, jnp.zeros_like(down_piece)), gated_low))
    if square:
        middle, channel_own = project_and_norm(
            gated_low, output_full, local_input, channel_scale, 3
        )
        both_pre, hidden_low, down_term, channel_full = feed_forward_gather(
            channel_own, feed_weight, upstream_full, 4
        )
        down_share = scatter_rows(down_term)
        middle_grad, channel_term, branch_own, feed_term = feed_back_scatter(
            after(upstream_full, down_term), both_pre, feed_weight, down_full, channel_full,
            middle, upstream, channel_scale, 6,
        )
        feed_share = scatter_rows(feed_term)
        branch_full = whole(branch_own, 7)
    else:
        middle = inputs + scatter_seq(product(gated_low, output_full).astype(BF), 3)
        channel_full = whole(normalize(middle, channel_scale).astype(BF), 4)
        gate_pre, up_pre, hidden_low = feed_forward(channel_full, feed_weight)
        down_share = scatter_rows(transposed_times(hidden_low, upstream_full).astype(BF))
        feed_low_grad, channel_part, hidden_part = feed_backward(
            upstream_full, gate_pre, up_pre, hidden_low, feed_weight, down_full
        )
        feed_share = scatter_rows(transposed_times(channel_full, feed_low_grad).astype(BF))
        middle_local, channel_terms = norm_back(
            middle, scatter_seq(channel_part, 6), channel_scale
        )
        channel_term = jnp.sum(channel_terms, axis=0)
        middle_grad = upstream.astype(F32) + middle_local
        branch_full = whole(middle_grad.astype(BF), 7)

    at_value, at_swish = 2 * qk, 2 * qk + vd_pad
    if square:
        swish_grad, retained_grad, swish_term, output_send, layer_output = gate_backward_scatter(
            after(branch_full, down_share), output_full, swish_pre, retained,
            channel_term, hidden_low, down_full, mixed_turned, gated_low, middle,
            per_device, vd_pad, cut, 5,
        )
        swish_share = scatter_rows(swish_term)
        key_grad, value_grad, merged_term, down_all = retention_backward_exchange(
            query_low, key_low, value_low, after(retained_grad, feed_share), table_back, cosine, sine,
            mixed_turned, output_send, down_share, per_device, vd_pad, 8,
        )
        merged_share = scatter_rows(merged_term)
        input_gradient, value_term, feed_all = input_backward(
            key_grad, value_grad, swish_grad, attention_weight, local_input, middle_grad,
            mixed_turned, mixer_scale, feed_share, (at_value, at_swish), vd, 9,
        )
    else:
        swish_grad, retained_grad = gate_backward(
            branch_full, output_full, swish_pre, retained, per_device, vd_pad
        )
        spare = lax.broadcasted_iota(jnp.int32, (width, vd_pad), 1) == vd
        swish_term = transposed_times(mixed_low, swish_grad)
        swish_term = jnp.where(spare, channel_term[:, None], swish_term).astype(BF)
        swish_share = scatter_rows(swish_term)
        layer_output = middle + scatter_seq(hidden_part, 5)
        key_grad, value_grad = retention_backward(
            query_low, key_low, value_low, retained_grad, table_back, cosine, sine, per_device, vd_pad
        )
        key_term = transposed_times(mixed_low, key_grad).astype(BF)
        key_share = scatter_rows(key_term)
        mixed_part = (
            times_transposed(key_grad, attention_weight[:, :at_value])
            + times_transposed(value_grad, attention_weight[:, at_value:at_swish])
            + times_transposed(swish_grad, attention_weight[:, at_swish:])
        )
        input_local, mixer_terms = norm_back(
            inputs, scatter_seq(mixed_part.astype(BF), 9), mixer_scale
        )
        mixer_term = jnp.sum(mixer_terms, axis=0)
        input_gradient = middle_grad + input_local
        output_term = transposed_times(gated_low, branch_full).astype(BF)
        output_term = output_term.reshape(blocks, own_rows, width)
        output_send = jnp.stack(
            [
                lax.slice_in_dim(output_term, cut.start(k), cut.start(k) + cut.width, axis=1)
                for k in range(seq_count)
            ]
        )
        output_swapped = exchange_seq(output_send, 8)
        output_share = scatter_rows(output_swapped.reshape(shards * cut.width, width))
        value_term = transposed_times(mixed_low, value_grad)
        value_term = jnp.where(spare, mixer_term[:, None], value_term).astype(BF)
    input_gradient = input_gradient.astype(BF).reshape(groups, local_length, width)
    value_share = scatter_rows(value_term)

    layer_output = layer_output.astype(BF).reshape(groups, local_length, width)
    if square:
        gelu_gradient, linear_gradient, down_gradient = unpack_feed(
            after(feed_all, value_term), down_all, cut, shards
        )
        swish_all = gather_seq(
            after(swish_share, gelu_gradient, layer_output, input_gradient), 13
        )
        swish_gradient, channel_own_gradient = unpack_columns(swish_all, vd)
        merged_all = gather_seq(after(merged_share, swish_gradient), 15)
        query_gradient, key_gradient, output_gradient = unpack_merged(merged_all, qk, cut, width)
        value_share = after(value_share, query_gradient)
    else:
        down_all = gather_seq(down_share, 10)
        feed_all = gather_seq(after(feed_share, down_all), 11)
        swish_all = gather_seq(after(swish_share, feed_all), 13)
        output_all = gather_seq(after(output_share, swish_all), 12)
        key_all = gather_seq(after(key_share, output_all), 15)
        value_share = after(value_share, key_all)
        swish_gradient, channel_own_gradient = unpack_columns(swish_all, vd)
        output_gradient = cut.assemble([output_all[k] for k in range(seq_count)], 0).astype(F32)
        gelu_gradient, linear_gradient, down_gradient = unpack_feed(
            feed_all, down_all, cut, shards
        )
        query_gradient, key_gradient = (
            jnp.concatenate(
                [key_all[k][:, at : at + qk] for k in range(seq_count)], axis=1
            ).astype(F32)
            for at in (0, qk)
        )
    value_all = gather_seq(value_share, 14)
    value_gradient, mixer_own_gradient = unpack_columns(value_all, vd)
    return (
        layer_output,
        input_gradient,
        mixer_own_gradient,
        query_gradient,
        key_gradient,
        value_gradient,
        swish_gradient,
        output_gradient,
        channel_own_gradient,
        gelu_gradient,
        linear_gradient,
        down_gradient,
    )


def solution(mesh):
    tokens, rows, vector = P("fsdp", "seq", None), P("fsdp", None), P("fsdp")
    return jax.shard_map(
        on_device,
        mesh=mesh,
        in_specs=(
            tokens, vector, rows, rows, rows, rows, rows, vector, rows, rows, rows, tokens,
        ),
        out_specs=(
            tokens, tokens, vector, rows, rows, rows, rows, rows, vector, rows, rows, rows,
        ),
        check_vma=False,
    )
```

```python
import functools
import math

import jax
import jax.numpy as jnp
from jax import lax
from jax.experimental import pallas as pl
from jax.experimental.pallas import tpu as pltpu
from jax.sharding import PartitionSpec as P

HEADS = 8
KEY_HEAD = 256
VAL_HEAD = 432
EPSILON = 1e-05
MESH = pl.DeviceIdType.MESH
BF = jnp.bfloat16
F32 = jnp.float32
IN_VMEM = pl.BlockSpec(memory_space=pltpu.VMEM)
ANYWHERE = pl.BlockSpec(memory_space=pl.ANY)


def product(left, right):
    return jnp.dot(left, right, preferred_element_type=F32)


def times_transposed(left, right):
    return lax.dot_general(left, right, (((1,), (1,)), ((), ())), preferred_element_type=F32)


def transposed_times(left, right):
    return lax.dot_general(left, right, (((0,), (0,)), ((), ())), preferred_element_type=F32)


def normalize(values, gain):
    centered = values - jnp.mean(values, axis=-1, keepdims=True)
    spread = lax.rsqrt(jnp.mean(centered * centered, axis=-1, keepdims=True) + EPSILON)
    return centered * spread * gain


def rotation_tables(length, half_width):
    rates = jnp.exp(-math.log(10000.0) * jnp.arange(half_width, dtype=F32) / (half_width - 1))
    turned = jnp.arange(length, dtype=F32)[:, None] * rates[None, :]
    return (jnp.cos(turned), jnp.sin(turned))


def pad_lanes(pieces, width):
    have = sum(piece.shape[1] for piece in pieces)
    if have < width:
        pieces = pieces + [jnp.zeros((pieces[0].shape[0], width - have), pieces[0].dtype)]
    return jnp.concatenate(pieces, axis=1) if len(pieces) > 1 else pieces[0]


def rotate_pair(values, cosine, sine, back=False):
    half = KEY_HEAD // 2
    first, second = values[:, :half], values[:, half:]
    if back:
        return jnp.concatenate([first * cosine + second * sine, second * cosine - first * sine], 1)
    return jnp.concatenate([first * cosine - second * sine, second * cosine + first * sine], 1)


BLOCK = 256


def decay_tables(head_ids, length):
    rates = jnp.log1p(-jnp.exp2(-5.0 - head_ids.astype(F32)))[:, None, None]
    short = jnp.arange(BLOCK, dtype=jnp.int32)
    long = jnp.arange(2 * length - BLOCK, dtype=jnp.int32)

    def decay(gap):
        far = jnp.exp(jnp.maximum(gap, 0).astype(F32)[None] * rates)
        return jnp.where(gap[None] >= 0, far, 0.0)

    by_row = decay(length - BLOCK + short[:, None] - long[None, :])
    by_column = decay(long[:, None] - (length - BLOCK) - short[None, :])
    return by_row, by_column


def norm_parts(values):
    centered = values - jnp.mean(values, axis=-1, keepdims=True)
    variance = jnp.mean(centered * centered, axis=-1, keepdims=True)
    factor = lax.rsqrt(jnp.maximum(variance, 1.0))
    return centered * factor, factor, variance > 1.0


def rows_of(block):
    return pl.ds(pl.multiple_of(block * BLOCK, BLOCK), BLOCK)


def head_lanes(head, width):
    return slice(head * width, (head + 1) * width)


class Moves:
    def __init__(self, sems):
        self.sems, self.used, self.open = sems, 0, []

    def start(self, source, target):
        copy = pltpu.make_async_copy(source, target, self.sems.at[self.used])
        self.used += 1
        copy.start()
        return copy

    def store(self, source, target):
        self.open.append(self.start(source, target))

    def close(self):
        for copy in self.open:
            copy.wait()


def norm_kernel(x_ref, gain_ref, out_ref, turned_ref):
    normed = normalize(x_ref[...].astype(F32), gain_ref[...])
    out_ref[...] = normed.astype(BF)
    turned_ref[...] = normed.T.astype(BF)


def norm_and_turn(x, gain):
    length, width = x.shape
    return pl.pallas_call(
        norm_kernel,
        grid=(length // BLOCK,),
        in_specs=[
            pl.BlockSpec((BLOCK, width), lambda i: (i, 0)),
            pl.BlockSpec((1, width), lambda i: (0, 0)),
        ],
        out_specs=[
            pl.BlockSpec((BLOCK, width), lambda i: (i, 0)),
            pl.BlockSpec((width, BLOCK), lambda i: (0, i)),
        ],
        out_shape=[
            jax.ShapeDtypeStruct((length, width), BF),
            jax.ShapeDtypeStruct((width, length), BF),
        ],
        compiler_params=pltpu.CompilerParams(vmem_limit_bytes=32 * 1024 * 1024),
        name="norm_and_turn",
    )(x, gain[None, :])


class Series:
    def __init__(self, moves, count, ends):
        self.sems, self.first, self.count, self.ends = moves.sems, moves.used, count, ends
        moves.used += count

    def copy(self, i):
        return pltpu.make_async_copy(*self.ends(i), self.sems.at[self.first + i])

    def start_all(self):
        for i in range(self.count):
            self.copy(i).start()
        return self

    def wait_all(self):
        for i in range(self.count):
            self.copy(i).wait()


def by_block(moves, count, source, target, rows=BLOCK):
    def ends(i):
        here = pl.ds(i * rows if isinstance(i, int) else pl.multiple_of(i * rows, rows), rows)
        if len(source.shape) == 3:
            return source.at[:, here], target.at[:, here]
        return source.at[here], target.at[here]

    return Series(moves, count, ends)


def retention_kernel(
    heads, offsets, mixed_any, w_any, cos_ref, sin_ref, table_ref,
    q_any, k_any, v_any, swish_any, retained_any, gated_any,
    mixed_ref, w_ref, q_ref, k_ref, v_ref, swish_ref, retained_ref, gated_ref, sems,
    between=None,
):
    at_key, at_value, at_swish = offsets
    length = mixed_ref.shape[0]
    blocks = length // BLOCK
    moves = sems if isinstance(sems, Moves) else Moves(sems)
    spans = (
        slice(0, at_key), slice(at_key, at_value), slice(at_value, at_swish),
        slice(at_swish, w_ref.shape[1]),
    )
    loads = by_block(moves, blocks, mixed_any, mixed_ref)
    loads.copy(0).start()
    weights = [moves.start(w_any.at[:, span], w_ref.at[:, span]) for span in spans]
    for i in range(1, blocks):
        loads.copy(i).start()
    stores = [
        by_block(moves, blocks, source, target)
        for source, target in (
            (q_ref, q_any), (k_ref, k_any), (v_ref, v_any), (swish_ref, swish_any),
            (retained_ref, retained_any), (gated_ref, gated_any),
        )
    ]
    k_ref[...] = jnp.zeros_like(k_ref)
    v_ref[...] = jnp.zeros_like(v_ref)
    if between is not None:
        between(-1)

    @pl.loop(0, blocks)
    def _(i):
        rows = rows_of(i)
        loads.copy(i).wait()
        mixed = mixed_ref[rows, :]
        cosine, sine = cos_ref[rows, :], sin_ref[rows, :]

        def projected(n):
            @pl.when(i == 0)
            def _():
                weights[n].wait()

            return product(mixed, w_ref[:, spans[n]])

        for n, (target, scale) in enumerate(((q_ref, 1.0), (k_ref, KEY_HEAD**-0.5))):
            pre = projected(n)
            for h in range(heads):
                lanes = head_lanes(h, KEY_HEAD)
                turned = rotate_pair(pre[:, lanes], cosine, sine)
                target[rows, lanes] = (turned * scale if n else turned).astype(BF)
        value = projected(2)
        for h in range(heads):
            v_ref[h, rows, :] = value[:, head_lanes(h, VAL_HEAD)].astype(BF)
        swish_ref[rows, :] = projected(3)[:, : heads * VAL_HEAD]
        gated = []
        for h in range(heads):
            lanes = head_lanes(h, KEY_HEAD)
            scores = times_transposed(q_ref[rows, lanes], k_ref[:, lanes])
            decay = table_ref[
                h, :, pl.ds(pl.multiple_of((blocks - 1 - i) * BLOCK, BLOCK), length)
            ]
            retained = product((scores * decay).astype(BF), v_ref[h]).astype(BF)
            retained_ref[h, rows, :] = retained
            unit, _, _ = norm_parts(retained.astype(F32))
            s = swish_ref[rows, head_lanes(h, VAL_HEAD)]
            gated.append((s * jax.nn.sigmoid(s) * unit).astype(BF))
        gated_ref[rows, :] = jnp.concatenate(gated, axis=1) if heads > 1 else gated[0]
        for store in stores:
            store.copy(i).start()
        if between is not None:
            between(i)

    for store in stores:
        store.wait_all()


def retention_outputs(length, heads):
    qk, vd = heads * KEY_HEAD, heads * VAL_HEAD
    return (
        ((length, qk), BF),
        ((length, qk), BF),
        ((heads, length, VAL_HEAD), BF),
        ((length, vd), F32),
        ((heads, length, VAL_HEAD), BF),
        ((length, vd), BF),
    )


def retention_forward(mixed, weight, cosine, sine, table, heads, offsets):
    length, width = mixed.shape
    outputs = retention_outputs(length, heads)
    blocks = length // BLOCK
    return pl.pallas_call(
        functools.partial(retention_kernel, heads, offsets),
        out_shape=tuple(jax.ShapeDtypeStruct(*out) for out in outputs),
        in_specs=[ANYWHERE, ANYWHERE, IN_VMEM, IN_VMEM, IN_VMEM],
        out_specs=(ANYWHERE,) * 6,
        scratch_shapes=[pltpu.VMEM(mixed.shape, BF), pltpu.VMEM(weight.shape, BF)]
        + [pltpu.VMEM(*out) for out in outputs]
        + [pltpu.SemaphoreType.DMA((4 + 7 * blocks,))],
        compiler_params=pltpu.CompilerParams(vmem_limit_bytes=60 * 1024 * 1024),
        cost_estimate=pl.CostEstimate(
            flops=30_000_000_000, bytes_accessed=0, transcendentals=0
        ),
        name="retention",
    )(mixed, weight, cosine, sine, table)


def gate_back_rows(heads, rows, branch, w_ref, swish_ref, retained_ref, dswish_ref, dret_ref):
    gated_grad = times_transposed(branch, w_ref[...])
    swish_parts = []
    for h in range(heads):
        lanes = head_lanes(h, VAL_HEAD)
        grad, s = gated_grad[:, lanes], swish_ref[rows, lanes]
        gate = jax.nn.sigmoid(s)
        unit, factor, above = norm_parts(retained_ref[h, rows, :].astype(F32))
        swish_parts.append((grad * unit * (gate * (1.0 + s * (1.0 - gate)))).astype(BF))
        g = grad * (s * gate)
        along = jnp.where(above, jnp.mean(g * unit, axis=-1, keepdims=True), 0.0)
        back = factor * (g - jnp.mean(g, axis=-1, keepdims=True) - unit * along)
        dret_ref[h, rows, :] = back.astype(BF)
    dswish_ref[rows, :] = pad_lanes(swish_parts, dswish_ref.shape[1])


def gate_back_kernel(heads, branch_ref, w_ref, swish_ref, retained_ref, dswish_ref, dret_ref):
    @pl.loop(0, branch_ref.shape[0] // BLOCK)
    def _(i):
        rows = rows_of(i)
        gate_back_rows(
            heads, rows, branch_ref[rows, :], w_ref, swish_ref, retained_ref, dswish_ref, dret_ref
        )


def gate_backward(branch, weight, swish, retained, heads, padded):
    length = branch.shape[0]
    return pl.pallas_call(
        functools.partial(gate_back_kernel, heads),
        out_shape=(
            jax.ShapeDtypeStruct((length, padded), BF),
            jax.ShapeDtypeStruct((heads, length, VAL_HEAD), BF),
        ),
        compiler_params=pltpu.CompilerParams(vmem_limit_bytes=48 * 1024 * 1024),
        name="gate_back",
    )(branch, weight, swish, retained)


def retention_back_head(
    h, heads, q_ref, k_ref, v_ref, dret_ref, table_ref, cos_ref, sin_ref, dqk_ref, dv_head,
    dq_sum,
):
    length = q_ref.shape[0]
    blocks = length // BLOCK
    lanes = head_lanes(h, KEY_HEAD)
    dq_sum[...] = jnp.zeros_like(dq_sum)

    @pl.loop(0, blocks)
    def _(j):
        there = rows_of(j)
        query, grad = q_ref[:, lanes], dret_ref[h]
        key, value = k_ref[there, lanes], v_ref[h, there, :]
        decay = table_ref[h, pl.ds(pl.multiple_of((blocks - 1 - j) * BLOCK, BLOCK), length), :]
        weights = (times_transposed(query, key) * decay).astype(BF)
        score = (times_transposed(grad, value) * decay).astype(BF)
        dq_sum[...] += product(score, key)
        dk = transposed_times(score, query).astype(BF).astype(F32)
        dk = rotate_pair(dk, cos_ref[there, :], sin_ref[there, :], back=True)
        dqk_ref[there, head_lanes(heads + h, KEY_HEAD)] = (dk * (KEY_HEAD**-0.5)).astype(BF)
        dv_head[there, :] = transposed_times(weights, grad).astype(BF)

    @pl.loop(0, blocks)
    def _(i):
        rows = rows_of(i)
        dq = dq_sum[rows, :].astype(BF).astype(F32)
        dqk_ref[rows, lanes] = rotate_pair(
            dq, cos_ref[rows, :], sin_ref[rows, :], back=True
        ).astype(BF)


def retention_back_kernel(
    heads, q_ref, k_ref, v_ref, dret_ref, table_ref, cos_ref, sin_ref, dqk_ref, dv_ref,
    dv_heads, dq_sum,
):
    for h in range(heads):
        retention_back_head(
            h, heads, q_ref, k_ref, v_ref, dret_ref, table_ref, cos_ref, sin_ref, dqk_ref,
            dv_heads.at[h], dq_sum,
        )
    dv_ref[...] = pad_lanes([dv_heads[h] for h in range(heads)], dv_ref.shape[1])


def retention_backward(q, k, v, dret, table, cosine, sine, heads, padded):
    length = q.shape[0]
    qk = heads * KEY_HEAD
    return pl.pallas_call(
        functools.partial(retention_back_kernel, heads),
        out_shape=(
            jax.ShapeDtypeStruct((length, 2 * qk), BF),
            jax.ShapeDtypeStruct((length, padded), BF),
        ),
        scratch_shapes=[
            pltpu.VMEM((heads, length, VAL_HEAD), BF),
            pltpu.VMEM((length, KEY_HEAD), F32),
        ],
        compiler_params=pltpu.CompilerParams(vmem_limit_bytes=48 * 1024 * 1024),
        name="retention_back",
    )(q, k, v, dret, table, cosine, sine)


def transfer_cost(elements):
    return pl.CostEstimate(flops=0, bytes_accessed=elements * 240, transcendentals=0)


def greet(peers):
    barrier = pltpu.get_barrier_semaphore()
    for peer in peers:
        pl.semaphore_signal(barrier, inc=1, device_id={"seq": peer}, device_id_type=MESH)
    pl.semaphore_wait(barrier, len(peers))


def remote(source, target, sends, recvs, k, to):
    return pltpu.make_async_remote_copy(
        src_ref=source,
        dst_ref=target,
        send_sem=sends.at[k],
        recv_sem=recvs.at[k],
        device_id={"seq": to},
        device_id_type=MESH,
    )


def gather_square_kernel(x_ref, o_ref, sends, recvs, local):
    me = lax.axis_index("seq")
    across, along = me ^ 1, me ^ 2
    half = x_ref.shape[0] // 2
    greet((across, along))
    own = pltpu.make_async_copy(x_ref, o_ref.at[me], local)
    own.start()

    def part(ref, i):
        return ref.at[pl.ds(i * half, half)]

    first = (
        remote(part(x_ref, 0), part(o_ref.at[me], 0), sends, recvs, 0, across),
        remote(part(x_ref, 1), part(o_ref.at[me], 1), sends, recvs, 1, along),
        remote(part(x_ref, 1), part(o_ref.at[me], 1), sends, recvs, 2, across),
        remote(part(x_ref, 0), part(o_ref.at[me], 0), sends, recvs, 3, along),
    )
    for copy in first:
        copy.start()
    first[0].wait_recv()
    on_along = remote(part(o_ref.at[across], 0), part(o_ref.at[across], 0), sends, recvs, 4, along)
    on_along.start()
    first[1].wait_recv()
    on_across = remote(part(o_ref.at[along], 1), part(o_ref.at[along], 1), sends, recvs, 5, across)
    on_across.start()
    first[2].wait_recv()
    first[3].wait_recv()
    on_along.wait_recv()
    on_across.wait_recv()
    for copy in first + (on_along, on_across):
        copy.wait_send()
    own.wait()


def gather_kernel(count, x_ref, o_ref, sends, recvs, local):
    me = lax.axis_index("seq")
    peers = [lax.rem(me + step, count) for step in range(1, count)]
    greet(peers)
    own = pltpu.make_async_copy(x_ref, o_ref.at[me], local)
    own.start()
    copies = [remote(x_ref, o_ref.at[me], sends, recvs, k, to) for k, to in enumerate(peers)]
    for copy in copies:
        copy.start()
    for copy in copies:
        copy.wait()
    own.wait()


def gather_seq(values, call):
    count = lax.axis_size("seq")
    square = count == 4 and values.shape[0] % 32 == 0
    body = gather_square_kernel if square else functools.partial(gather_kernel, count)
    copies = 6 if square else count - 1
    return pl.pallas_call(
        body,
        out_shape=jax.ShapeDtypeStruct((count,) + values.shape, values.dtype),
        in_specs=[pl.BlockSpec(memory_space=pl.ANY)],
        out_specs=pl.BlockSpec(memory_space=pl.ANY),
        scratch_shapes=[
            pltpu.SemaphoreType.DMA((copies,)),
            pltpu.SemaphoreType.DMA((copies,)),
            pltpu.SemaphoreType.DMA,
        ],
        compiler_params=pltpu.CompilerParams(collective_id=call, has_side_effects=True),
        cost_estimate=transfer_cost(values.size),
        name=f"gather_seq_{call}",
    )(values)


def gather_two_kernel(a_ref, b_ref, a_out, b_out, sends, recvs, locals_):
    me = lax.axis_index("seq")
    greet((me ^ 1, me ^ 2))
    moves = Moves(locals_)
    moves.store(a_ref, a_out.at[me])
    moves.store(b_ref, b_out.at[me])
    both = [
        square_pass(ref, out, sends, recvs, first, half_rows(ref.shape[0]))
        for ref, out, first in ((a_ref, a_out, 0), (b_ref, b_out, 6))
    ]
    for copies in both:
        for copy in copies[:4]:
            copy.start()
    for copies in both:
        pass_on(copies)
    for copies in both:
        for copy in copies[2:]:
            copy.wait_recv()
    moves.close()
    for copies in both:
        for copy in copies:
            copy.wait_send()


def gather_two(a, b, call):
    return comm_call(
        gather_two_kernel,
        [(a, False), (b, False)],
        [((4,) + a.shape, BF, False), ((4,) + b.shape, BF, False)],
        [],
        12,
        2,
        call,
        a.size + b.size,
        "gather_two",
    )


def exchange_kernel(count, x_ref, o_ref, sends, recvs, local):
    me = lax.axis_index("seq")
    peers = [lax.rem(me + step, count) for step in range(1, count)]
    greet(peers)
    own = pltpu.make_async_copy(x_ref.at[me], o_ref.at[me], local)
    own.start()
    copies = [remote(x_ref.at[to], o_ref.at[me], sends, recvs, k, to) for k, to in enumerate(peers)]
    for copy in copies:
        copy.start()
    for copy in copies:
        copy.wait()
    own.wait()


def exchange_seq(values, call):
    count = lax.axis_size("seq")
    return pl.pallas_call(
        functools.partial(exchange_kernel, count),
        out_shape=jax.ShapeDtypeStruct(values.shape, values.dtype),
        in_specs=[pl.BlockSpec(memory_space=pl.ANY)],
        out_specs=pl.BlockSpec(memory_space=pl.ANY),
        scratch_shapes=[
            pltpu.SemaphoreType.DMA((count - 1,)),
            pltpu.SemaphoreType.DMA((count - 1,)),
            pltpu.SemaphoreType.DMA,
        ],
        compiler_params=pltpu.CompilerParams(collective_id=call, has_side_effects=True),
        cost_estimate=transfer_cost(values.size),
        name=f"exchange_seq_{call}",
    )(values)


def scatter_square_kernel(p_ref, o_ref, inbox_x, inbox_y, via_x, via_y, out_x, out_y, sends, recvs):
    me = lax.axis_index("seq")
    across, along, corner = me ^ 1, me ^ 2, me ^ 3
    half = p_ref.shape[1] // 2
    low, high = pl.ds(0, half), pl.ds(half, half)
    greet((across, along))
    first = (
        remote(p_ref.at[corner, low], via_x, sends, recvs, 0, across),
        remote(p_ref.at[corner, high], via_y, sends, recvs, 1, along),
        remote(p_ref.at[across, low], inbox_x.at[low], sends, recvs, 2, across),
        remote(p_ref.at[along, high], inbox_y.at[high], sends, recvs, 3, along),
    )
    for copy in first:
        copy.start()
    first[0].wait_recv()
    out_y[...] = (p_ref[along, :half].astype(F32) + via_x[...].astype(F32)).astype(BF)
    to_along = remote(out_y, inbox_y.at[low], sends, recvs, 4, along)
    to_along.start()
    first[1].wait_recv()
    out_x[...] = (p_ref[across, half:].astype(F32) + via_y[...].astype(F32)).astype(BF)
    to_across = remote(out_x, inbox_x.at[high], sends, recvs, 5, across)
    to_across.start()
    first[2].wait_recv()
    first[3].wait_recv()
    to_along.wait_recv()
    to_across.wait_recv()
    o_ref[...] = (
        p_ref[me].astype(F32) + inbox_x[...].astype(F32) + inbox_y[...].astype(F32)
    )
    for copy in first + (to_along, to_across):
        copy.wait_send()


def scatter_kernel(count, p_ref, o_ref, inbox, sends, recvs):
    me = lax.axis_index("seq")
    peers = [lax.rem(me + step, count) for step in range(1, count)]
    greet(peers)
    copies = [remote(p_ref.at[to], inbox.at[k], sends, recvs, k, to) for k, to in enumerate(peers)]
    for copy in copies:
        copy.start()
    total = p_ref[me].astype(F32)
    for k, copy in enumerate(copies):
        copy.wait_recv()
        total = total + inbox[k].astype(F32)
    o_ref[...] = total
    for copy in copies:
        copy.wait_send()


def scatter_seq(parts, call):
    count = lax.axis_size("seq")
    rows, width = parts.shape[0] // count, parts.shape[1]
    parts = parts.reshape(count, rows, width)
    if count == 4 and rows % 32 == 0:
        body = scatter_square_kernel
        scratch = [pltpu.VMEM((rows, width), BF)] * 2 + [pltpu.VMEM((rows // 2, width), BF)] * 4
        copies = 6
    else:
        body = functools.partial(scatter_kernel, count)
        scratch = [pltpu.VMEM((count - 1, rows, width), BF)]
        copies = count - 1
    return pl.pallas_call(
        body,
        out_shape=jax.ShapeDtypeStruct((rows, width), F32),
        in_specs=[pl.BlockSpec(memory_space=pltpu.VMEM)],
        out_specs=pl.BlockSpec(memory_space=pltpu.VMEM),
        scratch_shapes=scratch
        + [pltpu.SemaphoreType.DMA((copies,)), pltpu.SemaphoreType.DMA((copies,))],
        compiler_params=pltpu.CompilerParams(
            collective_id=call, has_side_effects=True, vmem_limit_bytes=32 * 1024 * 1024
        ),
        cost_estimate=transfer_cost(rows * width),
        name=f"scatter_seq_{call}",
    )(parts)


def feed_forward_kernel(ff, x_ref, w_ref, gate_ref, up_ref, hidden_ref):
    both = product(x_ref[...], w_ref[...])
    gate, up = both[:, :ff], both[:, ff:]
    gate_ref[...] = gate
    up_ref[...] = up
    hidden_ref[...] = (gate * (0.5 + 0.5 * lax.erf(gate * math.sqrt(0.5))) * up).astype(BF)


def feed_back_kernel(
    ff, c_ref, gate_ref, up_ref, hidden_ref, w_ref, down_ref, both_ref, part_ref, out_ref
):
    gate, up = gate_ref[...], up_ref[...]
    out_ref[...] = product(hidden_ref[...], down_ref[...]).astype(BF)
    hidden_grad = times_transposed(c_ref[...], down_ref[...])
    bell = 0.5 + 0.5 * lax.erf(gate * math.sqrt(0.5))
    slope = bell + gate * (math.sqrt(0.5 / math.pi) * jnp.exp(-0.5 * gate * gate))
    both = jnp.concatenate([hidden_grad * up * slope, hidden_grad * (gate * bell)], axis=1)
    both = both.astype(BF)
    both_ref[...] = both
    part_ref[...] = times_transposed(both, w_ref[...]).astype(BF)


def by_rows(block, width):
    return pl.BlockSpec((block, width), lambda i: (i, 0))


def kept(shape):
    return pl.BlockSpec(shape, lambda i: (0, 0), pipeline_mode=pl.Buffered(1))


FEED_BLOCK = 256


def feed_forward(x, weight):
    length, width = x.shape
    ff = weight.shape[1] // 2
    return pl.pallas_call(
        functools.partial(feed_forward_kernel, ff),
        grid=(length // FEED_BLOCK,),
        in_specs=[by_rows(FEED_BLOCK, width), kept(weight.shape)],
        out_specs=[by_rows(FEED_BLOCK, ff)] * 3,
        out_shape=(
            jax.ShapeDtypeStruct((length, ff), F32),
            jax.ShapeDtypeStruct((length, ff), F32),
            jax.ShapeDtypeStruct((length, ff), BF),
        ),
        compiler_params=pltpu.CompilerParams(vmem_limit_bytes=48 * 1024 * 1024),
        cost_estimate=pl.CostEstimate(
            flops=4 * length * width * ff, bytes_accessed=weight.size * 4, transcendentals=0
        ),
        name="feed_forward",
    )(x, weight)


def feed_backward(cotangent, gate, up, hidden, weight, down):
    length, width = cotangent.shape
    ff = weight.shape[1] // 2
    return pl.pallas_call(
        functools.partial(feed_back_kernel, ff),
        grid=(length // FEED_BLOCK,),
        in_specs=[by_rows(FEED_BLOCK, width)]
        + [by_rows(FEED_BLOCK, ff)] * 3
        + [kept(weight.shape), kept(down.shape)],
        out_specs=[
            by_rows(FEED_BLOCK, 2 * ff),
            by_rows(FEED_BLOCK, width),
            by_rows(FEED_BLOCK, width),
        ],
        out_shape=(
            jax.ShapeDtypeStruct((length, 2 * ff), BF),
            jax.ShapeDtypeStruct((length, width), BF),
            jax.ShapeDtypeStruct((length, width), BF),
        ),
        compiler_params=pltpu.CompilerParams(vmem_limit_bytes=56 * 1024 * 1024),
        cost_estimate=pl.CostEstimate(
            flops=8 * length * width * ff, bytes_accessed=weight.size * 4, transcendentals=0
        ),
        name="feed_back",
    )(cotangent, gate, up, hidden, weight, down)


def square_parts(parts, boxes, sends, recvs, first):
    me = lax.axis_index("seq")
    across, along = me ^ 1, me ^ 2
    inbox_x, inbox_y, via_x, via_y, out_x, out_y = boxes
    half = via_x.shape[0]
    low, high = pl.ds(0, half), pl.ds(half, half)
    copies = [
        remote(parts.at[3, low], via_x, sends, recvs, first, across),
        remote(parts.at[3, high], via_y, sends, recvs, first + 1, along),
        remote(parts.at[1, low], inbox_x.at[low], sends, recvs, first + 2, across),
        remote(parts.at[2, high], inbox_y.at[high], sends, recvs, first + 3, along),
        remote(out_y, inbox_y.at[low], sends, recvs, first + 4, along),
        remote(out_x, inbox_x.at[high], sends, recvs, first + 5, across),
    ]

    def finish():
        forward_sums(copies, parts, boxes)
        for copy in copies[2:]:
            copy.wait_recv()

    def total(rows):
        return (
            parts[0, rows].astype(F32)
            + inbox_x[rows, :].astype(F32)
            + inbox_y[rows, :].astype(F32)
        )

    return copies, finish, total


def square_gather(own, out_ref, sends, recvs, first):
    me = lax.axis_index("seq")
    across, along = me ^ 1, me ^ 2
    half = own.shape[0] // 2

    def part(ref, i):
        return ref.at[pl.ds(i * half, half)]

    copies = [
        remote(part(own, 0), part(out_ref.at[me], 0), sends, recvs, first, across),
        remote(part(own, 1), part(out_ref.at[me], 1), sends, recvs, first + 1, along),
        remote(part(own, 1), part(out_ref.at[me], 1), sends, recvs, first + 2, across),
        remote(part(own, 0), part(out_ref.at[me], 0), sends, recvs, first + 3, along),
        remote(
            part(out_ref.at[across], 0), part(out_ref.at[across], 0), sends, recvs, first + 4, along
        ),
        remote(
            part(out_ref.at[along], 1), part(out_ref.at[along], 1), sends, recvs, first + 5, across
        ),
    ]

    def finish():
        copies[0].wait_recv()
        copies[4].start()
        copies[1].wait_recv()
        copies[5].start()
        for copy in copies[2:]:
            copy.wait_recv()

    return copies, finish


def block_rows(k, rows):
    return pl.ds(pl.multiple_of((lax.axis_index("seq") ^ k) * rows, rows), rows)


def forward_sums(copies, parts, boxes):
    inbox_x, inbox_y, via_x, via_y, out_x, out_y = boxes
    half = via_x.shape[0]
    copies[0].wait_recv()
    out_y[...] = (parts[2, :half].astype(F32) + via_x[...].astype(F32)).astype(BF)
    copies[4].start()
    copies[1].wait_recv()
    out_x[...] = (parts[1, half:].astype(F32) + via_y[...].astype(F32)).astype(BF)
    copies[5].start()


def send_parts(part, copies, then=None):
    @pl.loop(0, 4)
    def _(i):
        if then is not None:
            pl.when(i == 3)(then)
        part(jnp.where(i == 0, 3, jnp.where(i == 3, 0, i)))

        @pl.when(i == 0)
        def _():
            copies[0].start()
            copies[1].start()

        @pl.when(i == 1)
        def _():
            copies[2].start()

        @pl.when(i == 2)
        def _():
            copies[3].start()


def project_kernel(
    g_any, w_any, x_ref, gain_ref, middle_ref, own_ref,
    g_ref, w_ref, parts, inbox_x, inbox_y, via_x, via_y, out_x, out_y, sends, recvs, locals_,
):
    me = lax.axis_index("seq")
    rows = x_ref.shape[0]
    half = rows // 2
    moves = Moves(locals_)
    loads = [moves.start(w_any, w_ref), moves.start(g_any, g_ref)]
    greet((me ^ 1, me ^ 2))
    boxes = (inbox_x, inbox_y, via_x, via_y, out_x, out_y)
    copies, finish, total = square_parts(parts, boxes, sends, recvs, 0)

    def part(k):
        parts[k] = product(g_ref[block_rows(k, rows), :], w_ref[...]).astype(BF)

    for load in loads:
        load.wait()
    send_parts(part, copies)
    finish()

    @pl.loop(0, 2)
    def _(i):
        here = pl.ds(pl.multiple_of(i * half, half), half)
        middle = x_ref[here, :].astype(F32) + total(here)
        middle_ref[here, :] = middle
        own_ref[here, :] = normalize(middle, gain_ref[...]).astype(BF)

    for copy in copies:
        copy.wait_send()


def square_scratch(rows, width):
    return [
        pltpu.VMEM((4, rows, width), BF),
        pltpu.VMEM((rows, width), BF),
        pltpu.VMEM((rows, width), BF),
        pltpu.VMEM((rows // 2, width), BF),
        pltpu.VMEM((rows // 2, width), BF),
        pltpu.VMEM((rows // 2, width), BF),
        pltpu.VMEM((rows // 2, width), BF),
    ]


def square_call(body, out_shape, out_specs, scratch, inputs, call, cost, name):
    return pl.pallas_call(
        body,
        out_shape=out_shape,
        in_specs=[IN_VMEM] * len(inputs),
        out_specs=out_specs,
        scratch_shapes=scratch,
        compiler_params=pltpu.CompilerParams(
            collective_id=call, has_side_effects=True, vmem_limit_bytes=56 * 1024 * 1024
        ),
        cost_estimate=transfer_cost(cost),
        name=name,
    )(*inputs)


def core_sum(moves, make, send_ref, twin_ref, out_ref, targets, sends, recvs, first):
    shard = lax.axis_index("fsdp")
    core = lax.rem(shard, 2)
    count = out_ref.shape[0]

    def copy(t):
        return pltpu.make_async_remote_copy(
            src_ref=send_ref.at[t],
            dst_ref=twin_ref.at[t],
            send_sem=sends.at[first + t],
            recv_sem=recvs.at[first + t],
            device_id={"fsdp": shard ^ 1},
            device_id_type=MESH,
        )

    stores = Series(moves, count, lambda t: (out_ref.at[t], targets(t)))

    @pl.loop(0, count)
    def _(t):
        send_ref[t] = make(2 * t + 1 - core).astype(BF)
        copy(t).start()

    @pl.loop(0, count)
    def _(t):
        own = make(2 * t + core)
        copy(t).wait_recv()
        out_ref[t] = (own + twin_ref[t].astype(F32)).astype(BF)
        stores.copy(t).start()

    def finish():
        stores.wait_all()
        for t in range(count):
            copy(t).wait_send()

    return finish


def greet_near(me, shard):
    barrier = pltpu.get_barrier_semaphore()
    for k in (1, 2):
        pl.semaphore_signal(barrier, inc=1, device_id={"seq": me ^ k}, device_id_type=MESH)
    pl.semaphore_signal(barrier, inc=1, device_id={"fsdp": shard ^ 1}, device_id_type=MESH)
    pl.semaphore_wait(barrier, 3)


def core_scratch(rows, width):
    return [pltpu.VMEM((rows // (2 * BLOCK), BLOCK, width), BF)] * 3


def comm_call(body, inputs, outputs, scratch, remotes, moves, call, cost, name):
    return pl.pallas_call(
        body,
        out_shape=tuple(jax.ShapeDtypeStruct(shape, kind) for shape, kind, _ in outputs),
        in_specs=[IN_VMEM if whole else ANYWHERE for _, whole in inputs],
        out_specs=tuple(IN_VMEM if whole else ANYWHERE for _, _, whole in outputs),
        scratch_shapes=scratch
        + [
            pltpu.SemaphoreType.DMA((remotes,)),
            pltpu.SemaphoreType.DMA((remotes,)),
            pltpu.SemaphoreType.DMA((moves,)),
        ],
        compiler_params=pltpu.CompilerParams(
            collective_id=call, has_side_effects=True, vmem_limit_bytes=60 * 1024 * 1024
        ),
        cost_estimate=transfer_cost(cost),
        name=name,
    )(*[value for value, _ in inputs])


def retention_exchange_kernel(
    heads, offsets, cut, mixed_any, w_any, cos_ref, sin_ref, table_ref,
    q_any, k_any, v_any, swish_any, retained_any, gated_any, wo_any,
    mixed_ref, w_ref, q_ref, k_ref, v_ref, swish_ref, retained_ref, gated_ref, both_ref, wo_ref,
    via_x, via_y, sends, recvs, locals_,
):
    me = lax.axis_index("seq")
    shard = lax.axis_index("fsdp")
    core = lax.rem(shard, 2)
    step, wide = both_ref.shape[2:]
    moves = Moves(locals_)

    def piece(column):
        rows = pl.ds(pl.multiple_of((2 * column + core) * step, step), step)
        return w_any.at[rows, slice(w_ref.shape[1], w_ref.shape[1] + wide)]

    across, along, corner = me ^ 1, me ^ 2, me ^ 3
    half = step // 2
    low, high = slice(0, half), slice(half, step)
    swaps = [
        remote(piece(corner).at[low], via_x, sends, recvs, 0, across),
        remote(piece(corner).at[high], via_y, sends, recvs, 1, along),
        remote(piece(across), both_ref.at[core, me], sends, recvs, 2, across),
        remote(piece(along), both_ref.at[core, me], sends, recvs, 3, along),
        remote(via_x, both_ref.at[core, across, low], sends, recvs, 4, along),
        remote(via_y, both_ref.at[core, along, high], sends, recvs, 5, across),
    ]
    kept_here = []

    def twin(k):
        return pltpu.make_async_remote_copy(
            src_ref=both_ref.at[core, me ^ k],
            dst_ref=both_ref.at[core, me ^ k],
            send_sem=sends.at[6 + k],
            recv_sem=recvs.at[6 + k],
            device_id={"fsdp": shard ^ 1},
            device_id_type=MESH,
        )

    def between(i):
        if isinstance(i, int):
            greet_all(me, shard)
            for copy in swaps[:4]:
                copy.start()
            kept_here.append(moves.start(piece(me), both_ref.at[core, me]))
            return

        @pl.when(i == 0)
        def _():
            swaps[0].wait_recv()
            swaps[4].start()
            swaps[1].wait_recv()
            swaps[5].start()
            kept_here[0].wait()
            twin(0).start()

        @pl.when(i == 2)
        def _():
            for k in (1, 2):
                swaps[1 + k].wait_recv()
                twin(k).start()

        @pl.when(i == 3)
        def _():
            swaps[4].wait_recv()
            swaps[5].wait_recv()
            twin(3).start()

    retention_kernel(
        heads, offsets, mixed_any, w_any, cos_ref, sin_ref, table_ref,
        q_any, k_any, v_any, swish_any, retained_any, gated_any,
        mixed_ref, w_ref, q_ref, k_ref, v_ref, swish_ref, retained_ref, gated_ref, moves, between,
    )
    for k in range(4):
        twin(k).wait_recv()
    tile, lane = 16, 128

    @pl.loop(0, heads * (wo_ref.shape[1] // lane))
    def _(n):
        h, c = n // (wo_ref.shape[1] // lane), lax.rem(n, wo_ref.shape[1] // lane)
        lanes = pl.ds(pl.multiple_of(c * lane, lane), lane)
        for k in range(4):
            for r in range(cut.skip(k) // tile, cut.width // tile):
                at = pl.multiple_of(h * cut.rows + (cut.start(k) + r * tile), tile)
                wo_ref[pl.ds(at, tile), lanes] = both_ref[
                    h, k, pl.ds(pl.multiple_of(c * tile, tile), tile), head_lanes(r, lane)
                ]

    moves.start(wo_ref, wo_any).wait()
    for copy in swaps + [twin(k) for k in range(4)]:
        copy.wait_send()


def greet_all(me, shard):
    barrier = pltpu.get_barrier_semaphore()
    for k in (1, 2, 3):
        pl.semaphore_signal(barrier, inc=1, device_id={"seq": me ^ k}, device_id_type=MESH)
    pl.semaphore_signal(barrier, inc=1, device_id={"fsdp": shard ^ 1}, device_id_type=MESH)
    pl.semaphore_wait(barrier, 4)


def retention_exchange(mixed, weight, cosine, sine, table, heads, offsets, cut, call):
    length, width = mixed.shape
    wide = cut.width * width // 256
    outputs = retention_outputs(length, heads) + (((heads * VAL_HEAD, width), BF),)
    return comm_call(
        functools.partial(retention_exchange_kernel, heads, offsets, cut),
        [(mixed, False), (weight, False), (cosine, True), (sine, True), (table, True)],
        [(shape, kind, False) for shape, kind in outputs],
        [pltpu.VMEM(mixed.shape, BF), pltpu.VMEM((width, weight.shape[1] - wide), BF)]
        + [pltpu.VMEM(*out) for out in outputs[:-1]]
        + [pltpu.VMEM((heads, 4, 256, wide), BF), pltpu.VMEM(outputs[-1][0], BF)]
        + [pltpu.VMEM((128, wide), BF)] * 2,
        10,
        6 + 7 * (length // BLOCK),
        call,
        mixed.size // 2,
        "retention_exchange",
    )


def project_and_norm(gated, weight, x, gain, call):
    rows, width = x.shape
    return comm_call(
        project_kernel,
        [(gated, False), (weight, False), (x, True), (gain[None, :], True)],
        [((rows, width), F32, True), ((rows, width), BF, True)],
        [pltpu.VMEM(gated.shape, BF), pltpu.VMEM(weight.shape, BF)] + square_scratch(rows, width),
        6,
        2,
        call,
        x.size,
        "project_and_norm",
    )


def feed_forward_gather_kernel(
    ff, x_any, w_any, c_any, both_any, hidden_any, down_any, full_any,
    full, w_ref, c_ref, both_ref, hidden_ref, total, down_ref, sends, recvs, locals_,
):
    me = lax.axis_index("seq")
    rows = x_any.shape[0]
    moves = Moves(locals_)
    load_x = moves.start(x_any, full.at[me])
    load_w = moves.start(w_any, w_ref)
    load_c = moves.start(c_any, c_ref)
    greet((me ^ 1, me ^ 2))
    load_x.wait()
    copies, _ = square_gather(full.at[me], full, sends, recvs, 0)
    for copy in copies[:4]:
        copy.start()
    stores = [
        by_block(moves, 4, both_ref, both_any, rows),
        by_block(moves, 4, hidden_ref, hidden_any, rows),
        Series(moves, 4, lambda n: (full.at[n], full_any.at[n])),
    ]
    total[...] = jnp.zeros_like(total)
    load_w.wait()
    load_c.wait()

    @pl.loop(0, 4)
    def _(k):
        @pl.when(k == 1)
        def _():
            copies[0].wait_recv()
            copies[4].start()
            copies[1].wait_recv()
            copies[5].start()
            copies[2].wait_recv()

        @pl.when(k == 2)
        def _():
            copies[3].wait_recv()

        @pl.when(k == 3)
        def _():
            copies[4].wait_recv()
            copies[5].wait_recv()

        here = block_rows(k, rows)
        both = product(full[me ^ k], w_ref[...])
        gate, up = both[:, :ff], both[:, ff:]
        bell = 0.5 + 0.5 * lax.erf(gate * math.sqrt(0.5))
        passed = gate * bell
        slope = bell + gate * (math.sqrt(0.5 / math.pi) * jnp.exp(-0.5 * gate * gate))
        both_ref[here, :ff] = (up * slope).astype(BF)
        both_ref[here, ff:] = passed.astype(BF)
        hidden = (passed * up).astype(BF)
        hidden_ref[here, :] = hidden
        for store in stores:
            store.copy(me ^ k).start()
        total[...] += transposed_times(hidden, c_ref[here, :])

    down_ref[...] = total[...].astype(BF)
    moves.store(down_ref, down_any)
    for store in stores:
        store.wait_all()
    moves.close()
    for copy in copies:
        copy.wait_send()


def feed_forward_gather(own, weight, cotangent, call):
    rows, width = own.shape
    length, ff = 4 * rows, weight.shape[1] // 2
    both, hidden, down, full = comm_call(
        functools.partial(feed_forward_gather_kernel, ff),
        [(own, False), (weight, False), (cotangent, False)],
        [
            ((length, 2 * ff), BF, False),
            ((length, ff), BF, False),
            ((ff, width), BF, False),
            ((4, rows, width), BF, False),
        ],
        [
            pltpu.VMEM((4, rows, width), BF),
            pltpu.VMEM(weight.shape, BF),
            pltpu.VMEM(cotangent.shape, BF),
            pltpu.VMEM((length, 2 * ff), BF),
            pltpu.VMEM((length, ff), BF),
            pltpu.VMEM((ff, width), F32),
            pltpu.VMEM((ff, width), BF),
        ],
        6,
        16,
        call,
        own.size,
        "feed_forward_gather",
    )
    return both, hidden, down, full.reshape(length, width)


def column_of(halves):
    total = 0.0
    for terms in halves:
        ones = jnp.ones((terms.shape[0], 128), BF)
        total = total + transposed_times(terms.astype(BF), ones)
    return total


def feed_back_scatter_kernel(
    ff, c_any, both_any, w_any, down_any, x_any, m_ref, own_c_ref, gain_ref,
    grad_ref, term_ref, branch_ref, dw_any,
    c_ref, both_ref, w_ref, down_ref, x_ref, low, dw_send, dw_twin, dw_ref,
    parts, inbox_x, inbox_y, via_x, via_y, out_x, out_y, sends, recvs, locals_,
):
    me = lax.axis_index("seq")
    rows = own_c_ref.shape[0]
    half = rows // 2
    moves = Moves(locals_)
    load_c = by_block(moves, 4, c_any, c_ref, rows)
    load_both = by_block(moves, 4, both_any, both_ref, rows)
    load_c.copy(me ^ 3).start()
    load_down = moves.start(down_any, down_ref)
    load_both.copy(me ^ 3).start()
    load_w = moves.start(w_any, w_ref)
    for k in (1, 2, 0):
        load_c.copy(me ^ k).start()
        load_both.copy(me ^ k).start()
    load_x = moves.start(x_any, x_ref)
    greet_near(me, lax.axis_index("fsdp"))
    boxes = (inbox_x, inbox_y, via_x, via_y, out_x, out_y)
    copies, _, total = square_parts(parts, boxes, sends, recvs, 0)

    def part(k):
        here = block_rows(k, rows)
        load_c.copy(me ^ k).wait()
        load_both.copy(me ^ k).wait()
        hidden_grad = times_transposed(c_ref[here, :], down_ref[...])
        low[here, :ff] = (hidden_grad * both_ref[here, :ff].astype(F32)).astype(BF)
        low[here, ff:] = (hidden_grad * both_ref[here, ff:].astype(F32)).astype(BF)
        pl.when(k == 3)(load_w.wait)
        parts[k] = times_transposed(low[here, :], w_ref[...]).astype(BF)

    load_down.wait()
    send_parts(part, copies, lambda: forward_sums(copies, parts, boxes))
    load_x.wait()
    finish = core_sum(
        moves, lambda b: transposed_times(x_ref[:, rows_of(b)], low[...]), dw_send, dw_twin, dw_ref,
        lambda t: dw_any.at[rows_of(t)], sends, recvs, 6,
    )
    for copy in copies[2:]:
        copy.wait_recv()

    def back_half(i):
        here = slice(i * half, (i + 1) * half)
        back, term = norm_back(m_ref[here, :], total(here), gain_ref[...])
        grad = own_c_ref[here, :].astype(F32) + back
        grad_ref[here, :] = grad
        branch_ref[here, :] = grad.astype(BF)
        return term

    term_ref[...] = column_of([back_half(i) for i in range(2)])
    finish()
    for copy in copies:
        copy.wait_send()


def feed_back_scatter(cotangent, both, weight, down, x, middle, own_cotangent, gain, call):
    rows, width = own_cotangent.shape
    length, ff = cotangent.shape[0], weight.shape[1] // 2
    grad, term, branch, dw = comm_call(
        functools.partial(feed_back_scatter_kernel, ff),
        [
            (cotangent, False),
            (both, False),
            (weight, False),
            (down, False),
            (x, False),
            (middle, True),
            (own_cotangent, True),
            (gain[None, :], True),
        ],
        [
            ((rows, width), F32, True),
            ((width, 128), F32, True),
            ((rows, width), BF, True),
            ((width // 2, 2 * ff), BF, False),
        ],
        [
            pltpu.VMEM(cotangent.shape, BF),
            pltpu.VMEM(both.shape, BF),
            pltpu.VMEM(weight.shape, BF),
            pltpu.VMEM(down.shape, BF),
            pltpu.VMEM(x.shape, BF),
            pltpu.VMEM((length, 2 * ff), BF),
        ]
        + core_scratch(width, 2 * ff)
        + square_scratch(rows, width),
        6 + width // (2 * BLOCK),
        11 + width // (2 * BLOCK),
        call,
        own_cotangent.size,
        "feed_back_scatter",
    )
    return grad, term, branch, dw


def norm_back(values, grad, gain):
    centered = values - jnp.mean(values, axis=-1, keepdims=True)
    spread = lax.rsqrt(jnp.mean(centered * centered, axis=-1, keepdims=True) + EPSILON)
    unit = centered * spread
    g = grad * gain
    back = g - jnp.mean(g, axis=-1, keepdims=True)
    back = spread * (back - unit * jnp.mean(g * unit, axis=-1, keepdims=True))
    return back, grad * unit


def square_pass(own, out_ref, sends, recvs, first, half):
    me = lax.axis_index("seq")
    across, along = me ^ 1, me ^ 2
    spans = (slice(0, half), slice(half, own.shape[0]))

    def part(ref, i):
        return ref.at[spans[i]]

    return [
        remote(part(own, 0), part(out_ref.at[me], 0), sends, recvs, first, across),
        remote(part(own, 1), part(out_ref.at[me], 1), sends, recvs, first + 1, along),
        remote(part(own, 1), part(out_ref.at[me], 1), sends, recvs, first + 2, across),
        remote(part(own, 0), part(out_ref.at[me], 0), sends, recvs, first + 3, along),
        remote(
            part(out_ref.at[across], 0), part(out_ref.at[across], 0), sends, recvs, first + 4, along
        ),
        remote(
            part(out_ref.at[along], 1), part(out_ref.at[along], 1), sends, recvs, first + 5, across
        ),
    ]


def pass_on(copies):
    copies[0].wait_recv()
    copies[4].start()
    copies[1].wait_recv()
    copies[5].start()


def half_rows(rows):
    return -(-rows // 32) * 16


def put_column(ref, rows, at, column):
    first = ref.shape[1] - 128
    spare = lax.broadcasted_iota(jnp.int32, column.shape, 1) == at - first
    ref[rows, first:] = jnp.where(spare, column, ref[rows, first:].astype(F32)).astype(BF)


def gate_back_scatter_kernel(
    heads, cut, branch_any, w_any, swish_any, retained_any, column_any, hidden_any, down_any,
    mixed_any, gated_any, m_any, dswish_any, dret_any, dws_any, dwo_any, out_ref,
    branch_ref, w_ref, swish_ref, retained_ref, column_ref, hidden_ref, down_ref, mixed_ref,
    gated_ref, m_ref, dswish_ref, dret_ref, dws_send, dws_twin, dws_ref, dwo_ref,
    parts, inbox_x, inbox_y, via_x, via_y, out_x, out_y, sends, recvs, locals_,
):
    me = lax.axis_index("seq")
    rows = out_ref.shape[0]
    moves = Moves(locals_)
    load_down = moves.start(down_any, down_ref)
    load_hidden = moves.start(hidden_any, hidden_ref)
    load_gate = moves.start(w_any, w_ref)
    blocks = branch_ref.shape[0] // BLOCK
    load_rows = [
        by_block(moves, blocks, branch_any, branch_ref).start_all(),
        by_block(moves, blocks, swish_any, swish_ref).start_all(),
        by_block(moves, blocks, retained_any, retained_ref).start_all(),
    ]
    load_mixed = moves.start(mixed_any, mixed_ref)
    load_column = moves.start(column_any, column_ref)
    load_gated = moves.start(gated_any, gated_ref)
    load_m = moves.start(m_any, m_ref)
    greet_near(me, lax.axis_index("fsdp"))
    boxes = (inbox_x, inbox_y, via_x, via_y, out_x, out_y)
    copies, _, total = square_parts(parts, boxes, sends, recvs, 0)

    def part(k):
        here = block_rows(k, rows)
        parts[k] = product(hidden_ref[here, :], down_ref[...]).astype(BF)

    load_hidden.wait()
    load_down.wait()
    send_parts(part, copies)
    load_gate.wait()

    @pl.loop(0, blocks)
    def _(i):
        here = rows_of(i)
        for load in load_rows:
            load.copy(i).wait()
        gate_back_rows(
            heads, here, branch_ref[here, :], w_ref, swish_ref, retained_ref, dswish_ref, dret_ref
        )

    moves.store(dswish_ref, dswish_any)
    moves.store(dret_ref, dret_any)
    forward_sums(copies, parts, boxes)
    load_mixed.wait()
    load_column.wait()
    last = dswish_ref.shape[1] - 128
    spare = lax.broadcasted_iota(jnp.int32, (BLOCK, 128), 1) == heads * VAL_HEAD - last

    def make(b):
        here = rows_of(b)
        term = product(mixed_ref[here, :], dswish_ref[...])
        column = jnp.where(spare, column_ref[here, :], term[:, last:])
        return jnp.concatenate([term[:, :last], column], axis=1)

    finish = core_sum(
        moves, make, dws_send, dws_twin, dws_ref, lambda t: dws_any.at[rows_of(t)], sends, recvs, 6
    )
    load_gated.wait()
    step, tile, lane = 2 * BLOCK, 16, 128
    for h in range(heads):
        value_lanes = head_lanes(h, VAL_HEAD)

        @pl.loop(0, branch_ref.shape[1] // step)
        def _(b):
            lanes = pl.ds(pl.multiple_of(b * step, step), step)
            wide = transposed_times(gated_ref[:, value_lanes], branch_ref[:, lanes]).astype(BF)
            for k in range(4):
                for r in range(cut.width // tile):
                    at = cut.start(k) + r * tile
                    for c in range(step // lane):
                        to = pl.ds(pl.multiple_of((b * (step // lane) + c) * tile, tile), tile)
                        dwo_ref[h, k, to, head_lanes(r, lane)] = wide[
                            at : at + tile, head_lanes(c, lane)
                        ]

    moves.store(dwo_ref, dwo_any)
    load_m.wait()
    for copy in copies[2:]:
        copy.wait_recv()
    out_ref[...] = m_ref[...] + total(slice(0, rows))
    finish()
    moves.close()
    for copy in copies:
        copy.wait_send()


def gate_backward_scatter(
    branch, weight, swish, retained, column, hidden, down, mixed_t, gated, middle, heads, padded,
    cut, call,
):
    length, width = branch.shape
    rows = middle.shape[0]
    dwo = (heads, 4, width // 8, cut.width * 8)
    inputs = (branch, weight, swish, retained, column, hidden, down, mixed_t, gated, middle)
    outputs = [
        ((length, padded), BF, False),
        ((heads, length, VAL_HEAD), BF, False),
        ((width // 2, padded), BF, False),
        (dwo, BF, False),
        ((rows, width), F32, True),
    ]
    return comm_call(
        functools.partial(gate_back_scatter_kernel, heads, cut),
        [(value, False) for value in inputs],
        outputs,
        [pltpu.VMEM(v.shape, v.dtype) for v in inputs]
        + [pltpu.VMEM(shape, kind) for shape, kind, _ in outputs[:2]]
        + core_scratch(width, padded)
        + [pltpu.VMEM(dwo, BF)]
        + square_scratch(rows, width),
        6 + width // (2 * BLOCK),
        20 + 3 * length // BLOCK + width // (2 * BLOCK),
        call,
        middle.size,
        "gate_back_scatter",
    )


def retention_back_exchange_kernel(
    heads, q_any, k_any, v_any, dret_any, table_ref, cos_ref, sin_ref, mixed_any, send_any, share_any,
    dqk_any, dv_any, merged_any, full_any,
    q_ref, k_ref, v_ref, dret_ref, mixed_ref, send_ref, dqk_ref, dv_ref, dw_send, dw_twin, dw_ref,
    twin_ref, sum_ref, via_x, via_y, dv_heads, dq_sum, sends, recvs, locals_,
):
    me = lax.axis_index("seq")
    shard = lax.axis_index("fsdp")
    core = lax.rem(shard, 2)
    moves = Moves(locals_)
    load_send = moves.start(send_any, send_ref)
    loads = [
        moves.start(source, target)
        for source, target in (
            (q_any, q_ref), (k_any, k_ref), (v_any, v_ref), (dret_any, dret_ref)
        )
    ]
    load_mixed = moves.start(mixed_any, mixed_ref)
    greet_all(me, shard)
    load_send.wait()
    twin = pltpu.make_async_remote_copy(
        src_ref=send_ref.at[1 - core],
        dst_ref=twin_ref,
        send_sem=sends.at[12],
        recv_sem=recvs.at[12],
        device_id={"fsdp": shard ^ 1},
        device_id_type=MESH,
    )
    twin.start()
    passed = square_pass(share_any, full_any, sends, recvs, 0, half_rows(share_any.shape[0]))
    for copy in passed[:4]:
        copy.start()
    moves.store(share_any, full_any.at[me])
    step, wide = sum_ref.shape[1:]
    half = step // 2
    at = dqk_ref.shape[1]
    across, along, corner = me ^ 1, me ^ 2, me ^ 3

    def place(column, start, rows):
        here = pl.ds(pl.multiple_of(column * step + start, half), rows)
        return merged_any.at[here, slice(at, at + wide)]

    low, high = slice(0, half), slice(half, step)
    swaps = [
        remote(sum_ref.at[corner, low], via_x, sends, recvs, 6, across),
        remote(sum_ref.at[corner, high], via_y, sends, recvs, 7, along),
        remote(sum_ref.at[across], place(me, 0, step), sends, recvs, 8, across),
        remote(sum_ref.at[along], place(me, 0, step), sends, recvs, 9, along),
        remote(via_x, place(across, 0, half), sends, recvs, 10, along),
        remote(via_y, place(along, half, half), sends, recvs, 11, across),
    ]
    for load in loads:
        load.wait()
    for h in range(heads):
        retention_back_head(
            h, heads, q_ref, k_ref, v_ref, dret_ref, table_ref, cos_ref, sin_ref, dqk_ref,
            dv_heads.at[h], dq_sum,
        )
        if h == 0:
            twin.wait_recv()

            @pl.loop(0, 4)
            def _(k):
                sum_ref[k] = (send_ref[core, k].astype(F32) + twin_ref[k].astype(F32)).astype(BF)

            for copy in swaps[:4]:
                copy.start()
            moves.store(sum_ref.at[me], place(me, 0, step))
            pass_on(passed)
    pass_on(swaps)
    dv_ref[...] = pad_lanes([dv_heads[h] for h in range(heads)], dv_ref.shape[1])
    moves.store(dv_ref, dv_any)
    moves.store(dqk_ref, dqk_any)
    load_mixed.wait()
    finish = core_sum(
        moves, lambda b: product(mixed_ref[rows_of(b), :], dqk_ref[...]), dw_send, dw_twin, dw_ref,
        lambda t: merged_any.at[rows_of(t), slice(0, at)], sends, recvs, 13,
    )
    for copy in passed[2:] + swaps[2:]:
        copy.wait_recv()
    finish()
    moves.close()
    for copy in passed + swaps + [twin]:
        copy.wait_send()


def retention_backward_exchange(
    q, k, v, dret, table, cosine, sine, mixed_t, send, share, heads, padded, call
):
    width, length = mixed_t.shape
    qk = heads * KEY_HEAD
    inputs = (
        (q, False), (k, False), (v, False), (dret, False), (table, True), (cosine, True),
        (sine, True), (mixed_t, False), (send, False), (share, False),
    )
    staged = (q, k, v, dret, mixed_t, send)
    block = send.shape[1:]
    kept = width // 2
    return comm_call(
        functools.partial(retention_back_exchange_kernel, heads),
        inputs,
        [
            ((length, 2 * qk), BF, False),
            ((length, padded), BF, False),
            ((kept, 2 * qk + block[2]), BF, False),
            ((4,) + share.shape, BF, False),
        ],
        [pltpu.VMEM(value.shape, BF) for value in staged]
        + [
            pltpu.VMEM((length, 2 * qk), BF),
            pltpu.VMEM((length, padded), BF),
        ]
        + core_scratch(width, 2 * qk)
        + [
            pltpu.VMEM(block, BF),
            pltpu.VMEM(block, BF),
            pltpu.VMEM((block[1] // 2, block[2]), BF),
            pltpu.VMEM((block[1] // 2, block[2]), BF),
            pltpu.VMEM((heads, length, VAL_HEAD), BF),
            pltpu.VMEM((length, KEY_HEAD), F32),
        ],
        13 + kept // BLOCK,
        12 + kept // BLOCK,
        call,
        send.size // 4,
        "retention_back_exchange",
    )


def input_back_kernel(
    offsets, spare, dqk_any, dv_any, ds_any, w_any, x_any, grad_any, mixed_any, gain_ref, share_any,
    dx_ref, dwv_any, full_any, dqk_ref, dv_ref, ds_ref, w_ref, x_ref, grad_ref, mixed_ref, dwv_ref,
    parts, inbox_x, inbox_y, via_x, via_y, out_x, out_y, sends, recvs, locals_,
):
    at_value, at_swish = offsets
    me = lax.axis_index("seq")
    rows = x_ref.shape[0]
    half = rows // 2
    moves = Moves(locals_)
    spans = (slice(0, at_value), slice(at_value, at_swish), slice(at_swish, w_ref.shape[1]))
    grads = ((dqk_any, dqk_ref), (dv_any, dv_ref), (ds_any, ds_ref))
    loads = []
    for span, (source, target) in zip(spans, grads, strict=True):
        loads.append(moves.start(source, target))
        loads.append(moves.start(w_any.at[:, span], w_ref.at[:, span]))
    load_x = moves.start(x_any, x_ref)
    load_grad = moves.start(grad_any, grad_ref)
    load_mixed = moves.start(mixed_any, mixed_ref)
    greet((me ^ 1, me ^ 2))
    boxes = (inbox_x, inbox_y, via_x, via_y, out_x, out_y)
    copies, _, total = square_parts(parts, boxes, sends, recvs, 0)
    passed = square_pass(share_any, full_any, sends, recvs, 6, half_rows(share_any.shape[0]))
    passed[0].start()
    passed[1].start()
    moves.store(share_any, full_any.at[me])

    def part(k):
        here = block_rows(k, rows)
        whole = 0.0
        for n, (_, ref) in enumerate(grads):

            @pl.when(k == 3)
            def _():
                loads[2 * n].wait()
                loads[2 * n + 1].wait()

            whole = whole + times_transposed(ref[here, :], w_ref[:, spans[n]])
        parts[k] = whole.astype(BF)

    def pass_all():
        pass_on(passed)
        forward_sums(copies, parts, boxes)
        passed[2].start()
        passed[3].start()

    send_parts(part, copies, pass_all)
    load_mixed.wait()

    @pl.loop(0, dwv_ref.shape[0] // BLOCK)
    def _(b):
        here = rows_of(b)
        dwv_ref[here, :] = product(mixed_ref[here, :], dv_ref[...]).astype(BF)

    for copy in copies[2:]:
        copy.wait_recv()
    load_x.wait()
    load_grad.wait()
    terms = []
    for i in range(2):
        here = slice(i * half, (i + 1) * half)
        back, term = norm_back(x_ref[here, :].astype(F32), total(here), gain_ref[...])
        dx_ref[here, :] = grad_ref[here, :] + back
        terms.append(term)
    put_column(dwv_ref, slice(0, dwv_ref.shape[0]), spare, column_of(terms))
    moves.store(dwv_ref, dwv_any)
    for copy in passed[2:]:
        copy.wait_recv()
    moves.close()
    for copy in copies + passed:
        copy.wait_send()


def input_backward(dqk, dv, ds, weight, x, grad, mixed_t, gain, share, offsets, spare, call):
    rows, width = x.shape
    staged = (dqk, dv, ds, weight, x, grad, mixed_t)
    return comm_call(
        functools.partial(input_back_kernel, offsets, spare),
        [(value, False) for value in staged] + [(gain[None, :], True), (share, False)],
        [
            ((rows, width), F32, True),
            ((width, dv.shape[1]), BF, False),
            ((4,) + share.shape, BF, False),
        ],
        [pltpu.VMEM(value.shape, value.dtype) for value in staged[:3]]
        + [pltpu.VMEM((width, dqk.shape[1] + dv.shape[1] + ds.shape[1]), BF)]
        + [pltpu.VMEM(value.shape, value.dtype) for value in staged[4:]]
        + [pltpu.VMEM((width, dv.shape[1]), BF)]
        + square_scratch(rows, width),
        12,
        11,
        call,
        x.size + share.size,
        "input_backward",
    )


def join(pieces):
    return jnp.concatenate(pieces, axis=1) if len(pieces) > 1 else pieces[0]


def unpack_columns_kernel(width, in_ref, out_ref, gain_ref):
    count = in_ref.shape[0]
    out_ref[...] = join([in_ref[k][:, :width].astype(F32) for k in range(count)])
    last = in_ref.shape[2] - 128
    tile = sum(in_ref[k][:, last:].astype(F32) for k in range(count))
    gain_ref[...] = tile.T[width - last : width - last + 1, :]


def unpack_columns(gathered, width):
    count, rows, whole = gathered.shape
    block = min(rows, 128)
    out, gain = pl.pallas_call(
        functools.partial(unpack_columns_kernel, width),
        grid=(rows // block,),
        in_specs=[pl.BlockSpec((count, block, whole), lambda i: (0, i, 0))],
        out_specs=[
            pl.BlockSpec((block, count * width), lambda i: (i, 0)),
            pl.BlockSpec((1, block), lambda i: (0, i)),
        ],
        out_shape=[
            jax.ShapeDtypeStruct((rows, count * width), F32),
            jax.ShapeDtypeStruct((1, rows), F32),
        ],
        cost_estimate=pl.CostEstimate(flops=0, bytes_accessed=gathered.size * 4, transcendentals=0),
        name="unpack_columns",
    )(gathered)
    return out, gain[0]


def unpack_related_kernel(width, own_ref, across_ref, along_ref, corner_ref, out_ref, gain_ref):
    me = lax.axis_index("seq")
    pieces = [ref[...].astype(F32) for ref in (own_ref, across_ref, along_ref, corner_ref)]
    last = own_ref.shape[1] - 128
    tile = sum(piece[:, last:] for piece in pieces)
    gain_ref[...] = tile.T[width - last : width - last + 1, :]
    pieces = [piece[:, :width] for piece in pieces]
    low = [jnp.where(me % 2 == k, pieces[0], pieces[1]) for k in range(2)]
    high = [jnp.where(me % 2 == k, pieces[2], pieces[3]) for k in range(2)]
    order = [jnp.where(me < 2, low[k], high[k]) for k in range(2)]
    order += [jnp.where(me < 2, high[k], low[k]) for k in range(2)]
    out_ref[...] = join(order)


def unpack_related(pieces, width):
    rows, whole = pieces[0].shape
    block = min(rows, 128)
    out, gain = pl.pallas_call(
        functools.partial(unpack_related_kernel, width),
        grid=(rows // block,),
        in_specs=[pl.BlockSpec((block, whole), lambda i: (i, 0))] * 4,
        out_specs=[
            pl.BlockSpec((block, 4 * width), lambda i: (i, 0)),
            pl.BlockSpec((1, block), lambda i: (0, i)),
        ],
        out_shape=[
            jax.ShapeDtypeStruct((rows, 4 * width), F32),
            jax.ShapeDtypeStruct((1, rows), F32),
        ],
        compiler_params=pltpu.CompilerParams(vmem_limit_bytes=40 * 1024 * 1024),
        name="unpack_related",
    )(*pieces)
    return out, gain[0]


def swap(values, step):
    return lax.ppermute(values, "seq", [(k, k ^ step) for k in range(4)])


def unpack_feed_kernel(cut, shards, in_ref, down_ref, gate_ref, up_ref, out_ref):
    count = in_ref.shape[0]

    @pl.when(pl.program_id(0) == 0)
    def _():
        for k in range(count):
            if cut.skip(k) < cut.width:
                at = cut.start(k)
                out_ref[at + cut.skip(k) : at + cut.width, :] = down_ref[
                    k, cut.skip(k) : cut.width, :
                ].astype(F32)

    for n, target in enumerate((gate_ref, up_ref)):
        pieces = []
        for f in range(shards):
            for k in range(count):
                at = (n * shards + f) * cut.width
                if cut.skip(k) < cut.width:
                    piece = in_ref[k][:, at + cut.skip(k) : at + cut.width]
                    pieces.append(piece.astype(F32))
        target[...] = join(pieces)


def unpack_feed(gathered, down, cut, shards):
    count, rows, whole = gathered.shape
    block = rows // 4 if rows % 64 == 0 else rows
    wide, width = shards * cut.rows, down.shape[2]
    return pl.pallas_call(
        functools.partial(unpack_feed_kernel, cut, shards),
        grid=(rows // block,),
        in_specs=[
            pl.BlockSpec((count, block, whole), lambda i: (0, i, 0)),
            pl.BlockSpec(down.shape, lambda i: (0, 0, 0)),
        ],
        out_specs=[
            pl.BlockSpec((block, wide), lambda i: (i, 0)),
            pl.BlockSpec((block, wide), lambda i: (i, 0)),
            pl.BlockSpec((cut.rows, width), lambda i: (0, 0)),
        ],
        out_shape=[
            jax.ShapeDtypeStruct((rows, wide), F32),
            jax.ShapeDtypeStruct((rows, wide), F32),
            jax.ShapeDtypeStruct((cut.rows, width), F32),
        ],
        compiler_params=pltpu.CompilerParams(vmem_limit_bytes=40 * 1024 * 1024),
        cost_estimate=pl.CostEstimate(flops=0, bytes_accessed=gathered.size * 4, transcendentals=0),
        name="unpack_feed",
    )(gathered, down)


def unpack_merged_kernel(cut, in_ref, query_ref, key_ref, out_ref):
    tile, lane, count = 16, 128, in_ref.shape[0]
    wide = query_ref.shape[1] // count
    for k in range(count):
        query_ref[:, head_lanes(k, wide)] = in_ref[k, :, :wide].astype(F32)
        key_ref[:, head_lanes(k, wide)] = in_ref[k, :, wide : 2 * wide].astype(F32)
        for r in range(cut.skip(k) // tile, cut.width // tile):
            at = cut.start(k) + r * tile
            lanes = slice(2 * wide + r * lane, 2 * wide + (r + 1) * lane)
            for c in range(out_ref.shape[1] // lane):
                out_ref[at : at + tile, head_lanes(c, lane)] = in_ref[
                    k, c * tile : (c + 1) * tile, lanes
                ].astype(F32)


def unpack_merged(gathered, wide, cut, width):
    count, rows, _ = gathered.shape
    return pl.pallas_call(
        functools.partial(unpack_merged_kernel, cut),
        out_shape=(
            jax.ShapeDtypeStruct((rows, count * wide), F32),
            jax.ShapeDtypeStruct((rows, count * wide), F32),
            jax.ShapeDtypeStruct((cut.rows, width), F32),
        ),
        compiler_params=pltpu.CompilerParams(vmem_limit_bytes=40 * 1024 * 1024),
        cost_estimate=pl.CostEstimate(flops=0, bytes_accessed=gathered.size * 4, transcendentals=0),
        name="unpack_merged",
    )(gathered)


def after(values, *others, all_of=False):
    held = lax.optimization_barrier((values,) + others)
    return held if all_of else held[0]


class Cut:
    def __init__(self, rows, count):
        self.rows, self.count = rows, count
        self.width = -(-rows // (count * 16)) * 16

    def start(self, piece):
        if isinstance(piece, int):
            return min(piece * self.width, self.rows - self.width)
        return jnp.minimum(piece * self.width, self.rows - self.width)

    def skip(self, piece):
        if isinstance(piece, int):
            return min(piece * self.width - self.start(piece), self.width)
        return jnp.minimum(piece * self.width - self.start(piece), self.width)

    def assemble(self, pieces, axis):
        kept = []
        for k, piece in enumerate(pieces):
            if self.skip(k) < self.width:
                kept.append(lax.slice_in_dim(piece, self.skip(k), self.width, axis=axis))
        return jnp.concatenate(kept, axis=axis)


def columns_of(weight, index, width, padded):
    piece = lax.dynamic_slice_in_dim(weight, index * width, width, axis=1)
    return jnp.pad(piece, ((0, 0), (0, padded - width)))


def on_device(
    layer_input,
    mixer_gain,
    query_weight,
    key_weight,
    value_weight,
    swish_weight,
    output_weight,
    channel_gain,
    gelu_weight,
    linear_weight,
    down_weight,
    output_cotangent,
):
    groups, local_length, width = layer_input.shape
    seq_count = lax.axis_size("seq")
    shards = lax.axis_size("fsdp")
    me = lax.axis_index("seq")
    per_device = HEADS // seq_count
    rows_count = groups * local_length
    square = seq_count == 4 and shards == 8 and rows_count % 32 == 0
    length = local_length * seq_count
    key_scale = KEY_HEAD ** (-0.5)
    qk = query_weight.shape[1] // seq_count
    vd = value_weight.shape[1] // seq_count
    vd_pad = -(-vd // 128) * 128
    hidden_units = gelu_weight.shape[1]
    own_rows = down_weight.shape[0]
    cut = Cut(own_rows, seq_count)
    ff = shards * cut.width

    def gather_rows(values):
        return lax.all_gather(values, "fsdp", axis=0, tiled=True)

    def scatter_rows(values):
        return lax.psum_scatter(values.astype(BF), "fsdp", scatter_dimension=0, tiled=True)

    def scatter_parity(values):
        groups = [list(range(parity, shards, 2)) for parity in range(2)]
        return lax.psum_scatter(
            values, "fsdp", scatter_dimension=0, tiled=True, axis_index_groups=groups
        )

    output_piece = lax.dynamic_slice_in_dim(output_weight, cut.start(me), cut.width, axis=0)
    attention_pieces = [
        columns_of(query_weight, me, qk, qk),
        columns_of(key_weight, me, qk, qk),
        columns_of(value_weight, me, vd, vd_pad),
        columns_of(swish_weight, me, vd, vd_pad),
    ]
    if square:
        tiles = output_piece.reshape(cut.width // 16, 16, width // 128, 128)
        attention_pieces.append(tiles.transpose(2, 1, 0, 3).reshape(width // 8, cut.width * 8))
    else:
        output_pieces = gather_rows(output_piece)
    attention_weight = gather_rows(jnp.concatenate(attention_pieces, axis=1))
    column = lax.broadcasted_iota(jnp.int32, (hidden_units, ff), 0)
    slot = lax.broadcasted_iota(jnp.int32, (hidden_units, ff), 1)
    chosen = (slot // cut.width) * own_rows + cut.start(me) + slot % cut.width
    selector = (column == chosen).astype(BF)
    gate_piece = product(gelu_weight, selector).astype(BF)
    up_piece = product(linear_weight, selector).astype(BF)
    feed_piece = jnp.concatenate([gate_piece, up_piece], axis=1)
    down_piece = lax.dynamic_slice_in_dim(down_weight, cut.start(me), cut.width, axis=0)
    gains = lax.all_gather(jnp.stack([mixer_gain, channel_gain]), "fsdp", axis=1, tiled=True)
    mixer_scale, channel_scale = gains[0].astype(F32), gains[1].astype(F32)

    local_input = layer_input.reshape(rows_count, width)
    upstream = output_cotangent.reshape(rows_count, width)

    upstream = after(upstream, gains)

    def whole(values, call):
        gathered = gather_seq(values, call)
        return gathered.reshape(length * groups, width)

    input_full = whole(local_input, 0)
    upstream_full = whole(after(upstream, input_full), 1)
    inputs = local_input.astype(F32)

    blocks = shards // seq_count
    mixed_low, mixed_turned = norm_and_turn(input_full, mixer_scale)
    head_ids = me * per_device + jnp.arange(per_device, dtype=jnp.int32)
    table, table_back = decay_tables(head_ids, length)
    cosine, sine = rotation_tables(length, KEY_HEAD // 2)
    feed_weight = gather_rows(after(feed_piece, upstream_full))

    offsets = (qk, 2 * qk, 2 * qk + vd_pad)
    attention_weight = after(
        attention_weight, mixed_low, mixed_turned, table, table_back, cosine, feed_piece
    )
    if square:
        query_low, key_low, value_low, swish_pre, retained, gated_low, output_full = (
            retention_exchange(
                mixed_low, attention_weight, cosine, sine, table, per_device, offsets, cut, 2
            )
        )
    else:
        query_low, key_low, value_low, swish_pre, retained, gated_low = retention_forward(
            mixed_low, attention_weight, cosine, sine, table, per_device, offsets
        )
        swapped = exchange_seq(
            output_pieces.reshape(seq_count, blocks, cut.width, width), 2
        )
        output_full = jnp.concatenate(
            [
                cut.assemble([swapped[piece, block] for piece in range(seq_count)], 0)
                for block in range(blocks)
            ],
            axis=0,
        )

    kept_rows = lax.broadcasted_iota(jnp.int32, down_piece.shape, 0) >= cut.skip(me)
    down_full = gather_rows(after(jnp.where(kept_rows, down_piece, jnp.zeros_like(down_piece)), gated_low))
    if square:
        middle, channel_own = project_and_norm(
            gated_low, output_full, local_input, channel_scale, 3
        )
        both_pre, hidden_low, down_term, channel_full = feed_forward_gather(
            channel_own, feed_weight, upstream_full, 4
        )
        down_share = scatter_rows(down_term)
        middle_grad, channel_term, branch_own, feed_term = feed_back_scatter(
            after(upstream_full, down_term), both_pre, feed_weight, down_full, channel_full,
            middle, upstream, channel_scale, 6,
        )
        feed_share = scatter_parity(feed_term)
        branch_full = whole(branch_own, 7)
    else:
        middle = inputs + scatter_seq(product(gated_low, output_full).astype(BF), 3)
        channel_full = whole(normalize(middle, channel_scale).astype(BF), 4)
        gate_pre, up_pre, hidden_low = feed_forward(channel_full, feed_weight)
        down_share = scatter_rows(transposed_times(hidden_low, upstream_full).astype(BF))
        feed_low_grad, channel_part, hidden_part = feed_backward(
            upstream_full, gate_pre, up_pre, hidden_low, feed_weight, down_full
        )
        feed_share = scatter_rows(transposed_times(channel_full, feed_low_grad).astype(BF))
        middle_local, channel_terms = norm_back(
            middle, scatter_seq(channel_part, 6), channel_scale
        )
        channel_term = jnp.sum(channel_terms, axis=0)
        middle_grad = upstream.astype(F32) + middle_local
        branch_full = whole(middle_grad.astype(BF), 7)

    at_value, at_swish = 2 * qk, 2 * qk + vd_pad
    if square:
        swish_grad, retained_grad, swish_term, output_send, layer_output = gate_backward_scatter(
            after(branch_full, down_share), output_full, swish_pre, retained,
            channel_term, hidden_low, down_full, mixed_turned, gated_low, middle,
            per_device, vd_pad, cut, 5,
        )
        swish_share = scatter_parity(swish_term)
        key_grad, value_grad, merged_term, down_all = retention_backward_exchange(
            query_low, key_low, value_low, after(retained_grad, feed_share), table_back, cosine, sine,
            mixed_turned, output_send, down_share, per_device, vd_pad, 8,
        )
        merged_share = scatter_parity(merged_term)
        input_gradient, value_term, feed_all = input_backward(
            key_grad, value_grad, swish_grad, attention_weight, local_input, middle_grad,
            mixed_turned, mixer_scale, feed_share, (at_value, at_swish), vd, 9,
        )
    else:
        swish_grad, retained_grad = gate_backward(
            branch_full, output_full, swish_pre, retained, per_device, vd_pad
        )
        spare = lax.broadcasted_iota(jnp.int32, (width, vd_pad), 1) == vd
        swish_term = transposed_times(mixed_low, swish_grad)
        swish_term = jnp.where(spare, channel_term[:, None], swish_term).astype(BF)
        swish_share = scatter_rows(swish_term)
        layer_output = middle + scatter_seq(hidden_part, 5)
        key_grad, value_grad = retention_backward(
            query_low, key_low, value_low, retained_grad, table_back, cosine, sine, per_device, vd_pad
        )
        key_term = transposed_times(mixed_low, key_grad).astype(BF)
        key_share = scatter_rows(key_term)
        mixed_part = (
            times_transposed(key_grad, attention_weight[:, :at_value])
            + times_transposed(value_grad, attention_weight[:, at_value:at_swish])
            + times_transposed(swish_grad, attention_weight[:, at_swish:])
        )
        input_local, mixer_terms = norm_back(
            inputs, scatter_seq(mixed_part.astype(BF), 9), mixer_scale
        )
        mixer_term = jnp.sum(mixer_terms, axis=0)
        input_gradient = middle_grad + input_local
        output_term = transposed_times(gated_low, branch_full).astype(BF)
        output_term = output_term.reshape(blocks, own_rows, width)
        output_send = jnp.stack(
            [
                lax.slice_in_dim(output_term, cut.start(k), cut.start(k) + cut.width, axis=1)
                for k in range(seq_count)
            ]
        )
        output_swapped = exchange_seq(output_send, 8)
        output_share = scatter_rows(output_swapped.reshape(shards * cut.width, width))
        value_term = transposed_times(mixed_low, value_grad)
        value_term = jnp.where(spare, mixer_term[:, None], value_term).astype(BF)
    input_gradient = input_gradient.astype(BF).reshape(groups, local_length, width)
    value_share = scatter_rows(value_term)

    layer_output = layer_output.astype(BF).reshape(groups, local_length, width)
    if square:
        swish_all, merged_all = gather_two(
            after(swish_share, layer_output, input_gradient), merged_share, 13
        )
        value_share = after(value_share, swish_all)
        half = value_share.shape[0] // 2
        across, along = swap(value_share, 1), swap(value_share, 2)
        gelu_gradient, linear_gradient, down_gradient = unpack_feed(
            after(feed_all, swish_all), down_all, cut, shards
        )
        swish_gradient, channel_own_gradient = unpack_columns(swish_all, vd)
        across, along, gelu_gradient, swish_gradient = after(
            across, along, gelu_gradient, swish_gradient, all_of=True
        )
        corner_low, corner_high = swap(across[:half], 2), swap(along[half:], 1)
        query_gradient, key_gradient, output_gradient = unpack_merged(merged_all, qk, cut, width)
        corner_low, corner_high, query_gradient = after(
            corner_low, corner_high, query_gradient, all_of=True
        )
        corner = jnp.concatenate([corner_low, corner_high], axis=0)
        value_gradient, mixer_own_gradient = unpack_related(
            (value_share, across, along, corner), vd
        )
    else:
        down_all = gather_seq(down_share, 10)
        feed_all = gather_seq(after(feed_share, down_all), 11)
        swish_all = gather_seq(after(swish_share, feed_all), 13)
        output_all = gather_seq(after(output_share, swish_all), 12)
        key_all = gather_seq(after(key_share, output_all), 15)
        value_all = gather_seq(after(value_share, key_all), 14)
        swish_gradient, channel_own_gradient = unpack_columns(swish_all, vd)
        output_gradient = cut.assemble([output_all[k] for k in range(seq_count)], 0).astype(F32)
        gelu_gradient, linear_gradient, down_gradient = unpack_feed(
            feed_all, down_all, cut, shards
        )
        query_gradient, key_gradient = (
            jnp.concatenate(
                [key_all[k][:, at : at + qk] for k in range(seq_count)], axis=1
            ).astype(F32)
            for at in (0, qk)
        )
        value_gradient, mixer_own_gradient = unpack_columns(value_all, vd)
    return (
        layer_output,
        input_gradient,
        mixer_own_gradient,
        query_gradient,
        key_gradient,
        value_gradient,
        swish_gradient,
        output_gradient,
        channel_own_gradient,
        gelu_gradient,
        linear_gradient,
        down_gradient,
    )


def solution(mesh):
    tokens, rows, vector = P("fsdp", "seq", None), P("fsdp", None), P("fsdp")
    return jax.shard_map(
        on_device,
        mesh=mesh,
        in_specs=(
            tokens, vector, rows, rows, rows, rows, rows, vector, rows, rows, rows, tokens,
        ),
        out_specs=(
            tokens, tokens, vector, rows, rows, rows, rows, rows, vector, rows, rows, rows,
        ),
        check_vma=False,
    )
```

```python
import functools
import math

import jax
import jax.numpy as jnp
from jax import lax
from jax.experimental import pallas as pl
from jax.experimental.pallas import tpu as pltpu
from jax.sharding import PartitionSpec as P

HEADS = 8
KEY_HEAD = 256
VAL_HEAD = 432
EPSILON = 1e-05
MESH = pl.DeviceIdType.MESH
BF = jnp.bfloat16
F32 = jnp.float32
IN_VMEM = pl.BlockSpec(memory_space=pltpu.VMEM)
ANYWHERE = pl.BlockSpec(memory_space=pl.ANY)


def product(left, right):
    return jnp.dot(left, right, preferred_element_type=F32)


def times_transposed(left, right):
    return lax.dot_general(left, right, (((1,), (1,)), ((), ())), preferred_element_type=F32)


def transposed_times(left, right):
    return lax.dot_general(left, right, (((0,), (0,)), ((), ())), preferred_element_type=F32)


def normalize(values, gain):
    centered = values - jnp.mean(values, axis=-1, keepdims=True)
    spread = lax.rsqrt(jnp.mean(centered * centered, axis=-1, keepdims=True) + EPSILON)
    return centered * spread * gain


def rotation_tables(length, half_width):
    rates = jnp.exp(-math.log(10000.0) * jnp.arange(half_width, dtype=F32) / (half_width - 1))
    turned = jnp.arange(length, dtype=F32)[:, None] * rates[None, :]
    return (jnp.cos(turned), jnp.sin(turned))


def pad_lanes(pieces, width):
    have = sum(piece.shape[1] for piece in pieces)
    if have < width:
        pieces = pieces + [jnp.zeros((pieces[0].shape[0], width - have), pieces[0].dtype)]
    return jnp.concatenate(pieces, axis=1) if len(pieces) > 1 else pieces[0]


def rotate_pair(values, cosine, sine, back=False):
    half = KEY_HEAD // 2
    first, second = values[:, :half], values[:, half:]
    if back:
        return jnp.concatenate([first * cosine + second * sine, second * cosine - first * sine], 1)
    return jnp.concatenate([first * cosine - second * sine, second * cosine + first * sine], 1)


BLOCK = 256


def decay_tables(head_ids, length):
    rates = jnp.log1p(-jnp.exp2(-5.0 - head_ids.astype(F32)))[:, None, None]
    short = jnp.arange(BLOCK, dtype=jnp.int32)
    long = jnp.arange(2 * length - BLOCK, dtype=jnp.int32)

    def decay(gap):
        far = jnp.exp(jnp.maximum(gap, 0).astype(F32)[None] * rates)
        return jnp.where(gap[None] >= 0, far, 0.0)

    by_row = decay(length - BLOCK + short[:, None] - long[None, :])
    by_column = decay(long[:, None] - (length - BLOCK) - short[None, :])
    return by_row, by_column


def norm_parts(values):
    centered = values - jnp.mean(values, axis=-1, keepdims=True)
    variance = jnp.mean(centered * centered, axis=-1, keepdims=True)
    factor = lax.rsqrt(jnp.maximum(variance, 1.0))
    return centered * factor, factor, variance > 1.0


def rows_of(block):
    return pl.ds(pl.multiple_of(block * BLOCK, BLOCK), BLOCK)


def head_lanes(head, width):
    return slice(head * width, (head + 1) * width)


class Moves:
    def __init__(self, sems):
        self.sems, self.used, self.open = sems, 0, []

    def start(self, source, target):
        copy = pltpu.make_async_copy(source, target, self.sems.at[self.used])
        self.used += 1
        copy.start()
        return copy

    def store(self, source, target):
        self.open.append(self.start(source, target))

    def close(self):
        for copy in self.open:
            copy.wait()


def norm_kernel(x_ref, gain_ref, out_ref, turned_ref):
    normed = normalize(x_ref[...].astype(F32), gain_ref[...])
    out_ref[...] = normed.astype(BF)
    turned_ref[...] = normed.T.astype(BF)


def norm_and_turn(x, gain):
    length, width = x.shape
    return pl.pallas_call(
        norm_kernel,
        grid=(length // BLOCK,),
        in_specs=[
            pl.BlockSpec((BLOCK, width), lambda i: (i, 0)),
            pl.BlockSpec((1, width), lambda i: (0, 0)),
        ],
        out_specs=[
            pl.BlockSpec((BLOCK, width), lambda i: (i, 0)),
            pl.BlockSpec((width, BLOCK), lambda i: (0, i)),
        ],
        out_shape=[
            jax.ShapeDtypeStruct((length, width), BF),
            jax.ShapeDtypeStruct((width, length), BF),
        ],
        compiler_params=pltpu.CompilerParams(vmem_limit_bytes=32 * 1024 * 1024),
        name="norm_and_turn",
    )(x, gain[None, :])


class Series:
    def __init__(self, moves, count, ends):
        self.sems, self.first, self.count, self.ends = moves.sems, moves.used, count, ends
        moves.used += count

    def copy(self, i):
        return pltpu.make_async_copy(*self.ends(i), self.sems.at[self.first + i])

    def start_all(self):
        for i in range(self.count):
            self.copy(i).start()
        return self

    def wait_all(self):
        for i in range(self.count):
            self.copy(i).wait()


def by_block(moves, count, source, target, rows=BLOCK):
    def ends(i):
        here = pl.ds(i * rows if isinstance(i, int) else pl.multiple_of(i * rows, rows), rows)
        if len(source.shape) == 3:
            return source.at[:, here], target.at[:, here]
        return source.at[here], target.at[here]

    return Series(moves, count, ends)


def retention_kernel(
    heads, offsets, mixed_any, w_any, cos_ref, sin_ref, table_ref,
    q_any, k_any, v_any, swish_any, retained_any, gated_any,
    mixed_ref, w_ref, q_ref, k_ref, v_ref, swish_ref, retained_ref, gated_ref, sems,
    between=None,
):
    at_key, at_value, at_swish = offsets
    length = mixed_ref.shape[0]
    blocks = length // BLOCK
    moves = sems if isinstance(sems, Moves) else Moves(sems)
    spans = (
        slice(0, at_key), slice(at_key, at_value), slice(at_value, at_swish),
        slice(at_swish, w_ref.shape[1]),
    )
    loads = by_block(moves, blocks, mixed_any, mixed_ref)
    loads.copy(0).start()
    weights = [moves.start(w_any.at[:, span], w_ref.at[:, span]) for span in spans]
    for i in range(1, blocks):
        loads.copy(i).start()
    stores = [
        by_block(moves, blocks, source, target)
        for source, target in (
            (q_ref, q_any), (k_ref, k_any), (v_ref, v_any), (swish_ref, swish_any),
            (retained_ref, retained_any), (gated_ref, gated_any),
        )
    ]
    k_ref[...] = jnp.zeros_like(k_ref)
    v_ref[...] = jnp.zeros_like(v_ref)
    if between is not None:
        between(-1)

    @pl.loop(0, blocks)
    def _(i):
        rows = rows_of(i)
        loads.copy(i).wait()
        mixed = mixed_ref[rows, :]
        cosine, sine = cos_ref[rows, :], sin_ref[rows, :]

        def projected(n):
            @pl.when(i == 0)
            def _():
                weights[n].wait()

            return product(mixed, w_ref[:, spans[n]])

        for n, (target, scale) in enumerate(((q_ref, 1.0), (k_ref, KEY_HEAD**-0.5))):
            pre = projected(n)
            for h in range(heads):
                lanes = head_lanes(h, KEY_HEAD)
                turned = rotate_pair(pre[:, lanes], cosine, sine)
                target[rows, lanes] = (turned * scale if n else turned).astype(BF)
        value = projected(2)
        for h in range(heads):
            v_ref[h, rows, :] = value[:, head_lanes(h, VAL_HEAD)].astype(BF)
        swish_ref[rows, :] = projected(3)[:, : heads * VAL_HEAD]
        gated = []
        for h in range(heads):
            lanes = head_lanes(h, KEY_HEAD)
            scores = times_transposed(q_ref[rows, lanes], k_ref[:, lanes])
            decay = table_ref[
                h, :, pl.ds(pl.multiple_of((blocks - 1 - i) * BLOCK, BLOCK), length)
            ]
            retained = product((scores * decay).astype(BF), v_ref[h]).astype(BF)
            retained_ref[h, rows, :] = retained
            unit, _, _ = norm_parts(retained.astype(F32))
            s = swish_ref[rows, head_lanes(h, VAL_HEAD)]
            gated.append((s * jax.nn.sigmoid(s) * unit).astype(BF))
        gated_ref[rows, :] = jnp.concatenate(gated, axis=1) if heads > 1 else gated[0]
        for store in stores:
            store.copy(i).start()
        if between is not None:
            between(i)

    for store in stores:
        store.wait_all()


def retention_outputs(length, heads):
    qk, vd = heads * KEY_HEAD, heads * VAL_HEAD
    return (
        ((length, qk), BF),
        ((length, qk), BF),
        ((heads, length, VAL_HEAD), BF),
        ((length, vd), F32),
        ((heads, length, VAL_HEAD), BF),
        ((length, vd), BF),
    )


def retention_forward(mixed, weight, cosine, sine, table, heads, offsets):
    length, width = mixed.shape
    outputs = retention_outputs(length, heads)
    blocks = length // BLOCK
    return pl.pallas_call(
        functools.partial(retention_kernel, heads, offsets),
        out_shape=tuple(jax.ShapeDtypeStruct(*out) for out in outputs),
        in_specs=[ANYWHERE, ANYWHERE, IN_VMEM, IN_VMEM, IN_VMEM],
        out_specs=(ANYWHERE,) * 6,
        scratch_shapes=[pltpu.VMEM(mixed.shape, BF), pltpu.VMEM(weight.shape, BF)]
        + [pltpu.VMEM(*out) for out in outputs]
        + [pltpu.SemaphoreType.DMA((4 + 7 * blocks,))],
        compiler_params=pltpu.CompilerParams(vmem_limit_bytes=60 * 1024 * 1024),
        cost_estimate=pl.CostEstimate(
            flops=30_000_000_000, bytes_accessed=0, transcendentals=0
        ),
        name="retention",
    )(mixed, weight, cosine, sine, table)


def gate_back_rows(heads, rows, branch, w_ref, swish_ref, retained_ref, dswish_ref, dret_ref):
    gated_grad = times_transposed(branch, w_ref[...])
    swish_parts = []
    for h in range(heads):
        lanes = head_lanes(h, VAL_HEAD)
        grad, s = gated_grad[:, lanes], swish_ref[rows, lanes]
        gate = jax.nn.sigmoid(s)
        unit, factor, above = norm_parts(retained_ref[h, rows, :].astype(F32))
        swish_parts.append((grad * unit * (gate * (1.0 + s * (1.0 - gate)))).astype(BF))
        g = grad * (s * gate)
        along = jnp.where(above, jnp.mean(g * unit, axis=-1, keepdims=True), 0.0)
        back = factor * (g - jnp.mean(g, axis=-1, keepdims=True) - unit * along)
        dret_ref[h, rows, :] = back.astype(BF)
    dswish_ref[rows, :] = pad_lanes(swish_parts, dswish_ref.shape[1])


def gate_back_kernel(heads, branch_ref, w_ref, swish_ref, retained_ref, dswish_ref, dret_ref):
    @pl.loop(0, branch_ref.shape[0] // BLOCK)
    def _(i):
        rows = rows_of(i)
        gate_back_rows(
            heads, rows, branch_ref[rows, :], w_ref, swish_ref, retained_ref, dswish_ref, dret_ref
        )


def gate_backward(branch, weight, swish, retained, heads, padded):
    length = branch.shape[0]
    return pl.pallas_call(
        functools.partial(gate_back_kernel, heads),
        out_shape=(
            jax.ShapeDtypeStruct((length, padded), BF),
            jax.ShapeDtypeStruct((heads, length, VAL_HEAD), BF),
        ),
        compiler_params=pltpu.CompilerParams(vmem_limit_bytes=48 * 1024 * 1024),
        name="gate_back",
    )(branch, weight, swish, retained)


def retention_back_head(
    h, heads, q_ref, k_ref, v_ref, dret_ref, table_ref, cos_ref, sin_ref, dqk_ref, dv_head,
    dq_sum,
):
    length = q_ref.shape[0]
    blocks = length // BLOCK
    lanes = head_lanes(h, KEY_HEAD)
    dq_sum[...] = jnp.zeros_like(dq_sum)

    @pl.loop(0, blocks)
    def _(j):
        there = rows_of(j)
        query, grad = q_ref[:, lanes], dret_ref[h]
        key, value = k_ref[there, lanes], v_ref[h, there, :]
        decay = table_ref[h, pl.ds(pl.multiple_of((blocks - 1 - j) * BLOCK, BLOCK), length), :]
        weights = (times_transposed(query, key) * decay).astype(BF)
        score = (times_transposed(grad, value) * decay).astype(BF)
        dq_sum[...] += product(score, key)
        dk = transposed_times(score, query).astype(BF).astype(F32)
        dk = rotate_pair(dk, cos_ref[there, :], sin_ref[there, :], back=True)
        dqk_ref[there, head_lanes(heads + h, KEY_HEAD)] = (dk * (KEY_HEAD**-0.5)).astype(BF)
        dv_head[there, :] = transposed_times(weights, grad).astype(BF)

    @pl.loop(0, blocks)
    def _(i):
        rows = rows_of(i)
        dq = dq_sum[rows, :].astype(BF).astype(F32)
        dqk_ref[rows, lanes] = rotate_pair(
            dq, cos_ref[rows, :], sin_ref[rows, :], back=True
        ).astype(BF)


def retention_back_kernel(
    heads, q_ref, k_ref, v_ref, dret_ref, table_ref, cos_ref, sin_ref, dqk_ref, dv_ref,
    dv_heads, dq_sum,
):
    for h in range(heads):
        retention_back_head(
            h, heads, q_ref, k_ref, v_ref, dret_ref, table_ref, cos_ref, sin_ref, dqk_ref,
            dv_heads.at[h], dq_sum,
        )
    dv_ref[...] = pad_lanes([dv_heads[h] for h in range(heads)], dv_ref.shape[1])


def retention_backward(q, k, v, dret, table, cosine, sine, heads, padded):
    length = q.shape[0]
    qk = heads * KEY_HEAD
    return pl.pallas_call(
        functools.partial(retention_back_kernel, heads),
        out_shape=(
            jax.ShapeDtypeStruct((length, 2 * qk), BF),
            jax.ShapeDtypeStruct((length, padded), BF),
        ),
        scratch_shapes=[
            pltpu.VMEM((heads, length, VAL_HEAD), BF),
            pltpu.VMEM((length, KEY_HEAD), F32),
        ],
        compiler_params=pltpu.CompilerParams(vmem_limit_bytes=48 * 1024 * 1024),
        name="retention_back",
    )(q, k, v, dret, table, cosine, sine)


def transfer_cost(elements):
    return pl.CostEstimate(flops=0, bytes_accessed=elements * 240, transcendentals=0)


def greet(peers):
    barrier = pltpu.get_barrier_semaphore()
    for peer in peers:
        pl.semaphore_signal(barrier, inc=1, device_id={"seq": peer}, device_id_type=MESH)
    pl.semaphore_wait(barrier, len(peers))


def remote(source, target, sends, recvs, k, to):
    return pltpu.make_async_remote_copy(
        src_ref=source,
        dst_ref=target,
        send_sem=sends.at[k],
        recv_sem=recvs.at[k],
        device_id={"seq": to},
        device_id_type=MESH,
    )


def gather_square_kernel(x_ref, o_ref, sends, recvs, local):
    me = lax.axis_index("seq")
    across, along = me ^ 1, me ^ 2
    half = x_ref.shape[0] // 2
    greet((across, along))
    own = pltpu.make_async_copy(x_ref, o_ref.at[me], local)
    own.start()

    def part(ref, i):
        return ref.at[pl.ds(i * half, half)]

    first = (
        remote(part(x_ref, 0), part(o_ref.at[me], 0), sends, recvs, 0, across),
        remote(part(x_ref, 1), part(o_ref.at[me], 1), sends, recvs, 1, along),
        remote(part(x_ref, 1), part(o_ref.at[me], 1), sends, recvs, 2, across),
        remote(part(x_ref, 0), part(o_ref.at[me], 0), sends, recvs, 3, along),
    )
    for copy in first:
        copy.start()
    first[0].wait_recv()
    on_along = remote(part(o_ref.at[across], 0), part(o_ref.at[across], 0), sends, recvs, 4, along)
    on_along.start()
    first[1].wait_recv()
    on_across = remote(part(o_ref.at[along], 1), part(o_ref.at[along], 1), sends, recvs, 5, across)
    on_across.start()
    first[2].wait_recv()
    first[3].wait_recv()
    on_along.wait_recv()
    on_across.wait_recv()
    for copy in first + (on_along, on_across):
        copy.wait_send()
    own.wait()


def gather_kernel(count, x_ref, o_ref, sends, recvs, local):
    me = lax.axis_index("seq")
    peers = [lax.rem(me + step, count) for step in range(1, count)]
    greet(peers)
    own = pltpu.make_async_copy(x_ref, o_ref.at[me], local)
    own.start()
    copies = [remote(x_ref, o_ref.at[me], sends, recvs, k, to) for k, to in enumerate(peers)]
    for copy in copies:
        copy.start()
    for copy in copies:
        copy.wait()
    own.wait()


def gather_seq(values, call):
    count = lax.axis_size("seq")
    square = count == 4 and values.shape[0] % 32 == 0
    body = gather_square_kernel if square else functools.partial(gather_kernel, count)
    copies = 6 if square else count - 1
    return pl.pallas_call(
        body,
        out_shape=jax.ShapeDtypeStruct((count,) + values.shape, values.dtype),
        in_specs=[pl.BlockSpec(memory_space=pl.ANY)],
        out_specs=pl.BlockSpec(memory_space=pl.ANY),
        scratch_shapes=[
            pltpu.SemaphoreType.DMA((copies,)),
            pltpu.SemaphoreType.DMA((copies,)),
            pltpu.SemaphoreType.DMA,
        ],
        compiler_params=pltpu.CompilerParams(collective_id=call, has_side_effects=True),
        cost_estimate=transfer_cost(values.size),
        name=f"gather_seq_{call}",
    )(values)


def gather_two_kernel(a_ref, b_ref, a_out, b_out, sends, recvs, locals_):
    me = lax.axis_index("seq")
    greet((me ^ 1, me ^ 2))
    moves = Moves(locals_)
    moves.store(a_ref, a_out.at[me])
    moves.store(b_ref, b_out.at[me])
    both = [
        square_pass(ref, out, sends, recvs, first, half_rows(ref.shape[0]))
        for ref, out, first in ((a_ref, a_out, 0), (b_ref, b_out, 6))
    ]
    for copies in both:
        for copy in copies[:4]:
            copy.start()
    for copies in both:
        pass_on(copies)
    for copies in both:
        for copy in copies[2:]:
            copy.wait_recv()
    moves.close()
    for copies in both:
        for copy in copies:
            copy.wait_send()


def gather_two(a, b, call):
    return comm_call(
        gather_two_kernel,
        [(a, False), (b, False)],
        [((4,) + a.shape, BF, False), ((4,) + b.shape, BF, False)],
        [],
        12,
        2,
        call,
        a.size + b.size,
        "gather_two",
    )


def exchange_kernel(count, x_ref, o_ref, sends, recvs, local):
    me = lax.axis_index("seq")
    peers = [lax.rem(me + step, count) for step in range(1, count)]
    greet(peers)
    own = pltpu.make_async_copy(x_ref.at[me], o_ref.at[me], local)
    own.start()
    copies = [remote(x_ref.at[to], o_ref.at[me], sends, recvs, k, to) for k, to in enumerate(peers)]
    for copy in copies:
        copy.start()
    for copy in copies:
        copy.wait()
    own.wait()


def exchange_seq(values, call):
    count = lax.axis_size("seq")
    return pl.pallas_call(
        functools.partial(exchange_kernel, count),
        out_shape=jax.ShapeDtypeStruct(values.shape, values.dtype),
        in_specs=[pl.BlockSpec(memory_space=pl.ANY)],
        out_specs=pl.BlockSpec(memory_space=pl.ANY),
        scratch_shapes=[
            pltpu.SemaphoreType.DMA((count - 1,)),
            pltpu.SemaphoreType.DMA((count - 1,)),
            pltpu.SemaphoreType.DMA,
        ],
        compiler_params=pltpu.CompilerParams(collective_id=call, has_side_effects=True),
        cost_estimate=transfer_cost(values.size),
        name=f"exchange_seq_{call}",
    )(values)


def scatter_square_kernel(p_ref, o_ref, inbox_x, inbox_y, via_x, via_y, out_x, out_y, sends, recvs):
    me = lax.axis_index("seq")
    across, along, corner = me ^ 1, me ^ 2, me ^ 3
    half = p_ref.shape[1] // 2
    low, high = pl.ds(0, half), pl.ds(half, half)
    greet((across, along))
    first = (
        remote(p_ref.at[corner, low], via_x, sends, recvs, 0, across),
        remote(p_ref.at[corner, high], via_y, sends, recvs, 1, along),
        remote(p_ref.at[across, low], inbox_x.at[low], sends, recvs, 2, across),
        remote(p_ref.at[along, high], inbox_y.at[high], sends, recvs, 3, along),
    )
    for copy in first:
        copy.start()
    first[0].wait_recv()
    out_y[...] = (p_ref[along, :half].astype(F32) + via_x[...].astype(F32)).astype(BF)
    to_along = remote(out_y, inbox_y.at[low], sends, recvs, 4, along)
    to_along.start()
    first[1].wait_recv()
    out_x[...] = (p_ref[across, half:].astype(F32) + via_y[...].astype(F32)).astype(BF)
    to_across = remote(out_x, inbox_x.at[high], sends, recvs, 5, across)
    to_across.start()
    first[2].wait_recv()
    first[3].wait_recv()
    to_along.wait_recv()
    to_across.wait_recv()
    o_ref[...] = (
        p_ref[me].astype(F32) + inbox_x[...].astype(F32) + inbox_y[...].astype(F32)
    )
    for copy in first + (to_along, to_across):
        copy.wait_send()


def scatter_kernel(count, p_ref, o_ref, inbox, sends, recvs):
    me = lax.axis_index("seq")
    peers = [lax.rem(me + step, count) for step in range(1, count)]
    greet(peers)
    copies = [remote(p_ref.at[to], inbox.at[k], sends, recvs, k, to) for k, to in enumerate(peers)]
    for copy in copies:
        copy.start()
    total = p_ref[me].astype(F32)
    for k, copy in enumerate(copies):
        copy.wait_recv()
        total = total + inbox[k].astype(F32)
    o_ref[...] = total
    for copy in copies:
        copy.wait_send()


def scatter_seq(parts, call):
    count = lax.axis_size("seq")
    rows, width = parts.shape[0] // count, parts.shape[1]
    parts = parts.reshape(count, rows, width)
    if count == 4 and rows % 32 == 0:
        body = scatter_square_kernel
        scratch = [pltpu.VMEM((rows, width), BF)] * 2 + [pltpu.VMEM((rows // 2, width), BF)] * 4
        copies = 6
    else:
        body = functools.partial(scatter_kernel, count)
        scratch = [pltpu.VMEM((count - 1, rows, width), BF)]
        copies = count - 1
    return pl.pallas_call(
        body,
        out_shape=jax.ShapeDtypeStruct((rows, width), F32),
        in_specs=[pl.BlockSpec(memory_space=pltpu.VMEM)],
        out_specs=pl.BlockSpec(memory_space=pltpu.VMEM),
        scratch_shapes=scratch
        + [pltpu.SemaphoreType.DMA((copies,)), pltpu.SemaphoreType.DMA((copies,))],
        compiler_params=pltpu.CompilerParams(
            collective_id=call, has_side_effects=True, vmem_limit_bytes=32 * 1024 * 1024
        ),
        cost_estimate=transfer_cost(rows * width),
        name=f"scatter_seq_{call}",
    )(parts)


def feed_forward_kernel(ff, x_ref, w_ref, gate_ref, up_ref, hidden_ref):
    both = product(x_ref[...], w_ref[...])
    gate, up = both[:, :ff], both[:, ff:]
    gate_ref[...] = gate
    up_ref[...] = up
    hidden_ref[...] = (gate * (0.5 + 0.5 * lax.erf(gate * math.sqrt(0.5))) * up).astype(BF)


def feed_back_kernel(
    ff, c_ref, gate_ref, up_ref, hidden_ref, w_ref, down_ref, both_ref, part_ref, out_ref
):
    gate, up = gate_ref[...], up_ref[...]
    out_ref[...] = product(hidden_ref[...], down_ref[...]).astype(BF)
    hidden_grad = times_transposed(c_ref[...], down_ref[...])
    bell = 0.5 + 0.5 * lax.erf(gate * math.sqrt(0.5))
    slope = bell + gate * (math.sqrt(0.5 / math.pi) * jnp.exp(-0.5 * gate * gate))
    both = jnp.concatenate([hidden_grad * up * slope, hidden_grad * (gate * bell)], axis=1)
    both = both.astype(BF)
    both_ref[...] = both
    part_ref[...] = times_transposed(both, w_ref[...]).astype(BF)


def by_rows(block, width):
    return pl.BlockSpec((block, width), lambda i: (i, 0))


def kept(shape):
    return pl.BlockSpec(shape, lambda i: (0, 0), pipeline_mode=pl.Buffered(1))


FEED_BLOCK = 256


def feed_forward(x, weight):
    length, width = x.shape
    ff = weight.shape[1] // 2
    return pl.pallas_call(
        functools.partial(feed_forward_kernel, ff),
        grid=(length // FEED_BLOCK,),
        in_specs=[by_rows(FEED_BLOCK, width), kept(weight.shape)],
        out_specs=[by_rows(FEED_BLOCK, ff)] * 3,
        out_shape=(
            jax.ShapeDtypeStruct((length, ff), F32),
            jax.ShapeDtypeStruct((length, ff), F32),
            jax.ShapeDtypeStruct((length, ff), BF),
        ),
        compiler_params=pltpu.CompilerParams(vmem_limit_bytes=48 * 1024 * 1024),
        cost_estimate=pl.CostEstimate(
            flops=4 * length * width * ff, bytes_accessed=weight.size * 4, transcendentals=0
        ),
        name="feed_forward",
    )(x, weight)


def feed_backward(cotangent, gate, up, hidden, weight, down):
    length, width = cotangent.shape
    ff = weight.shape[1] // 2
    return pl.pallas_call(
        functools.partial(feed_back_kernel, ff),
        grid=(length // FEED_BLOCK,),
        in_specs=[by_rows(FEED_BLOCK, width)]
        + [by_rows(FEED_BLOCK, ff)] * 3
        + [kept(weight.shape), kept(down.shape)],
        out_specs=[
            by_rows(FEED_BLOCK, 2 * ff),
            by_rows(FEED_BLOCK, width),
            by_rows(FEED_BLOCK, width),
        ],
        out_shape=(
            jax.ShapeDtypeStruct((length, 2 * ff), BF),
            jax.ShapeDtypeStruct((length, width), BF),
            jax.ShapeDtypeStruct((length, width), BF),
        ),
        compiler_params=pltpu.CompilerParams(vmem_limit_bytes=56 * 1024 * 1024),
        cost_estimate=pl.CostEstimate(
            flops=8 * length * width * ff, bytes_accessed=weight.size * 4, transcendentals=0
        ),
        name="feed_back",
    )(cotangent, gate, up, hidden, weight, down)


def square_parts(parts, boxes, sends, recvs, first):
    me = lax.axis_index("seq")
    across, along = me ^ 1, me ^ 2
    inbox_x, inbox_y, via_x, via_y, out_x, out_y = boxes
    half = via_x.shape[0]
    low, high = pl.ds(0, half), pl.ds(half, half)
    copies = [
        remote(parts.at[3, low], via_x, sends, recvs, first, across),
        remote(parts.at[3, high], via_y, sends, recvs, first + 1, along),
        remote(parts.at[1, low], inbox_x.at[low], sends, recvs, first + 2, across),
        remote(parts.at[2, high], inbox_y.at[high], sends, recvs, first + 3, along),
        remote(out_y, inbox_y.at[low], sends, recvs, first + 4, along),
        remote(out_x, inbox_x.at[high], sends, recvs, first + 5, across),
    ]

    def finish():
        forward_sums(copies, parts, boxes)
        for copy in copies[2:]:
            copy.wait_recv()

    def total(rows):
        return (
            parts[0, rows].astype(F32)
            + inbox_x[rows, :].astype(F32)
            + inbox_y[rows, :].astype(F32)
        )

    return copies, finish, total


def square_gather(own, out_ref, sends, recvs, first):
    me = lax.axis_index("seq")
    across, along = me ^ 1, me ^ 2
    half = own.shape[0] // 2

    def part(ref, i):
        return ref.at[pl.ds(i * half, half)]

    copies = [
        remote(part(own, 0), part(out_ref.at[me], 0), sends, recvs, first, across),
        remote(part(own, 1), part(out_ref.at[me], 1), sends, recvs, first + 1, along),
        remote(part(own, 1), part(out_ref.at[me], 1), sends, recvs, first + 2, across),
        remote(part(own, 0), part(out_ref.at[me], 0), sends, recvs, first + 3, along),
        remote(
            part(out_ref.at[across], 0), part(out_ref.at[across], 0), sends, recvs, first + 4, along
        ),
        remote(
            part(out_ref.at[along], 1), part(out_ref.at[along], 1), sends, recvs, first + 5, across
        ),
    ]

    def finish():
        copies[0].wait_recv()
        copies[4].start()
        copies[1].wait_recv()
        copies[5].start()
        for copy in copies[2:]:
            copy.wait_recv()

    return copies, finish


def block_rows(k, rows):
    return pl.ds(pl.multiple_of((lax.axis_index("seq") ^ k) * rows, rows), rows)


def forward_sums(copies, parts, boxes):
    inbox_x, inbox_y, via_x, via_y, out_x, out_y = boxes
    half = via_x.shape[0]
    copies[0].wait_recv()
    out_y[...] = (parts[2, :half].astype(F32) + via_x[...].astype(F32)).astype(BF)
    copies[4].start()
    copies[1].wait_recv()
    out_x[...] = (parts[1, half:].astype(F32) + via_y[...].astype(F32)).astype(BF)
    copies[5].start()


def send_parts(part, copies, then=None):
    @pl.loop(0, 4)
    def _(i):
        if then is not None:
            pl.when(i == 3)(then)
        part(jnp.where(i == 0, 3, jnp.where(i == 3, 0, i)))

        @pl.when(i == 0)
        def _():
            copies[0].start()
            copies[1].start()

        @pl.when(i == 1)
        def _():
            copies[2].start()

        @pl.when(i == 2)
        def _():
            copies[3].start()


def project_kernel(
    g_any, w_any, x_ref, gain_ref, middle_ref, own_ref,
    g_ref, w_ref, parts, inbox_x, inbox_y, via_x, via_y, out_x, out_y, sends, recvs, locals_,
):
    me = lax.axis_index("seq")
    rows = x_ref.shape[0]
    half = rows // 2
    moves = Moves(locals_)
    loads = [moves.start(w_any, w_ref), moves.start(g_any, g_ref)]
    greet((me ^ 1, me ^ 2))
    boxes = (inbox_x, inbox_y, via_x, via_y, out_x, out_y)
    copies, finish, total = square_parts(parts, boxes, sends, recvs, 0)

    def part(k):
        parts[k] = product(g_ref[block_rows(k, rows), :], w_ref[...]).astype(BF)

    for load in loads:
        load.wait()
    send_parts(part, copies)
    finish()

    @pl.loop(0, 2)
    def _(i):
        here = pl.ds(pl.multiple_of(i * half, half), half)
        middle = x_ref[here, :].astype(F32) + total(here)
        middle_ref[here, :] = middle
        own_ref[here, :] = normalize(middle, gain_ref[...]).astype(BF)

    for copy in copies:
        copy.wait_send()


def square_scratch(rows, width):
    return [
        pltpu.VMEM((4, rows, width), BF),
        pltpu.VMEM((rows, width), BF),
        pltpu.VMEM((rows, width), BF),
        pltpu.VMEM((rows // 2, width), BF),
        pltpu.VMEM((rows // 2, width), BF),
        pltpu.VMEM((rows // 2, width), BF),
        pltpu.VMEM((rows // 2, width), BF),
    ]


def square_call(body, out_shape, out_specs, scratch, inputs, call, cost, name):
    return pl.pallas_call(
        body,
        out_shape=out_shape,
        in_specs=[IN_VMEM] * len(inputs),
        out_specs=out_specs,
        scratch_shapes=scratch,
        compiler_params=pltpu.CompilerParams(
            collective_id=call, has_side_effects=True, vmem_limit_bytes=56 * 1024 * 1024
        ),
        cost_estimate=transfer_cost(cost),
        name=name,
    )(*inputs)


def core_sum(moves, make, send_ref, twin_ref, out_ref, targets, sends, recvs, first):
    shard = lax.axis_index("fsdp")
    core = lax.rem(shard, 2)
    count = out_ref.shape[0]

    def copy(t):
        return pltpu.make_async_remote_copy(
            src_ref=send_ref.at[t],
            dst_ref=twin_ref.at[t],
            send_sem=sends.at[first + t],
            recv_sem=recvs.at[first + t],
            device_id={"fsdp": shard ^ 1},
            device_id_type=MESH,
        )

    stores = Series(moves, count, lambda t: (out_ref.at[t], targets(t)))

    @pl.loop(0, count)
    def _(t):
        send_ref[t] = make(2 * t + 1 - core).astype(BF)
        copy(t).start()

    @pl.loop(0, count)
    def _(t):
        own = make(2 * t + core)
        copy(t).wait_recv()
        out_ref[t] = (own + twin_ref[t].astype(F32)).astype(BF)
        stores.copy(t).start()

    def finish():
        stores.wait_all()
        for t in range(count):
            copy(t).wait_send()

    return finish


def greet_near(me, shard):
    barrier = pltpu.get_barrier_semaphore()
    for k in (1, 2):
        pl.semaphore_signal(barrier, inc=1, device_id={"seq": me ^ k}, device_id_type=MESH)
    pl.semaphore_signal(barrier, inc=1, device_id={"fsdp": shard ^ 1}, device_id_type=MESH)
    pl.semaphore_wait(barrier, 3)


def core_scratch(rows, width):
    return [pltpu.VMEM((rows // (2 * BLOCK), BLOCK, width), BF)] * 3


def comm_call(body, inputs, outputs, scratch, remotes, moves, call, cost, name):
    return pl.pallas_call(
        body,
        out_shape=tuple(jax.ShapeDtypeStruct(shape, kind) for shape, kind, _ in outputs),
        in_specs=[IN_VMEM if whole else ANYWHERE for _, whole in inputs],
        out_specs=tuple(IN_VMEM if whole else ANYWHERE for _, _, whole in outputs),
        scratch_shapes=scratch
        + [
            pltpu.SemaphoreType.DMA((remotes,)),
            pltpu.SemaphoreType.DMA((remotes,)),
            pltpu.SemaphoreType.DMA((moves,)),
        ],
        compiler_params=pltpu.CompilerParams(
            collective_id=call, has_side_effects=True, vmem_limit_bytes=60 * 1024 * 1024
        ),
        cost_estimate=transfer_cost(cost),
        name=name,
    )(*[value for value, _ in inputs])


def retention_exchange_kernel(
    heads, offsets, cut, mixed_any, w_any, cos_ref, sin_ref, table_ref,
    q_any, k_any, v_any, swish_any, retained_any, gated_any, wo_any,
    mixed_ref, w_ref, q_ref, k_ref, v_ref, swish_ref, retained_ref, gated_ref, both_ref, wo_ref,
    via_x, via_y, sends, recvs, locals_,
):
    me = lax.axis_index("seq")
    shard = lax.axis_index("fsdp")
    core = lax.rem(shard, 2)
    step, wide = both_ref.shape[2:]
    moves = Moves(locals_)

    def piece(column):
        rows = pl.ds(pl.multiple_of((2 * column + core) * step, step), step)
        return w_any.at[rows, slice(w_ref.shape[1], w_ref.shape[1] + wide)]

    across, along, corner = me ^ 1, me ^ 2, me ^ 3
    half = step // 2
    low, high = slice(0, half), slice(half, step)
    swaps = [
        remote(piece(corner).at[low], via_x, sends, recvs, 0, across),
        remote(piece(corner).at[high], via_y, sends, recvs, 1, along),
        remote(piece(across), both_ref.at[core, me], sends, recvs, 2, across),
        remote(piece(along), both_ref.at[core, me], sends, recvs, 3, along),
        remote(via_x, both_ref.at[core, across, low], sends, recvs, 4, along),
        remote(via_y, both_ref.at[core, along, high], sends, recvs, 5, across),
    ]
    kept_here = []

    def twin(k):
        return pltpu.make_async_remote_copy(
            src_ref=both_ref.at[core, me ^ k],
            dst_ref=both_ref.at[core, me ^ k],
            send_sem=sends.at[6 + k],
            recv_sem=recvs.at[6 + k],
            device_id={"fsdp": shard ^ 1},
            device_id_type=MESH,
        )

    def between(i):
        if isinstance(i, int):
            greet_all(me, shard)
            for copy in swaps[:4]:
                copy.start()
            kept_here.append(moves.start(piece(me), both_ref.at[core, me]))
            return

        @pl.when(i == 0)
        def _():
            swaps[0].wait_recv()
            swaps[4].start()
            swaps[1].wait_recv()
            swaps[5].start()
            kept_here[0].wait()
            twin(0).start()

        @pl.when(i == 2)
        def _():
            for k in (1, 2):
                swaps[1 + k].wait_recv()
                twin(k).start()

        @pl.when(i == 3)
        def _():
            swaps[4].wait_recv()
            swaps[5].wait_recv()
            twin(3).start()

    retention_kernel(
        heads, offsets, mixed_any, w_any, cos_ref, sin_ref, table_ref,
        q_any, k_any, v_any, swish_any, retained_any, gated_any,
        mixed_ref, w_ref, q_ref, k_ref, v_ref, swish_ref, retained_ref, gated_ref, moves, between,
    )
    for k in range(4):
        twin(k).wait_recv()
    tile, lane = 16, 128

    @pl.loop(0, heads * (wo_ref.shape[1] // lane))
    def _(n):
        h, c = n // (wo_ref.shape[1] // lane), lax.rem(n, wo_ref.shape[1] // lane)
        lanes = pl.ds(pl.multiple_of(c * lane, lane), lane)
        for k in range(4):
            for r in range(cut.skip(k) // tile, cut.width // tile):
                at = pl.multiple_of(h * cut.rows + (cut.start(k) + r * tile), tile)
                wo_ref[pl.ds(at, tile), lanes] = both_ref[
                    h, k, pl.ds(pl.multiple_of(c * tile, tile), tile), head_lanes(r, lane)
                ]

    moves.start(wo_ref, wo_any).wait()
    for copy in swaps + [twin(k) for k in range(4)]:
        copy.wait_send()


def greet_all(me, shard):
    barrier = pltpu.get_barrier_semaphore()
    for k in (1, 2, 3):
        pl.semaphore_signal(barrier, inc=1, device_id={"seq": me ^ k}, device_id_type=MESH)
    pl.semaphore_signal(barrier, inc=1, device_id={"fsdp": shard ^ 1}, device_id_type=MESH)
    pl.semaphore_wait(barrier, 4)


def retention_exchange(mixed, weight, cosine, sine, table, heads, offsets, cut, call):
    length, width = mixed.shape
    wide = cut.width * width // 256
    outputs = retention_outputs(length, heads) + (((heads * VAL_HEAD, width), BF),)
    return comm_call(
        functools.partial(retention_exchange_kernel, heads, offsets, cut),
        [(mixed, False), (weight, False), (cosine, True), (sine, True), (table, True)],
        [(shape, kind, False) for shape, kind in outputs],
        [pltpu.VMEM(mixed.shape, BF), pltpu.VMEM((width, weight.shape[1] - wide), BF)]
        + [pltpu.VMEM(*out) for out in outputs[:-1]]
        + [pltpu.VMEM((heads, 4, 256, wide), BF), pltpu.VMEM(outputs[-1][0], BF)]
        + [pltpu.VMEM((128, wide), BF)] * 2,
        10,
        6 + 7 * (length // BLOCK),
        call,
        mixed.size // 2,
        "retention_exchange",
    )


def project_and_norm(gated, weight, x, gain, call):
    rows, width = x.shape
    return comm_call(
        project_kernel,
        [(gated, False), (weight, False), (x, True), (gain[None, :], True)],
        [((rows, width), F32, True), ((rows, width), BF, True)],
        [pltpu.VMEM(gated.shape, BF), pltpu.VMEM(weight.shape, BF)] + square_scratch(rows, width),
        6,
        2,
        call,
        x.size,
        "project_and_norm",
    )


def feed_forward_gather_kernel(
    ff, x_any, w_any, c_any, both_any, hidden_any, down_any, full_any,
    full, w_ref, c_ref, both_ref, hidden_ref, total, down_ref, sends, recvs, locals_,
):
    me = lax.axis_index("seq")
    rows = x_any.shape[0]
    moves = Moves(locals_)
    load_x = moves.start(x_any, full.at[me])
    load_w = moves.start(w_any, w_ref)
    load_c = moves.start(c_any, c_ref)
    greet((me ^ 1, me ^ 2))
    load_x.wait()
    copies, _ = square_gather(full.at[me], full, sends, recvs, 0)
    for copy in copies[:4]:
        copy.start()
    stores = [
        by_block(moves, 4, both_ref, both_any, rows),
        by_block(moves, 4, hidden_ref, hidden_any, rows),
        Series(moves, 4, lambda n: (full.at[n], full_any.at[n])),
    ]
    total[...] = jnp.zeros_like(total)
    load_w.wait()
    load_c.wait()

    @pl.loop(0, 4)
    def _(k):
        @pl.when(k == 1)
        def _():
            copies[0].wait_recv()
            copies[4].start()
            copies[1].wait_recv()
            copies[5].start()
            copies[2].wait_recv()

        @pl.when(k == 2)
        def _():
            copies[3].wait_recv()

        @pl.when(k == 3)
        def _():
            copies[4].wait_recv()
            copies[5].wait_recv()

        here = block_rows(k, rows)
        both = product(full[me ^ k], w_ref[...])
        gate, up = both[:, :ff], both[:, ff:]
        bell = 0.5 + 0.5 * lax.erf(gate * math.sqrt(0.5))
        passed = gate * bell
        slope = bell + gate * (math.sqrt(0.5 / math.pi) * jnp.exp(-0.5 * gate * gate))
        both_ref[here, :ff] = (up * slope).astype(BF)
        both_ref[here, ff:] = passed.astype(BF)
        hidden = (passed * up).astype(BF)
        hidden_ref[here, :] = hidden
        for store in stores:
            store.copy(me ^ k).start()
        total[...] += transposed_times(hidden, c_ref[here, :])

    down_ref[...] = total[...].astype(BF)
    moves.store(down_ref, down_any)
    for store in stores:
        store.wait_all()
    moves.close()
    for copy in copies:
        copy.wait_send()


def feed_forward_gather(own, weight, cotangent, call):
    rows, width = own.shape
    length, ff = 4 * rows, weight.shape[1] // 2
    both, hidden, down, full = comm_call(
        functools.partial(feed_forward_gather_kernel, ff),
        [(own, False), (weight, False), (cotangent, False)],
        [
            ((length, 2 * ff), BF, False),
            ((length, ff), BF, False),
            ((ff, width), BF, False),
            ((4, rows, width), BF, False),
        ],
        [
            pltpu.VMEM((4, rows, width), BF),
            pltpu.VMEM(weight.shape, BF),
            pltpu.VMEM(cotangent.shape, BF),
            pltpu.VMEM((length, 2 * ff), BF),
            pltpu.VMEM((length, ff), BF),
            pltpu.VMEM((ff, width), F32),
            pltpu.VMEM((ff, width), BF),
        ],
        6,
        16,
        call,
        own.size,
        "feed_forward_gather",
    )
    return both, hidden, down, full.reshape(length, width)


def column_of(halves):
    total = 0.0
    for terms in halves:
        ones = jnp.ones((terms.shape[0], 128), BF)
        total = total + transposed_times(terms.astype(BF), ones)
    return total


def feed_back_scatter_kernel(
    ff, c_any, both_any, w_any, down_any, x_any, m_ref, own_c_ref, gain_ref,
    grad_ref, term_ref, branch_ref, dw_any,
    c_ref, both_ref, w_ref, down_ref, x_ref, low, dw_send, dw_twin, dw_ref,
    parts, inbox_x, inbox_y, via_x, via_y, out_x, out_y, sends, recvs, locals_,
):
    me = lax.axis_index("seq")
    rows = own_c_ref.shape[0]
    half = rows // 2
    moves = Moves(locals_)
    load_c = by_block(moves, 4, c_any, c_ref, rows)
    load_both = by_block(moves, 4, both_any, both_ref, rows)
    load_c.copy(me ^ 3).start()
    load_down = moves.start(down_any, down_ref)
    load_both.copy(me ^ 3).start()
    load_w = moves.start(w_any, w_ref)
    for k in (1, 2, 0):
        load_c.copy(me ^ k).start()
        load_both.copy(me ^ k).start()
    load_x = moves.start(x_any, x_ref)
    greet_near(me, lax.axis_index("fsdp"))
    boxes = (inbox_x, inbox_y, via_x, via_y, out_x, out_y)
    copies, _, total = square_parts(parts, boxes, sends, recvs, 0)

    def part(k):
        here = block_rows(k, rows)
        load_c.copy(me ^ k).wait()
        load_both.copy(me ^ k).wait()
        hidden_grad = times_transposed(c_ref[here, :], down_ref[...])
        low[here, :ff] = (hidden_grad * both_ref[here, :ff].astype(F32)).astype(BF)
        low[here, ff:] = (hidden_grad * both_ref[here, ff:].astype(F32)).astype(BF)
        pl.when(k == 3)(load_w.wait)
        parts[k] = times_transposed(low[here, :], w_ref[...]).astype(BF)

    load_down.wait()
    send_parts(part, copies, lambda: forward_sums(copies, parts, boxes))
    load_x.wait()
    finish = core_sum(
        moves, lambda b: transposed_times(x_ref[:, rows_of(b)], low[...]), dw_send, dw_twin, dw_ref,
        lambda t: dw_any.at[rows_of(t)], sends, recvs, 6,
    )
    for copy in copies[2:]:
        copy.wait_recv()

    def back_half(i):
        here = slice(i * half, (i + 1) * half)
        back, term = norm_back(m_ref[here, :], total(here), gain_ref[...])
        grad = own_c_ref[here, :].astype(F32) + back
        grad_ref[here, :] = grad
        branch_ref[here, :] = grad.astype(BF)
        return term

    term_ref[...] = column_of([back_half(i) for i in range(2)])
    finish()
    for copy in copies:
        copy.wait_send()


def feed_back_scatter(cotangent, both, weight, down, x, middle, own_cotangent, gain, call):
    rows, width = own_cotangent.shape
    length, ff = cotangent.shape[0], weight.shape[1] // 2
    grad, term, branch, dw = comm_call(
        functools.partial(feed_back_scatter_kernel, ff),
        [
            (cotangent, False),
            (both, False),
            (weight, False),
            (down, False),
            (x, False),
            (middle, True),
            (own_cotangent, True),
            (gain[None, :], True),
        ],
        [
            ((rows, width), F32, True),
            ((width, 128), F32, True),
            ((rows, width), BF, True),
            ((width // 2, 2 * ff), BF, False),
        ],
        [
            pltpu.VMEM(cotangent.shape, BF),
            pltpu.VMEM(both.shape, BF),
            pltpu.VMEM(weight.shape, BF),
            pltpu.VMEM(down.shape, BF),
            pltpu.VMEM(x.shape, BF),
            pltpu.VMEM((length, 2 * ff), BF),
        ]
        + core_scratch(width, 2 * ff)
        + square_scratch(rows, width),
        6 + width // (2 * BLOCK),
        11 + width // (2 * BLOCK),
        call,
        own_cotangent.size,
        "feed_back_scatter",
    )
    return grad, term, branch, dw


def norm_back(values, grad, gain):
    centered = values - jnp.mean(values, axis=-1, keepdims=True)
    spread = lax.rsqrt(jnp.mean(centered * centered, axis=-1, keepdims=True) + EPSILON)
    unit = centered * spread
    g = grad * gain
    back = g - jnp.mean(g, axis=-1, keepdims=True)
    back = spread * (back - unit * jnp.mean(g * unit, axis=-1, keepdims=True))
    return back, grad * unit


def square_pass(own, out_ref, sends, recvs, first, half):
    me = lax.axis_index("seq")
    across, along = me ^ 1, me ^ 2
    spans = (slice(0, half), slice(half, own.shape[0]))

    def part(ref, i):
        return ref.at[spans[i]]

    return [
        remote(part(own, 0), part(out_ref.at[me], 0), sends, recvs, first, across),
        remote(part(own, 1), part(out_ref.at[me], 1), sends, recvs, first + 1, along),
        remote(part(own, 1), part(out_ref.at[me], 1), sends, recvs, first + 2, across),
        remote(part(own, 0), part(out_ref.at[me], 0), sends, recvs, first + 3, along),
        remote(
            part(out_ref.at[across], 0), part(out_ref.at[across], 0), sends, recvs, first + 4, along
        ),
        remote(
            part(out_ref.at[along], 1), part(out_ref.at[along], 1), sends, recvs, first + 5, across
        ),
    ]


def pass_on(copies):
    copies[0].wait_recv()
    copies[4].start()
    copies[1].wait_recv()
    copies[5].start()


def half_rows(rows):
    return -(-rows // 32) * 16


def put_column(ref, rows, at, column):
    first = ref.shape[1] - 128
    spare = lax.broadcasted_iota(jnp.int32, column.shape, 1) == at - first
    ref[rows, first:] = jnp.where(spare, column, ref[rows, first:].astype(F32)).astype(BF)


def gate_back_scatter_kernel(
    heads, cut, branch_any, w_any, swish_any, retained_any, column_any, hidden_any, down_any,
    mixed_any, gated_any, m_any, dswish_any, dret_any, dws_any, dwo_any, out_ref,
    branch_ref, w_ref, swish_ref, retained_ref, column_ref, hidden_ref, down_ref, mixed_ref,
    gated_ref, m_ref, dswish_ref, dret_ref, dws_send, dws_twin, dws_ref, dwo_ref,
    parts, inbox_x, inbox_y, via_x, via_y, out_x, out_y, sends, recvs, locals_,
):
    me = lax.axis_index("seq")
    rows = out_ref.shape[0]
    moves = Moves(locals_)
    load_down = moves.start(down_any, down_ref)
    load_hidden = moves.start(hidden_any, hidden_ref)
    load_gate = moves.start(w_any, w_ref)
    blocks = branch_ref.shape[0] // BLOCK
    load_rows = [
        by_block(moves, blocks, branch_any, branch_ref).start_all(),
        by_block(moves, blocks, swish_any, swish_ref).start_all(),
        by_block(moves, blocks, retained_any, retained_ref).start_all(),
    ]
    load_mixed = moves.start(mixed_any, mixed_ref)
    load_column = moves.start(column_any, column_ref)
    load_gated = moves.start(gated_any, gated_ref)
    load_m = moves.start(m_any, m_ref)
    greet_near(me, lax.axis_index("fsdp"))
    boxes = (inbox_x, inbox_y, via_x, via_y, out_x, out_y)
    copies, _, total = square_parts(parts, boxes, sends, recvs, 0)

    def part(k):
        here = block_rows(k, rows)
        parts[k] = product(hidden_ref[here, :], down_ref[...]).astype(BF)

    load_hidden.wait()
    load_down.wait()
    send_parts(part, copies)
    load_gate.wait()

    @pl.loop(0, blocks)
    def _(i):
        here = rows_of(i)
        for load in load_rows:
            load.copy(i).wait()
        gate_back_rows(
            heads, here, branch_ref[here, :], w_ref, swish_ref, retained_ref, dswish_ref, dret_ref
        )

    moves.store(dswish_ref, dswish_any)
    moves.store(dret_ref, dret_any)
    forward_sums(copies, parts, boxes)
    load_mixed.wait()
    load_column.wait()
    last = dswish_ref.shape[1] - 128
    spare = lax.broadcasted_iota(jnp.int32, (BLOCK, 128), 1) == heads * VAL_HEAD - last

    def make(b):
        here = rows_of(b)
        term = product(mixed_ref[here, :], dswish_ref[...])
        column = jnp.where(spare, column_ref[here, :], term[:, last:])
        return jnp.concatenate([term[:, :last], column], axis=1)

    finish = core_sum(
        moves, make, dws_send, dws_twin, dws_ref, lambda t: dws_any.at[rows_of(t)], sends, recvs, 6
    )
    load_gated.wait()
    step, tile, lane = 2 * BLOCK, 16, 128
    for h in range(heads):
        value_lanes = head_lanes(h, VAL_HEAD)

        @pl.loop(0, branch_ref.shape[1] // step)
        def _(b):
            lanes = pl.ds(pl.multiple_of(b * step, step), step)
            wide = transposed_times(gated_ref[:, value_lanes], branch_ref[:, lanes]).astype(BF)
            for k in range(4):
                for r in range(cut.width // tile):
                    at = cut.start(k) + r * tile
                    for c in range(step // lane):
                        to = pl.ds(pl.multiple_of((b * (step // lane) + c) * tile, tile), tile)
                        dwo_ref[h, k, to, head_lanes(r, lane)] = wide[
                            at : at + tile, head_lanes(c, lane)
                        ]

    moves.store(dwo_ref, dwo_any)
    load_m.wait()
    for copy in copies[2:]:
        copy.wait_recv()
    out_ref[...] = m_ref[...] + total(slice(0, rows))
    finish()
    moves.close()
    for copy in copies:
        copy.wait_send()


def gate_backward_scatter(
    branch, weight, swish, retained, column, hidden, down, mixed_t, gated, middle, heads, padded,
    cut, call,
):
    length, width = branch.shape
    rows = middle.shape[0]
    dwo = (heads, 4, width // 8, cut.width * 8)
    inputs = (branch, weight, swish, retained, column, hidden, down, mixed_t, gated, middle)
    outputs = [
        ((length, padded), BF, False),
        ((heads, length, VAL_HEAD), BF, False),
        ((width // 2, padded), BF, False),
        (dwo, BF, False),
        ((rows, width), F32, True),
    ]
    return comm_call(
        functools.partial(gate_back_scatter_kernel, heads, cut),
        [(value, False) for value in inputs],
        outputs,
        [pltpu.VMEM(v.shape, v.dtype) for v in inputs]
        + [pltpu.VMEM(shape, kind) for shape, kind, _ in outputs[:2]]
        + core_scratch(width, padded)
        + [pltpu.VMEM(dwo, BF)]
        + square_scratch(rows, width),
        6 + width // (2 * BLOCK),
        20 + 3 * length // BLOCK + width // (2 * BLOCK),
        call,
        middle.size,
        "gate_back_scatter",
    )


def retention_back_exchange_kernel(
    heads, q_any, k_any, v_any, dret_any, table_ref, cos_ref, sin_ref, mixed_any, send_any, share_any,
    dqk_any, dv_any, merged_any, full_any,
    q_ref, k_ref, v_ref, dret_ref, mixed_ref, send_ref, dqk_ref, dv_ref, dw_send, dw_twin, dw_ref,
    twin_ref, sum_ref, via_x, via_y, dv_heads, dq_sum, sends, recvs, locals_,
):
    me = lax.axis_index("seq")
    shard = lax.axis_index("fsdp")
    core = lax.rem(shard, 2)
    moves = Moves(locals_)
    load_send = moves.start(send_any, send_ref)
    loads = [
        moves.start(source, target)
        for source, target in (
            (q_any, q_ref), (k_any, k_ref), (v_any, v_ref), (dret_any, dret_ref)
        )
    ]
    load_mixed = moves.start(mixed_any, mixed_ref)
    greet_all(me, shard)
    load_send.wait()
    twin = pltpu.make_async_remote_copy(
        src_ref=send_ref.at[1 - core],
        dst_ref=twin_ref,
        send_sem=sends.at[12],
        recv_sem=recvs.at[12],
        device_id={"fsdp": shard ^ 1},
        device_id_type=MESH,
    )
    twin.start()
    passed = square_pass(share_any, full_any, sends, recvs, 0, half_rows(share_any.shape[0]))
    for copy in passed[:4]:
        copy.start()
    moves.store(share_any, full_any.at[me])
    step, wide = sum_ref.shape[1:]
    half = step // 2
    at = dqk_ref.shape[1]
    across, along, corner = me ^ 1, me ^ 2, me ^ 3

    def place(column, start, rows):
        here = pl.ds(pl.multiple_of(column * step + start, half), rows)
        return merged_any.at[here, slice(at, at + wide)]

    low, high = slice(0, half), slice(half, step)
    swaps = [
        remote(sum_ref.at[corner, low], via_x, sends, recvs, 6, across),
        remote(sum_ref.at[corner, high], via_y, sends, recvs, 7, along),
        remote(sum_ref.at[across], place(me, 0, step), sends, recvs, 8, across),
        remote(sum_ref.at[along], place(me, 0, step), sends, recvs, 9, along),
        remote(via_x, place(across, 0, half), sends, recvs, 10, along),
        remote(via_y, place(along, half, half), sends, recvs, 11, across),
    ]
    for load in loads:
        load.wait()
    for h in range(heads):
        retention_back_head(
            h, heads, q_ref, k_ref, v_ref, dret_ref, table_ref, cos_ref, sin_ref, dqk_ref,
            dv_heads.at[h], dq_sum,
        )
        if h == 0:
            twin.wait_recv()

            @pl.loop(0, 4)
            def _(k):
                sum_ref[k] = (send_ref[core, k].astype(F32) + twin_ref[k].astype(F32)).astype(BF)

            for copy in swaps[:4]:
                copy.start()
            moves.store(sum_ref.at[me], place(me, 0, step))
            pass_on(passed)
    pass_on(swaps)
    dv_ref[...] = pad_lanes([dv_heads[h] for h in range(heads)], dv_ref.shape[1])
    moves.store(dv_ref, dv_any)
    moves.store(dqk_ref, dqk_any)
    load_mixed.wait()
    finish = core_sum(
        moves, lambda b: product(mixed_ref[rows_of(b), :], dqk_ref[...]), dw_send, dw_twin, dw_ref,
        lambda t: merged_any.at[rows_of(t), slice(0, at)], sends, recvs, 13,
    )
    for copy in passed[2:] + swaps[2:]:
        copy.wait_recv()
    finish()
    moves.close()
    for copy in passed + swaps + [twin]:
        copy.wait_send()


def retention_backward_exchange(
    q, k, v, dret, table, cosine, sine, mixed_t, send, share, heads, padded, call
):
    width, length = mixed_t.shape
    qk = heads * KEY_HEAD
    inputs = (
        (q, False), (k, False), (v, False), (dret, False), (table, True), (cosine, True),
        (sine, True), (mixed_t, False), (send, False), (share, False),
    )
    staged = (q, k, v, dret, mixed_t, send)
    block = send.shape[1:]
    kept = width // 2
    return comm_call(
        functools.partial(retention_back_exchange_kernel, heads),
        inputs,
        [
            ((length, 2 * qk), BF, False),
            ((length, padded), BF, False),
            ((kept, 2 * qk + block[2]), BF, False),
            ((4,) + share.shape, BF, False),
        ],
        [pltpu.VMEM(value.shape, BF) for value in staged]
        + [
            pltpu.VMEM((length, 2 * qk), BF),
            pltpu.VMEM((length, padded), BF),
        ]
        + core_scratch(width, 2 * qk)
        + [
            pltpu.VMEM(block, BF),
            pltpu.VMEM(block, BF),
            pltpu.VMEM((block[1] // 2, block[2]), BF),
            pltpu.VMEM((block[1] // 2, block[2]), BF),
            pltpu.VMEM((heads, length, VAL_HEAD), BF),
            pltpu.VMEM((length, KEY_HEAD), F32),
        ],
        13 + kept // BLOCK,
        12 + kept // BLOCK,
        call,
        send.size // 4,
        "retention_back_exchange",
    )


def input_back_kernel(
    offsets, spare, dqk_any, dv_any, ds_any, w_any, x_any, grad_any, mixed_any, gain_ref, share_any,
    dx_ref, dwv_any, full_any, dqk_ref, dv_ref, ds_ref, w_ref, x_ref, grad_ref, mixed_ref, dwv_ref,
    parts, inbox_x, inbox_y, via_x, via_y, out_x, out_y, sends, recvs, locals_,
):
    at_value, at_swish = offsets
    me = lax.axis_index("seq")
    rows = x_ref.shape[0]
    half = rows // 2
    moves = Moves(locals_)
    spans = (slice(0, at_value), slice(at_value, at_swish), slice(at_swish, w_ref.shape[1]))
    grads = ((dqk_any, dqk_ref), (dv_any, dv_ref), (ds_any, ds_ref))
    loads = []
    for span, (source, target) in zip(spans, grads, strict=True):
        loads.append(moves.start(source, target))
        loads.append(moves.start(w_any.at[:, span], w_ref.at[:, span]))
    load_x = moves.start(x_any, x_ref)
    load_grad = moves.start(grad_any, grad_ref)
    load_mixed = moves.start(mixed_any, mixed_ref)
    greet((me ^ 1, me ^ 2))
    boxes = (inbox_x, inbox_y, via_x, via_y, out_x, out_y)
    copies, _, total = square_parts(parts, boxes, sends, recvs, 0)
    passed = square_pass(share_any, full_any, sends, recvs, 6, half_rows(share_any.shape[0]))
    passed[0].start()
    passed[1].start()
    moves.store(share_any, full_any.at[me])

    def part(k):
        here = block_rows(k, rows)
        whole = 0.0
        for n, (_, ref) in enumerate(grads):

            @pl.when(k == 3)
            def _():
                loads[2 * n].wait()
                loads[2 * n + 1].wait()

            whole = whole + times_transposed(ref[here, :], w_ref[:, spans[n]])
        parts[k] = whole.astype(BF)

    def pass_all():
        pass_on(passed)
        forward_sums(copies, parts, boxes)
        passed[2].start()
        passed[3].start()

    send_parts(part, copies, pass_all)
    load_mixed.wait()

    @pl.loop(0, dwv_ref.shape[0] // BLOCK)
    def _(b):
        here = rows_of(b)
        dwv_ref[here, :] = product(mixed_ref[here, :], dv_ref[...]).astype(BF)

    for copy in copies[2:]:
        copy.wait_recv()
    load_x.wait()
    load_grad.wait()
    terms = []
    for i in range(2):
        here = slice(i * half, (i + 1) * half)
        back, term = norm_back(x_ref[here, :].astype(F32), total(here), gain_ref[...])
        dx_ref[here, :] = grad_ref[here, :] + back
        terms.append(term)
    put_column(dwv_ref, slice(0, dwv_ref.shape[0]), spare, column_of(terms))
    moves.store(dwv_ref, dwv_any)
    for copy in passed[2:]:
        copy.wait_recv()
    moves.close()
    for copy in copies + passed:
        copy.wait_send()


def input_backward(dqk, dv, ds, weight, x, grad, mixed_t, gain, share, offsets, spare, call):
    rows, width = x.shape
    staged = (dqk, dv, ds, weight, x, grad, mixed_t)
    return comm_call(
        functools.partial(input_back_kernel, offsets, spare),
        [(value, False) for value in staged] + [(gain[None, :], True), (share, False)],
        [
            ((rows, width), F32, True),
            ((width, dv.shape[1]), BF, False),
            ((4,) + share.shape, BF, False),
        ],
        [pltpu.VMEM(value.shape, value.dtype) for value in staged[:3]]
        + [pltpu.VMEM((width, dqk.shape[1] + dv.shape[1] + ds.shape[1]), BF)]
        + [pltpu.VMEM(value.shape, value.dtype) for value in staged[4:]]
        + [pltpu.VMEM((width, dv.shape[1]), BF)]
        + square_scratch(rows, width),
        12,
        11,
        call,
        x.size + share.size,
        "input_backward",
    )


def join(pieces):
    return jnp.concatenate(pieces, axis=1) if len(pieces) > 1 else pieces[0]


def unpack_columns_kernel(width, in_ref, out_ref, gain_ref):
    count = in_ref.shape[0]
    out_ref[...] = join([in_ref[k][:, :width].astype(F32) for k in range(count)])
    last = in_ref.shape[2] - 128
    tile = sum(in_ref[k][:, last:].astype(F32) for k in range(count))
    gain_ref[...] = tile.T[width - last : width - last + 1, :]


def unpack_columns(gathered, width):
    count, rows, whole = gathered.shape
    block = min(rows, 128)
    out, gain = pl.pallas_call(
        functools.partial(unpack_columns_kernel, width),
        grid=(rows // block,),
        in_specs=[pl.BlockSpec((count, block, whole), lambda i: (0, i, 0))],
        out_specs=[
            pl.BlockSpec((block, count * width), lambda i: (i, 0)),
            pl.BlockSpec((1, block), lambda i: (0, i)),
        ],
        out_shape=[
            jax.ShapeDtypeStruct((rows, count * width), F32),
            jax.ShapeDtypeStruct((1, rows), F32),
        ],
        cost_estimate=pl.CostEstimate(flops=0, bytes_accessed=gathered.size * 4, transcendentals=0),
        name="unpack_columns",
    )(gathered)
    return out, gain[0]


def unpack_related_kernel(width, own_ref, across_ref, along_ref, corner_ref, out_ref, gain_ref):
    me = lax.axis_index("seq")
    pieces = [ref[...].astype(F32) for ref in (own_ref, across_ref, along_ref, corner_ref)]
    last = own_ref.shape[1] - 128
    tile = sum(piece[:, last:] for piece in pieces)
    gain_ref[...] = tile.T[width - last : width - last + 1, :]
    pieces = [piece[:, :width] for piece in pieces]
    low = [jnp.where(me % 2 == k, pieces[0], pieces[1]) for k in range(2)]
    high = [jnp.where(me % 2 == k, pieces[2], pieces[3]) for k in range(2)]
    order = [jnp.where(me < 2, low[k], high[k]) for k in range(2)]
    order += [jnp.where(me < 2, high[k], low[k]) for k in range(2)]
    out_ref[...] = join(order)


def unpack_related(pieces, width):
    rows, whole = pieces[0].shape
    block = min(rows, 128)
    out, gain = pl.pallas_call(
        functools.partial(unpack_related_kernel, width),
        grid=(rows // block,),
        in_specs=[pl.BlockSpec((block, whole), lambda i: (i, 0))] * 4,
        out_specs=[
            pl.BlockSpec((block, 4 * width), lambda i: (i, 0)),
            pl.BlockSpec((1, block), lambda i: (0, i)),
        ],
        out_shape=[
            jax.ShapeDtypeStruct((rows, 4 * width), F32),
            jax.ShapeDtypeStruct((1, rows), F32),
        ],
        compiler_params=pltpu.CompilerParams(vmem_limit_bytes=40 * 1024 * 1024),
        name="unpack_related",
    )(*pieces)
    return out, gain[0]


def swap(values, step):
    return lax.ppermute(values, "seq", [(k, k ^ step) for k in range(4)])


def unpack_feed_kernel(cut, shards, in_ref, down_ref, gate_ref, up_ref, out_ref):
    count = in_ref.shape[0]

    @pl.when(pl.program_id(0) == 0)
    def _():
        for k in range(count):
            if cut.skip(k) < cut.width:
                at = cut.start(k)
                out_ref[at + cut.skip(k) : at + cut.width, :] = down_ref[
                    k, cut.skip(k) : cut.width, :
                ].astype(F32)

    for n, target in enumerate((gate_ref, up_ref)):
        pieces = []
        for f in range(shards):
            for k in range(count):
                at = (n * shards + f) * cut.width
                if cut.skip(k) < cut.width:
                    piece = in_ref[k][:, at + cut.skip(k) : at + cut.width]
                    pieces.append(piece.astype(F32))
        target[...] = join(pieces)


def unpack_feed(gathered, down, cut, shards):
    count, rows, whole = gathered.shape
    block = rows // 4 if rows % 64 == 0 else rows
    wide, width = shards * cut.rows, down.shape[2]
    return pl.pallas_call(
        functools.partial(unpack_feed_kernel, cut, shards),
        grid=(rows // block,),
        in_specs=[
            pl.BlockSpec((count, block, whole), lambda i: (0, i, 0)),
            pl.BlockSpec(down.shape, lambda i: (0, 0, 0)),
        ],
        out_specs=[
            pl.BlockSpec((block, wide), lambda i: (i, 0)),
            pl.BlockSpec((block, wide), lambda i: (i, 0)),
            pl.BlockSpec((cut.rows, width), lambda i: (0, 0)),
        ],
        out_shape=[
            jax.ShapeDtypeStruct((rows, wide), F32),
            jax.ShapeDtypeStruct((rows, wide), F32),
            jax.ShapeDtypeStruct((cut.rows, width), F32),
        ],
        compiler_params=pltpu.CompilerParams(vmem_limit_bytes=40 * 1024 * 1024),
        cost_estimate=pl.CostEstimate(flops=0, bytes_accessed=gathered.size * 4, transcendentals=0),
        name="unpack_feed",
    )(gathered, down)


def unpack_merged_kernel(cut, in_ref, query_ref, key_ref, out_ref):
    tile, lane, count = 16, 128, in_ref.shape[0]
    wide = query_ref.shape[1] // count
    for k in range(count):
        query_ref[:, head_lanes(k, wide)] = in_ref[k, :, :wide].astype(F32)
        key_ref[:, head_lanes(k, wide)] = in_ref[k, :, wide : 2 * wide].astype(F32)
        for r in range(cut.skip(k) // tile, cut.width // tile):
            at = cut.start(k) + r * tile
            lanes = slice(2 * wide + r * lane, 2 * wide + (r + 1) * lane)
            for c in range(out_ref.shape[1] // lane):
                out_ref[at : at + tile, head_lanes(c, lane)] = in_ref[
                    k, c * tile : (c + 1) * tile, lanes
                ].astype(F32)


def unpack_merged(gathered, wide, cut, width):
    count, rows, _ = gathered.shape
    return pl.pallas_call(
        functools.partial(unpack_merged_kernel, cut),
        out_shape=(
            jax.ShapeDtypeStruct((rows, count * wide), F32),
            jax.ShapeDtypeStruct((rows, count * wide), F32),
            jax.ShapeDtypeStruct((cut.rows, width), F32),
        ),
        compiler_params=pltpu.CompilerParams(vmem_limit_bytes=40 * 1024 * 1024),
        cost_estimate=pl.CostEstimate(flops=0, bytes_accessed=gathered.size * 4, transcendentals=0),
        name="unpack_merged",
    )(gathered)


def after(values, *others, all_of=False):
    held = lax.optimization_barrier((values,) + others)
    return held if all_of else held[0]


class Cut:
    def __init__(self, rows, count):
        self.rows, self.count = rows, count
        self.width = -(-rows // (count * 16)) * 16

    def start(self, piece):
        if isinstance(piece, int):
            return min(piece * self.width, self.rows - self.width)
        return jnp.minimum(piece * self.width, self.rows - self.width)

    def skip(self, piece):
        if isinstance(piece, int):
            return min(piece * self.width - self.start(piece), self.width)
        return jnp.minimum(piece * self.width - self.start(piece), self.width)

    def assemble(self, pieces, axis):
        kept = []
        for k, piece in enumerate(pieces):
            if self.skip(k) < self.width:
                kept.append(lax.slice_in_dim(piece, self.skip(k), self.width, axis=axis))
        return jnp.concatenate(kept, axis=axis)


def pack_kernel(
    cut, qk, vd, padded, q_any, k_any, v_any, s_any, o_any, out_any,
    qk_ref, v_ref, s_ref, o_ref, values_ref, tiles_ref, sems,
):
    me = lax.axis_index("seq")
    moves = Moves(sems)
    total, wide = v_any.shape[1], v_ref.shape[1]
    base = jnp.minimum((me * vd) // 128 * 128, total - wide)
    window = pl.ds(pl.multiple_of(base, 128), wide)
    loads = [
        moves.start(v_any.at[:, window], v_ref),
        moves.start(s_any.at[:, window], s_ref),
        moves.start(o_any.at[pl.ds(pl.multiple_of(cut.start(me), 16), cut.width)], o_ref),
    ]
    own = pl.ds(pl.multiple_of(me * qk, 128), qk)
    loads += [
        moves.start(q_any.at[:, own], qk_ref.at[:, slice(0, qk)]),
        moves.start(k_any.at[:, own], qk_ref.at[:, slice(qk, 2 * qk)]),
    ]
    tile, lane = 16, 128
    loads[2].wait()
    for r in range(cut.width // tile):
        for c in range(o_ref.shape[1] // lane):
            tiles_ref[c * tile : (c + 1) * tile, head_lanes(r, lane)] = o_ref[
                r * tile : (r + 1) * tile, head_lanes(c, lane)
            ]
    at = 2 * qk + 2 * padded
    moves.store(tiles_ref, out_any.at[:, slice(at, at + tiles_ref.shape[1])])
    loads[0].wait()
    loads[1].wait()
    for k in range(4):
        shift = k * vd - min(k * vd // 128 * 128, total - wide)

        @pl.when(me == k)
        def _():
            for n, ref in enumerate((v_ref, s_ref)):
                values_ref[:, head_lanes(n, padded)] = pad_lanes([ref[:, shift : shift + vd]], padded)

    moves.store(values_ref, out_any.at[:, slice(2 * qk, at)])
    loads[3].wait()
    loads[4].wait()
    moves.store(qk_ref, out_any.at[:, slice(0, 2 * qk)])
    moves.close()


def pack(query, key, value, swish, output, cut, qk, vd, padded):
    rows, width = query.shape
    wide = min(padded + 128, value.shape[1])
    tiles = cut.width * width // rows
    return pl.pallas_call(
        functools.partial(pack_kernel, cut, qk, vd, padded),
        out_shape=jax.ShapeDtypeStruct((rows, 2 * qk + 2 * padded + tiles), BF),
        in_specs=[ANYWHERE] * 5,
        out_specs=ANYWHERE,
        scratch_shapes=[
            pltpu.VMEM((rows, 2 * qk), BF),
            pltpu.VMEM((rows, wide), BF),
            pltpu.VMEM((rows, wide), BF),
            pltpu.VMEM((cut.width, width), BF),
            pltpu.VMEM((rows, 2 * padded), BF),
            pltpu.VMEM((rows, tiles), BF),
            pltpu.SemaphoreType.DMA((8,)),
        ],
        compiler_params=pltpu.CompilerParams(vmem_limit_bytes=60 * 1024 * 1024),
        name="pack",
    )(query, key, value, swish, output)


def columns_of(weight, index, width, padded):
    piece = lax.dynamic_slice_in_dim(weight, index * width, width, axis=1)
    return jnp.pad(piece, ((0, 0), (0, padded - width)))


def on_device(
    layer_input,
    mixer_gain,
    query_weight,
    key_weight,
    value_weight,
    swish_weight,
    output_weight,
    channel_gain,
    gelu_weight,
    linear_weight,
    down_weight,
    output_cotangent,
):
    groups, local_length, width = layer_input.shape
    seq_count = lax.axis_size("seq")
    shards = lax.axis_size("fsdp")
    me = lax.axis_index("seq")
    per_device = HEADS // seq_count
    rows_count = groups * local_length
    square = seq_count == 4 and shards == 8 and rows_count % 32 == 0
    length = local_length * seq_count
    key_scale = KEY_HEAD ** (-0.5)
    qk = query_weight.shape[1] // seq_count
    vd = value_weight.shape[1] // seq_count
    vd_pad = -(-vd // 128) * 128
    hidden_units = gelu_weight.shape[1]
    own_rows = down_weight.shape[0]
    cut = Cut(own_rows, seq_count)
    ff = shards * cut.width

    def gather_rows(values):
        return lax.all_gather(values, "fsdp", axis=0, tiled=True)

    def scatter_rows(values):
        return lax.psum_scatter(values.astype(BF), "fsdp", scatter_dimension=0, tiled=True)

    def scatter_parity(values):
        groups = [list(range(parity, shards, 2)) for parity in range(2)]
        return lax.psum_scatter(
            values, "fsdp", scatter_dimension=0, tiled=True, axis_index_groups=groups
        )

    if square:
        attention_piece = pack(
            query_weight, key_weight, value_weight, swish_weight, output_weight, cut, qk, vd, vd_pad
        )
    else:
        output_pieces = gather_rows(
            lax.dynamic_slice_in_dim(output_weight, cut.start(me), cut.width, axis=0)
        )
        attention_piece = jnp.concatenate(
            [
                columns_of(query_weight, me, qk, qk),
                columns_of(key_weight, me, qk, qk),
                columns_of(value_weight, me, vd, vd_pad),
                columns_of(swish_weight, me, vd, vd_pad),
            ],
            axis=1,
        )
    attention_weight = gather_rows(attention_piece)
    column = lax.broadcasted_iota(jnp.int32, (hidden_units, ff), 0)
    slot = lax.broadcasted_iota(jnp.int32, (hidden_units, ff), 1)
    chosen = (slot // cut.width) * own_rows + cut.start(me) + slot % cut.width
    selector = (column == chosen).astype(BF)
    gate_piece = product(gelu_weight, selector).astype(BF)
    up_piece = product(linear_weight, selector).astype(BF)
    feed_piece = jnp.concatenate([gate_piece, up_piece], axis=1)
    down_piece = lax.dynamic_slice_in_dim(down_weight, cut.start(me), cut.width, axis=0)
    gains = lax.all_gather(jnp.stack([mixer_gain, channel_gain]), "fsdp", axis=1, tiled=True)
    mixer_scale, channel_scale = gains[0].astype(F32), gains[1].astype(F32)

    local_input = layer_input.reshape(rows_count, width)
    upstream = output_cotangent.reshape(rows_count, width)

    upstream = after(upstream, gains)

    def whole(values, call):
        gathered = gather_seq(values, call)
        return gathered.reshape(length * groups, width)

    input_full = whole(local_input, 0)
    upstream_full = whole(after(upstream, input_full), 1)
    inputs = local_input.astype(F32)

    blocks = shards // seq_count
    mixed_low, mixed_turned = norm_and_turn(input_full, mixer_scale)
    head_ids = me * per_device + jnp.arange(per_device, dtype=jnp.int32)
    table, table_back = decay_tables(head_ids, length)
    cosine, sine = rotation_tables(length, KEY_HEAD // 2)
    feed_weight = gather_rows(after(feed_piece, upstream_full))

    offsets = (qk, 2 * qk, 2 * qk + vd_pad)
    attention_weight = after(
        attention_weight, mixed_low, mixed_turned, table, table_back, cosine, feed_piece
    )
    if square:
        query_low, key_low, value_low, swish_pre, retained, gated_low, output_full = (
            retention_exchange(
                mixed_low, attention_weight, cosine, sine, table, per_device, offsets, cut, 2
            )
        )
    else:
        query_low, key_low, value_low, swish_pre, retained, gated_low = retention_forward(
            mixed_low, attention_weight, cosine, sine, table, per_device, offsets
        )
        swapped = exchange_seq(
            output_pieces.reshape(seq_count, blocks, cut.width, width), 2
        )
        output_full = jnp.concatenate(
            [
                cut.assemble([swapped[piece, block] for piece in range(seq_count)], 0)
                for block in range(blocks)
            ],
            axis=0,
        )

    kept_rows = lax.broadcasted_iota(jnp.int32, down_piece.shape, 0) >= cut.skip(me)
    down_full = gather_rows(after(jnp.where(kept_rows, down_piece, jnp.zeros_like(down_piece)), gated_low))
    if square:
        middle, channel_own = project_and_norm(
            gated_low, output_full, local_input, channel_scale, 3
        )
        both_pre, hidden_low, down_term, channel_full = feed_forward_gather(
            channel_own, feed_weight, upstream_full, 4
        )
        down_share = scatter_rows(down_term)
        middle_grad, channel_term, branch_own, feed_term = feed_back_scatter(
            after(upstream_full, down_term), both_pre, feed_weight, down_full, channel_full,
            middle, upstream, channel_scale, 6,
        )
        feed_share = scatter_parity(feed_term)
        branch_full = whole(branch_own, 7)
    else:
        middle = inputs + scatter_seq(product(gated_low, output_full).astype(BF), 3)
        channel_full = whole(normalize(middle, channel_scale).astype(BF), 4)
        gate_pre, up_pre, hidden_low = feed_forward(channel_full, feed_weight)
        down_share = scatter_rows(transposed_times(hidden_low, upstream_full).astype(BF))
        feed_low_grad, channel_part, hidden_part = feed_backward(
            upstream_full, gate_pre, up_pre, hidden_low, feed_weight, down_full
        )
        feed_share = scatter_rows(transposed_times(channel_full, feed_low_grad).astype(BF))
        middle_local, channel_terms = norm_back(
            middle, scatter_seq(channel_part, 6), channel_scale
        )
        channel_term = jnp.sum(channel_terms, axis=0)
        middle_grad = upstream.astype(F32) + middle_local
        branch_full = whole(middle_grad.astype(BF), 7)

    at_value, at_swish = 2 * qk, 2 * qk + vd_pad
    if square:
        swish_grad, retained_grad, swish_term, output_send, layer_output = gate_backward_scatter(
            after(branch_full, down_share), output_full, swish_pre, retained,
            channel_term, hidden_low, down_full, mixed_turned, gated_low, middle,
            per_device, vd_pad, cut, 5,
        )
        swish_share = scatter_parity(swish_term)
        key_grad, value_grad, merged_term, down_all = retention_backward_exchange(
            query_low, key_low, value_low, after(retained_grad, feed_share), table_back, cosine, sine,
            mixed_turned, output_send, down_share, per_device, vd_pad, 8,
        )
        merged_share = scatter_parity(merged_term)
        input_gradient, value_term, feed_all = input_backward(
            key_grad, value_grad, swish_grad, attention_weight, local_input, middle_grad,
            mixed_turned, mixer_scale, feed_share, (at_value, at_swish), vd, 9,
        )
    else:
        swish_grad, retained_grad = gate_backward(
            branch_full, output_full, swish_pre, retained, per_device, vd_pad
        )
        spare = lax.broadcasted_iota(jnp.int32, (width, vd_pad), 1) == vd
        swish_term = transposed_times(mixed_low, swish_grad)
        swish_term = jnp.where(spare, channel_term[:, None], swish_term).astype(BF)
        swish_share = scatter_rows(swish_term)
        layer_output = middle + scatter_seq(hidden_part, 5)
        key_grad, value_grad = retention_backward(
            query_low, key_low, value_low, retained_grad, table_back, cosine, sine, per_device, vd_pad
        )
        key_term = transposed_times(mixed_low, key_grad).astype(BF)
        key_share = scatter_rows(key_term)
        mixed_part = (
            times_transposed(key_grad, attention_weight[:, :at_value])
            + times_transposed(value_grad, attention_weight[:, at_value:at_swish])
            + times_transposed(swish_grad, attention_weight[:, at_swish:])
        )
        input_local, mixer_terms = norm_back(
            inputs, scatter_seq(mixed_part.astype(BF), 9), mixer_scale
        )
        mixer_term = jnp.sum(mixer_terms, axis=0)
        input_gradient = middle_grad + input_local
        output_term = transposed_times(gated_low, branch_full).astype(BF)
        output_term = output_term.reshape(blocks, own_rows, width)
        output_send = jnp.stack(
            [
                lax.slice_in_dim(output_term, cut.start(k), cut.start(k) + cut.width, axis=1)
                for k in range(seq_count)
            ]
        )
        output_swapped = exchange_seq(output_send, 8)
        output_share = scatter_rows(output_swapped.reshape(shards * cut.width, width))
        value_term = transposed_times(mixed_low, value_grad)
        value_term = jnp.where(spare, mixer_term[:, None], value_term).astype(BF)
    input_gradient = input_gradient.astype(BF).reshape(groups, local_length, width)
    value_share = scatter_rows(value_term)

    layer_output = layer_output.astype(BF).reshape(groups, local_length, width)
    if square:
        swish_all, merged_all = gather_two(
            after(swish_share, layer_output, input_gradient), merged_share, 13
        )
        value_share = after(value_share, swish_all)
        half = value_share.shape[0] // 2
        across, along = swap(value_share, 1), swap(value_share, 2)
        gelu_gradient, linear_gradient, down_gradient = unpack_feed(
            after(feed_all, swish_all), down_all, cut, shards
        )
        swish_gradient, channel_own_gradient = unpack_columns(swish_all, vd)
        across, along, gelu_gradient, swish_gradient = after(
            across, along, gelu_gradient, swish_gradient, all_of=True
        )
        corner_low, corner_high = swap(across[:half], 2), swap(along[half:], 1)
        query_gradient, key_gradient, output_gradient = unpack_merged(merged_all, qk, cut, width)
        corner_low, corner_high, query_gradient = after(
            corner_low, corner_high, query_gradient, all_of=True
        )
        corner = jnp.concatenate([corner_low, corner_high], axis=0)
        value_gradient, mixer_own_gradient = unpack_related(
            (value_share, across, along, corner), vd
        )
    else:
        down_all = gather_seq(down_share, 10)
        feed_all = gather_seq(after(feed_share, down_all), 11)
        swish_all = gather_seq(after(swish_share, feed_all), 13)
        output_all = gather_seq(after(output_share, swish_all), 12)
        key_all = gather_seq(after(key_share, output_all), 15)
        value_all = gather_seq(after(value_share, key_all), 14)
        swish_gradient, channel_own_gradient = unpack_columns(swish_all, vd)
        output_gradient = cut.assemble([output_all[k] for k in range(seq_count)], 0).astype(F32)
        gelu_gradient, linear_gradient, down_gradient = unpack_feed(
            feed_all, down_all, cut, shards
        )
        query_gradient, key_gradient = (
            jnp.concatenate(
                [key_all[k][:, at : at + qk] for k in range(seq_count)], axis=1
            ).astype(F32)
            for at in (0, qk)
        )
        value_gradient, mixer_own_gradient = unpack_columns(value_all, vd)
    return (
        layer_output,
        input_gradient,
        mixer_own_gradient,
        query_gradient,
        key_gradient,
        value_gradient,
        swish_gradient,
        output_gradient,
        channel_own_gradient,
        gelu_gradient,
        linear_gradient,
        down_gradient,
    )


def solution(mesh):
    tokens, rows, vector = P("fsdp", "seq", None), P("fsdp", None), P("fsdp")
    return jax.shard_map(
        on_device,
        mesh=mesh,
        in_specs=(
            tokens, vector, rows, rows, rows, rows, rows, vector, rows, rows, rows, tokens,
        ),
        out_specs=(
            tokens, tokens, vector, rows, rows, rows, rows, rows, vector, rows, rows, rows,
        ),
        check_vma=False,
    )
```

```python
import functools
import math

import jax
import jax.numpy as jnp
from jax import lax
from jax.experimental import pallas as pl
from jax.experimental.pallas import tpu as pltpu
from jax.sharding import PartitionSpec as P

HEADS = 8
KEY_HEAD = 256
VAL_HEAD = 432
EPSILON = 1e-05
MESH = pl.DeviceIdType.MESH
BF = jnp.bfloat16
F32 = jnp.float32
IN_VMEM = pl.BlockSpec(memory_space=pltpu.VMEM)
ANYWHERE = pl.BlockSpec(memory_space=pl.ANY)


def product(left, right):
    return jnp.dot(left, right, preferred_element_type=F32)


def times_transposed(left, right):
    return lax.dot_general(left, right, (((1,), (1,)), ((), ())), preferred_element_type=F32)


def transposed_times(left, right):
    return lax.dot_general(left, right, (((0,), (0,)), ((), ())), preferred_element_type=F32)


def normalize(values, gain):
    centered = values - jnp.mean(values, axis=-1, keepdims=True)
    spread = lax.rsqrt(jnp.mean(centered * centered, axis=-1, keepdims=True) + EPSILON)
    return centered * spread * gain


def rotation_tables(length, half_width):
    rates = jnp.exp(-math.log(10000.0) * jnp.arange(half_width, dtype=F32) / (half_width - 1))
    turned = jnp.arange(length, dtype=F32)[:, None] * rates[None, :]
    return (jnp.cos(turned), jnp.sin(turned))


def pad_lanes(pieces, width):
    have = sum(piece.shape[1] for piece in pieces)
    if have < width:
        pieces = pieces + [jnp.zeros((pieces[0].shape[0], width - have), pieces[0].dtype)]
    return jnp.concatenate(pieces, axis=1) if len(pieces) > 1 else pieces[0]


def rotate_pair(values, cosine, sine, back=False):
    half = KEY_HEAD // 2
    first, second = values[:, :half], values[:, half:]
    if back:
        return jnp.concatenate([first * cosine + second * sine, second * cosine - first * sine], 1)
    return jnp.concatenate([first * cosine - second * sine, second * cosine + first * sine], 1)


BLOCK = 256


def decay_tables(head_ids, length):
    rates = jnp.log1p(-jnp.exp2(-5.0 - head_ids.astype(F32)))[:, None, None]
    short = jnp.arange(BLOCK, dtype=jnp.int32)
    long = jnp.arange(2 * length - BLOCK, dtype=jnp.int32)

    def decay(gap):
        far = jnp.exp(jnp.maximum(gap, 0).astype(F32)[None] * rates)
        return jnp.where(gap[None] >= 0, far, 0.0)

    by_row = decay(length - BLOCK + short[:, None] - long[None, :])
    by_column = decay(long[:, None] - (length - BLOCK) - short[None, :])
    return by_row, by_column


def norm_parts(values):
    centered = values - jnp.mean(values, axis=-1, keepdims=True)
    variance = jnp.mean(centered * centered, axis=-1, keepdims=True)
    factor = lax.rsqrt(jnp.maximum(variance, 1.0))
    return centered * factor, factor, variance > 1.0


def rows_of(block):
    return pl.ds(pl.multiple_of(block * BLOCK, BLOCK), BLOCK)


def head_lanes(head, width):
    return slice(head * width, (head + 1) * width)


class Moves:
    def __init__(self, sems):
        self.sems, self.used, self.open = sems, 0, []

    def start(self, source, target):
        copy = pltpu.make_async_copy(source, target, self.sems.at[self.used])
        self.used += 1
        copy.start()
        return copy

    def store(self, source, target):
        self.open.append(self.start(source, target))

    def close(self):
        for copy in self.open:
            copy.wait()


def norm_kernel(x_ref, gain_ref, out_ref, turned_ref):
    normed = normalize(x_ref[...].astype(F32), gain_ref[...])
    out_ref[...] = normed.astype(BF)
    turned_ref[...] = normed.T.astype(BF)


def norm_and_turn(x, gain):
    length, width = x.shape
    return pl.pallas_call(
        norm_kernel,
        grid=(length // BLOCK,),
        in_specs=[
            pl.BlockSpec((BLOCK, width), lambda i: (i, 0)),
            pl.BlockSpec((1, width), lambda i: (0, 0)),
        ],
        out_specs=[
            pl.BlockSpec((BLOCK, width), lambda i: (i, 0)),
            pl.BlockSpec((width, BLOCK), lambda i: (0, i)),
        ],
        out_shape=[
            jax.ShapeDtypeStruct((length, width), BF),
            jax.ShapeDtypeStruct((width, length), BF),
        ],
        compiler_params=pltpu.CompilerParams(vmem_limit_bytes=32 * 1024 * 1024),
        name="norm_and_turn",
    )(x, gain[None, :])


class Series:
    def __init__(self, moves, count, ends):
        self.sems, self.first, self.count, self.ends = moves.sems, moves.used, count, ends
        moves.used += count

    def copy(self, i):
        return pltpu.make_async_copy(*self.ends(i), self.sems.at[self.first + i])

    def start_all(self):
        for i in range(self.count):
            self.copy(i).start()
        return self

    def wait_all(self):
        for i in range(self.count):
            self.copy(i).wait()


def by_block(moves, count, source, target, rows=BLOCK):
    def ends(i):
        here = pl.ds(i * rows if isinstance(i, int) else pl.multiple_of(i * rows, rows), rows)
        if len(source.shape) == 3:
            return source.at[:, here], target.at[:, here]
        return source.at[here], target.at[here]

    return Series(moves, count, ends)


def retention_kernel(
    heads, offsets, mixed_any, w_any, cos_ref, sin_ref, table_ref,
    q_any, k_any, v_any, swish_any, retained_any, gated_any,
    mixed_ref, w_ref, q_ref, k_ref, v_ref, swish_ref, retained_ref, gated_ref, sems,
    between=None,
):
    at_key, at_value, at_swish = offsets
    length = mixed_ref.shape[0]
    blocks = length // BLOCK
    moves = sems if isinstance(sems, Moves) else Moves(sems)
    spans = (
        slice(0, at_key), slice(at_key, at_value), slice(at_value, at_swish),
        slice(at_swish, w_ref.shape[1]),
    )
    loads = by_block(moves, blocks, mixed_any, mixed_ref)
    loads.copy(0).start()
    weights = [moves.start(w_any.at[:, span], w_ref.at[:, span]) for span in spans]
    for i in range(1, blocks):
        loads.copy(i).start()
    stores = [
        by_block(moves, blocks, source, target)
        for source, target in (
            (q_ref, q_any), (k_ref, k_any), (v_ref, v_any), (swish_ref, swish_any),
            (retained_ref, retained_any), (gated_ref, gated_any),
        )
    ]
    k_ref[...] = jnp.zeros_like(k_ref)
    v_ref[...] = jnp.zeros_like(v_ref)
    if between is not None:
        between(-1)

    @pl.loop(0, blocks)
    def _(i):
        rows = rows_of(i)
        loads.copy(i).wait()
        mixed = mixed_ref[rows, :]
        cosine, sine = cos_ref[rows, :], sin_ref[rows, :]

        def projected(n):
            @pl.when(i == 0)
            def _():
                weights[n].wait()

            return product(mixed, w_ref[:, spans[n]])

        for n, (target, scale) in enumerate(((q_ref, 1.0), (k_ref, KEY_HEAD**-0.5))):
            pre = projected(n)
            for h in range(heads):
                lanes = head_lanes(h, KEY_HEAD)
                turned = rotate_pair(pre[:, lanes], cosine, sine)
                target[rows, lanes] = (turned * scale if n else turned).astype(BF)
        value = projected(2)
        for h in range(heads):
            v_ref[h, rows, :] = value[:, head_lanes(h, VAL_HEAD)].astype(BF)
        swish_ref[rows, :] = projected(3)[:, : heads * VAL_HEAD]
        gated = []
        for h in range(heads):
            lanes = head_lanes(h, KEY_HEAD)
            scores = times_transposed(q_ref[rows, lanes], k_ref[:, lanes])
            decay = table_ref[
                h, :, pl.ds(pl.multiple_of((blocks - 1 - i) * BLOCK, BLOCK), length)
            ]
            retained = product((scores * decay).astype(BF), v_ref[h]).astype(BF)
            retained_ref[h, rows, :] = retained
            unit, _, _ = norm_parts(retained.astype(F32))
            s = swish_ref[rows, head_lanes(h, VAL_HEAD)]
            gated.append((s * jax.nn.sigmoid(s) * unit).astype(BF))
        gated_ref[rows, :] = jnp.concatenate(gated, axis=1) if heads > 1 else gated[0]
        for store in stores:
            store.copy(i).start()
        if between is not None:
            between(i)

    for store in stores:
        store.wait_all()


def retention_outputs(length, heads):
    qk, vd = heads * KEY_HEAD, heads * VAL_HEAD
    return (
        ((length, qk), BF),
        ((length, qk), BF),
        ((heads, length, VAL_HEAD), BF),
        ((length, vd), F32),
        ((heads, length, VAL_HEAD), BF),
        ((length, vd), BF),
    )


def retention_forward(mixed, weight, cosine, sine, table, heads, offsets):
    length, width = mixed.shape
    outputs = retention_outputs(length, heads)
    blocks = length // BLOCK
    return pl.pallas_call(
        functools.partial(retention_kernel, heads, offsets),
        out_shape=tuple(jax.ShapeDtypeStruct(*out) for out in outputs),
        in_specs=[ANYWHERE, ANYWHERE, IN_VMEM, IN_VMEM, IN_VMEM],
        out_specs=(ANYWHERE,) * 6,
        scratch_shapes=[pltpu.VMEM(mixed.shape, BF), pltpu.VMEM(weight.shape, BF)]
        + [pltpu.VMEM(*out) for out in outputs]
        + [pltpu.SemaphoreType.DMA((4 + 7 * blocks,))],
        compiler_params=pltpu.CompilerParams(vmem_limit_bytes=60 * 1024 * 1024),
        cost_estimate=pl.CostEstimate(
            flops=30_000_000_000, bytes_accessed=0, transcendentals=0
        ),
        name="retention",
    )(mixed, weight, cosine, sine, table)


def gate_back_rows(heads, rows, branch, w_ref, swish_ref, retained_ref, dswish_ref, dret_ref):
    gated_grad = times_transposed(branch, w_ref[...])
    swish_parts = []
    for h in range(heads):
        lanes = head_lanes(h, VAL_HEAD)
        grad, s = gated_grad[:, lanes], swish_ref[rows, lanes]
        gate = jax.nn.sigmoid(s)
        unit, factor, above = norm_parts(retained_ref[h, rows, :].astype(F32))
        swish_parts.append((grad * unit * (gate * (1.0 + s * (1.0 - gate)))).astype(BF))
        g = grad * (s * gate)
        along = jnp.where(above, jnp.mean(g * unit, axis=-1, keepdims=True), 0.0)
        back = factor * (g - jnp.mean(g, axis=-1, keepdims=True) - unit * along)
        dret_ref[h, rows, :] = back.astype(BF)
    dswish_ref[rows, :] = pad_lanes(swish_parts, dswish_ref.shape[1])


def gate_back_kernel(heads, branch_ref, w_ref, swish_ref, retained_ref, dswish_ref, dret_ref):
    @pl.loop(0, branch_ref.shape[0] // BLOCK)
    def _(i):
        rows = rows_of(i)
        gate_back_rows(
            heads, rows, branch_ref[rows, :], w_ref, swish_ref, retained_ref, dswish_ref, dret_ref
        )


def gate_backward(branch, weight, swish, retained, heads, padded):
    length = branch.shape[0]
    return pl.pallas_call(
        functools.partial(gate_back_kernel, heads),
        out_shape=(
            jax.ShapeDtypeStruct((length, padded), BF),
            jax.ShapeDtypeStruct((heads, length, VAL_HEAD), BF),
        ),
        compiler_params=pltpu.CompilerParams(vmem_limit_bytes=48 * 1024 * 1024),
        name="gate_back",
    )(branch, weight, swish, retained)


def retention_back_head(
    h, heads, q_ref, k_ref, v_ref, dret_ref, table_ref, cos_ref, sin_ref, dqk_ref, dv_head,
    dq_sum,
):
    length = q_ref.shape[0]
    blocks = length // BLOCK
    lanes = head_lanes(h, KEY_HEAD)
    dq_sum[...] = jnp.zeros_like(dq_sum)

    @pl.loop(0, blocks)
    def _(j):
        there = rows_of(j)
        query, grad = q_ref[:, lanes], dret_ref[h]
        key, value = k_ref[there, lanes], v_ref[h, there, :]
        decay = table_ref[h, pl.ds(pl.multiple_of((blocks - 1 - j) * BLOCK, BLOCK), length), :]
        weights = (times_transposed(query, key) * decay).astype(BF)
        score = (times_transposed(grad, value) * decay).astype(BF)
        dq_sum[...] += product(score, key)
        dk = transposed_times(score, query).astype(BF).astype(F32)
        dk = rotate_pair(dk, cos_ref[there, :], sin_ref[there, :], back=True)
        dqk_ref[there, head_lanes(heads + h, KEY_HEAD)] = (dk * (KEY_HEAD**-0.5)).astype(BF)
        dv_head[there, :] = transposed_times(weights, grad).astype(BF)

    @pl.loop(0, blocks)
    def _(i):
        rows = rows_of(i)
        dq = dq_sum[rows, :].astype(BF).astype(F32)
        dqk_ref[rows, lanes] = rotate_pair(
            dq, cos_ref[rows, :], sin_ref[rows, :], back=True
        ).astype(BF)


def retention_back_kernel(
    heads, q_ref, k_ref, v_ref, dret_ref, table_ref, cos_ref, sin_ref, dqk_ref, dv_ref,
    dv_heads, dq_sum,
):
    for h in range(heads):
        retention_back_head(
            h, heads, q_ref, k_ref, v_ref, dret_ref, table_ref, cos_ref, sin_ref, dqk_ref,
            dv_heads.at[h], dq_sum,
        )
    dv_ref[...] = pad_lanes([dv_heads[h] for h in range(heads)], dv_ref.shape[1])


def retention_backward(q, k, v, dret, table, cosine, sine, heads, padded):
    length = q.shape[0]
    qk = heads * KEY_HEAD
    return pl.pallas_call(
        functools.partial(retention_back_kernel, heads),
        out_shape=(
            jax.ShapeDtypeStruct((length, 2 * qk), BF),
            jax.ShapeDtypeStruct((length, padded), BF),
        ),
        scratch_shapes=[
            pltpu.VMEM((heads, length, VAL_HEAD), BF),
            pltpu.VMEM((length, KEY_HEAD), F32),
        ],
        compiler_params=pltpu.CompilerParams(vmem_limit_bytes=48 * 1024 * 1024),
        name="retention_back",
    )(q, k, v, dret, table, cosine, sine)


def transfer_cost(elements):
    return pl.CostEstimate(flops=0, bytes_accessed=elements * 240, transcendentals=0)


def greet(peers):
    barrier = pltpu.get_barrier_semaphore()
    for peer in peers:
        pl.semaphore_signal(barrier, inc=1, device_id={"seq": peer}, device_id_type=MESH)
    pl.semaphore_wait(barrier, len(peers))


def remote(source, target, sends, recvs, k, to):
    return pltpu.make_async_remote_copy(
        src_ref=source,
        dst_ref=target,
        send_sem=sends.at[k],
        recv_sem=recvs.at[k],
        device_id={"seq": to},
        device_id_type=MESH,
    )


def gather_square_kernel(x_ref, o_ref, sends, recvs, local):
    me = lax.axis_index("seq")
    across, along = me ^ 1, me ^ 2
    half = x_ref.shape[0] // 2
    greet((across, along))
    own = pltpu.make_async_copy(x_ref, o_ref.at[me], local)
    own.start()

    def part(ref, i):
        return ref.at[pl.ds(i * half, half)]

    first = (
        remote(part(x_ref, 0), part(o_ref.at[me], 0), sends, recvs, 0, across),
        remote(part(x_ref, 1), part(o_ref.at[me], 1), sends, recvs, 1, along),
        remote(part(x_ref, 1), part(o_ref.at[me], 1), sends, recvs, 2, across),
        remote(part(x_ref, 0), part(o_ref.at[me], 0), sends, recvs, 3, along),
    )
    for copy in first:
        copy.start()
    first[0].wait_recv()
    on_along = remote(part(o_ref.at[across], 0), part(o_ref.at[across], 0), sends, recvs, 4, along)
    on_along.start()
    first[1].wait_recv()
    on_across = remote(part(o_ref.at[along], 1), part(o_ref.at[along], 1), sends, recvs, 5, across)
    on_across.start()
    first[2].wait_recv()
    first[3].wait_recv()
    on_along.wait_recv()
    on_across.wait_recv()
    for copy in first + (on_along, on_across):
        copy.wait_send()
    own.wait()


def gather_kernel(count, x_ref, o_ref, sends, recvs, local):
    me = lax.axis_index("seq")
    peers = [lax.rem(me + step, count) for step in range(1, count)]
    greet(peers)
    own = pltpu.make_async_copy(x_ref, o_ref.at[me], local)
    own.start()
    copies = [remote(x_ref, o_ref.at[me], sends, recvs, k, to) for k, to in enumerate(peers)]
    for copy in copies:
        copy.start()
    for copy in copies:
        copy.wait()
    own.wait()


def gather_seq(values, call):
    count = lax.axis_size("seq")
    square = count == 4 and values.shape[0] % 32 == 0
    body = gather_square_kernel if square else functools.partial(gather_kernel, count)
    copies = 6 if square else count - 1
    return pl.pallas_call(
        body,
        out_shape=jax.ShapeDtypeStruct((count,) + values.shape, values.dtype),
        in_specs=[pl.BlockSpec(memory_space=pl.ANY)],
        out_specs=pl.BlockSpec(memory_space=pl.ANY),
        scratch_shapes=[
            pltpu.SemaphoreType.DMA((copies,)),
            pltpu.SemaphoreType.DMA((copies,)),
            pltpu.SemaphoreType.DMA,
        ],
        compiler_params=pltpu.CompilerParams(collective_id=call, has_side_effects=True),
        cost_estimate=transfer_cost(values.size),
        name=f"gather_seq_{call}",
    )(values)


def gather_two_kernel(a_ref, b_ref, a_out, b_out, sends, recvs, locals_):
    me = lax.axis_index("seq")
    greet((me ^ 1, me ^ 2))
    moves = Moves(locals_)
    moves.store(a_ref, a_out.at[me])
    moves.store(b_ref, b_out.at[me])
    both = [
        square_pass(ref, out, sends, recvs, first, half_rows(ref.shape[0]))
        for ref, out, first in ((a_ref, a_out, 0), (b_ref, b_out, 6))
    ]
    for copies in both:
        for copy in copies[:4]:
            copy.start()
    for copies in both:
        pass_on(copies)
    for copies in both:
        for copy in copies[2:]:
            copy.wait_recv()
    moves.close()
    for copies in both:
        for copy in copies:
            copy.wait_send()


def gather_two(a, b, call):
    return comm_call(
        gather_two_kernel,
        [(a, False), (b, False)],
        [((4,) + a.shape, BF, False), ((4,) + b.shape, BF, False)],
        [],
        12,
        2,
        call,
        a.size + b.size,
        "gather_two",
    )


def exchange_kernel(count, x_ref, o_ref, sends, recvs, local):
    me = lax.axis_index("seq")
    peers = [lax.rem(me + step, count) for step in range(1, count)]
    greet(peers)
    own = pltpu.make_async_copy(x_ref.at[me], o_ref.at[me], local)
    own.start()
    copies = [remote(x_ref.at[to], o_ref.at[me], sends, recvs, k, to) for k, to in enumerate(peers)]
    for copy in copies:
        copy.start()
    for copy in copies:
        copy.wait()
    own.wait()


def exchange_seq(values, call):
    count = lax.axis_size("seq")
    return pl.pallas_call(
        functools.partial(exchange_kernel, count),
        out_shape=jax.ShapeDtypeStruct(values.shape, values.dtype),
        in_specs=[pl.BlockSpec(memory_space=pl.ANY)],
        out_specs=pl.BlockSpec(memory_space=pl.ANY),
        scratch_shapes=[
            pltpu.SemaphoreType.DMA((count - 1,)),
            pltpu.SemaphoreType.DMA((count - 1,)),
            pltpu.SemaphoreType.DMA,
        ],
        compiler_params=pltpu.CompilerParams(collective_id=call, has_side_effects=True),
        cost_estimate=transfer_cost(values.size),
        name=f"exchange_seq_{call}",
    )(values)


def scatter_square_kernel(p_ref, o_ref, inbox_x, inbox_y, via_x, via_y, out_x, out_y, sends, recvs):
    me = lax.axis_index("seq")
    across, along, corner = me ^ 1, me ^ 2, me ^ 3
    half = p_ref.shape[1] // 2
    low, high = pl.ds(0, half), pl.ds(half, half)
    greet((across, along))
    first = (
        remote(p_ref.at[corner, low], via_x, sends, recvs, 0, across),
        remote(p_ref.at[corner, high], via_y, sends, recvs, 1, along),
        remote(p_ref.at[across, low], inbox_x.at[low], sends, recvs, 2, across),
        remote(p_ref.at[along, high], inbox_y.at[high], sends, recvs, 3, along),
    )
    for copy in first:
        copy.start()
    first[0].wait_recv()
    out_y[...] = (p_ref[along, :half].astype(F32) + via_x[...].astype(F32)).astype(BF)
    to_along = remote(out_y, inbox_y.at[low], sends, recvs, 4, along)
    to_along.start()
    first[1].wait_recv()
    out_x[...] = (p_ref[across, half:].astype(F32) + via_y[...].astype(F32)).astype(BF)
    to_across = remote(out_x, inbox_x.at[high], sends, recvs, 5, across)
    to_across.start()
    first[2].wait_recv()
    first[3].wait_recv()
    to_along.wait_recv()
    to_across.wait_recv()
    o_ref[...] = (
        p_ref[me].astype(F32) + inbox_x[...].astype(F32) + inbox_y[...].astype(F32)
    )
    for copy in first + (to_along, to_across):
        copy.wait_send()


def scatter_kernel(count, p_ref, o_ref, inbox, sends, recvs):
    me = lax.axis_index("seq")
    peers = [lax.rem(me + step, count) for step in range(1, count)]
    greet(peers)
    copies = [remote(p_ref.at[to], inbox.at[k], sends, recvs, k, to) for k, to in enumerate(peers)]
    for copy in copies:
        copy.start()
    total = p_ref[me].astype(F32)
    for k, copy in enumerate(copies):
        copy.wait_recv()
        total = total + inbox[k].astype(F32)
    o_ref[...] = total
    for copy in copies:
        copy.wait_send()


def scatter_seq(parts, call):
    count = lax.axis_size("seq")
    rows, width = parts.shape[0] // count, parts.shape[1]
    parts = parts.reshape(count, rows, width)
    if count == 4 and rows % 32 == 0:
        body = scatter_square_kernel
        scratch = [pltpu.VMEM((rows, width), BF)] * 2 + [pltpu.VMEM((rows // 2, width), BF)] * 4
        copies = 6
    else:
        body = functools.partial(scatter_kernel, count)
        scratch = [pltpu.VMEM((count - 1, rows, width), BF)]
        copies = count - 1
    return pl.pallas_call(
        body,
        out_shape=jax.ShapeDtypeStruct((rows, width), F32),
        in_specs=[pl.BlockSpec(memory_space=pltpu.VMEM)],
        out_specs=pl.BlockSpec(memory_space=pltpu.VMEM),
        scratch_shapes=scratch
        + [pltpu.SemaphoreType.DMA((copies,)), pltpu.SemaphoreType.DMA((copies,))],
        compiler_params=pltpu.CompilerParams(
            collective_id=call, has_side_effects=True, vmem_limit_bytes=32 * 1024 * 1024
        ),
        cost_estimate=transfer_cost(rows * width),
        name=f"scatter_seq_{call}",
    )(parts)


def feed_forward_kernel(ff, x_ref, w_ref, gate_ref, up_ref, hidden_ref):
    both = product(x_ref[...], w_ref[...])
    gate, up = both[:, :ff], both[:, ff:]
    gate_ref[...] = gate
    up_ref[...] = up
    hidden_ref[...] = (gate * (0.5 + 0.5 * lax.erf(gate * math.sqrt(0.5))) * up).astype(BF)


def feed_back_kernel(
    ff, c_ref, gate_ref, up_ref, hidden_ref, w_ref, down_ref, both_ref, part_ref, out_ref
):
    gate, up = gate_ref[...], up_ref[...]
    out_ref[...] = product(hidden_ref[...], down_ref[...]).astype(BF)
    hidden_grad = times_transposed(c_ref[...], down_ref[...])
    bell = 0.5 + 0.5 * lax.erf(gate * math.sqrt(0.5))
    slope = bell + gate * (math.sqrt(0.5 / math.pi) * jnp.exp(-0.5 * gate * gate))
    both = jnp.concatenate([hidden_grad * up * slope, hidden_grad * (gate * bell)], axis=1)
    both = both.astype(BF)
    both_ref[...] = both
    part_ref[...] = times_transposed(both, w_ref[...]).astype(BF)


def by_rows(block, width):
    return pl.BlockSpec((block, width), lambda i: (i, 0))


def kept(shape):
    return pl.BlockSpec(shape, lambda i: (0, 0), pipeline_mode=pl.Buffered(1))


FEED_BLOCK = 256


def feed_forward(x, weight):
    length, width = x.shape
    ff = weight.shape[1] // 2
    return pl.pallas_call(
        functools.partial(feed_forward_kernel, ff),
        grid=(length // FEED_BLOCK,),
        in_specs=[by_rows(FEED_BLOCK, width), kept(weight.shape)],
        out_specs=[by_rows(FEED_BLOCK, ff)] * 3,
        out_shape=(
            jax.ShapeDtypeStruct((length, ff), F32),
            jax.ShapeDtypeStruct((length, ff), F32),
            jax.ShapeDtypeStruct((length, ff), BF),
        ),
        compiler_params=pltpu.CompilerParams(vmem_limit_bytes=48 * 1024 * 1024),
        cost_estimate=pl.CostEstimate(
            flops=4 * length * width * ff, bytes_accessed=weight.size * 4, transcendentals=0
        ),
        name="feed_forward",
    )(x, weight)


def feed_backward(cotangent, gate, up, hidden, weight, down):
    length, width = cotangent.shape
    ff = weight.shape[1] // 2
    return pl.pallas_call(
        functools.partial(feed_back_kernel, ff),
        grid=(length // FEED_BLOCK,),
        in_specs=[by_rows(FEED_BLOCK, width)]
        + [by_rows(FEED_BLOCK, ff)] * 3
        + [kept(weight.shape), kept(down.shape)],
        out_specs=[
            by_rows(FEED_BLOCK, 2 * ff),
            by_rows(FEED_BLOCK, width),
            by_rows(FEED_BLOCK, width),
        ],
        out_shape=(
            jax.ShapeDtypeStruct((length, 2 * ff), BF),
            jax.ShapeDtypeStruct((length, width), BF),
            jax.ShapeDtypeStruct((length, width), BF),
        ),
        compiler_params=pltpu.CompilerParams(vmem_limit_bytes=56 * 1024 * 1024),
        cost_estimate=pl.CostEstimate(
            flops=8 * length * width * ff, bytes_accessed=weight.size * 4, transcendentals=0
        ),
        name="feed_back",
    )(cotangent, gate, up, hidden, weight, down)


def square_parts(parts, boxes, sends, recvs, first):
    me = lax.axis_index("seq")
    across, along = me ^ 1, me ^ 2
    inbox_x, inbox_y, via_x, via_y, out_x, out_y = boxes
    half = via_x.shape[0]
    low, high = pl.ds(0, half), pl.ds(half, half)
    copies = [
        remote(parts.at[3, low], via_x, sends, recvs, first, across),
        remote(parts.at[3, high], via_y, sends, recvs, first + 1, along),
        remote(parts.at[1, low], inbox_x.at[low], sends, recvs, first + 2, across),
        remote(parts.at[2, high], inbox_y.at[high], sends, recvs, first + 3, along),
        remote(out_y, inbox_y.at[low], sends, recvs, first + 4, along),
        remote(out_x, inbox_x.at[high], sends, recvs, first + 5, across),
    ]

    def finish():
        forward_sums(copies, parts, boxes)
        for copy in copies[2:]:
            copy.wait_recv()

    def total(rows):
        return (
            parts[0, rows].astype(F32)
            + inbox_x[rows, :].astype(F32)
            + inbox_y[rows, :].astype(F32)
        )

    return copies, finish, total


def square_gather(own, out_ref, sends, recvs, first):
    me = lax.axis_index("seq")
    across, along = me ^ 1, me ^ 2
    half = own.shape[0] // 2

    def part(ref, i):
        return ref.at[pl.ds(i * half, half)]

    copies = [
        remote(part(own, 0), part(out_ref.at[me], 0), sends, recvs, first, across),
        remote(part(own, 1), part(out_ref.at[me], 1), sends, recvs, first + 1, along),
        remote(part(own, 1), part(out_ref.at[me], 1), sends, recvs, first + 2, across),
        remote(part(own, 0), part(out_ref.at[me], 0), sends, recvs, first + 3, along),
        remote(
            part(out_ref.at[across], 0), part(out_ref.at[across], 0), sends, recvs, first + 4, along
        ),
        remote(
            part(out_ref.at[along], 1), part(out_ref.at[along], 1), sends, recvs, first + 5, across
        ),
    ]

    def finish():
        copies[0].wait_recv()
        copies[4].start()
        copies[1].wait_recv()
        copies[5].start()
        for copy in copies[2:]:
            copy.wait_recv()

    return copies, finish


def block_rows(k, rows):
    return pl.ds(pl.multiple_of((lax.axis_index("seq") ^ k) * rows, rows), rows)


def forward_sums(copies, parts, boxes):
    inbox_x, inbox_y, via_x, via_y, out_x, out_y = boxes
    half = via_x.shape[0]
    copies[0].wait_recv()
    out_y[...] = (parts[2, :half].astype(F32) + via_x[...].astype(F32)).astype(BF)
    copies[4].start()
    copies[1].wait_recv()
    out_x[...] = (parts[1, half:].astype(F32) + via_y[...].astype(F32)).astype(BF)
    copies[5].start()


def send_parts(part, copies, then=None):
    @pl.loop(0, 4)
    def _(i):
        if then is not None:
            pl.when(i == 3)(then)
        part(jnp.where(i == 0, 3, jnp.where(i == 3, 0, i)))

        @pl.when(i == 0)
        def _():
            copies[0].start()
            copies[1].start()

        @pl.when(i == 1)
        def _():
            copies[2].start()

        @pl.when(i == 2)
        def _():
            copies[3].start()


def project_kernel(
    g_any, w_any, x_ref, gain_ref, middle_ref, own_ref,
    g_ref, w_ref, parts, inbox_x, inbox_y, via_x, via_y, out_x, out_y, sends, recvs, locals_,
):
    me = lax.axis_index("seq")
    rows = x_ref.shape[0]
    half = rows // 2
    moves = Moves(locals_)
    loads = [moves.start(w_any, w_ref), moves.start(g_any, g_ref)]
    greet((me ^ 1, me ^ 2))
    boxes = (inbox_x, inbox_y, via_x, via_y, out_x, out_y)
    copies, finish, total = square_parts(parts, boxes, sends, recvs, 0)

    def part(k):
        parts[k] = product(g_ref[block_rows(k, rows), :], w_ref[...]).astype(BF)

    for load in loads:
        load.wait()
    send_parts(part, copies)
    finish()

    @pl.loop(0, 2)
    def _(i):
        here = pl.ds(pl.multiple_of(i * half, half), half)
        middle = x_ref[here, :].astype(F32) + total(here)
        middle_ref[here, :] = middle
        own_ref[here, :] = normalize(middle, gain_ref[...]).astype(BF)

    for copy in copies:
        copy.wait_send()


def square_scratch(rows, width):
    return [
        pltpu.VMEM((4, rows, width), BF),
        pltpu.VMEM((rows, width), BF),
        pltpu.VMEM((rows, width), BF),
        pltpu.VMEM((rows // 2, width), BF),
        pltpu.VMEM((rows // 2, width), BF),
        pltpu.VMEM((rows // 2, width), BF),
        pltpu.VMEM((rows // 2, width), BF),
    ]


def square_call(body, out_shape, out_specs, scratch, inputs, call, cost, name):
    return pl.pallas_call(
        body,
        out_shape=out_shape,
        in_specs=[IN_VMEM] * len(inputs),
        out_specs=out_specs,
        scratch_shapes=scratch,
        compiler_params=pltpu.CompilerParams(
            collective_id=call, has_side_effects=True, vmem_limit_bytes=56 * 1024 * 1024
        ),
        cost_estimate=transfer_cost(cost),
        name=name,
    )(*inputs)


def core_sum(moves, make, send_ref, twin_ref, out_ref, targets, sends, recvs, first):
    shard = lax.axis_index("fsdp")
    core = lax.rem(shard, 2)
    count = out_ref.shape[0]

    def copy(t):
        return pltpu.make_async_remote_copy(
            src_ref=send_ref.at[t],
            dst_ref=twin_ref.at[t],
            send_sem=sends.at[first + t],
            recv_sem=recvs.at[first + t],
            device_id={"fsdp": shard ^ 1},
            device_id_type=MESH,
        )

    stores = Series(moves, count, lambda t: (out_ref.at[t], targets(t)))

    @pl.loop(0, count)
    def _(t):
        send_ref[t] = make(2 * t + 1 - core).astype(BF)
        copy(t).start()

    @pl.loop(0, count)
    def _(t):
        own = make(2 * t + core)
        copy(t).wait_recv()
        out_ref[t] = (own + twin_ref[t].astype(F32)).astype(BF)
        stores.copy(t).start()

    def finish():
        stores.wait_all()
        for t in range(count):
            copy(t).wait_send()

    return finish


def greet_near(me, shard):
    barrier = pltpu.get_barrier_semaphore()
    for k in (1, 2):
        pl.semaphore_signal(barrier, inc=1, device_id={"seq": me ^ k}, device_id_type=MESH)
    pl.semaphore_signal(barrier, inc=1, device_id={"fsdp": shard ^ 1}, device_id_type=MESH)
    pl.semaphore_wait(barrier, 3)


def core_scratch(rows, width):
    return [pltpu.VMEM((rows // (2 * BLOCK), BLOCK, width), BF)] * 3


def comm_call(body, inputs, outputs, scratch, remotes, moves, call, cost, name):
    return pl.pallas_call(
        body,
        out_shape=tuple(jax.ShapeDtypeStruct(shape, kind) for shape, kind, _ in outputs),
        in_specs=[IN_VMEM if whole else ANYWHERE for _, whole in inputs],
        out_specs=tuple(IN_VMEM if whole else ANYWHERE for _, _, whole in outputs),
        scratch_shapes=scratch
        + [
            pltpu.SemaphoreType.DMA((remotes,)),
            pltpu.SemaphoreType.DMA((remotes,)),
            pltpu.SemaphoreType.DMA((moves,)),
        ],
        compiler_params=pltpu.CompilerParams(
            collective_id=call, has_side_effects=True, vmem_limit_bytes=60 * 1024 * 1024
        ),
        cost_estimate=transfer_cost(cost),
        name=name,
    )(*[value for value, _ in inputs])


def retention_exchange_kernel(
    heads, offsets, cut, mixed_any, w_any, cos_ref, sin_ref, table_ref,
    q_any, k_any, v_any, swish_any, retained_any, gated_any, wo_any,
    mixed_ref, w_ref, q_ref, k_ref, v_ref, swish_ref, retained_ref, gated_ref, both_ref, wo_ref,
    via_x, via_y, sends, recvs, locals_,
):
    me = lax.axis_index("seq")
    shard = lax.axis_index("fsdp")
    core = lax.rem(shard, 2)
    step, wide = both_ref.shape[2:]
    moves = Moves(locals_)

    def piece(column):
        rows = pl.ds(pl.multiple_of((2 * column + core) * step, step), step)
        return w_any.at[rows, slice(w_ref.shape[1], w_ref.shape[1] + wide)]

    across, along, corner = me ^ 1, me ^ 2, me ^ 3
    half = step // 2
    low, high = slice(0, half), slice(half, step)
    swaps = [
        remote(piece(corner).at[low], via_x, sends, recvs, 0, across),
        remote(piece(corner).at[high], via_y, sends, recvs, 1, along),
        remote(piece(across), both_ref.at[core, me], sends, recvs, 2, across),
        remote(piece(along), both_ref.at[core, me], sends, recvs, 3, along),
        remote(via_x, both_ref.at[core, across, low], sends, recvs, 4, along),
        remote(via_y, both_ref.at[core, along, high], sends, recvs, 5, across),
    ]
    kept_here = []

    def twin(k):
        return pltpu.make_async_remote_copy(
            src_ref=both_ref.at[core, me ^ k],
            dst_ref=both_ref.at[core, me ^ k],
            send_sem=sends.at[6 + k],
            recv_sem=recvs.at[6 + k],
            device_id={"fsdp": shard ^ 1},
            device_id_type=MESH,
        )

    def between(i):
        if isinstance(i, int):
            greet_all(me, shard)
            for copy in swaps[:4]:
                copy.start()
            kept_here.append(moves.start(piece(me), both_ref.at[core, me]))
            return

        @pl.when(i == 0)
        def _():
            swaps[0].wait_recv()
            swaps[4].start()
            swaps[1].wait_recv()
            swaps[5].start()
            kept_here[0].wait()
            twin(0).start()

        @pl.when(i == 2)
        def _():
            for k in (1, 2):
                swaps[1 + k].wait_recv()
                twin(k).start()

        @pl.when(i == 3)
        def _():
            swaps[4].wait_recv()
            swaps[5].wait_recv()
            twin(3).start()

    retention_kernel(
        heads, offsets, mixed_any, w_any, cos_ref, sin_ref, table_ref,
        q_any, k_any, v_any, swish_any, retained_any, gated_any,
        mixed_ref, w_ref, q_ref, k_ref, v_ref, swish_ref, retained_ref, gated_ref, moves, between,
    )
    for k in range(4):
        twin(k).wait_recv()
    tile, lane = 16, 128

    @pl.loop(0, heads * (wo_ref.shape[1] // lane))
    def _(n):
        h, c = n // (wo_ref.shape[1] // lane), lax.rem(n, wo_ref.shape[1] // lane)
        lanes = pl.ds(pl.multiple_of(c * lane, lane), lane)
        for k in range(4):
            for r in range(cut.skip(k) // tile, cut.width // tile):
                at = pl.multiple_of(h * cut.rows + (cut.start(k) + r * tile), tile)
                wo_ref[pl.ds(at, tile), lanes] = both_ref[
                    h, k, pl.ds(pl.multiple_of(c * tile, tile), tile), head_lanes(r, lane)
                ]

    moves.start(wo_ref, wo_any).wait()
    for copy in swaps + [twin(k) for k in range(4)]:
        copy.wait_send()


def greet_all(me, shard):
    barrier = pltpu.get_barrier_semaphore()
    for k in (1, 2, 3):
        pl.semaphore_signal(barrier, inc=1, device_id={"seq": me ^ k}, device_id_type=MESH)
    pl.semaphore_signal(barrier, inc=1, device_id={"fsdp": shard ^ 1}, device_id_type=MESH)
    pl.semaphore_wait(barrier, 4)


def retention_exchange(mixed, weight, cosine, sine, table, heads, offsets, cut, call):
    length, width = mixed.shape
    wide = cut.width * width // 256
    outputs = retention_outputs(length, heads) + (((heads * VAL_HEAD, width), BF),)
    return comm_call(
        functools.partial(retention_exchange_kernel, heads, offsets, cut),
        [(mixed, False), (weight, False), (cosine, True), (sine, True), (table, True)],
        [(shape, kind, False) for shape, kind in outputs],
        [pltpu.VMEM(mixed.shape, BF), pltpu.VMEM((width, weight.shape[1] - wide), BF)]
        + [pltpu.VMEM(*out) for out in outputs[:-1]]
        + [pltpu.VMEM((heads, 4, 256, wide), BF), pltpu.VMEM(outputs[-1][0], BF)]
        + [pltpu.VMEM((128, wide), BF)] * 2,
        10,
        6 + 7 * (length // BLOCK),
        call,
        mixed.size // 2,
        "retention_exchange",
    )


def project_and_norm(gated, weight, x, gain, call):
    rows, width = x.shape
    return comm_call(
        project_kernel,
        [(gated, False), (weight, False), (x, True), (gain[None, :], True)],
        [((rows, width), F32, True), ((rows, width), BF, True)],
        [pltpu.VMEM(gated.shape, BF), pltpu.VMEM(weight.shape, BF)] + square_scratch(rows, width),
        6,
        2,
        call,
        x.size,
        "project_and_norm",
    )


def feed_forward_gather_kernel(
    ff, x_any, w_any, c_any, both_any, hidden_any, down_any, full_any,
    full, w_ref, c_ref, both_ref, hidden_ref, total, down_ref, sends, recvs, locals_,
):
    me = lax.axis_index("seq")
    rows = x_any.shape[0]
    moves = Moves(locals_)
    load_x = moves.start(x_any, full.at[me])
    load_w = moves.start(w_any, w_ref)
    load_c = moves.start(c_any, c_ref)
    greet((me ^ 1, me ^ 2))
    load_x.wait()
    copies, _ = square_gather(full.at[me], full, sends, recvs, 0)
    for copy in copies[:4]:
        copy.start()
    stores = [
        by_block(moves, 4, both_ref, both_any, rows),
        by_block(moves, 4, hidden_ref, hidden_any, rows),
        Series(moves, 4, lambda n: (full.at[n], full_any.at[n])),
    ]
    total[...] = jnp.zeros_like(total)
    load_w.wait()
    load_c.wait()

    @pl.loop(0, 4)
    def _(k):
        @pl.when(k == 1)
        def _():
            copies[0].wait_recv()
            copies[4].start()
            copies[1].wait_recv()
            copies[5].start()
            copies[2].wait_recv()

        @pl.when(k == 2)
        def _():
            copies[3].wait_recv()

        @pl.when(k == 3)
        def _():
            copies[4].wait_recv()
            copies[5].wait_recv()

        here = block_rows(k, rows)
        both = product(full[me ^ k], w_ref[...])
        gate, up = both[:, :ff], both[:, ff:]
        bell = 0.5 + 0.5 * lax.erf(gate * math.sqrt(0.5))
        passed = gate * bell
        slope = bell + gate * (math.sqrt(0.5 / math.pi) * jnp.exp(-0.5 * gate * gate))
        both_ref[here, :ff] = (up * slope).astype(BF)
        both_ref[here, ff:] = passed.astype(BF)
        hidden = (passed * up).astype(BF)
        hidden_ref[here, :] = hidden
        for store in stores:
            store.copy(me ^ k).start()
        total[...] += transposed_times(hidden, c_ref[here, :])

    down_ref[...] = total[...].astype(BF)
    moves.store(down_ref, down_any)
    for store in stores:
        store.wait_all()
    moves.close()
    for copy in copies:
        copy.wait_send()


def feed_forward_gather(own, weight, cotangent, call):
    rows, width = own.shape
    length, ff = 4 * rows, weight.shape[1] // 2
    both, hidden, down, full = comm_call(
        functools.partial(feed_forward_gather_kernel, ff),
        [(own, False), (weight, False), (cotangent, False)],
        [
            ((length, 2 * ff), BF, False),
            ((length, ff), BF, False),
            ((ff, width), BF, False),
            ((4, rows, width), BF, False),
        ],
        [
            pltpu.VMEM((4, rows, width), BF),
            pltpu.VMEM(weight.shape, BF),
            pltpu.VMEM(cotangent.shape, BF),
            pltpu.VMEM((length, 2 * ff), BF),
            pltpu.VMEM((length, ff), BF),
            pltpu.VMEM((ff, width), F32),
            pltpu.VMEM((ff, width), BF),
        ],
        6,
        16,
        call,
        own.size,
        "feed_forward_gather",
    )
    return both, hidden, down, full.reshape(length, width)


def column_of(halves):
    total = 0.0
    for terms in halves:
        ones = jnp.ones((terms.shape[0], 128), BF)
        total = total + transposed_times(terms.astype(BF), ones)
    return total


def feed_back_scatter_kernel(
    ff, c_any, both_any, w_any, down_any, x_any, m_ref, own_c_ref, gain_ref,
    grad_ref, term_ref, branch_ref, dw_any,
    c_ref, both_ref, w_ref, down_ref, x_ref, low, dw_send, dw_twin, dw_ref,
    parts, inbox_x, inbox_y, via_x, via_y, out_x, out_y, sends, recvs, locals_,
):
    me = lax.axis_index("seq")
    rows = own_c_ref.shape[0]
    half = rows // 2
    moves = Moves(locals_)
    load_c = by_block(moves, 4, c_any, c_ref, rows)
    load_both = by_block(moves, 4, both_any, both_ref, rows)
    load_c.copy(me ^ 3).start()
    load_down = moves.start(down_any, down_ref)
    load_both.copy(me ^ 3).start()
    load_w = moves.start(w_any, w_ref)
    for k in (1, 2, 0):
        load_c.copy(me ^ k).start()
        load_both.copy(me ^ k).start()
    load_x = moves.start(x_any, x_ref)
    greet_near(me, lax.axis_index("fsdp"))
    boxes = (inbox_x, inbox_y, via_x, via_y, out_x, out_y)
    copies, _, total = square_parts(parts, boxes, sends, recvs, 0)

    def part(k):
        here = block_rows(k, rows)
        load_c.copy(me ^ k).wait()
        load_both.copy(me ^ k).wait()
        hidden_grad = times_transposed(c_ref[here, :], down_ref[...])
        low[here, :ff] = (hidden_grad * both_ref[here, :ff].astype(F32)).astype(BF)
        low[here, ff:] = (hidden_grad * both_ref[here, ff:].astype(F32)).astype(BF)
        pl.when(k == 3)(load_w.wait)
        parts[k] = times_transposed(low[here, :], w_ref[...]).astype(BF)

    load_down.wait()
    send_parts(part, copies, lambda: forward_sums(copies, parts, boxes))
    load_x.wait()
    finish = core_sum(
        moves, lambda b: transposed_times(x_ref[:, rows_of(b)], low[...]), dw_send, dw_twin, dw_ref,
        lambda t: dw_any.at[rows_of(t)], sends, recvs, 6,
    )
    for copy in copies[2:]:
        copy.wait_recv()

    def back_half(i):
        here = slice(i * half, (i + 1) * half)
        back, term = norm_back(m_ref[here, :], total(here), gain_ref[...])
        grad = own_c_ref[here, :].astype(F32) + back
        grad_ref[here, :] = grad
        branch_ref[here, :] = grad.astype(BF)
        return term

    term_ref[...] = column_of([back_half(i) for i in range(2)])
    finish()
    for copy in copies:
        copy.wait_send()


def feed_back_scatter(cotangent, both, weight, down, x, middle, own_cotangent, gain, call):
    rows, width = own_cotangent.shape
    length, ff = cotangent.shape[0], weight.shape[1] // 2
    grad, term, branch, dw = comm_call(
        functools.partial(feed_back_scatter_kernel, ff),
        [
            (cotangent, False),
            (both, False),
            (weight, False),
            (down, False),
            (x, False),
            (middle, True),
            (own_cotangent, True),
            (gain[None, :], True),
        ],
        [
            ((rows, width), F32, True),
            ((width, 128), F32, True),
            ((rows, width), BF, True),
            ((width // 2, 2 * ff), BF, False),
        ],
        [
            pltpu.VMEM(cotangent.shape, BF),
            pltpu.VMEM(both.shape, BF),
            pltpu.VMEM(weight.shape, BF),
            pltpu.VMEM(down.shape, BF),
            pltpu.VMEM(x.shape, BF),
            pltpu.VMEM((length, 2 * ff), BF),
        ]
        + core_scratch(width, 2 * ff)
        + square_scratch(rows, width),
        6 + width // (2 * BLOCK),
        11 + width // (2 * BLOCK),
        call,
        own_cotangent.size,
        "feed_back_scatter",
    )
    return grad, term, branch, dw


def norm_back(values, grad, gain):
    centered = values - jnp.mean(values, axis=-1, keepdims=True)
    spread = lax.rsqrt(jnp.mean(centered * centered, axis=-1, keepdims=True) + EPSILON)
    unit = centered * spread
    g = grad * gain
    back = g - jnp.mean(g, axis=-1, keepdims=True)
    back = spread * (back - unit * jnp.mean(g * unit, axis=-1, keepdims=True))
    return back, grad * unit


def square_pass(own, out_ref, sends, recvs, first, half):
    me = lax.axis_index("seq")
    across, along = me ^ 1, me ^ 2
    spans = (slice(0, half), slice(half, own.shape[0]))

    def part(ref, i):
        return ref.at[spans[i]]

    return [
        remote(part(own, 0), part(out_ref.at[me], 0), sends, recvs, first, across),
        remote(part(own, 1), part(out_ref.at[me], 1), sends, recvs, first + 1, along),
        remote(part(own, 1), part(out_ref.at[me], 1), sends, recvs, first + 2, across),
        remote(part(own, 0), part(out_ref.at[me], 0), sends, recvs, first + 3, along),
        remote(
            part(out_ref.at[across], 0), part(out_ref.at[across], 0), sends, recvs, first + 4, along
        ),
        remote(
            part(out_ref.at[along], 1), part(out_ref.at[along], 1), sends, recvs, first + 5, across
        ),
    ]


def pass_on(copies):
    copies[0].wait_recv()
    copies[4].start()
    copies[1].wait_recv()
    copies[5].start()


def half_rows(rows):
    return -(-rows // 32) * 16


def put_column(ref, rows, at, column):
    first = ref.shape[1] - 128
    spare = lax.broadcasted_iota(jnp.int32, column.shape, 1) == at - first
    ref[rows, first:] = jnp.where(spare, column, ref[rows, first:].astype(F32)).astype(BF)


def gate_back_scatter_kernel(
    heads, cut, branch_any, w_any, swish_any, retained_any, column_any, hidden_any, down_any,
    mixed_any, gated_any, m_any, dswish_any, dret_any, dws_any, dwo_any, out_ref,
    branch_ref, w_ref, swish_ref, retained_ref, column_ref, hidden_ref, down_ref, mixed_ref,
    gated_ref, m_ref, dswish_ref, dret_ref, dws_send, dws_twin, dws_ref, dwo_ref,
    parts, inbox_x, inbox_y, via_x, via_y, out_x, out_y, sends, recvs, locals_,
):
    me = lax.axis_index("seq")
    rows = out_ref.shape[0]
    moves = Moves(locals_)
    load_down = moves.start(down_any, down_ref)
    load_hidden = moves.start(hidden_any, hidden_ref)
    load_gate = moves.start(w_any, w_ref)
    blocks = branch_ref.shape[0] // BLOCK
    load_rows = [
        by_block(moves, blocks, branch_any, branch_ref).start_all(),
        by_block(moves, blocks, swish_any, swish_ref).start_all(),
        by_block(moves, blocks, retained_any, retained_ref).start_all(),
    ]
    load_mixed = moves.start(mixed_any, mixed_ref)
    load_column = moves.start(column_any, column_ref)
    load_gated = moves.start(gated_any, gated_ref)
    load_m = moves.start(m_any, m_ref)
    greet_near(me, lax.axis_index("fsdp"))
    boxes = (inbox_x, inbox_y, via_x, via_y, out_x, out_y)
    copies, _, total = square_parts(parts, boxes, sends, recvs, 0)

    def part(k):
        here = block_rows(k, rows)
        parts[k] = product(hidden_ref[here, :], down_ref[...]).astype(BF)

    load_hidden.wait()
    load_down.wait()
    send_parts(part, copies)
    load_gate.wait()

    @pl.loop(0, blocks)
    def _(i):
        here = rows_of(i)
        for load in load_rows:
            load.copy(i).wait()
        gate_back_rows(
            heads, here, branch_ref[here, :], w_ref, swish_ref, retained_ref, dswish_ref, dret_ref
        )

    moves.store(dswish_ref, dswish_any)
    moves.store(dret_ref, dret_any)
    forward_sums(copies, parts, boxes)
    load_mixed.wait()
    load_column.wait()
    last = dswish_ref.shape[1] - 128
    spare = lax.broadcasted_iota(jnp.int32, (BLOCK, 128), 1) == heads * VAL_HEAD - last

    def make(b):
        here = rows_of(b)
        term = product(mixed_ref[here, :], dswish_ref[...])
        column = jnp.where(spare, column_ref[here, :], term[:, last:])
        return jnp.concatenate([term[:, :last], column], axis=1)

    finish = core_sum(
        moves, make, dws_send, dws_twin, dws_ref, lambda t: dws_any.at[rows_of(t)], sends, recvs, 6
    )
    load_gated.wait()
    step, tile, lane = 2 * BLOCK, 16, 128
    for h in range(heads):
        value_lanes = head_lanes(h, VAL_HEAD)

        @pl.loop(0, branch_ref.shape[1] // step)
        def _(b):
            lanes = pl.ds(pl.multiple_of(b * step, step), step)
            wide = transposed_times(gated_ref[:, value_lanes], branch_ref[:, lanes]).astype(BF)
            for k in range(4):
                for r in range(cut.width // tile):
                    at = cut.start(k) + r * tile
                    for c in range(step // lane):
                        to = pl.ds(pl.multiple_of((b * (step // lane) + c) * tile, tile), tile)
                        dwo_ref[h, k, to, head_lanes(r, lane)] = wide[
                            at : at + tile, head_lanes(c, lane)
                        ]

    moves.store(dwo_ref, dwo_any)
    load_m.wait()
    for copy in copies[2:]:
        copy.wait_recv()
    out_ref[...] = m_ref[...] + total(slice(0, rows))
    finish()
    moves.close()
    for copy in copies:
        copy.wait_send()


def gate_backward_scatter(
    branch, weight, swish, retained, column, hidden, down, mixed_t, gated, middle, heads, padded,
    cut, call,
):
    length, width = branch.shape
    rows = middle.shape[0]
    dwo = (heads, 4, width // 8, cut.width * 8)
    inputs = (branch, weight, swish, retained, column, hidden, down, mixed_t, gated, middle)
    outputs = [
        ((length, padded), BF, False),
        ((heads, length, VAL_HEAD), BF, False),
        ((width // 2, padded), BF, False),
        (dwo, BF, False),
        ((rows, width), F32, True),
    ]
    return comm_call(
        functools.partial(gate_back_scatter_kernel, heads, cut),
        [(value, False) for value in inputs],
        outputs,
        [pltpu.VMEM(v.shape, v.dtype) for v in inputs]
        + [pltpu.VMEM(shape, kind) for shape, kind, _ in outputs[:2]]
        + core_scratch(width, padded)
        + [pltpu.VMEM(dwo, BF)]
        + square_scratch(rows, width),
        6 + width // (2 * BLOCK),
        20 + 3 * length // BLOCK + width // (2 * BLOCK),
        call,
        middle.size,
        "gate_back_scatter",
    )


def retention_back_exchange_kernel(
    heads, q_any, k_any, v_any, dret_any, table_ref, cos_ref, sin_ref, mixed_any, send_any, share_any,
    dqk_any, dv_any, merged_any, full_any,
    q_ref, k_ref, v_ref, dret_ref, mixed_ref, send_ref, dqk_ref, dv_ref, dw_send, dw_twin, dw_ref,
    twin_ref, sum_ref, via_x, via_y, dv_heads, dq_sum, sends, recvs, locals_,
):
    me = lax.axis_index("seq")
    shard = lax.axis_index("fsdp")
    core = lax.rem(shard, 2)
    moves = Moves(locals_)
    load_send = moves.start(send_any, send_ref)
    loads = [
        moves.start(source, target)
        for source, target in (
            (q_any, q_ref), (k_any, k_ref), (v_any, v_ref), (dret_any, dret_ref)
        )
    ]
    load_mixed = moves.start(mixed_any, mixed_ref)
    greet_all(me, shard)
    load_send.wait()
    twin = pltpu.make_async_remote_copy(
        src_ref=send_ref.at[1 - core],
        dst_ref=twin_ref,
        send_sem=sends.at[12],
        recv_sem=recvs.at[12],
        device_id={"fsdp": shard ^ 1},
        device_id_type=MESH,
    )
    twin.start()
    passed = square_pass(share_any, full_any, sends, recvs, 0, half_rows(share_any.shape[0]))
    for copy in passed[:4]:
        copy.start()
    moves.store(share_any, full_any.at[me])
    step, wide = sum_ref.shape[1:]
    half = step // 2
    at = dqk_ref.shape[1]
    across, along, corner = me ^ 1, me ^ 2, me ^ 3

    def place(column, start, rows):
        here = pl.ds(pl.multiple_of(column * step + start, half), rows)
        return merged_any.at[here, slice(at, at + wide)]

    low, high = slice(0, half), slice(half, step)
    swaps = [
        remote(sum_ref.at[corner, low], via_x, sends, recvs, 6, across),
        remote(sum_ref.at[corner, high], via_y, sends, recvs, 7, along),
        remote(sum_ref.at[across], place(me, 0, step), sends, recvs, 8, across),
        remote(sum_ref.at[along], place(me, 0, step), sends, recvs, 9, along),
        remote(via_x, place(across, 0, half), sends, recvs, 10, along),
        remote(via_y, place(along, half, half), sends, recvs, 11, across),
    ]
    for load in loads:
        load.wait()
    for h in range(heads):
        retention_back_head(
            h, heads, q_ref, k_ref, v_ref, dret_ref, table_ref, cos_ref, sin_ref, dqk_ref,
            dv_heads.at[h], dq_sum,
        )
        if h == 0:
            twin.wait_recv()

            @pl.loop(0, 4)
            def _(k):
                sum_ref[k] = (send_ref[core, k].astype(F32) + twin_ref[k].astype(F32)).astype(BF)

            for copy in swaps[:4]:
                copy.start()
            moves.store(sum_ref.at[me], place(me, 0, step))
            pass_on(passed)
    pass_on(swaps)
    dv_ref[...] = pad_lanes([dv_heads[h] for h in range(heads)], dv_ref.shape[1])
    moves.store(dv_ref, dv_any)
    moves.store(dqk_ref, dqk_any)
    load_mixed.wait()
    finish = core_sum(
        moves, lambda b: product(mixed_ref[rows_of(b), :], dqk_ref[...]), dw_send, dw_twin, dw_ref,
        lambda t: merged_any.at[rows_of(t), slice(0, at)], sends, recvs, 13,
    )
    for copy in passed[2:] + swaps[2:]:
        copy.wait_recv()
    finish()
    moves.close()
    for copy in passed + swaps + [twin]:
        copy.wait_send()


def retention_backward_exchange(
    q, k, v, dret, table, cosine, sine, mixed_t, send, share, heads, padded, call
):
    width, length = mixed_t.shape
    qk = heads * KEY_HEAD
    inputs = (
        (q, False), (k, False), (v, False), (dret, False), (table, True), (cosine, True),
        (sine, True), (mixed_t, False), (send, False), (share, False),
    )
    staged = (q, k, v, dret, mixed_t, send)
    block = send.shape[1:]
    kept = width // 2
    return comm_call(
        functools.partial(retention_back_exchange_kernel, heads),
        inputs,
        [
            ((length, 2 * qk), BF, False),
            ((length, padded), BF, False),
            ((kept, 2 * qk + block[2]), BF, False),
            ((4,) + share.shape, BF, False),
        ],
        [pltpu.VMEM(value.shape, BF) for value in staged]
        + [
            pltpu.VMEM((length, 2 * qk), BF),
            pltpu.VMEM((length, padded), BF),
        ]
        + core_scratch(width, 2 * qk)
        + [
            pltpu.VMEM(block, BF),
            pltpu.VMEM(block, BF),
            pltpu.VMEM((block[1] // 2, block[2]), BF),
            pltpu.VMEM((block[1] // 2, block[2]), BF),
            pltpu.VMEM((heads, length, VAL_HEAD), BF),
            pltpu.VMEM((length, KEY_HEAD), F32),
        ],
        13 + kept // BLOCK,
        12 + kept // BLOCK,
        call,
        send.size // 4,
        "retention_back_exchange",
    )


def input_back_kernel(
    offsets, spare, dqk_any, dv_any, ds_any, w_any, x_any, grad_any, mixed_any, gain_ref, share_any,
    dx_ref, dwv_any, full_any, dqk_ref, dv_ref, ds_ref, w_ref, x_ref, grad_ref, mixed_ref, dwv_ref,
    parts, inbox_x, inbox_y, via_x, via_y, out_x, out_y, sends, recvs, locals_,
):
    at_value, at_swish = offsets
    me = lax.axis_index("seq")
    rows = x_ref.shape[0]
    half = rows // 2
    moves = Moves(locals_)
    spans = (slice(0, at_value), slice(at_value, at_swish), slice(at_swish, w_ref.shape[1]))
    grads = ((dqk_any, dqk_ref), (dv_any, dv_ref), (ds_any, ds_ref))
    loads = []
    for span, (source, target) in zip(spans, grads, strict=True):
        loads.append(moves.start(source, target))
        loads.append(moves.start(w_any.at[:, span], w_ref.at[:, span]))
    load_x = moves.start(x_any, x_ref)
    load_grad = moves.start(grad_any, grad_ref)
    load_mixed = moves.start(mixed_any, mixed_ref)
    greet((me ^ 1, me ^ 2))
    boxes = (inbox_x, inbox_y, via_x, via_y, out_x, out_y)
    copies, _, total = square_parts(parts, boxes, sends, recvs, 0)
    passed = square_pass(share_any, full_any, sends, recvs, 6, half_rows(share_any.shape[0]))
    passed[0].start()
    passed[1].start()
    moves.store(share_any, full_any.at[me])

    def part(k):
        here = block_rows(k, rows)
        whole = 0.0
        for n, (_, ref) in enumerate(grads):

            @pl.when(k == 3)
            def _():
                loads[2 * n].wait()
                loads[2 * n + 1].wait()

            whole = whole + times_transposed(ref[here, :], w_ref[:, spans[n]])
        parts[k] = whole.astype(BF)

    def pass_all():
        pass_on(passed)
        forward_sums(copies, parts, boxes)
        passed[2].start()
        passed[3].start()

    send_parts(part, copies, pass_all)
    load_mixed.wait()

    @pl.loop(0, dwv_ref.shape[0] // BLOCK)
    def _(b):
        here = rows_of(b)
        dwv_ref[here, :] = product(mixed_ref[here, :], dv_ref[...]).astype(BF)

    for copy in copies[2:]:
        copy.wait_recv()
    load_x.wait()
    load_grad.wait()
    terms = []
    for i in range(2):
        here = slice(i * half, (i + 1) * half)
        back, term = norm_back(x_ref[here, :].astype(F32), total(here), gain_ref[...])
        dx_ref[here, :] = grad_ref[here, :] + back
        terms.append(term)
    put_column(dwv_ref, slice(0, dwv_ref.shape[0]), spare, column_of(terms))
    moves.store(dwv_ref, dwv_any)
    for copy in passed[2:]:
        copy.wait_recv()
    moves.close()
    for copy in copies + passed:
        copy.wait_send()


def input_backward(dqk, dv, ds, weight, x, grad, mixed_t, gain, share, offsets, spare, call):
    rows, width = x.shape
    staged = (dqk, dv, ds, weight, x, grad, mixed_t)
    return comm_call(
        functools.partial(input_back_kernel, offsets, spare),
        [(value, False) for value in staged] + [(gain[None, :], True), (share, False)],
        [
            ((rows, width), F32, True),
            ((width, dv.shape[1]), BF, False),
            ((4,) + share.shape, BF, False),
        ],
        [pltpu.VMEM(value.shape, value.dtype) for value in staged[:3]]
        + [pltpu.VMEM((width, dqk.shape[1] + dv.shape[1] + ds.shape[1]), BF)]
        + [pltpu.VMEM(value.shape, value.dtype) for value in staged[4:]]
        + [pltpu.VMEM((width, dv.shape[1]), BF)]
        + square_scratch(rows, width),
        12,
        11,
        call,
        x.size + share.size,
        "input_backward",
    )


def join(pieces):
    return jnp.concatenate(pieces, axis=1) if len(pieces) > 1 else pieces[0]


def unpack_columns_kernel(width, in_ref, out_ref, gain_ref):
    count = in_ref.shape[0]
    out_ref[...] = join([in_ref[k][:, :width].astype(F32) for k in range(count)])
    last = in_ref.shape[2] - 128
    tile = sum(in_ref[k][:, last:].astype(F32) for k in range(count))
    gain_ref[...] = tile.T[width - last : width - last + 1, :]


def unpack_columns(gathered, width):
    count, rows, whole = gathered.shape
    block = min(rows, 128)
    out, gain = pl.pallas_call(
        functools.partial(unpack_columns_kernel, width),
        grid=(rows // block,),
        in_specs=[pl.BlockSpec((count, block, whole), lambda i: (0, i, 0))],
        out_specs=[
            pl.BlockSpec((block, count * width), lambda i: (i, 0)),
            pl.BlockSpec((1, block), lambda i: (0, i)),
        ],
        out_shape=[
            jax.ShapeDtypeStruct((rows, count * width), F32),
            jax.ShapeDtypeStruct((1, rows), F32),
        ],
        cost_estimate=pl.CostEstimate(flops=0, bytes_accessed=gathered.size * 4, transcendentals=0),
        name="unpack_columns",
    )(gathered)
    return out, gain[0]


def in_order(pieces):
    me = lax.axis_index("seq")
    low = [jnp.where(me % 2 == k, pieces[0], pieces[1]) for k in range(2)]
    high = [jnp.where(me % 2 == k, pieces[2], pieces[3]) for k in range(2)]
    order = [jnp.where(me < 2, low[k], high[k]) for k in range(2)]
    return order + [jnp.where(me < 2, high[k], low[k]) for k in range(2)]


def unpack_related_kernel(width, own_ref, across_ref, along_ref, corner_ref, out_ref, gain_ref):
    pieces = [ref[...].astype(F32) for ref in (own_ref, across_ref, along_ref, corner_ref)]
    last = own_ref.shape[1] - 128
    tile = sum(piece[:, last:] for piece in pieces)
    gain_ref[...] = tile.T[width - last : width - last + 1, :]
    out_ref[...] = join(in_order([piece[:, :width] for piece in pieces]))


def unpack_related(pieces, width):
    rows, whole = pieces[0].shape
    block = min(rows, 128)
    out, gain = pl.pallas_call(
        functools.partial(unpack_related_kernel, width),
        grid=(rows // block,),
        in_specs=[pl.BlockSpec((block, whole), lambda i: (i, 0))] * 4,
        out_specs=[
            pl.BlockSpec((block, 4 * width), lambda i: (i, 0)),
            pl.BlockSpec((1, block), lambda i: (0, i)),
        ],
        out_shape=[
            jax.ShapeDtypeStruct((rows, 4 * width), F32),
            jax.ShapeDtypeStruct((1, rows), F32),
        ],
        compiler_params=pltpu.CompilerParams(vmem_limit_bytes=40 * 1024 * 1024),
        cost_estimate=pl.CostEstimate(
            flops=0, bytes_accessed=pieces[0].size * 16, transcendentals=0
        ),
        name="unpack_related",
    )(*pieces)
    return out, gain[0]


def swap(values, step):
    return lax.ppermute(values, "seq", [(k, k ^ step) for k in range(4)])


def unpack_feed_kernel(cut, shards, in_ref, down_ref, gate_ref, up_ref, out_ref):
    count = in_ref.shape[0]

    @pl.when(pl.program_id(0) == 0)
    def _():
        for k in range(count):
            if cut.skip(k) < cut.width:
                at = cut.start(k)
                out_ref[at + cut.skip(k) : at + cut.width, :] = down_ref[
                    k, cut.skip(k) : cut.width, :
                ].astype(F32)

    for n, target in enumerate((gate_ref, up_ref)):
        pieces = []
        for f in range(shards):
            for k in range(count):
                at = (n * shards + f) * cut.width
                if cut.skip(k) < cut.width:
                    piece = in_ref[k][:, at + cut.skip(k) : at + cut.width]
                    pieces.append(piece.astype(F32))
        target[...] = join(pieces)


def unpack_feed(gathered, down, cut, shards):
    count, rows, whole = gathered.shape
    block = rows // 4 if rows % 64 == 0 else rows
    wide, width = shards * cut.rows, down.shape[2]
    return pl.pallas_call(
        functools.partial(unpack_feed_kernel, cut, shards),
        grid=(rows // block,),
        in_specs=[
            pl.BlockSpec((count, block, whole), lambda i: (0, i, 0)),
            pl.BlockSpec(down.shape, lambda i: (0, 0, 0)),
        ],
        out_specs=[
            pl.BlockSpec((block, wide), lambda i: (i, 0)),
            pl.BlockSpec((block, wide), lambda i: (i, 0)),
            pl.BlockSpec((cut.rows, width), lambda i: (0, 0)),
        ],
        out_shape=[
            jax.ShapeDtypeStruct((rows, wide), F32),
            jax.ShapeDtypeStruct((rows, wide), F32),
            jax.ShapeDtypeStruct((cut.rows, width), F32),
        ],
        compiler_params=pltpu.CompilerParams(vmem_limit_bytes=40 * 1024 * 1024),
        cost_estimate=pl.CostEstimate(flops=0, bytes_accessed=gathered.size * 4, transcendentals=0),
        name="unpack_feed",
    )(gathered, down)


def unpack_merged_kernel(
    cut, own_ref, across_ref, along_ref, corner_ref, query_ref, key_ref, out_ref, ordered
):
    tile, lane, count = 16, 128, 4
    wide = query_ref.shape[1] // count
    rows = own_ref.shape[0] // 4

    @pl.loop(0, 4)
    def _(i):
        here = pl.ds(pl.multiple_of(i * rows, rows), rows)
        refs = (own_ref, across_ref, along_ref, corner_ref)
        for k, piece in enumerate(in_order([ref[here, :] for ref in refs])):
            query_ref[here, head_lanes(k, wide)] = piece[:, :wide].astype(F32)
            key_ref[here, head_lanes(k, wide)] = piece[:, wide : 2 * wide].astype(F32)
            ordered[k, here, :] = piece[:, 2 * wide :]

    for k in range(count):
        for r in range(cut.skip(k) // tile, cut.width // tile):
            at = cut.start(k) + r * tile
            for c in range(out_ref.shape[1] // lane):
                out_ref[at : at + tile, head_lanes(c, lane)] = ordered[
                    k, c * tile : (c + 1) * tile, head_lanes(r, lane)
                ].astype(F32)


def unpack_merged(pieces, wide, cut, width):
    rows, whole = pieces[0].shape
    return pl.pallas_call(
        functools.partial(unpack_merged_kernel, cut),
        out_shape=(
            jax.ShapeDtypeStruct((rows, 4 * wide), F32),
            jax.ShapeDtypeStruct((rows, 4 * wide), F32),
            jax.ShapeDtypeStruct((cut.rows, width), F32),
        ),
        scratch_shapes=[pltpu.VMEM((4, rows, whole - 2 * wide), BF)],
        compiler_params=pltpu.CompilerParams(vmem_limit_bytes=40 * 1024 * 1024),
        cost_estimate=pl.CostEstimate(
            flops=0, bytes_accessed=pieces[0].size * 16, transcendentals=0
        ),
        name="unpack_merged",
    )(*pieces)


def after(values, *others, all_of=False):
    held = lax.optimization_barrier((values,) + others)
    return held if all_of else held[0]


class Cut:
    def __init__(self, rows, count):
        self.rows, self.count = rows, count
        self.width = -(-rows // (count * 16)) * 16

    def start(self, piece):
        if isinstance(piece, int):
            return min(piece * self.width, self.rows - self.width)
        return jnp.minimum(piece * self.width, self.rows - self.width)

    def skip(self, piece):
        if isinstance(piece, int):
            return min(piece * self.width - self.start(piece), self.width)
        return jnp.minimum(piece * self.width - self.start(piece), self.width)

    def assemble(self, pieces, axis):
        kept = []
        for k, piece in enumerate(pieces):
            if self.skip(k) < self.width:
                kept.append(lax.slice_in_dim(piece, self.skip(k), self.width, axis=axis))
        return jnp.concatenate(kept, axis=axis)


def pack_kernel(
    cut, qk, vd, padded, q_any, k_any, v_any, s_any, o_any, out_any,
    qk_ref, v_ref, s_ref, o_ref, values_ref, tiles_ref, sems,
):
    me = lax.axis_index("seq")
    moves = Moves(sems)
    total, wide = v_any.shape[1], v_ref.shape[1]
    base = jnp.minimum((me * vd) // 128 * 128, total - wide)
    window = pl.ds(pl.multiple_of(base, 128), wide)
    loads = [
        moves.start(v_any.at[:, window], v_ref),
        moves.start(s_any.at[:, window], s_ref),
        moves.start(o_any.at[pl.ds(pl.multiple_of(cut.start(me), 16), cut.width)], o_ref),
    ]
    own = pl.ds(pl.multiple_of(me * qk, 128), qk)
    loads += [
        moves.start(q_any.at[:, own], qk_ref.at[:, slice(0, qk)]),
        moves.start(k_any.at[:, own], qk_ref.at[:, slice(qk, 2 * qk)]),
    ]
    tile, lane = 16, 128
    loads[2].wait()
    for r in range(cut.width // tile):
        for c in range(o_ref.shape[1] // lane):
            tiles_ref[c * tile : (c + 1) * tile, head_lanes(r, lane)] = o_ref[
                r * tile : (r + 1) * tile, head_lanes(c, lane)
            ]
    at = 2 * qk + 2 * padded
    moves.store(tiles_ref, out_any.at[:, slice(at, at + tiles_ref.shape[1])])
    loads[0].wait()
    loads[1].wait()
    for k in range(4):
        shift = k * vd - min(k * vd // 128 * 128, total - wide)

        @pl.when(me == k)
        def _():
            for n, ref in enumerate((v_ref, s_ref)):
                values_ref[:, head_lanes(n, padded)] = pad_lanes([ref[:, shift : shift + vd]], padded)

    moves.store(values_ref, out_any.at[:, slice(2 * qk, at)])
    loads[3].wait()
    loads[4].wait()
    moves.store(qk_ref, out_any.at[:, slice(0, 2 * qk)])
    moves.close()


def pack(query, key, value, swish, output, cut, qk, vd, padded):
    rows, width = query.shape
    wide = min(padded + 128, value.shape[1])
    tiles = cut.width * width // rows
    return pl.pallas_call(
        functools.partial(pack_kernel, cut, qk, vd, padded),
        out_shape=jax.ShapeDtypeStruct((rows, 2 * qk + 2 * padded + tiles), BF),
        in_specs=[ANYWHERE] * 5,
        out_specs=ANYWHERE,
        scratch_shapes=[
            pltpu.VMEM((rows, 2 * qk), BF),
            pltpu.VMEM((rows, wide), BF),
            pltpu.VMEM((rows, wide), BF),
            pltpu.VMEM((cut.width, width), BF),
            pltpu.VMEM((rows, 2 * padded), BF),
            pltpu.VMEM((rows, tiles), BF),
            pltpu.SemaphoreType.DMA((8,)),
        ],
        compiler_params=pltpu.CompilerParams(vmem_limit_bytes=60 * 1024 * 1024),
        name="pack",
    )(query, key, value, swish, output)


def columns_of(weight, index, width, padded):
    piece = lax.dynamic_slice_in_dim(weight, index * width, width, axis=1)
    return jnp.pad(piece, ((0, 0), (0, padded - width)))


def on_device(
    layer_input,
    mixer_gain,
    query_weight,
    key_weight,
    value_weight,
    swish_weight,
    output_weight,
    channel_gain,
    gelu_weight,
    linear_weight,
    down_weight,
    output_cotangent,
):
    groups, local_length, width = layer_input.shape
    seq_count = lax.axis_size("seq")
    shards = lax.axis_size("fsdp")
    me = lax.axis_index("seq")
    per_device = HEADS // seq_count
    rows_count = groups * local_length
    square = seq_count == 4 and shards == 8 and rows_count % 32 == 0
    length = local_length * seq_count
    key_scale = KEY_HEAD ** (-0.5)
    qk = query_weight.shape[1] // seq_count
    vd = value_weight.shape[1] // seq_count
    vd_pad = -(-vd // 128) * 128
    hidden_units = gelu_weight.shape[1]
    own_rows = down_weight.shape[0]
    cut = Cut(own_rows, seq_count)
    ff = shards * cut.width

    def gather_rows(values):
        return lax.all_gather(values, "fsdp", axis=0, tiled=True)

    def scatter_rows(values):
        return lax.psum_scatter(values.astype(BF), "fsdp", scatter_dimension=0, tiled=True)

    def scatter_parity(values):
        groups = [list(range(parity, shards, 2)) for parity in range(2)]
        return lax.psum_scatter(
            values, "fsdp", scatter_dimension=0, tiled=True, axis_index_groups=groups
        )

    if square:
        attention_piece = pack(
            query_weight, key_weight, value_weight, swish_weight, output_weight, cut, qk, vd, vd_pad
        )
    else:
        output_pieces = gather_rows(
            lax.dynamic_slice_in_dim(output_weight, cut.start(me), cut.width, axis=0)
        )
        attention_piece = jnp.concatenate(
            [
                columns_of(query_weight, me, qk, qk),
                columns_of(key_weight, me, qk, qk),
                columns_of(value_weight, me, vd, vd_pad),
                columns_of(swish_weight, me, vd, vd_pad),
            ],
            axis=1,
        )
    attention_weight = gather_rows(attention_piece)
    column = lax.broadcasted_iota(jnp.int32, (hidden_units, ff), 0)
    slot = lax.broadcasted_iota(jnp.int32, (hidden_units, ff), 1)
    chosen = (slot // cut.width) * own_rows + cut.start(me) + slot % cut.width
    selector = (column == chosen).astype(BF)
    gate_piece = product(gelu_weight, selector).astype(BF)
    up_piece = product(linear_weight, selector).astype(BF)
    feed_piece = jnp.concatenate([gate_piece, up_piece], axis=1)
    down_piece = lax.dynamic_slice_in_dim(down_weight, cut.start(me), cut.width, axis=0)
    gains = lax.all_gather(jnp.stack([mixer_gain, channel_gain]), "fsdp", axis=1, tiled=True)
    mixer_scale, channel_scale = gains[0].astype(F32), gains[1].astype(F32)

    local_input = layer_input.reshape(rows_count, width)
    upstream = output_cotangent.reshape(rows_count, width)

    upstream = after(upstream, gains)

    def whole(values, call):
        gathered = gather_seq(values, call)
        return gathered.reshape(length * groups, width)

    input_full = whole(local_input, 0)
    upstream_full = whole(after(upstream, input_full), 1)
    inputs = local_input.astype(F32)

    blocks = shards // seq_count
    mixed_low, mixed_turned = norm_and_turn(input_full, mixer_scale)
    head_ids = me * per_device + jnp.arange(per_device, dtype=jnp.int32)
    table, table_back = decay_tables(head_ids, length)
    cosine, sine = rotation_tables(length, KEY_HEAD // 2)
    feed_weight = gather_rows(after(feed_piece, upstream_full))

    offsets = (qk, 2 * qk, 2 * qk + vd_pad)
    attention_weight = after(
        attention_weight, mixed_low, mixed_turned, table, table_back, cosine, feed_piece
    )
    if square:
        query_low, key_low, value_low, swish_pre, retained, gated_low, output_full = (
            retention_exchange(
                mixed_low, attention_weight, cosine, sine, table, per_device, offsets, cut, 2
            )
        )
    else:
        query_low, key_low, value_low, swish_pre, retained, gated_low = retention_forward(
            mixed_low, attention_weight, cosine, sine, table, per_device, offsets
        )
        swapped = exchange_seq(
            output_pieces.reshape(seq_count, blocks, cut.width, width), 2
        )
        output_full = jnp.concatenate(
            [
                cut.assemble([swapped[piece, block] for piece in range(seq_count)], 0)
                for block in range(blocks)
            ],
            axis=0,
        )

    kept_rows = lax.broadcasted_iota(jnp.int32, down_piece.shape, 0) >= cut.skip(me)
    down_full = gather_rows(after(jnp.where(kept_rows, down_piece, jnp.zeros_like(down_piece)), gated_low))
    if square:
        middle, channel_own = project_and_norm(
            gated_low, output_full, local_input, channel_scale, 3
        )
        both_pre, hidden_low, down_term, channel_full = feed_forward_gather(
            channel_own, feed_weight, upstream_full, 4
        )
        down_share = scatter_rows(down_term)
        middle_grad, channel_term, branch_own, feed_term = feed_back_scatter(
            after(upstream_full, down_term), both_pre, feed_weight, down_full, channel_full,
            middle, upstream, channel_scale, 6,
        )
        feed_share = scatter_parity(feed_term)
        branch_full = whole(branch_own, 7)
    else:
        middle = inputs + scatter_seq(product(gated_low, output_full).astype(BF), 3)
        channel_full = whole(normalize(middle, channel_scale).astype(BF), 4)
        gate_pre, up_pre, hidden_low = feed_forward(channel_full, feed_weight)
        down_share = scatter_rows(transposed_times(hidden_low, upstream_full).astype(BF))
        feed_low_grad, channel_part, hidden_part = feed_backward(
            upstream_full, gate_pre, up_pre, hidden_low, feed_weight, down_full
        )
        feed_share = scatter_rows(transposed_times(channel_full, feed_low_grad).astype(BF))
        middle_local, channel_terms = norm_back(
            middle, scatter_seq(channel_part, 6), channel_scale
        )
        channel_term = jnp.sum(channel_terms, axis=0)
        middle_grad = upstream.astype(F32) + middle_local
        branch_full = whole(middle_grad.astype(BF), 7)

    at_value, at_swish = 2 * qk, 2 * qk + vd_pad
    if square:
        swish_grad, retained_grad, swish_term, output_send, layer_output = gate_backward_scatter(
            after(branch_full, down_share), output_full, swish_pre, retained,
            channel_term, hidden_low, down_full, mixed_turned, gated_low, middle,
            per_device, vd_pad, cut, 5,
        )
        swish_share = scatter_parity(swish_term)
        key_grad, value_grad, merged_term, down_all = retention_backward_exchange(
            query_low, key_low, value_low, after(retained_grad, feed_share), table_back, cosine, sine,
            mixed_turned, output_send, down_share, per_device, vd_pad, 8,
        )
        merged_share = scatter_parity(merged_term)
        input_gradient, value_term, feed_all = input_backward(
            key_grad, value_grad, swish_grad, attention_weight, local_input, middle_grad,
            mixed_turned, mixer_scale, feed_share, (at_value, at_swish), vd, 9,
        )
    else:
        swish_grad, retained_grad = gate_backward(
            branch_full, output_full, swish_pre, retained, per_device, vd_pad
        )
        spare = lax.broadcasted_iota(jnp.int32, (width, vd_pad), 1) == vd
        swish_term = transposed_times(mixed_low, swish_grad)
        swish_term = jnp.where(spare, channel_term[:, None], swish_term).astype(BF)
        swish_share = scatter_rows(swish_term)
        layer_output = middle + scatter_seq(hidden_part, 5)
        key_grad, value_grad = retention_backward(
            query_low, key_low, value_low, retained_grad, table_back, cosine, sine, per_device, vd_pad
        )
        key_term = transposed_times(mixed_low, key_grad).astype(BF)
        key_share = scatter_rows(key_term)
        mixed_part = (
            times_transposed(key_grad, attention_weight[:, :at_value])
            + times_transposed(value_grad, attention_weight[:, at_value:at_swish])
            + times_transposed(swish_grad, attention_weight[:, at_swish:])
        )
        input_local, mixer_terms = norm_back(
            inputs, scatter_seq(mixed_part.astype(BF), 9), mixer_scale
        )
        mixer_term = jnp.sum(mixer_terms, axis=0)
        input_gradient = middle_grad + input_local
        output_term = transposed_times(gated_low, branch_full).astype(BF)
        output_term = output_term.reshape(blocks, own_rows, width)
        output_send = jnp.stack(
            [
                lax.slice_in_dim(output_term, cut.start(k), cut.start(k) + cut.width, axis=1)
                for k in range(seq_count)
            ]
        )
        output_swapped = exchange_seq(output_send, 8)
        output_share = scatter_rows(output_swapped.reshape(shards * cut.width, width))
        value_term = transposed_times(mixed_low, value_grad)
        value_term = jnp.where(spare, mixer_term[:, None], value_term).astype(BF)
    input_gradient = input_gradient.astype(BF).reshape(groups, local_length, width)
    value_share = scatter_rows(value_term)

    layer_output = layer_output.astype(BF).reshape(groups, local_length, width)
    if square:
        swish_all = gather_seq(swish_share, 13)
        merged_share = after(merged_share, swish_all)
        second = (swap(merged_share, 1), swap(merged_share, 2))
        gelu_gradient, linear_gradient, down_gradient = unpack_feed(
            after(feed_all, swish_all, layer_output, input_gradient), down_all, cut, shards
        )
        swish_gradient, channel_own_gradient = unpack_columns(swish_all, vd)
        second, gelu_gradient, swish_gradient = after(
            second, gelu_gradient, swish_gradient, all_of=True
        )

        def corners(pair):
            half = pair[0].shape[0] // 2
            return swap(pair[0][:half], 2), swap(pair[1][half:], 1)

        def pieces(own, pair, halves):
            return (own,) + tuple(pair) + (jnp.concatenate(halves, axis=0),)

        second_corner = corners(second)
        second_corner, value_share = after(second_corner, value_share, all_of=True)
        third = (swap(value_share, 1), swap(value_share, 2))
        query_gradient, key_gradient, output_gradient = unpack_merged(
            pieces(merged_share, second, second_corner), qk, cut, width
        )
        third, query_gradient = after(third, query_gradient, all_of=True)
        value_gradient, mixer_own_gradient = unpack_related(
            pieces(value_share, third, corners(third)), vd
        )
    else:
        down_all = gather_seq(down_share, 10)
        feed_all = gather_seq(after(feed_share, down_all), 11)
        swish_all = gather_seq(after(swish_share, feed_all), 13)
        output_all = gather_seq(after(output_share, swish_all), 12)
        key_all = gather_seq(after(key_share, output_all), 15)
        value_all = gather_seq(after(value_share, key_all), 14)
        swish_gradient, channel_own_gradient = unpack_columns(swish_all, vd)
        output_gradient = cut.assemble([output_all[k] for k in range(seq_count)], 0).astype(F32)
        gelu_gradient, linear_gradient, down_gradient = unpack_feed(
            feed_all, down_all, cut, shards
        )
        query_gradient, key_gradient = (
            jnp.concatenate(
                [key_all[k][:, at : at + qk] for k in range(seq_count)], axis=1
            ).astype(F32)
            for at in (0, qk)
        )
        value_gradient, mixer_own_gradient = unpack_columns(value_all, vd)
    return (
        layer_output,
        input_gradient,
        mixer_own_gradient,
        query_gradient,
        key_gradient,
        value_gradient,
        swish_gradient,
        output_gradient,
        channel_own_gradient,
        gelu_gradient,
        linear_gradient,
        down_gradient,
    )


def solution(mesh):
    tokens, rows, vector = P("fsdp", "seq", None), P("fsdp", None), P("fsdp")
    return jax.shard_map(
        on_device,
        mesh=mesh,
        in_specs=(
            tokens, vector, rows, rows, rows, rows, rows, vector, rows, rows, rows, tokens,
        ),
        out_specs=(
            tokens, tokens, vector, rows, rows, rows, rows, rows, vector, rows, rows, rows,
        ),
        check_vma=False,
    )
```

```python
import functools
import math

import jax
import jax.numpy as jnp
from jax import lax
from jax.experimental import pallas as pl
from jax.experimental.pallas import tpu as pltpu
from jax.sharding import PartitionSpec as P

HEADS = 8
KEY_HEAD = 256
VAL_HEAD = 432
EPSILON = 1e-05
MESH = pl.DeviceIdType.MESH
BF = jnp.bfloat16
F32 = jnp.float32
IN_VMEM = pl.BlockSpec(memory_space=pltpu.VMEM)
ANYWHERE = pl.BlockSpec(memory_space=pl.ANY)


def product(left, right):
    return jnp.dot(left, right, preferred_element_type=F32)


def times_transposed(left, right):
    return lax.dot_general(left, right, (((1,), (1,)), ((), ())), preferred_element_type=F32)


def transposed_times(left, right):
    return lax.dot_general(left, right, (((0,), (0,)), ((), ())), preferred_element_type=F32)


def normalize(values, gain):
    centered = values - jnp.mean(values, axis=-1, keepdims=True)
    spread = lax.rsqrt(jnp.mean(centered * centered, axis=-1, keepdims=True) + EPSILON)
    return centered * spread * gain


def rotation_tables(length, half_width):
    rates = jnp.exp(-math.log(10000.0) * jnp.arange(half_width, dtype=F32) / (half_width - 1))
    turned = jnp.arange(length, dtype=F32)[:, None] * rates[None, :]
    return (jnp.cos(turned), jnp.sin(turned))


def pad_lanes(pieces, width):
    have = sum(piece.shape[1] for piece in pieces)
    if have < width:
        pieces = pieces + [jnp.zeros((pieces[0].shape[0], width - have), pieces[0].dtype)]
    return jnp.concatenate(pieces, axis=1) if len(pieces) > 1 else pieces[0]


def rotate_pair(values, cosine, sine, back=False):
    half = KEY_HEAD // 2
    first, second = values[:, :half], values[:, half:]
    if back:
        return jnp.concatenate([first * cosine + second * sine, second * cosine - first * sine], 1)
    return jnp.concatenate([first * cosine - second * sine, second * cosine + first * sine], 1)


BLOCK = 256


def decay_tables(head_ids, length):
    rates = jnp.log1p(-jnp.exp2(-5.0 - head_ids.astype(F32)))[:, None, None]
    short = jnp.arange(BLOCK, dtype=jnp.int32)
    long = jnp.arange(2 * length - BLOCK, dtype=jnp.int32)

    def decay(gap):
        far = jnp.exp(jnp.maximum(gap, 0).astype(F32)[None] * rates)
        return jnp.where(gap[None] >= 0, far, 0.0)

    by_row = decay(length - BLOCK + short[:, None] - long[None, :])
    by_column = decay(long[:, None] - (length - BLOCK) - short[None, :])
    return by_row, by_column


def norm_parts(values):
    centered = values - jnp.mean(values, axis=-1, keepdims=True)
    variance = jnp.mean(centered * centered, axis=-1, keepdims=True)
    factor = lax.rsqrt(jnp.maximum(variance, 1.0))
    return centered * factor, factor, variance > 1.0


def rows_of(block):
    return pl.ds(pl.multiple_of(block * BLOCK, BLOCK), BLOCK)


def head_lanes(head, width):
    return slice(head * width, (head + 1) * width)


class Moves:
    def __init__(self, sems):
        self.sems, self.used, self.open = sems, 0, []

    def start(self, source, target):
        copy = pltpu.make_async_copy(source, target, self.sems.at[self.used])
        self.used += 1
        copy.start()
        return copy

    def store(self, source, target):
        self.open.append(self.start(source, target))

    def close(self):
        for copy in self.open:
            copy.wait()


def norm_kernel(x_ref, gain_ref, out_ref, turned_ref):
    normed = normalize(x_ref[...].astype(F32), gain_ref[...])
    out_ref[...] = normed.astype(BF)
    turned_ref[...] = normed.T.astype(BF)


def norm_and_turn(x, gain):
    length, width = x.shape
    return pl.pallas_call(
        norm_kernel,
        grid=(length // BLOCK,),
        in_specs=[
            pl.BlockSpec((BLOCK, width), lambda i: (i, 0)),
            pl.BlockSpec((1, width), lambda i: (0, 0)),
        ],
        out_specs=[
            pl.BlockSpec((BLOCK, width), lambda i: (i, 0)),
            pl.BlockSpec((width, BLOCK), lambda i: (0, i)),
        ],
        out_shape=[
            jax.ShapeDtypeStruct((length, width), BF),
            jax.ShapeDtypeStruct((width, length), BF),
        ],
        compiler_params=pltpu.CompilerParams(vmem_limit_bytes=32 * 1024 * 1024),
        name="norm_and_turn",
    )(x, gain[None, :])


class Series:
    def __init__(self, moves, count, ends):
        self.sems, self.first, self.count, self.ends = moves.sems, moves.used, count, ends
        moves.used += count

    def copy(self, i):
        return pltpu.make_async_copy(*self.ends(i), self.sems.at[self.first + i])

    def start_all(self):
        for i in range(self.count):
            self.copy(i).start()
        return self

    def wait_all(self):
        for i in range(self.count):
            self.copy(i).wait()


def by_block(moves, count, source, target, rows=BLOCK):
    def ends(i):
        here = pl.ds(i * rows if isinstance(i, int) else pl.multiple_of(i * rows, rows), rows)
        if len(source.shape) == 3:
            return source.at[:, here], target.at[:, here]
        return source.at[here], target.at[here]

    return Series(moves, count, ends)


def retention_kernel(
    heads, offsets, mixed_any, w_any, cos_ref, sin_ref, table_ref,
    q_any, k_any, v_any, swish_any, retained_any, gated_any,
    mixed_ref, w_ref, q_ref, k_ref, v_ref, swish_ref, retained_ref, gated_ref, sems,
    between=None,
):
    at_key, at_value, at_swish = offsets
    length = mixed_ref.shape[0]
    blocks = length // BLOCK
    moves = sems if isinstance(sems, Moves) else Moves(sems)
    spans = (
        slice(0, at_key), slice(at_key, at_value), slice(at_value, at_swish),
        slice(at_swish, w_ref.shape[1]),
    )
    loads = by_block(moves, blocks, mixed_any, mixed_ref)
    loads.copy(0).start()
    weights = [moves.start(w_any.at[:, span], w_ref.at[:, span]) for span in spans]
    for i in range(1, blocks):
        loads.copy(i).start()
    stores = [
        by_block(moves, blocks, source, target)
        for source, target in (
            (q_ref, q_any), (k_ref, k_any), (v_ref, v_any), (swish_ref, swish_any),
            (retained_ref, retained_any), (gated_ref, gated_any),
        )
    ]
    k_ref[...] = jnp.zeros_like(k_ref)
    v_ref[...] = jnp.zeros_like(v_ref)
    if between is not None:
        between(-1)

    @pl.loop(0, blocks)
    def _(i):
        rows = rows_of(i)
        loads.copy(i).wait()
        mixed = mixed_ref[rows, :]
        cosine, sine = cos_ref[rows, :], sin_ref[rows, :]

        def projected(n):
            @pl.when(i == 0)
            def _():
                weights[n].wait()

            return product(mixed, w_ref[:, spans[n]])

        for n, (target, scale) in enumerate(((q_ref, 1.0), (k_ref, KEY_HEAD**-0.5))):
            pre = projected(n)
            for h in range(heads):
                lanes = head_lanes(h, KEY_HEAD)
                turned = rotate_pair(pre[:, lanes], cosine, sine)
                target[rows, lanes] = (turned * scale if n else turned).astype(BF)
        value = projected(2)
        for h in range(heads):
            v_ref[h, rows, :] = value[:, head_lanes(h, VAL_HEAD)].astype(BF)
        swish_ref[rows, :] = projected(3)[:, : heads * VAL_HEAD]
        gated = []
        for h in range(heads):
            lanes = head_lanes(h, KEY_HEAD)
            scores = times_transposed(q_ref[rows, lanes], k_ref[:, lanes])
            decay = table_ref[
                h, :, pl.ds(pl.multiple_of((blocks - 1 - i) * BLOCK, BLOCK), length)
            ]
            retained = product((scores * decay).astype(BF), v_ref[h]).astype(BF)
            retained_ref[h, rows, :] = retained
            unit, _, _ = norm_parts(retained.astype(F32))
            s = swish_ref[rows, head_lanes(h, VAL_HEAD)]
            gated.append((s * jax.nn.sigmoid(s) * unit).astype(BF))
        gated_ref[rows, :] = jnp.concatenate(gated, axis=1) if heads > 1 else gated[0]
        for store in stores:
            store.copy(i).start()
        if between is not None:
            between(i)

    for store in stores:
        store.wait_all()


def retention_outputs(length, heads):
    qk, vd = heads * KEY_HEAD, heads * VAL_HEAD
    return (
        ((length, qk), BF),
        ((length, qk), BF),
        ((heads, length, VAL_HEAD), BF),
        ((length, vd), F32),
        ((heads, length, VAL_HEAD), BF),
        ((length, vd), BF),
    )


def retention_forward(mixed, weight, cosine, sine, table, heads, offsets):
    length, width = mixed.shape
    outputs = retention_outputs(length, heads)
    blocks = length // BLOCK
    return pl.pallas_call(
        functools.partial(retention_kernel, heads, offsets),
        out_shape=tuple(jax.ShapeDtypeStruct(*out) for out in outputs),
        in_specs=[ANYWHERE, ANYWHERE, IN_VMEM, IN_VMEM, IN_VMEM],
        out_specs=(ANYWHERE,) * 6,
        scratch_shapes=[pltpu.VMEM(mixed.shape, BF), pltpu.VMEM(weight.shape, BF)]
        + [pltpu.VMEM(*out) for out in outputs]
        + [pltpu.SemaphoreType.DMA((4 + 7 * blocks,))],
        compiler_params=pltpu.CompilerParams(vmem_limit_bytes=60 * 1024 * 1024),
        cost_estimate=pl.CostEstimate(
            flops=30_000_000_000, bytes_accessed=0, transcendentals=0
        ),
        name="retention",
    )(mixed, weight, cosine, sine, table)


def gate_back_rows(heads, rows, branch, w_ref, swish_ref, retained_ref, dswish_ref, dret_ref):
    gated_grad = times_transposed(branch, w_ref[...])
    swish_parts = []
    for h in range(heads):
        lanes = head_lanes(h, VAL_HEAD)
        grad, s = gated_grad[:, lanes], swish_ref[rows, lanes]
        gate = jax.nn.sigmoid(s)
        unit, factor, above = norm_parts(retained_ref[h, rows, :].astype(F32))
        swish_parts.append((grad * unit * (gate * (1.0 + s * (1.0 - gate)))).astype(BF))
        g = grad * (s * gate)
        along = jnp.where(above, jnp.mean(g * unit, axis=-1, keepdims=True), 0.0)
        back = factor * (g - jnp.mean(g, axis=-1, keepdims=True) - unit * along)
        dret_ref[h, rows, :] = back.astype(BF)
    dswish_ref[rows, :] = pad_lanes(swish_parts, dswish_ref.shape[1])


def gate_back_kernel(heads, branch_ref, w_ref, swish_ref, retained_ref, dswish_ref, dret_ref):
    @pl.loop(0, branch_ref.shape[0] // BLOCK)
    def _(i):
        rows = rows_of(i)
        gate_back_rows(
            heads, rows, branch_ref[rows, :], w_ref, swish_ref, retained_ref, dswish_ref, dret_ref
        )


def gate_backward(branch, weight, swish, retained, heads, padded):
    length = branch.shape[0]
    return pl.pallas_call(
        functools.partial(gate_back_kernel, heads),
        out_shape=(
            jax.ShapeDtypeStruct((length, padded), BF),
            jax.ShapeDtypeStruct((heads, length, VAL_HEAD), BF),
        ),
        compiler_params=pltpu.CompilerParams(vmem_limit_bytes=48 * 1024 * 1024),
        name="gate_back",
    )(branch, weight, swish, retained)


def retention_back_head(
    h, heads, q_ref, k_ref, v_ref, dret_ref, table_ref, cos_ref, sin_ref, dqk_ref, dv_head,
    dq_sum,
):
    length = q_ref.shape[0]
    blocks = length // BLOCK
    lanes = head_lanes(h, KEY_HEAD)
    dq_sum[...] = jnp.zeros_like(dq_sum)

    @pl.loop(0, blocks)
    def _(j):
        there = rows_of(j)
        query, grad = q_ref[:, lanes], dret_ref[h]
        key, value = k_ref[there, lanes], v_ref[h, there, :]
        decay = table_ref[h, pl.ds(pl.multiple_of((blocks - 1 - j) * BLOCK, BLOCK), length), :]
        weights = (times_transposed(query, key) * decay).astype(BF)
        score = (times_transposed(grad, value) * decay).astype(BF)
        dq_sum[...] += product(score, key)
        dk = transposed_times(score, query).astype(BF).astype(F32)
        dk = rotate_pair(dk, cos_ref[there, :], sin_ref[there, :], back=True)
        dqk_ref[there, head_lanes(heads + h, KEY_HEAD)] = (dk * (KEY_HEAD**-0.5)).astype(BF)
        dv_head[there, :] = transposed_times(weights, grad).astype(BF)

    @pl.loop(0, blocks)
    def _(i):
        rows = rows_of(i)
        dq = dq_sum[rows, :].astype(BF).astype(F32)
        dqk_ref[rows, lanes] = rotate_pair(
            dq, cos_ref[rows, :], sin_ref[rows, :], back=True
        ).astype(BF)


def retention_back_kernel(
    heads, q_ref, k_ref, v_ref, dret_ref, table_ref, cos_ref, sin_ref, dqk_ref, dv_ref,
    dv_heads, dq_sum,
):
    for h in range(heads):
        retention_back_head(
            h, heads, q_ref, k_ref, v_ref, dret_ref, table_ref, cos_ref, sin_ref, dqk_ref,
            dv_heads.at[h], dq_sum,
        )
    dv_ref[...] = pad_lanes([dv_heads[h] for h in range(heads)], dv_ref.shape[1])


def retention_backward(q, k, v, dret, table, cosine, sine, heads, padded):
    length = q.shape[0]
    qk = heads * KEY_HEAD
    return pl.pallas_call(
        functools.partial(retention_back_kernel, heads),
        out_shape=(
            jax.ShapeDtypeStruct((length, 2 * qk), BF),
            jax.ShapeDtypeStruct((length, padded), BF),
        ),
        scratch_shapes=[
            pltpu.VMEM((heads, length, VAL_HEAD), BF),
            pltpu.VMEM((length, KEY_HEAD), F32),
        ],
        compiler_params=pltpu.CompilerParams(vmem_limit_bytes=48 * 1024 * 1024),
        name="retention_back",
    )(q, k, v, dret, table, cosine, sine)


def transfer_cost(elements):
    return pl.CostEstimate(flops=0, bytes_accessed=elements * 240, transcendentals=0)


def greet(peers):
    barrier = pltpu.get_barrier_semaphore()
    for peer in peers:
        pl.semaphore_signal(barrier, inc=1, device_id={"seq": peer}, device_id_type=MESH)
    pl.semaphore_wait(barrier, len(peers))


def remote(source, target, sends, recvs, k, to):
    return pltpu.make_async_remote_copy(
        src_ref=source,
        dst_ref=target,
        send_sem=sends.at[k],
        recv_sem=recvs.at[k],
        device_id={"seq": to},
        device_id_type=MESH,
    )


def gather_square_kernel(x_ref, o_ref, sends, recvs, local):
    me = lax.axis_index("seq")
    across, along = me ^ 1, me ^ 2
    half = x_ref.shape[0] // 2
    greet((across, along))
    own = pltpu.make_async_copy(x_ref, o_ref.at[me], local)
    own.start()

    def part(ref, i):
        return ref.at[pl.ds(i * half, half)]

    first = (
        remote(part(x_ref, 0), part(o_ref.at[me], 0), sends, recvs, 0, across),
        remote(part(x_ref, 1), part(o_ref.at[me], 1), sends, recvs, 1, along),
        remote(part(x_ref, 1), part(o_ref.at[me], 1), sends, recvs, 2, across),
        remote(part(x_ref, 0), part(o_ref.at[me], 0), sends, recvs, 3, along),
    )
    for copy in first:
        copy.start()
    first[0].wait_recv()
    on_along = remote(part(o_ref.at[across], 0), part(o_ref.at[across], 0), sends, recvs, 4, along)
    on_along.start()
    first[1].wait_recv()
    on_across = remote(part(o_ref.at[along], 1), part(o_ref.at[along], 1), sends, recvs, 5, across)
    on_across.start()
    first[2].wait_recv()
    first[3].wait_recv()
    on_along.wait_recv()
    on_across.wait_recv()
    for copy in first + (on_along, on_across):
        copy.wait_send()
    own.wait()


def gather_kernel(count, x_ref, o_ref, sends, recvs, local):
    me = lax.axis_index("seq")
    peers = [lax.rem(me + step, count) for step in range(1, count)]
    greet(peers)
    own = pltpu.make_async_copy(x_ref, o_ref.at[me], local)
    own.start()
    copies = [remote(x_ref, o_ref.at[me], sends, recvs, k, to) for k, to in enumerate(peers)]
    for copy in copies:
        copy.start()
    for copy in copies:
        copy.wait()
    own.wait()


def gather_seq(values, call):
    count = lax.axis_size("seq")
    square = count == 4 and values.shape[0] % 32 == 0
    body = gather_square_kernel if square else functools.partial(gather_kernel, count)
    copies = 6 if square else count - 1
    return pl.pallas_call(
        body,
        out_shape=jax.ShapeDtypeStruct((count,) + values.shape, values.dtype),
        in_specs=[pl.BlockSpec(memory_space=pl.ANY)],
        out_specs=pl.BlockSpec(memory_space=pl.ANY),
        scratch_shapes=[
            pltpu.SemaphoreType.DMA((copies,)),
            pltpu.SemaphoreType.DMA((copies,)),
            pltpu.SemaphoreType.DMA,
        ],
        compiler_params=pltpu.CompilerParams(collective_id=call, has_side_effects=True),
        cost_estimate=transfer_cost(values.size),
        name=f"gather_seq_{call}",
    )(values)


def gather_two_kernel(a_ref, b_ref, a_out, b_out, sends, recvs, locals_):
    me = lax.axis_index("seq")
    greet((me ^ 1, me ^ 2))
    moves = Moves(locals_)
    moves.store(a_ref, a_out.at[me])
    moves.store(b_ref, b_out.at[me])
    both = [
        square_pass(ref, out, sends, recvs, first, half_rows(ref.shape[0]))
        for ref, out, first in ((a_ref, a_out, 0), (b_ref, b_out, 6))
    ]
    for copies in both:
        for copy in copies[:4]:
            copy.start()
    for copies in both:
        pass_on(copies)
    for copies in both:
        for copy in copies[2:]:
            copy.wait_recv()
    moves.close()
    for copies in both:
        for copy in copies:
            copy.wait_send()


def gather_two(a, b, call):
    return comm_call(
        gather_two_kernel,
        [(a, False), (b, False)],
        [((4,) + a.shape, BF, False), ((4,) + b.shape, BF, False)],
        [],
        12,
        2,
        call,
        a.size + b.size,
        "gather_two",
    )


def exchange_kernel(count, x_ref, o_ref, sends, recvs, local):
    me = lax.axis_index("seq")
    peers = [lax.rem(me + step, count) for step in range(1, count)]
    greet(peers)
    own = pltpu.make_async_copy(x_ref.at[me], o_ref.at[me], local)
    own.start()
    copies = [remote(x_ref.at[to], o_ref.at[me], sends, recvs, k, to) for k, to in enumerate(peers)]
    for copy in copies:
        copy.start()
    for copy in copies:
        copy.wait()
    own.wait()


def exchange_seq(values, call):
    count = lax.axis_size("seq")
    return pl.pallas_call(
        functools.partial(exchange_kernel, count),
        out_shape=jax.ShapeDtypeStruct(values.shape, values.dtype),
        in_specs=[pl.BlockSpec(memory_space=pl.ANY)],
        out_specs=pl.BlockSpec(memory_space=pl.ANY),
        scratch_shapes=[
            pltpu.SemaphoreType.DMA((count - 1,)),
            pltpu.SemaphoreType.DMA((count - 1,)),
            pltpu.SemaphoreType.DMA,
        ],
        compiler_params=pltpu.CompilerParams(collective_id=call, has_side_effects=True),
        cost_estimate=transfer_cost(values.size),
        name=f"exchange_seq_{call}",
    )(values)


def scatter_square_kernel(p_ref, o_ref, inbox_x, inbox_y, via_x, via_y, out_x, out_y, sends, recvs):
    me = lax.axis_index("seq")
    across, along, corner = me ^ 1, me ^ 2, me ^ 3
    half = p_ref.shape[1] // 2
    low, high = pl.ds(0, half), pl.ds(half, half)
    greet((across, along))
    first = (
        remote(p_ref.at[corner, low], via_x, sends, recvs, 0, across),
        remote(p_ref.at[corner, high], via_y, sends, recvs, 1, along),
        remote(p_ref.at[across, low], inbox_x.at[low], sends, recvs, 2, across),
        remote(p_ref.at[along, high], inbox_y.at[high], sends, recvs, 3, along),
    )
    for copy in first:
        copy.start()
    first[0].wait_recv()
    out_y[...] = (p_ref[along, :half].astype(F32) + via_x[...].astype(F32)).astype(BF)
    to_along = remote(out_y, inbox_y.at[low], sends, recvs, 4, along)
    to_along.start()
    first[1].wait_recv()
    out_x[...] = (p_ref[across, half:].astype(F32) + via_y[...].astype(F32)).astype(BF)
    to_across = remote(out_x, inbox_x.at[high], sends, recvs, 5, across)
    to_across.start()
    first[2].wait_recv()
    first[3].wait_recv()
    to_along.wait_recv()
    to_across.wait_recv()
    o_ref[...] = (
        p_ref[me].astype(F32) + inbox_x[...].astype(F32) + inbox_y[...].astype(F32)
    )
    for copy in first + (to_along, to_across):
        copy.wait_send()


def scatter_kernel(count, p_ref, o_ref, inbox, sends, recvs):
    me = lax.axis_index("seq")
    peers = [lax.rem(me + step, count) for step in range(1, count)]
    greet(peers)
    copies = [remote(p_ref.at[to], inbox.at[k], sends, recvs, k, to) for k, to in enumerate(peers)]
    for copy in copies:
        copy.start()
    total = p_ref[me].astype(F32)
    for k, copy in enumerate(copies):
        copy.wait_recv()
        total = total + inbox[k].astype(F32)
    o_ref[...] = total
    for copy in copies:
        copy.wait_send()


def scatter_seq(parts, call):
    count = lax.axis_size("seq")
    rows, width = parts.shape[0] // count, parts.shape[1]
    parts = parts.reshape(count, rows, width)
    if count == 4 and rows % 32 == 0:
        body = scatter_square_kernel
        scratch = [pltpu.VMEM((rows, width), BF)] * 2 + [pltpu.VMEM((rows // 2, width), BF)] * 4
        copies = 6
    else:
        body = functools.partial(scatter_kernel, count)
        scratch = [pltpu.VMEM((count - 1, rows, width), BF)]
        copies = count - 1
    return pl.pallas_call(
        body,
        out_shape=jax.ShapeDtypeStruct((rows, width), F32),
        in_specs=[pl.BlockSpec(memory_space=pltpu.VMEM)],
        out_specs=pl.BlockSpec(memory_space=pltpu.VMEM),
        scratch_shapes=scratch
        + [pltpu.SemaphoreType.DMA((copies,)), pltpu.SemaphoreType.DMA((copies,))],
        compiler_params=pltpu.CompilerParams(
            collective_id=call, has_side_effects=True, vmem_limit_bytes=32 * 1024 * 1024
        ),
        cost_estimate=transfer_cost(rows * width),
        name=f"scatter_seq_{call}",
    )(parts)


def feed_forward_kernel(ff, x_ref, w_ref, gate_ref, up_ref, hidden_ref):
    both = product(x_ref[...], w_ref[...])
    gate, up = both[:, :ff], both[:, ff:]
    gate_ref[...] = gate
    up_ref[...] = up
    hidden_ref[...] = (gate * (0.5 + 0.5 * lax.erf(gate * math.sqrt(0.5))) * up).astype(BF)


def feed_back_kernel(
    ff, c_ref, gate_ref, up_ref, hidden_ref, w_ref, down_ref, both_ref, part_ref, out_ref
):
    gate, up = gate_ref[...], up_ref[...]
    out_ref[...] = product(hidden_ref[...], down_ref[...]).astype(BF)
    hidden_grad = times_transposed(c_ref[...], down_ref[...])
    bell = 0.5 + 0.5 * lax.erf(gate * math.sqrt(0.5))
    slope = bell + gate * (math.sqrt(0.5 / math.pi) * jnp.exp(-0.5 * gate * gate))
    both = jnp.concatenate([hidden_grad * up * slope, hidden_grad * (gate * bell)], axis=1)
    both = both.astype(BF)
    both_ref[...] = both
    part_ref[...] = times_transposed(both, w_ref[...]).astype(BF)


def by_rows(block, width):
    return pl.BlockSpec((block, width), lambda i: (i, 0))


def kept(shape):
    return pl.BlockSpec(shape, lambda i: (0, 0), pipeline_mode=pl.Buffered(1))


FEED_BLOCK = 256


def feed_forward(x, weight):
    length, width = x.shape
    ff = weight.shape[1] // 2
    return pl.pallas_call(
        functools.partial(feed_forward_kernel, ff),
        grid=(length // FEED_BLOCK,),
        in_specs=[by_rows(FEED_BLOCK, width), kept(weight.shape)],
        out_specs=[by_rows(FEED_BLOCK, ff)] * 3,
        out_shape=(
            jax.ShapeDtypeStruct((length, ff), F32),
            jax.ShapeDtypeStruct((length, ff), F32),
            jax.ShapeDtypeStruct((length, ff), BF),
        ),
        compiler_params=pltpu.CompilerParams(vmem_limit_bytes=48 * 1024 * 1024),
        cost_estimate=pl.CostEstimate(
            flops=4 * length * width * ff, bytes_accessed=weight.size * 4, transcendentals=0
        ),
        name="feed_forward",
    )(x, weight)


def feed_backward(cotangent, gate, up, hidden, weight, down):
    length, width = cotangent.shape
    ff = weight.shape[1] // 2
    return pl.pallas_call(
        functools.partial(feed_back_kernel, ff),
        grid=(length // FEED_BLOCK,),
        in_specs=[by_rows(FEED_BLOCK, width)]
        + [by_rows(FEED_BLOCK, ff)] * 3
        + [kept(weight.shape), kept(down.shape)],
        out_specs=[
            by_rows(FEED_BLOCK, 2 * ff),
            by_rows(FEED_BLOCK, width),
            by_rows(FEED_BLOCK, width),
        ],
        out_shape=(
            jax.ShapeDtypeStruct((length, 2 * ff), BF),
            jax.ShapeDtypeStruct((length, width), BF),
            jax.ShapeDtypeStruct((length, width), BF),
        ),
        compiler_params=pltpu.CompilerParams(vmem_limit_bytes=56 * 1024 * 1024),
        cost_estimate=pl.CostEstimate(
            flops=8 * length * width * ff, bytes_accessed=weight.size * 4, transcendentals=0
        ),
        name="feed_back",
    )(cotangent, gate, up, hidden, weight, down)


def square_parts(parts, boxes, sends, recvs, first):
    me = lax.axis_index("seq")
    across, along = me ^ 1, me ^ 2
    inbox_x, inbox_y, via_x, via_y, out_x, out_y = boxes
    half = via_x.shape[0]
    low, high = pl.ds(0, half), pl.ds(half, half)
    copies = [
        remote(parts.at[3, low], via_x, sends, recvs, first, across),
        remote(parts.at[3, high], via_y, sends, recvs, first + 1, along),
        remote(parts.at[1, low], inbox_x.at[low], sends, recvs, first + 2, across),
        remote(parts.at[2, high], inbox_y.at[high], sends, recvs, first + 3, along),
        remote(out_y, inbox_y.at[low], sends, recvs, first + 4, along),
        remote(out_x, inbox_x.at[high], sends, recvs, first + 5, across),
    ]

    def finish():
        forward_sums(copies, parts, boxes)
        for copy in copies[2:]:
            copy.wait_recv()

    def total(rows):
        return (
            parts[0, rows].astype(F32)
            + inbox_x[rows, :].astype(F32)
            + inbox_y[rows, :].astype(F32)
        )

    return copies, finish, total


def square_gather(own, out_ref, sends, recvs, first):
    me = lax.axis_index("seq")
    across, along = me ^ 1, me ^ 2
    half = own.shape[0] // 2

    def part(ref, i):
        return ref.at[pl.ds(i * half, half)]

    copies = [
        remote(part(own, 0), part(out_ref.at[me], 0), sends, recvs, first, across),
        remote(part(own, 1), part(out_ref.at[me], 1), sends, recvs, first + 1, along),
        remote(part(own, 1), part(out_ref.at[me], 1), sends, recvs, first + 2, across),
        remote(part(own, 0), part(out_ref.at[me], 0), sends, recvs, first + 3, along),
        remote(
            part(out_ref.at[across], 0), part(out_ref.at[across], 0), sends, recvs, first + 4, along
        ),
        remote(
            part(out_ref.at[along], 1), part(out_ref.at[along], 1), sends, recvs, first + 5, across
        ),
    ]

    def finish():
        copies[0].wait_recv()
        copies[4].start()
        copies[1].wait_recv()
        copies[5].start()
        for copy in copies[2:]:
            copy.wait_recv()

    return copies, finish


def block_rows(k, rows):
    return pl.ds(pl.multiple_of((lax.axis_index("seq") ^ k) * rows, rows), rows)


def forward_sums(copies, parts, boxes):
    inbox_x, inbox_y, via_x, via_y, out_x, out_y = boxes
    half = via_x.shape[0]
    copies[0].wait_recv()
    out_y[...] = (parts[2, :half].astype(F32) + via_x[...].astype(F32)).astype(BF)
    copies[4].start()
    copies[1].wait_recv()
    out_x[...] = (parts[1, half:].astype(F32) + via_y[...].astype(F32)).astype(BF)
    copies[5].start()


def send_parts(part, copies, then=None):
    @pl.loop(0, 4)
    def _(i):
        if then is not None:
            pl.when(i == 3)(then)
        part(jnp.where(i == 0, 3, jnp.where(i == 3, 0, i)))

        @pl.when(i == 0)
        def _():
            copies[0].start()
            copies[1].start()

        @pl.when(i == 1)
        def _():
            copies[2].start()

        @pl.when(i == 2)
        def _():
            copies[3].start()


def project_kernel(
    g_any, w_any, x_ref, gain_ref, middle_any, own_any,
    middle_ref, own_ref, g_ref, w_ref, parts, inbox_x, inbox_y, via_x, via_y, out_x, out_y, sends, recvs, locals_,
):
    me = lax.axis_index("seq")
    rows = x_ref.shape[0]
    half = rows // 2
    moves = Moves(locals_)
    loads = [moves.start(w_any, w_ref), moves.start(g_any, g_ref)]
    greet((me ^ 1, me ^ 2))
    boxes = (inbox_x, inbox_y, via_x, via_y, out_x, out_y)
    copies, finish, total = square_parts(parts, boxes, sends, recvs, 0)

    def part(k):
        parts[k] = product(g_ref[block_rows(k, rows), :], w_ref[...]).astype(BF)

    for load in loads:
        load.wait()
    send_parts(part, copies)
    finish()

    stores = [
        by_block(moves, 2, middle_ref, middle_any, half),
        by_block(moves, 2, own_ref, own_any, half),
    ]

    @pl.loop(0, 2)
    def _(i):
        here = pl.ds(pl.multiple_of(i * half, half), half)
        middle = x_ref[here, :].astype(F32) + total(here)
        middle_ref[here, :] = middle
        own_ref[here, :] = normalize(middle, gain_ref[...]).astype(BF)
        for store in stores:
            store.copy(i).start()

    for store in stores:
        store.wait_all()
    for copy in copies:
        copy.wait_send()


def square_scratch(rows, width):
    return [
        pltpu.VMEM((4, rows, width), BF),
        pltpu.VMEM((rows, width), BF),
        pltpu.VMEM((rows, width), BF),
        pltpu.VMEM((rows // 2, width), BF),
        pltpu.VMEM((rows // 2, width), BF),
        pltpu.VMEM((rows // 2, width), BF),
        pltpu.VMEM((rows // 2, width), BF),
    ]


def square_call(body, out_shape, out_specs, scratch, inputs, call, cost, name):
    return pl.pallas_call(
        body,
        out_shape=out_shape,
        in_specs=[IN_VMEM] * len(inputs),
        out_specs=out_specs,
        scratch_shapes=scratch,
        compiler_params=pltpu.CompilerParams(
            collective_id=call, has_side_effects=True, vmem_limit_bytes=56 * 1024 * 1024
        ),
        cost_estimate=transfer_cost(cost),
        name=name,
    )(*inputs)


def core_sum(moves, make, send_ref, twin_ref, out_ref, targets, sends, recvs, first):
    shard = lax.axis_index("fsdp")
    core = lax.rem(shard, 2)
    count = out_ref.shape[0]

    def copy(t):
        return pltpu.make_async_remote_copy(
            src_ref=send_ref.at[t],
            dst_ref=twin_ref.at[t],
            send_sem=sends.at[first + t],
            recv_sem=recvs.at[first + t],
            device_id={"fsdp": shard ^ 1},
            device_id_type=MESH,
        )

    stores = Series(moves, count, lambda t: (out_ref.at[t], targets(t)))

    @pl.loop(0, count)
    def _(t):
        send_ref[t] = make(2 * t + 1 - core).astype(BF)
        copy(t).start()

    @pl.loop(0, count)
    def _(t):
        own = make(2 * t + core)
        copy(t).wait_recv()
        out_ref[t] = (own + twin_ref[t].astype(F32)).astype(BF)
        stores.copy(t).start()

    def finish():
        stores.wait_all()
        for t in range(count):
            copy(t).wait_send()

    return finish


def greet_near(me, shard):
    barrier = pltpu.get_barrier_semaphore()
    for k in (1, 2):
        pl.semaphore_signal(barrier, inc=1, device_id={"seq": me ^ k}, device_id_type=MESH)
    pl.semaphore_signal(barrier, inc=1, device_id={"fsdp": shard ^ 1}, device_id_type=MESH)
    pl.semaphore_wait(barrier, 3)


def core_scratch(rows, width):
    return [pltpu.VMEM((rows // (2 * BLOCK), BLOCK, width), BF)] * 3


def comm_call(body, inputs, outputs, scratch, remotes, moves, call, cost, name):
    return pl.pallas_call(
        body,
        out_shape=tuple(jax.ShapeDtypeStruct(shape, kind) for shape, kind, _ in outputs),
        in_specs=[IN_VMEM if whole else ANYWHERE for _, whole in inputs],
        out_specs=tuple(IN_VMEM if whole else ANYWHERE for _, _, whole in outputs),
        scratch_shapes=scratch
        + [
            pltpu.SemaphoreType.DMA((remotes,)),
            pltpu.SemaphoreType.DMA((remotes,)),
            pltpu.SemaphoreType.DMA((moves,)),
        ],
        compiler_params=pltpu.CompilerParams(
            collective_id=call, has_side_effects=True, vmem_limit_bytes=60 * 1024 * 1024
        ),
        cost_estimate=transfer_cost(cost),
        name=name,
    )(*[value for value, _ in inputs])


def retention_exchange_kernel(
    heads, offsets, cut, mixed_any, w_any, cos_ref, sin_ref, table_ref,
    q_any, k_any, v_any, swish_any, retained_any, gated_any, wo_any,
    mixed_ref, w_ref, q_ref, k_ref, v_ref, swish_ref, retained_ref, gated_ref, both_ref, wo_ref,
    via_x, via_y, sends, recvs, locals_,
):
    me = lax.axis_index("seq")
    shard = lax.axis_index("fsdp")
    core = lax.rem(shard, 2)
    step, wide = both_ref.shape[2:]
    moves = Moves(locals_)

    def piece(column):
        rows = pl.ds(pl.multiple_of((2 * column + core) * step, step), step)
        return w_any.at[rows, slice(w_ref.shape[1], w_ref.shape[1] + wide)]

    across, along, corner = me ^ 1, me ^ 2, me ^ 3
    half = step // 2
    low, high = slice(0, half), slice(half, step)
    swaps = [
        remote(piece(corner).at[low], via_x, sends, recvs, 0, across),
        remote(piece(corner).at[high], via_y, sends, recvs, 1, along),
        remote(piece(across), both_ref.at[core, me], sends, recvs, 2, across),
        remote(piece(along), both_ref.at[core, me], sends, recvs, 3, along),
        remote(via_x, both_ref.at[core, across, low], sends, recvs, 4, along),
        remote(via_y, both_ref.at[core, along, high], sends, recvs, 5, across),
    ]
    kept_here = []

    def twin(k):
        return pltpu.make_async_remote_copy(
            src_ref=both_ref.at[core, me ^ k],
            dst_ref=both_ref.at[core, me ^ k],
            send_sem=sends.at[6 + k],
            recv_sem=recvs.at[6 + k],
            device_id={"fsdp": shard ^ 1},
            device_id_type=MESH,
        )

    def between(i):
        if isinstance(i, int):
            greet_all(me, shard)
            for copy in swaps[:4]:
                copy.start()
            kept_here.append(moves.start(piece(me), both_ref.at[core, me]))
            return

        @pl.when(i == 0)
        def _():
            swaps[0].wait_recv()
            swaps[4].start()
            swaps[1].wait_recv()
            swaps[5].start()
            kept_here[0].wait()
            twin(0).start()

        @pl.when(i == 2)
        def _():
            for k in (1, 2):
                swaps[1 + k].wait_recv()
                twin(k).start()

        @pl.when(i == 3)
        def _():
            swaps[4].wait_recv()
            swaps[5].wait_recv()
            twin(3).start()

    retention_kernel(
        heads, offsets, mixed_any, w_any, cos_ref, sin_ref, table_ref,
        q_any, k_any, v_any, swish_any, retained_any, gated_any,
        mixed_ref, w_ref, q_ref, k_ref, v_ref, swish_ref, retained_ref, gated_ref, moves, between,
    )
    for k in range(4):
        twin(k).wait_recv()
    tile, lane = 16, 128

    @pl.loop(0, heads * (wo_ref.shape[1] // lane))
    def _(n):
        h, c = n // (wo_ref.shape[1] // lane), lax.rem(n, wo_ref.shape[1] // lane)
        lanes = pl.ds(pl.multiple_of(c * lane, lane), lane)
        for k in range(4):
            for r in range(cut.skip(k) // tile, cut.width // tile):
                at = pl.multiple_of(h * cut.rows + (cut.start(k) + r * tile), tile)
                wo_ref[pl.ds(at, tile), lanes] = both_ref[
                    h, k, pl.ds(pl.multiple_of(c * tile, tile), tile), head_lanes(r, lane)
                ]

    moves.start(wo_ref, wo_any).wait()
    for copy in swaps + [twin(k) for k in range(4)]:
        copy.wait_send()


def greet_all(me, shard):
    barrier = pltpu.get_barrier_semaphore()
    for k in (1, 2, 3):
        pl.semaphore_signal(barrier, inc=1, device_id={"seq": me ^ k}, device_id_type=MESH)
    pl.semaphore_signal(barrier, inc=1, device_id={"fsdp": shard ^ 1}, device_id_type=MESH)
    pl.semaphore_wait(barrier, 4)


def retention_exchange(mixed, weight, cosine, sine, table, heads, offsets, cut, call):
    length, width = mixed.shape
    wide = cut.width * width // 256
    outputs = retention_outputs(length, heads) + (((heads * VAL_HEAD, width), BF),)
    return comm_call(
        functools.partial(retention_exchange_kernel, heads, offsets, cut),
        [(mixed, False), (weight, False), (cosine, True), (sine, True), (table, True)],
        [(shape, kind, False) for shape, kind in outputs],
        [pltpu.VMEM(mixed.shape, BF), pltpu.VMEM((width, weight.shape[1] - wide), BF)]
        + [pltpu.VMEM(*out) for out in outputs[:-1]]
        + [pltpu.VMEM((heads, 4, 256, wide), BF), pltpu.VMEM(outputs[-1][0], BF)]
        + [pltpu.VMEM((128, wide), BF)] * 2,
        10,
        6 + 7 * (length // BLOCK),
        call,
        mixed.size // 2,
        "retention_exchange",
    )


def project_and_norm(gated, weight, x, gain, call):
    rows, width = x.shape
    return comm_call(
        project_kernel,
        [(gated, False), (weight, False), (x, True), (gain[None, :], True)],
        [((rows, width), F32, False), ((rows, width), BF, False)],
        [pltpu.VMEM((rows, width), F32), pltpu.VMEM((rows, width), BF)]
        + [pltpu.VMEM(gated.shape, BF), pltpu.VMEM(weight.shape, BF)]
        + square_scratch(rows, width),
        6,
        6,
        call,
        x.size,
        "project_and_norm",
    )


def feed_forward_gather_kernel(
    ff, x_any, w_any, c_any, both_any, hidden_any, down_any, full_any,
    full, w_ref, c_ref, both_ref, hidden_ref, total, down_ref, sends, recvs, locals_,
):
    me = lax.axis_index("seq")
    rows = x_any.shape[0]
    moves = Moves(locals_)
    load_x = moves.start(x_any, full.at[me])
    load_w = moves.start(w_any, w_ref)
    load_c = moves.start(c_any, c_ref)
    greet((me ^ 1, me ^ 2))
    load_x.wait()
    copies, _ = square_gather(full.at[me], full, sends, recvs, 0)
    for copy in copies[:4]:
        copy.start()
    stores = [
        by_block(moves, 4, both_ref, both_any, rows),
        by_block(moves, 4, hidden_ref, hidden_any, rows),
        Series(moves, 4, lambda n: (full.at[n], full_any.at[n])),
    ]
    total[...] = jnp.zeros_like(total)
    load_w.wait()
    load_c.wait()

    @pl.loop(0, 4)
    def _(k):
        @pl.when(k == 1)
        def _():
            copies[0].wait_recv()
            copies[4].start()
            copies[1].wait_recv()
            copies[5].start()
            copies[2].wait_recv()

        @pl.when(k == 2)
        def _():
            copies[3].wait_recv()

        @pl.when(k == 3)
        def _():
            copies[4].wait_recv()
            copies[5].wait_recv()

        here = block_rows(k, rows)
        both = product(full[me ^ k], w_ref[...])
        gate, up = both[:, :ff], both[:, ff:]
        bell = 0.5 + 0.5 * lax.erf(gate * math.sqrt(0.5))
        passed = gate * bell
        slope = bell + gate * (math.sqrt(0.5 / math.pi) * jnp.exp(-0.5 * gate * gate))
        both_ref[here, :ff] = (up * slope).astype(BF)
        both_ref[here, ff:] = passed.astype(BF)
        hidden = (passed * up).astype(BF)
        hidden_ref[here, :] = hidden
        for store in stores:
            store.copy(me ^ k).start()
        total[...] += transposed_times(hidden, c_ref[here, :])

    piece = ff // 4
    downs = by_block(moves, 4, down_ref, down_any, piece)

    @pl.loop(0, 4)
    def _(n):
        here = pl.ds(pl.multiple_of(n * piece, piece), piece)
        down_ref[here, :] = total[here, :].astype(BF)
        downs.copy(n).start()

    for store in stores + [downs]:
        store.wait_all()
    moves.close()
    for copy in copies:
        copy.wait_send()


def feed_forward_gather(own, weight, cotangent, call):
    rows, width = own.shape
    length, ff = 4 * rows, weight.shape[1] // 2
    both, hidden, down, full = comm_call(
        functools.partial(feed_forward_gather_kernel, ff),
        [(own, False), (weight, False), (cotangent, False)],
        [
            ((length, 2 * ff), BF, False),
            ((length, ff), BF, False),
            ((ff, width), BF, False),
            ((4, rows, width), BF, False),
        ],
        [
            pltpu.VMEM((4, rows, width), BF),
            pltpu.VMEM(weight.shape, BF),
            pltpu.VMEM(cotangent.shape, BF),
            pltpu.VMEM((length, 2 * ff), BF),
            pltpu.VMEM((length, ff), BF),
            pltpu.VMEM((ff, width), F32),
            pltpu.VMEM((ff, width), BF),
        ],
        6,
        19,
        call,
        own.size,
        "feed_forward_gather",
    )
    return both, hidden, down, full.reshape(length, width)


def column_of(halves):
    total = 0.0
    for terms in halves:
        ones = jnp.ones((terms.shape[0], 128), BF)
        total = total + transposed_times(terms.astype(BF), ones)
    return total


def feed_back_scatter_kernel(
    ff, c_any, both_any, w_any, down_any, x_any, m_ref, own_c_ref, gain_ref,
    grad_any, term_ref, branch_any, dw_any,
    grad_ref, branch_ref, c_ref, both_ref, w_ref, down_ref, x_ref, low, dw_send, dw_twin, dw_ref,
    parts, inbox_x, inbox_y, via_x, via_y, out_x, out_y, sends, recvs, locals_,
):
    me = lax.axis_index("seq")
    rows = own_c_ref.shape[0]
    half = rows // 2
    moves = Moves(locals_)
    load_c = by_block(moves, 4, c_any, c_ref, rows)
    load_both = by_block(moves, 4, both_any, both_ref, rows)
    load_c.copy(me ^ 3).start()
    load_down = moves.start(down_any, down_ref)
    load_both.copy(me ^ 3).start()
    load_w = moves.start(w_any, w_ref)
    for k in (1, 2, 0):
        load_c.copy(me ^ k).start()
        load_both.copy(me ^ k).start()
    load_x = moves.start(x_any, x_ref)
    greet_near(me, lax.axis_index("fsdp"))
    boxes = (inbox_x, inbox_y, via_x, via_y, out_x, out_y)
    copies, _, total = square_parts(parts, boxes, sends, recvs, 0)

    def part(k):
        here = block_rows(k, rows)
        load_c.copy(me ^ k).wait()
        load_both.copy(me ^ k).wait()
        hidden_grad = times_transposed(c_ref[here, :], down_ref[...])
        low[here, :ff] = (hidden_grad * both_ref[here, :ff].astype(F32)).astype(BF)
        low[here, ff:] = (hidden_grad * both_ref[here, ff:].astype(F32)).astype(BF)
        pl.when(k == 3)(load_w.wait)
        parts[k] = times_transposed(low[here, :], w_ref[...]).astype(BF)

    load_down.wait()
    send_parts(part, copies, lambda: forward_sums(copies, parts, boxes))
    load_x.wait()
    finish = core_sum(
        moves, lambda b: transposed_times(x_ref[:, rows_of(b)], low[...]), dw_send, dw_twin, dw_ref,
        lambda t: dw_any.at[rows_of(t)], sends, recvs, 6,
    )
    for copy in copies[2:]:
        copy.wait_recv()

    def back_half(i):
        here = slice(i * half, (i + 1) * half)
        back, term = norm_back(m_ref[here, :], total(here), gain_ref[...])
        grad = own_c_ref[here, :].astype(F32) + back
        grad_ref[here, :] = grad
        branch_ref[here, :] = grad.astype(BF)
        moves.store(grad_ref.at[here], grad_any.at[here])
        moves.store(branch_ref.at[here], branch_any.at[here])
        return term

    term_ref[...] = column_of([back_half(i) for i in range(2)])
    finish()
    moves.close()
    for copy in copies:
        copy.wait_send()


def feed_back_scatter(cotangent, both, weight, down, x, middle, own_cotangent, gain, call):
    rows, width = own_cotangent.shape
    length, ff = cotangent.shape[0], weight.shape[1] // 2
    grad, term, branch, dw = comm_call(
        functools.partial(feed_back_scatter_kernel, ff),
        [
            (cotangent, False),
            (both, False),
            (weight, False),
            (down, False),
            (x, False),
            (middle, True),
            (own_cotangent, True),
            (gain[None, :], True),
        ],
        [
            ((rows, width), F32, False),
            ((width, 128), F32, True),
            ((rows, width), BF, False),
            ((width // 2, 2 * ff), BF, False),
        ],
        [
            pltpu.VMEM((rows, width), F32),
            pltpu.VMEM((rows, width), BF),
            pltpu.VMEM(cotangent.shape, BF),
            pltpu.VMEM(both.shape, BF),
            pltpu.VMEM(weight.shape, BF),
            pltpu.VMEM(down.shape, BF),
            pltpu.VMEM(x.shape, BF),
            pltpu.VMEM((length, 2 * ff), BF),
        ]
        + core_scratch(width, 2 * ff)
        + square_scratch(rows, width),
        6 + width // (2 * BLOCK),
        15 + width // (2 * BLOCK),
        call,
        own_cotangent.size,
        "feed_back_scatter",
    )
    return grad, term, branch, dw


def norm_back(values, grad, gain):
    centered = values - jnp.mean(values, axis=-1, keepdims=True)
    spread = lax.rsqrt(jnp.mean(centered * centered, axis=-1, keepdims=True) + EPSILON)
    unit = centered * spread
    g = grad * gain
    back = g - jnp.mean(g, axis=-1, keepdims=True)
    back = spread * (back - unit * jnp.mean(g * unit, axis=-1, keepdims=True))
    return back, grad * unit


def square_pass(own, out_ref, sends, recvs, first, half):
    me = lax.axis_index("seq")
    across, along = me ^ 1, me ^ 2
    spans = (slice(0, half), slice(half, own.shape[0]))

    def part(ref, i):
        return ref.at[spans[i]]

    return [
        remote(part(own, 0), part(out_ref.at[me], 0), sends, recvs, first, across),
        remote(part(own, 1), part(out_ref.at[me], 1), sends, recvs, first + 1, along),
        remote(part(own, 1), part(out_ref.at[me], 1), sends, recvs, first + 2, across),
        remote(part(own, 0), part(out_ref.at[me], 0), sends, recvs, first + 3, along),
        remote(
            part(out_ref.at[across], 0), part(out_ref.at[across], 0), sends, recvs, first + 4, along
        ),
        remote(
            part(out_ref.at[along], 1), part(out_ref.at[along], 1), sends, recvs, first + 5, across
        ),
    ]


def pass_on(copies):
    copies[0].wait_recv()
    copies[4].start()
    copies[1].wait_recv()
    copies[5].start()


def half_rows(rows):
    return -(-rows // 32) * 16


def put_column(ref, rows, at, column):
    first = ref.shape[1] - 128
    spare = lax.broadcasted_iota(jnp.int32, column.shape, 1) == at - first
    ref[rows, first:] = jnp.where(spare, column, ref[rows, first:].astype(F32)).astype(BF)


def gate_back_scatter_kernel(
    heads, cut, branch_any, w_any, swish_any, retained_any, column_any, hidden_any, down_any,
    mixed_any, gated_any, m_any, dswish_any, dret_any, dws_any, dwo_any, out_ref,
    branch_ref, w_ref, swish_ref, retained_ref, column_ref, hidden_ref, down_ref, mixed_ref,
    gated_ref, m_ref, dswish_ref, dret_ref, dws_send, dws_twin, dws_ref, dwo_ref,
    parts, inbox_x, inbox_y, via_x, via_y, out_x, out_y, sends, recvs, locals_,
):
    me = lax.axis_index("seq")
    rows = out_ref.shape[0]
    moves = Moves(locals_)
    load_down = moves.start(down_any, down_ref)
    load_hidden = moves.start(hidden_any, hidden_ref)
    load_gate = moves.start(w_any, w_ref)
    blocks = branch_ref.shape[0] // BLOCK
    load_rows = [
        by_block(moves, blocks, branch_any, branch_ref).start_all(),
        by_block(moves, blocks, swish_any, swish_ref).start_all(),
        by_block(moves, blocks, retained_any, retained_ref).start_all(),
    ]
    load_mixed = moves.start(mixed_any, mixed_ref)
    load_column = moves.start(column_any, column_ref)
    load_gated = moves.start(gated_any, gated_ref)
    load_m = moves.start(m_any, m_ref)
    greet_near(me, lax.axis_index("fsdp"))
    boxes = (inbox_x, inbox_y, via_x, via_y, out_x, out_y)
    copies, _, total = square_parts(parts, boxes, sends, recvs, 0)

    def part(k):
        here = block_rows(k, rows)
        parts[k] = product(hidden_ref[here, :], down_ref[...]).astype(BF)

    load_hidden.wait()
    load_down.wait()
    send_parts(part, copies)
    load_gate.wait()

    @pl.loop(0, blocks)
    def _(i):
        here = rows_of(i)
        for load in load_rows:
            load.copy(i).wait()
        gate_back_rows(
            heads, here, branch_ref[here, :], w_ref, swish_ref, retained_ref, dswish_ref, dret_ref
        )

    moves.store(dswish_ref, dswish_any)
    moves.store(dret_ref, dret_any)
    forward_sums(copies, parts, boxes)
    load_mixed.wait()
    load_column.wait()
    last = dswish_ref.shape[1] - 128
    spare = lax.broadcasted_iota(jnp.int32, (BLOCK, 128), 1) == heads * VAL_HEAD - last

    def make(b):
        here = rows_of(b)
        term = product(mixed_ref[here, :], dswish_ref[...])
        column = jnp.where(spare, column_ref[here, :], term[:, last:])
        return jnp.concatenate([term[:, :last], column], axis=1)

    finish = core_sum(
        moves, make, dws_send, dws_twin, dws_ref, lambda t: dws_any.at[rows_of(t)], sends, recvs, 6
    )
    load_gated.wait()
    step, tile, lane = 2 * BLOCK, 16, 128
    for h in range(heads):
        value_lanes = head_lanes(h, VAL_HEAD)

        @pl.loop(0, branch_ref.shape[1] // step)
        def _(b):
            lanes = pl.ds(pl.multiple_of(b * step, step), step)
            wide = transposed_times(gated_ref[:, value_lanes], branch_ref[:, lanes]).astype(BF)
            for k in range(4):
                for r in range(cut.width // tile):
                    at = cut.start(k) + r * tile
                    for c in range(step // lane):
                        to = pl.ds(pl.multiple_of((b * (step // lane) + c) * tile, tile), tile)
                        dwo_ref[h, k, to, head_lanes(r, lane)] = wide[
                            at : at + tile, head_lanes(c, lane)
                        ]

    moves.store(dwo_ref, dwo_any)
    load_m.wait()
    for copy in copies[2:]:
        copy.wait_recv()
    out_ref[...] = m_ref[...] + total(slice(0, rows))
    finish()
    moves.close()
    for copy in copies:
        copy.wait_send()


def gate_backward_scatter(
    branch, weight, swish, retained, column, hidden, down, mixed_t, gated, middle, heads, padded,
    cut, call,
):
    length, width = branch.shape
    rows = middle.shape[0]
    dwo = (heads, 4, width // 8, cut.width * 8)
    inputs = (branch, weight, swish, retained, column, hidden, down, mixed_t, gated, middle)
    outputs = [
        ((length, padded), BF, False),
        ((heads, length, VAL_HEAD), BF, False),
        ((width // 2, padded), BF, False),
        (dwo, BF, False),
        ((rows, width), F32, True),
    ]
    return comm_call(
        functools.partial(gate_back_scatter_kernel, heads, cut),
        [(value, False) for value in inputs],
        outputs,
        [pltpu.VMEM(v.shape, v.dtype) for v in inputs]
        + [pltpu.VMEM(shape, kind) for shape, kind, _ in outputs[:2]]
        + core_scratch(width, padded)
        + [pltpu.VMEM(dwo, BF)]
        + square_scratch(rows, width),
        6 + width // (2 * BLOCK),
        20 + 3 * length // BLOCK + width // (2 * BLOCK),
        call,
        middle.size,
        "gate_back_scatter",
    )


def retention_back_exchange_kernel(
    heads, q_any, k_any, v_any, dret_any, table_ref, cos_ref, sin_ref, mixed_any, send_any, share_any,
    dqk_any, dv_any, merged_any, full_any,
    q_ref, k_ref, v_ref, dret_ref, mixed_ref, send_ref, dqk_ref, dv_ref, dw_send, dw_twin, dw_ref,
    twin_ref, sum_ref, via_x, via_y, dv_heads, dq_sum, sends, recvs, locals_,
):
    me = lax.axis_index("seq")
    shard = lax.axis_index("fsdp")
    core = lax.rem(shard, 2)
    moves = Moves(locals_)
    load_send = moves.start(send_any, send_ref)
    loads = [
        moves.start(source, target)
        for source, target in (
            (q_any, q_ref), (k_any, k_ref), (v_any, v_ref), (dret_any, dret_ref)
        )
    ]
    load_mixed = moves.start(mixed_any, mixed_ref)
    greet_all(me, shard)
    load_send.wait()
    twin = pltpu.make_async_remote_copy(
        src_ref=send_ref.at[1 - core],
        dst_ref=twin_ref,
        send_sem=sends.at[12],
        recv_sem=recvs.at[12],
        device_id={"fsdp": shard ^ 1},
        device_id_type=MESH,
    )
    twin.start()
    passed = square_pass(share_any, full_any, sends, recvs, 0, half_rows(share_any.shape[0]))
    for copy in passed[:4]:
        copy.start()
    moves.store(share_any, full_any.at[me])
    step, wide = sum_ref.shape[1:]
    half = step // 2
    at = dqk_ref.shape[1]
    across, along, corner = me ^ 1, me ^ 2, me ^ 3

    def place(column, start, rows):
        here = pl.ds(pl.multiple_of(column * step + start, half), rows)
        return merged_any.at[here, slice(at, at + wide)]

    low, high = slice(0, half), slice(half, step)
    swaps = [
        remote(sum_ref.at[corner, low], via_x, sends, recvs, 6, across),
        remote(sum_ref.at[corner, high], via_y, sends, recvs, 7, along),
        remote(sum_ref.at[across], place(me, 0, step), sends, recvs, 8, across),
        remote(sum_ref.at[along], place(me, 0, step), sends, recvs, 9, along),
        remote(via_x, place(across, 0, half), sends, recvs, 10, along),
        remote(via_y, place(along, half, half), sends, recvs, 11, across),
    ]
    for load in loads:
        load.wait()
    for h in range(heads):
        retention_back_head(
            h, heads, q_ref, k_ref, v_ref, dret_ref, table_ref, cos_ref, sin_ref, dqk_ref,
            dv_heads.at[h], dq_sum,
        )
        if h == 0:
            twin.wait_recv()

            @pl.loop(0, 4)
            def _(k):
                sum_ref[k] = (send_ref[core, k].astype(F32) + twin_ref[k].astype(F32)).astype(BF)

            for copy in swaps[:4]:
                copy.start()
            moves.store(sum_ref.at[me], place(me, 0, step))
            pass_on(passed)
    pass_on(swaps)
    dv_ref[...] = pad_lanes([dv_heads[h] for h in range(heads)], dv_ref.shape[1])
    moves.store(dv_ref, dv_any)
    moves.store(dqk_ref, dqk_any)
    load_mixed.wait()
    finish = core_sum(
        moves, lambda b: product(mixed_ref[rows_of(b), :], dqk_ref[...]), dw_send, dw_twin, dw_ref,
        lambda t: merged_any.at[rows_of(t), slice(0, at)], sends, recvs, 13,
    )
    for copy in passed[2:] + swaps[2:]:
        copy.wait_recv()
    finish()
    moves.close()
    for copy in passed + swaps + [twin]:
        copy.wait_send()


def retention_backward_exchange(
    q, k, v, dret, table, cosine, sine, mixed_t, send, share, heads, padded, call
):
    width, length = mixed_t.shape
    qk = heads * KEY_HEAD
    inputs = (
        (q, False), (k, False), (v, False), (dret, False), (table, True), (cosine, True),
        (sine, True), (mixed_t, False), (send, False), (share, False),
    )
    staged = (q, k, v, dret, mixed_t, send)
    block = send.shape[1:]
    kept = width // 2
    return comm_call(
        functools.partial(retention_back_exchange_kernel, heads),
        inputs,
        [
            ((length, 2 * qk), BF, False),
            ((length, padded), BF, False),
            ((kept, 2 * qk + block[2]), BF, False),
            ((4,) + share.shape, BF, False),
        ],
        [pltpu.VMEM(value.shape, BF) for value in staged]
        + [
            pltpu.VMEM((length, 2 * qk), BF),
            pltpu.VMEM((length, padded), BF),
        ]
        + core_scratch(width, 2 * qk)
        + [
            pltpu.VMEM(block, BF),
            pltpu.VMEM(block, BF),
            pltpu.VMEM((block[1] // 2, block[2]), BF),
            pltpu.VMEM((block[1] // 2, block[2]), BF),
            pltpu.VMEM((heads, length, VAL_HEAD), BF),
            pltpu.VMEM((length, KEY_HEAD), F32),
        ],
        13 + kept // BLOCK,
        12 + kept // BLOCK,
        call,
        send.size // 4,
        "retention_back_exchange",
    )


def input_back_kernel(
    offsets, spare, dqk_any, dv_any, ds_any, w_any, x_any, grad_any, mixed_any, gain_ref, share_any,
    dx_ref, dwv_any, full_any, dqk_ref, dv_ref, ds_ref, w_ref, x_ref, grad_ref, mixed_ref, dwv_ref,
    parts, inbox_x, inbox_y, via_x, via_y, out_x, out_y, sends, recvs, locals_,
):
    at_value, at_swish = offsets
    me = lax.axis_index("seq")
    rows = x_ref.shape[0]
    half = rows // 2
    moves = Moves(locals_)
    spans = (slice(0, at_value), slice(at_value, at_swish), slice(at_swish, w_ref.shape[1]))
    grads = ((dqk_any, dqk_ref), (dv_any, dv_ref), (ds_any, ds_ref))
    loads = []
    for span, (source, target) in zip(spans, grads, strict=True):
        loads.append(moves.start(source, target))
        loads.append(moves.start(w_any.at[:, span], w_ref.at[:, span]))
    load_x = moves.start(x_any, x_ref)
    load_grad = moves.start(grad_any, grad_ref)
    load_mixed = moves.start(mixed_any, mixed_ref)
    greet((me ^ 1, me ^ 2))
    boxes = (inbox_x, inbox_y, via_x, via_y, out_x, out_y)
    copies, _, total = square_parts(parts, boxes, sends, recvs, 0)
    passed = square_pass(share_any, full_any, sends, recvs, 6, half_rows(share_any.shape[0]))
    passed[0].start()
    passed[1].start()
    moves.store(share_any, full_any.at[me])

    def part(k):
        here = block_rows(k, rows)
        whole = 0.0
        for n, (_, ref) in enumerate(grads):

            @pl.when(k == 3)
            def _():
                loads[2 * n].wait()
                loads[2 * n + 1].wait()

            whole = whole + times_transposed(ref[here, :], w_ref[:, spans[n]])
        parts[k] = whole.astype(BF)

    def pass_all():
        pass_on(passed)
        forward_sums(copies, parts, boxes)
        passed[2].start()
        passed[3].start()

    send_parts(part, copies, pass_all)
    load_mixed.wait()

    @pl.loop(0, dwv_ref.shape[0] // BLOCK)
    def _(b):
        here = rows_of(b)
        dwv_ref[here, :] = product(mixed_ref[here, :], dv_ref[...]).astype(BF)

    for copy in copies[2:]:
        copy.wait_recv()
    load_x.wait()
    load_grad.wait()
    terms = []
    for i in range(2):
        here = slice(i * half, (i + 1) * half)
        back, term = norm_back(x_ref[here, :].astype(F32), total(here), gain_ref[...])
        dx_ref[here, :] = grad_ref[here, :] + back
        terms.append(term)
    put_column(dwv_ref, slice(0, dwv_ref.shape[0]), spare, column_of(terms))
    moves.store(dwv_ref, dwv_any)
    for copy in passed[2:]:
        copy.wait_recv()
    moves.close()
    for copy in copies + passed:
        copy.wait_send()


def input_backward(dqk, dv, ds, weight, x, grad, mixed_t, gain, share, offsets, spare, call):
    rows, width = x.shape
    staged = (dqk, dv, ds, weight, x, grad, mixed_t)
    return comm_call(
        functools.partial(input_back_kernel, offsets, spare),
        [(value, False) for value in staged] + [(gain[None, :], True), (share, False)],
        [
            ((rows, width), F32, True),
            ((width, dv.shape[1]), BF, False),
            ((4,) + share.shape, BF, False),
        ],
        [pltpu.VMEM(value.shape, value.dtype) for value in staged[:3]]
        + [pltpu.VMEM((width, dqk.shape[1] + dv.shape[1] + ds.shape[1]), BF)]
        + [pltpu.VMEM(value.shape, value.dtype) for value in staged[4:]]
        + [pltpu.VMEM((width, dv.shape[1]), BF)]
        + square_scratch(rows, width),
        12,
        11,
        call,
        x.size + share.size,
        "input_backward",
    )


def join(pieces):
    return jnp.concatenate(pieces, axis=1) if len(pieces) > 1 else pieces[0]


def unpack_columns_kernel(width, in_ref, out_ref, gain_ref):
    count = in_ref.shape[0]
    out_ref[...] = join([in_ref[k][:, :width].astype(F32) for k in range(count)])
    last = in_ref.shape[2] - 128
    tile = sum(in_ref[k][:, last:].astype(F32) for k in range(count))
    gain_ref[...] = tile.T[width - last : width - last + 1, :]


def unpack_columns(gathered, width):
    count, rows, whole = gathered.shape
    block = min(rows, 128)
    out, gain = pl.pallas_call(
        functools.partial(unpack_columns_kernel, width),
        grid=(rows // block,),
        in_specs=[pl.BlockSpec((count, block, whole), lambda i: (0, i, 0))],
        out_specs=[
            pl.BlockSpec((block, count * width), lambda i: (i, 0)),
            pl.BlockSpec((1, block), lambda i: (0, i)),
        ],
        out_shape=[
            jax.ShapeDtypeStruct((rows, count * width), F32),
            jax.ShapeDtypeStruct((1, rows), F32),
        ],
        cost_estimate=pl.CostEstimate(flops=0, bytes_accessed=gathered.size * 4, transcendentals=0),
        name="unpack_columns",
    )(gathered)
    return out, gain[0]


def in_order(pieces):
    me = lax.axis_index("seq")
    low = [jnp.where(me % 2 == k, pieces[0], pieces[1]) for k in range(2)]
    high = [jnp.where(me % 2 == k, pieces[2], pieces[3]) for k in range(2)]
    order = [jnp.where(me < 2, low[k], high[k]) for k in range(2)]
    return order + [jnp.where(me < 2, high[k], low[k]) for k in range(2)]


def unpack_related_kernel(width, own_ref, across_ref, along_ref, corner_ref, out_ref, gain_ref):
    pieces = [ref[...].astype(F32) for ref in (own_ref, across_ref, along_ref, corner_ref)]
    last = own_ref.shape[1] - 128
    tile = sum(piece[:, last:] for piece in pieces)
    gain_ref[...] = tile.T[width - last : width - last + 1, :]
    out_ref[...] = join(in_order([piece[:, :width] for piece in pieces]))


def unpack_related(pieces, width):
    rows, whole = pieces[0].shape
    block = min(rows, 128)
    out, gain = pl.pallas_call(
        functools.partial(unpack_related_kernel, width),
        grid=(rows // block,),
        in_specs=[pl.BlockSpec((block, whole), lambda i: (i, 0))] * 4,
        out_specs=[
            pl.BlockSpec((block, 4 * width), lambda i: (i, 0)),
            pl.BlockSpec((1, block), lambda i: (0, i)),
        ],
        out_shape=[
            jax.ShapeDtypeStruct((rows, 4 * width), F32),
            jax.ShapeDtypeStruct((1, rows), F32),
        ],
        compiler_params=pltpu.CompilerParams(vmem_limit_bytes=40 * 1024 * 1024),
        cost_estimate=pl.CostEstimate(
            flops=0, bytes_accessed=pieces[0].size * 16, transcendentals=0
        ),
        name="unpack_related",
    )(*pieces)
    return out, gain[0]


def swap(values, step):
    return lax.ppermute(values, "seq", [(k, k ^ step) for k in range(4)])


def unpack_feed_kernel(cut, shards, in_ref, down_ref, gate_ref, up_ref, out_ref):
    count = in_ref.shape[0]

    @pl.when(pl.program_id(0) == 0)
    def _():
        for k in range(count):
            if cut.skip(k) < cut.width:
                at = cut.start(k)
                out_ref[at + cut.skip(k) : at + cut.width, :] = down_ref[
                    k, cut.skip(k) : cut.width, :
                ].astype(F32)

    for n, target in enumerate((gate_ref, up_ref)):
        pieces = []
        for f in range(shards):
            for k in range(count):
                at = (n * shards + f) * cut.width
                if cut.skip(k) < cut.width:
                    piece = in_ref[k][:, at + cut.skip(k) : at + cut.width]
                    pieces.append(piece.astype(F32))
        target[...] = join(pieces)


def unpack_feed(gathered, down, cut, shards):
    count, rows, whole = gathered.shape
    block = rows // 4 if rows % 64 == 0 else rows
    wide, width = shards * cut.rows, down.shape[2]
    return pl.pallas_call(
        functools.partial(unpack_feed_kernel, cut, shards),
        grid=(rows // block,),
        in_specs=[
            pl.BlockSpec((count, block, whole), lambda i: (0, i, 0)),
            pl.BlockSpec(down.shape, lambda i: (0, 0, 0)),
        ],
        out_specs=[
            pl.BlockSpec((block, wide), lambda i: (i, 0)),
            pl.BlockSpec((block, wide), lambda i: (i, 0)),
            pl.BlockSpec((cut.rows, width), lambda i: (0, 0)),
        ],
        out_shape=[
            jax.ShapeDtypeStruct((rows, wide), F32),
            jax.ShapeDtypeStruct((rows, wide), F32),
            jax.ShapeDtypeStruct((cut.rows, width), F32),
        ],
        compiler_params=pltpu.CompilerParams(vmem_limit_bytes=40 * 1024 * 1024),
        cost_estimate=pl.CostEstimate(flops=0, bytes_accessed=gathered.size * 4, transcendentals=0),
        name="unpack_feed",
    )(gathered, down)


def unpack_merged_kernel(
    cut, own_ref, across_ref, along_ref, corner_ref, query_ref, key_ref, out_ref, ordered
):
    tile, lane, count = 16, 128, 4
    wide = query_ref.shape[1] // count
    rows = own_ref.shape[0] // 4

    @pl.loop(0, 4)
    def _(i):
        here = pl.ds(pl.multiple_of(i * rows, rows), rows)
        refs = (own_ref, across_ref, along_ref, corner_ref)
        for k, piece in enumerate(in_order([ref[here, :] for ref in refs])):
            query_ref[here, head_lanes(k, wide)] = piece[:, :wide].astype(F32)
            key_ref[here, head_lanes(k, wide)] = piece[:, wide : 2 * wide].astype(F32)
            ordered[k, here, :] = piece[:, 2 * wide :]

    for k in range(count):
        for r in range(cut.skip(k) // tile, cut.width // tile):
            at = cut.start(k) + r * tile
            for c in range(out_ref.shape[1] // lane):
                out_ref[at : at + tile, head_lanes(c, lane)] = ordered[
                    k, c * tile : (c + 1) * tile, head_lanes(r, lane)
                ].astype(F32)


def unpack_merged(pieces, wide, cut, width):
    rows, whole = pieces[0].shape
    return pl.pallas_call(
        functools.partial(unpack_merged_kernel, cut),
        out_shape=(
            jax.ShapeDtypeStruct((rows, 4 * wide), F32),
            jax.ShapeDtypeStruct((rows, 4 * wide), F32),
            jax.ShapeDtypeStruct((cut.rows, width), F32),
        ),
        scratch_shapes=[pltpu.VMEM((4, rows, whole - 2 * wide), BF)],
        compiler_params=pltpu.CompilerParams(vmem_limit_bytes=40 * 1024 * 1024),
        cost_estimate=pl.CostEstimate(
            flops=0, bytes_accessed=pieces[0].size * 16, transcendentals=0
        ),
        name="unpack_merged",
    )(*pieces)


def after(values, *others, all_of=False):
    held = lax.optimization_barrier((values,) + others)
    return held if all_of else held[0]


class Cut:
    def __init__(self, rows, count):
        self.rows, self.count = rows, count
        self.width = -(-rows // (count * 16)) * 16

    def start(self, piece):
        if isinstance(piece, int):
            return min(piece * self.width, self.rows - self.width)
        return jnp.minimum(piece * self.width, self.rows - self.width)

    def skip(self, piece):
        if isinstance(piece, int):
            return min(piece * self.width - self.start(piece), self.width)
        return jnp.minimum(piece * self.width - self.start(piece), self.width)

    def assemble(self, pieces, axis):
        kept = []
        for k, piece in enumerate(pieces):
            if self.skip(k) < self.width:
                kept.append(lax.slice_in_dim(piece, self.skip(k), self.width, axis=axis))
        return jnp.concatenate(kept, axis=axis)


def pack_kernel(
    cut, qk, vd, padded, q_any, k_any, v_any, s_any, o_any, out_any,
    qk_ref, v_ref, s_ref, o_ref, values_ref, tiles_ref, sems,
):
    me = lax.axis_index("seq")
    moves = Moves(sems)
    total, wide = v_any.shape[1], v_ref.shape[1]
    base = jnp.minimum((me * vd) // 128 * 128, total - wide)
    window = pl.ds(pl.multiple_of(base, 128), wide)
    loads = [
        moves.start(v_any.at[:, window], v_ref),
        moves.start(s_any.at[:, window], s_ref),
        moves.start(o_any.at[pl.ds(pl.multiple_of(cut.start(me), 16), cut.width)], o_ref),
    ]
    own = pl.ds(pl.multiple_of(me * qk, 128), qk)
    loads += [
        moves.start(q_any.at[:, own], qk_ref.at[:, slice(0, qk)]),
        moves.start(k_any.at[:, own], qk_ref.at[:, slice(qk, 2 * qk)]),
    ]
    tile, lane = 16, 128
    loads[2].wait()
    for r in range(cut.width // tile):
        for c in range(o_ref.shape[1] // lane):
            tiles_ref[c * tile : (c + 1) * tile, head_lanes(r, lane)] = o_ref[
                r * tile : (r + 1) * tile, head_lanes(c, lane)
            ]
    at = 2 * qk + 2 * padded
    moves.store(tiles_ref, out_any.at[:, slice(at, at + tiles_ref.shape[1])])
    loads[0].wait()
    loads[1].wait()
    for k in range(4):
        shift = k * vd - min(k * vd // 128 * 128, total - wide)

        @pl.when(me == k)
        def _():
            for n, ref in enumerate((v_ref, s_ref)):
                values_ref[:, head_lanes(n, padded)] = pad_lanes([ref[:, shift : shift + vd]], padded)

    moves.store(values_ref, out_any.at[:, slice(2 * qk, at)])
    loads[3].wait()
    loads[4].wait()
    moves.store(qk_ref, out_any.at[:, slice(0, 2 * qk)])
    moves.close()


def pack(query, key, value, swish, output, cut, qk, vd, padded):
    rows, width = query.shape
    wide = min(padded + 128, value.shape[1])
    tiles = cut.width * width // rows
    return pl.pallas_call(
        functools.partial(pack_kernel, cut, qk, vd, padded),
        out_shape=jax.ShapeDtypeStruct((rows, 2 * qk + 2 * padded + tiles), BF),
        in_specs=[ANYWHERE] * 5,
        out_specs=ANYWHERE,
        scratch_shapes=[
            pltpu.VMEM((rows, 2 * qk), BF),
            pltpu.VMEM((rows, wide), BF),
            pltpu.VMEM((rows, wide), BF),
            pltpu.VMEM((cut.width, width), BF),
            pltpu.VMEM((rows, 2 * padded), BF),
            pltpu.VMEM((rows, tiles), BF),
            pltpu.SemaphoreType.DMA((8,)),
        ],
        compiler_params=pltpu.CompilerParams(vmem_limit_bytes=60 * 1024 * 1024),
        name="pack",
    )(query, key, value, swish, output)


def columns_of(weight, index, width, padded):
    piece = lax.dynamic_slice_in_dim(weight, index * width, width, axis=1)
    return jnp.pad(piece, ((0, 0), (0, padded - width)))


def on_device(
    layer_input,
    mixer_gain,
    query_weight,
    key_weight,
    value_weight,
    swish_weight,
    output_weight,
    channel_gain,
    gelu_weight,
    linear_weight,
    down_weight,
    output_cotangent,
):
    groups, local_length, width = layer_input.shape
    seq_count = lax.axis_size("seq")
    shards = lax.axis_size("fsdp")
    me = lax.axis_index("seq")
    per_device = HEADS // seq_count
    rows_count = groups * local_length
    square = seq_count == 4 and shards == 8 and rows_count % 32 == 0
    length = local_length * seq_count
    key_scale = KEY_HEAD ** (-0.5)
    qk = query_weight.shape[1] // seq_count
    vd = value_weight.shape[1] // seq_count
    vd_pad = -(-vd // 128) * 128
    hidden_units = gelu_weight.shape[1]
    own_rows = down_weight.shape[0]
    cut = Cut(own_rows, seq_count)
    ff = shards * cut.width

    def gather_rows(values):
        return lax.all_gather(values, "fsdp", axis=0, tiled=True)

    def scatter_rows(values):
        return lax.psum_scatter(values.astype(BF), "fsdp", scatter_dimension=0, tiled=True)

    def scatter_parity(values):
        groups = [list(range(parity, shards, 2)) for parity in range(2)]
        return lax.psum_scatter(
            values, "fsdp", scatter_dimension=0, tiled=True, axis_index_groups=groups
        )

    if square:
        attention_piece = pack(
            query_weight, key_weight, value_weight, swish_weight, output_weight, cut, qk, vd, vd_pad
        )
    else:
        output_pieces = gather_rows(
            lax.dynamic_slice_in_dim(output_weight, cut.start(me), cut.width, axis=0)
        )
        attention_piece = jnp.concatenate(
            [
                columns_of(query_weight, me, qk, qk),
                columns_of(key_weight, me, qk, qk),
                columns_of(value_weight, me, vd, vd_pad),
                columns_of(swish_weight, me, vd, vd_pad),
            ],
            axis=1,
        )
    attention_weight = gather_rows(attention_piece)
    column = lax.broadcasted_iota(jnp.int32, (hidden_units, ff), 0)
    slot = lax.broadcasted_iota(jnp.int32, (hidden_units, ff), 1)
    chosen = (slot // cut.width) * own_rows + cut.start(me) + slot % cut.width
    selector = (column == chosen).astype(BF)
    gate_piece = product(gelu_weight, selector).astype(BF)
    up_piece = product(linear_weight, selector).astype(BF)
    feed_piece = jnp.concatenate([gate_piece, up_piece], axis=1)
    down_piece = lax.dynamic_slice_in_dim(down_weight, cut.start(me), cut.width, axis=0)
    gains = lax.all_gather(jnp.stack([mixer_gain, channel_gain]), "fsdp", axis=1, tiled=True)
    mixer_scale, channel_scale = gains[0].astype(F32), gains[1].astype(F32)

    local_input = layer_input.reshape(rows_count, width)
    upstream = output_cotangent.reshape(rows_count, width)

    upstream = after(upstream, gains)

    def whole(values, call):
        gathered = gather_seq(values, call)
        return gathered.reshape(length * groups, width)

    input_full = whole(local_input, 0)
    upstream_full = whole(after(upstream, input_full), 1)
    inputs = local_input.astype(F32)

    blocks = shards // seq_count
    mixed_low, mixed_turned = norm_and_turn(input_full, mixer_scale)
    head_ids = me * per_device + jnp.arange(per_device, dtype=jnp.int32)
    table, table_back = decay_tables(head_ids, length)
    cosine, sine = rotation_tables(length, KEY_HEAD // 2)
    feed_weight = gather_rows(after(feed_piece, upstream_full))

    offsets = (qk, 2 * qk, 2 * qk + vd_pad)
    attention_weight = after(
        attention_weight, mixed_low, mixed_turned, table, table_back, cosine, feed_piece
    )
    if square:
        query_low, key_low, value_low, swish_pre, retained, gated_low, output_full = (
            retention_exchange(
                mixed_low, attention_weight, cosine, sine, table, per_device, offsets, cut, 2
            )
        )
    else:
        query_low, key_low, value_low, swish_pre, retained, gated_low = retention_forward(
            mixed_low, attention_weight, cosine, sine, table, per_device, offsets
        )
        swapped = exchange_seq(
            output_pieces.reshape(seq_count, blocks, cut.width, width), 2
        )
        output_full = jnp.concatenate(
            [
                cut.assemble([swapped[piece, block] for piece in range(seq_count)], 0)
                for block in range(blocks)
            ],
            axis=0,
        )

    kept_rows = lax.broadcasted_iota(jnp.int32, down_piece.shape, 0) >= cut.skip(me)
    down_full = gather_rows(after(jnp.where(kept_rows, down_piece, jnp.zeros_like(down_piece)), gated_low))
    if square:
        middle, channel_own = project_and_norm(
            gated_low, output_full, local_input, channel_scale, 3
        )
        both_pre, hidden_low, down_term, channel_full = feed_forward_gather(
            channel_own, feed_weight, upstream_full, 4
        )
        down_share = scatter_rows(down_term)
        middle_grad, channel_term, branch_own, feed_term = feed_back_scatter(
            after(upstream_full, down_term), both_pre, feed_weight, down_full, channel_full,
            middle, upstream, channel_scale, 6,
        )
        feed_share = scatter_parity(feed_term)
        branch_full = whole(branch_own, 7)
    else:
        middle = inputs + scatter_seq(product(gated_low, output_full).astype(BF), 3)
        channel_full = whole(normalize(middle, channel_scale).astype(BF), 4)
        gate_pre, up_pre, hidden_low = feed_forward(channel_full, feed_weight)
        down_share = scatter_rows(transposed_times(hidden_low, upstream_full).astype(BF))
        feed_low_grad, channel_part, hidden_part = feed_backward(
            upstream_full, gate_pre, up_pre, hidden_low, feed_weight, down_full
        )
        feed_share = scatter_rows(transposed_times(channel_full, feed_low_grad).astype(BF))
        middle_local, channel_terms = norm_back(
            middle, scatter_seq(channel_part, 6), channel_scale
        )
        channel_term = jnp.sum(channel_terms, axis=0)
        middle_grad = upstream.astype(F32) + middle_local
        branch_full = whole(middle_grad.astype(BF), 7)

    at_value, at_swish = 2 * qk, 2 * qk + vd_pad
    if square:
        swish_grad, retained_grad, swish_term, output_send, layer_output = gate_backward_scatter(
            after(branch_full, down_share), output_full, swish_pre, retained,
            channel_term, hidden_low, down_full, mixed_turned, gated_low, middle,
            per_device, vd_pad, cut, 5,
        )
        swish_share = scatter_parity(swish_term)
        key_grad, value_grad, merged_term, down_all = retention_backward_exchange(
            query_low, key_low, value_low, after(retained_grad, feed_share), table_back, cosine, sine,
            mixed_turned, output_send, down_share, per_device, vd_pad, 8,
        )
        merged_share = scatter_parity(merged_term)
        input_gradient, value_term, feed_all = input_backward(
            key_grad, value_grad, swish_grad, attention_weight, local_input, middle_grad,
            mixed_turned, mixer_scale, feed_share, (at_value, at_swish), vd, 9,
        )
    else:
        swish_grad, retained_grad = gate_backward(
            branch_full, output_full, swish_pre, retained, per_device, vd_pad
        )
        spare = lax.broadcasted_iota(jnp.int32, (width, vd_pad), 1) == vd
        swish_term = transposed_times(mixed_low, swish_grad)
        swish_term = jnp.where(spare, channel_term[:, None], swish_term).astype(BF)
        swish_share = scatter_rows(swish_term)
        layer_output = middle + scatter_seq(hidden_part, 5)
        key_grad, value_grad = retention_backward(
            query_low, key_low, value_low, retained_grad, table_back, cosine, sine, per_device, vd_pad
        )
        key_term = transposed_times(mixed_low, key_grad).astype(BF)
        key_share = scatter_rows(key_term)
        mixed_part = (
            times_transposed(key_grad, attention_weight[:, :at_value])
            + times_transposed(value_grad, attention_weight[:, at_value:at_swish])
            + times_transposed(swish_grad, attention_weight[:, at_swish:])
        )
        input_local, mixer_terms = norm_back(
            inputs, scatter_seq(mixed_part.astype(BF), 9), mixer_scale
        )
        mixer_term = jnp.sum(mixer_terms, axis=0)
        input_gradient = middle_grad + input_local
        output_term = transposed_times(gated_low, branch_full).astype(BF)
        output_term = output_term.reshape(blocks, own_rows, width)
        output_send = jnp.stack(
            [
                lax.slice_in_dim(output_term, cut.start(k), cut.start(k) + cut.width, axis=1)
                for k in range(seq_count)
            ]
        )
        output_swapped = exchange_seq(output_send, 8)
        output_share = scatter_rows(output_swapped.reshape(shards * cut.width, width))
        value_term = transposed_times(mixed_low, value_grad)
        value_term = jnp.where(spare, mixer_term[:, None], value_term).astype(BF)
    input_gradient = input_gradient.astype(BF).reshape(groups, local_length, width)
    value_share = scatter_rows(value_term)

    layer_output = layer_output.astype(BF).reshape(groups, local_length, width)
    if square:
        swish_all = gather_seq(swish_share, 13)
        merged_share = after(merged_share, swish_all)
        second = (swap(merged_share, 1), swap(merged_share, 2))
        gelu_gradient, linear_gradient, down_gradient = unpack_feed(
            after(feed_all, swish_all, layer_output, input_gradient), down_all, cut, shards
        )
        swish_gradient, channel_own_gradient = unpack_columns(swish_all, vd)
        second, gelu_gradient, swish_gradient = after(
            second, gelu_gradient, swish_gradient, all_of=True
        )

        def corners(pair):
            half = pair[0].shape[0] // 2
            return swap(pair[0][:half], 2), swap(pair[1][half:], 1)

        def pieces(own, pair, halves):
            return (own,) + tuple(pair) + (jnp.concatenate(halves, axis=0),)

        second_corner = corners(second)
        second_corner, value_share = after(second_corner, value_share, all_of=True)
        third = (swap(value_share, 1), swap(value_share, 2))
        query_gradient, key_gradient, output_gradient = unpack_merged(
            pieces(merged_share, second, second_corner), qk, cut, width
        )
        third, query_gradient = after(third, query_gradient, all_of=True)
        value_gradient, mixer_own_gradient = unpack_related(
            pieces(value_share, third, corners(third)), vd
        )
    else:
        down_all = gather_seq(down_share, 10)
        feed_all = gather_seq(after(feed_share, down_all), 11)
        swish_all = gather_seq(after(swish_share, feed_all), 13)
        output_all = gather_seq(after(output_share, swish_all), 12)
        key_all = gather_seq(after(key_share, output_all), 15)
        value_all = gather_seq(after(value_share, key_all), 14)
        swish_gradient, channel_own_gradient = unpack_columns(swish_all, vd)
        output_gradient = cut.assemble([output_all[k] for k in range(seq_count)], 0).astype(F32)
        gelu_gradient, linear_gradient, down_gradient = unpack_feed(
            feed_all, down_all, cut, shards
        )
        query_gradient, key_gradient = (
            jnp.concatenate(
                [key_all[k][:, at : at + qk] for k in range(seq_count)], axis=1
            ).astype(F32)
            for at in (0, qk)
        )
        value_gradient, mixer_own_gradient = unpack_columns(value_all, vd)
    return (
        layer_output,
        input_gradient,
        mixer_own_gradient,
        query_gradient,
        key_gradient,
        value_gradient,
        swish_gradient,
        output_gradient,
        channel_own_gradient,
        gelu_gradient,
        linear_gradient,
        down_gradient,
    )


def solution(mesh):
    tokens, rows, vector = P("fsdp", "seq", None), P("fsdp", None), P("fsdp")
    return jax.shard_map(
        on_device,
        mesh=mesh,
        in_specs=(
            tokens, vector, rows, rows, rows, rows, rows, vector, rows, rows, rows, tokens,
        ),
        out_specs=(
            tokens, tokens, vector, rows, rows, rows, rows, rows, vector, rows, rows, rows,
        ),
        check_vma=False,
    )
```
